32 devices in a mesh: groups: 2 (over y), samples: 8 (over z, x), section: 1, mp: 2 (over core).
Axes of the slice: x: 2, y: 2, z: 4, core: 2. Of those that a mesh axis runs over, the one named last changes fastest.
Arguments:
- stored_inputs: bfloat16 [1, 16, 128, 2048], P('section', ('groups', 'samples'), None, 'mp'), parts along dimension 1
- top_cotangent: bfloat16 [16, 128, 2048], P(('groups', 'samples'), None, 'mp'), parts along dimension 0, may hold values from -0.375 to 0.375
- layer_weights: bfloat16 [1, 2048, 2048], P('section', 'samples', 'mp'), may hold values from -0.125 to 0.125
- block_layout: int32 [1, 2, 2], P('section'), may hold values 0 or 1
- region_mask: int32 [128], replicated, may hold values from 0 to 1, as said below
- partner_samples: int32 [16], P('groups'), parts along dimension 0, may hold values from 0 to 7, as said below
- spins: int32 [16, 128], P(('groups', 'samples')), parts along dimension 0, may hold values from 0 to 1
Outputs:
- weight_grad: float32 [2, 2048, 2048], P(('groups', 'section'), 'samples', 'mp'), parts along dimension 0
- layer_cotangents: bfloat16 [1, 16, 128, 2048], P('section', ('groups', 'samples'), None, 'mp'), parts along dimension 1
- embed_grad: float32 [4, 2048], P('groups', 'mp'), parts along dimension 0
The draws below stay inside these ranges and needn't reach their ends.
There are 2 independent parts, one for each index of `groups`. The reference program is written for one: setup_inputs(seed, part) draws one part's arguments, and reference() takes and returns one part's arrays. A program takes and returns all parts, laid end to end along the dimension named above; an argument that names none is the same for every part. Nothing has to cross between parts.
Inputs may be any that keep to these rules, and one draw needn't show every extreme that they name: `region_mask`: exactly 64 of the 128 entries are 1, the others 0. The samples pair up: partner_samples[partner_samples[r]] = r and partner_samples[r] != r for every sample r. `block_layout`: a query block always sees its own block, whatever the diagonal entry holds.
All inputs are finite; a program needn't handle non-finite values.
Results may differ from the reference program's by a relative error of at most 0.03.
Values may be sent and summed in bfloat16 or wider, within the bound.
No kernel may reach another device: no remote copies, remote signals or barrier semaphores. Data moves between devices by JAX's collectives and lax.ppermute only.
A program may use at most 64 MiB of HBM per device.

```python
import jax
import jax.numpy as jnp
from jax import lax

D = 2048
HEAD = 128
BLOCK = 64
SEQ = 128
SPINS = 2
MB = 1
LAYERS = 1
SHARDS = 8
SAMPLES = 8
NB = 2
NA = 64


def draw_stored_inputs(key, part):
    first_key = jax.random.fold_in(key, 0)
    shape = (LAYERS, SAMPLES, SEQ, D)
    return jnp.clip(jax.random.normal(first_key, shape, jnp.float32), -6.0, 6.0).astype(jnp.bfloat16)


def draw_region_mask(key, part):
    order = jax.random.permutation(key, SEQ)
    return jnp.zeros((SEQ,), jnp.int32).at[order[:NA]].set(1)


def draw_partner_samples(key, part):
    shard_key, slot_key, other_key, order_key = jax.random.split(jax.random.fold_in(key, 7), 4)
    shard = jax.random.randint(shard_key, (), 0, SHARDS, dtype=jnp.int32)
    slot_first = jax.random.randint(slot_key, (), 0, MB, dtype=jnp.int32)
    slot_second = jax.random.randint(other_key, (), 0, MB, dtype=jnp.int32)
    first = (shard * MB + slot_first).astype(jnp.int32)
    second = ((shard + SHARDS - 1) % SHARDS * MB + slot_second).astype(jnp.int32)
    scores = jax.random.permutation(order_key, SAMPLES).astype(jnp.int32)
    scores = scores.at[first].set(-2).at[second].set(-1)
    order = jnp.argsort(scores, stable=True).astype(jnp.int32)
    firsts = order[0::2]
    seconds = order[1::2]
    swap_partner = jnp.zeros((SAMPLES,), jnp.int32).at[firsts].set(seconds).at[seconds].set(firsts)
    return swap_partner.astype(jnp.int32)


def touch_ends(values, key, least, top_value):
    extent = values.shape
    place = [jax.random.randint(jax.random.fold_in(key, axis), (), 0, extent[axis]) for axis in range(len(extent))]
    values = values.at[tuple(place)].set(least)
    longest = extent.index(max(extent))
    place[longest] = (place[longest] + 1) % extent[longest]
    return values.at[tuple(place)].set(top_value)


def strengthened(entries, own_key, source, target, parts, factor):
    def block_of(dim):
        return (jnp.arange(entries.shape[dim]) // (entries.shape[dim] // parts)).reshape((-1,) + (1,) * (entries.ndim - 1 - dim))

    near = jax.random.permutation(own_key, parts)[block_of(target)]
    far = (block_of(target) + parts // 2) % parts
    return jnp.where((block_of(source) == near) | (block_of(source) == far), factor * entries, entries)


def level_of(key, dims, cuts, least, high):
    factor_of = 1.0
    for position, parts in cuts:
        draws = jax.random.uniform(jax.random.fold_in(jax.random.fold_in(key, 6), position), (parts,), jnp.float32, least / len(cuts), high / len(cuts))
        factor_of = factor_of * jnp.repeat(jnp.exp(draws), dims[position] // parts).reshape((-1,) + (1,) * (len(dims) - 1 - position))
    return factor_of


def bell_draw(own_key, shape, scale, bound, pieces=(), kind=jnp.bfloat16):
    entries = jax.random.normal(own_key, shape, jnp.float32) * scale
    if len(pieces) > 0:
        entries = level_of(own_key, shape, pieces, -0.22, 0.18) * entries
    return jnp.clip(entries, min=-bound, max=bound).astype(kind)


def bell_draw_with(key, shape, width, most, cuts, heavy, kind=jnp.bfloat16):
    result = width * jax.random.normal(key, shape, jnp.float32)
    if cuts:
        result = result * level_of(key, shape, cuts, -0.22, 0.18)
    return jnp.clip(strengthened(result, jax.random.fold_in(key, 3), *heavy), -most, most).astype(kind)


def setup_inputs(seed: int = 0, part: int = 0) -> dict:
    splits = jax.random.split(jax.random.key(seed), 8)
    part_splits = jax.random.split(jax.random.fold_in(splits[7], part), 8)
    stored_inputs = draw_stored_inputs(jax.random.fold_in(jax.random.fold_in(splits[7], part), 71), part)
    top_cotangent = bell_draw_with(part_splits[1], (SAMPLES, SEQ, D), 0.0625, 0.375, ((0, 8), (2, 2)), (0, 2, 8, 2.0))
    layer_weights = bell_draw(splits[2], (LAYERS, D, D), D ** -0.5, 0.125, ((1, 8), (2, 2)))
    block_layout = touch_ends((jax.random.randint(splits[3], (LAYERS, NB, NB), 0, 2) < 1).astype(jnp.int32), jax.random.fold_in(splits[3], 1), 0, 1)
    region_mask = draw_region_mask(jax.random.fold_in(splits[7], 71), part)
    partner_samples = draw_partner_samples(jax.random.fold_in(jax.random.fold_in(splits[7], part), 71), part)
    spins = touch_ends(jax.random.randint(part_splits[6], (SAMPLES, SEQ), 0, SPINS), jax.random.fold_in(part_splits[6], 1), 0, SPINS - 1).astype(jnp.int32)
    return {"stored_inputs": stored_inputs, "top_cotangent": top_cotangent, "layer_weights": layer_weights, "block_layout": block_layout, "region_mask": region_mask, "partner_samples": partner_samples, "spins": spins}


def rounded(value):
    return lax.optimization_barrier(value.astype(jnp.bfloat16)).astype(jnp.float32)


def layer_backward(grad_out, inputs, weight, allowed, attention_scale):
    head_count = D // HEAD
    inputs_h = inputs.astype(jnp.float32).reshape(SAMPLES, SEQ, head_count, HEAD)
    grad_attn = jnp.dot(grad_out.reshape(SAMPLES * SEQ, D), weight, preferred_element_type=jnp.float32)
    grad_attn = rounded(grad_attn).reshape(SAMPLES, SEQ, head_count, HEAD)
    scores = jnp.einsum('bqhd,bkhd->bhqk', inputs_h, inputs_h) * attention_scale
    scores = jnp.where(allowed, scores, -jnp.inf)
    top_score = jnp.max(scores, axis=-1, keepdims=True)
    expo_terms = jnp.exp(scores - top_score)
    probs = expo_terms / jnp.sum(expo_terms, axis=-1, keepdims=True)
    probs_low = rounded(probs)
    attended = rounded(jnp.einsum('bhqk,bkhd->bqhd', probs_low, inputs_h))
    grad_probs = jnp.einsum('bqhd,bkhd->bhqk', grad_attn, inputs_h)
    grad_scores = rounded(probs * (grad_probs - jnp.sum(grad_probs * probs, axis=-1, keepdims=True)))
    grad_in = grad_out.astype(jnp.float32).reshape(SAMPLES, SEQ, head_count, HEAD)
    grad_in = grad_in + jnp.einsum('bhqk,bqhd->bkhd', probs_low, grad_attn)
    grad_in = grad_in + attention_scale * (jnp.einsum('bhqk,bkhd->bqhd', grad_scores, inputs_h) + jnp.einsum('bhqk,bqhd->bkhd', grad_scores, inputs_h))
    return grad_in.reshape(SAMPLES, SEQ, D).astype(jnp.bfloat16), attended.reshape(SAMPLES, SEQ, D).astype(jnp.bfloat16)


def shard_term(total, pair):
    grad_rows, attended_rows = pair
    term = jnp.dot(grad_rows.T, attended_rows, preferred_element_type=jnp.float32)
    return total + rounded(term), None


def reference(stored_inputs, top_cotangent, layer_weights, block_layout, region_mask, partner_samples, spins):
    attention_scale = 4.0 / HEAD
    pos_block = jnp.arange(SEQ) // BLOCK
    grad_now = top_cotangent
    cotangents = [None] * LAYERS
    gradients = [None] * LAYERS
    for layer in reversed(range(LAYERS)):
        allowed = (block_layout[layer][pos_block[:, None], pos_block[None, :]] > 0) | (pos_block[:, None] == pos_block[None, :])
        grad_in, attended = layer_backward(grad_now, stored_inputs[layer], layer_weights[layer], allowed, attention_scale)
        grad_rows = grad_now.reshape(SHARDS, MB * SEQ, D)
        attended_rows = attended.reshape(SHARDS, MB * SEQ, D)
        total, unused = lax.scan(shard_term, jnp.zeros((D, D), jnp.float32), (grad_rows, attended_rows))
        gradients[layer] = total
        cotangents[layer] = grad_in
        grad_now = grad_in
    partner_ids = partner_samples.astype(jnp.int32)
    first = cotangents[0]
    site = jnp.where(region_mask[None, :, None] > 0, first[partner_ids], first)
    cotangents[0] = site
    onehot = (spins[:, :, None] == jnp.arange(SPINS, dtype=jnp.int32)[None, None, :]).astype(jnp.float32)
    embed_grad = jnp.einsum('btv,btd->vd', onehot, site.astype(jnp.float32))
    return jnp.stack(gradients), jnp.stack(cotangents), embed_grad
```

```python
import jax
import jax.numpy as jnp
from jax import lax
from jax.sharding import PartitionSpec as P

HEAD = 128
BLOCK = 64
SPINS = 2


def for_sending(value):

    def short(part):
        return part.astype(jnp.bfloat16) if part.dtype == jnp.float32 else part

    return jax.tree.map(short, value)


def passed_along(block, axis, distance):
    devices = range(lax.axis_size(axis))
    route = [(i - distance, i) for i in devices if i - distance in devices]
    return lax.ppermute(block, axis, route)


def softmax_parts(inputs_h, allowed, attention_scale):
    scores = (
        jnp.einsum("qhd,khd->hqk", inputs_h, inputs_h, preferred_element_type=jnp.float32)
        * attention_scale
    )
    scores = jnp.where(allowed[None], scores, -jnp.inf)
    top_score = jnp.max(scores, axis=-1, keepdims=True)
    expo_terms = jnp.exp(scores - top_score)
    probs = expo_terms / jnp.sum(expo_terms, axis=-1, keepdims=True)
    return (probs, probs.astype(jnp.bfloat16))


def local(
    stored_inputs, top_cotangent, layer_weights, block_layout, region_mask, partner_samples, spins
):
    section_index = lax.axis_index("section")
    section_count = lax.axis_size("section")
    micro_count = stored_inputs.shape[1]
    seq_len = stored_inputs.shape[2]
    half_width = stored_inputs.shape[3]
    head_count = half_width // HEAD
    attention_scale = 4.0 / HEAD
    weights = lax.all_gather(layer_weights[0], "samples", axis=0, tiled=True)
    pos_block = jnp.arange(seq_len) // BLOCK
    block_onehot = (pos_block[:, None] == jnp.arange(block_layout.shape[1])[None, :]).astype(
        jnp.float32
    )
    linked = jnp.dot(jnp.dot(block_onehot, block_layout[0].astype(jnp.float32)), block_onehot.T)
    allowed = (linked > 0.5) | (pos_block[:, None] == pos_block[None, :])
    every_layer_input = stored_inputs[0]
    inputs_h = every_layer_input[0].reshape(seq_len, head_count, HEAD)
    probs, probs_low = softmax_parts(inputs_h, allowed, attention_scale)
    attended = jnp.einsum(
        "hqk,khd->qhd", probs_low, inputs_h, preferred_element_type=jnp.float32
    ).astype(jnp.bfloat16)
    probs_list = [probs]
    low_list = [probs_low]
    attend_list = [attended.reshape(seq_len, half_width)]
    probs_all = jnp.stack(probs_list)
    low_all = jnp.stack(low_list)
    attend_store = jnp.stack(attend_list)

    def layer_back(grad_full, grad_own, inputs, probs, probs_low):
        grad_attn = jnp.dot(grad_full, weights, preferred_element_type=jnp.float32).astype(
            jnp.bfloat16
        )
        inputs_h = inputs.reshape(seq_len, head_count, HEAD)
        grad_h = grad_attn.reshape(seq_len, head_count, HEAD)
        grad_probs = jnp.einsum(
            "qhd,khd->hqk", grad_h, inputs_h, preferred_element_type=jnp.float32
        )
        grad_scores = (
            probs * (grad_probs - jnp.sum(grad_probs * probs, axis=-1, keepdims=True))
        ).astype(jnp.bfloat16)
        through = jnp.einsum("hqk,qhd->khd", probs_low, grad_h, preferred_element_type=jnp.float32)
        through = through + attention_scale * (
            jnp.einsum("hqk,khd->qhd", grad_scores, inputs_h, preferred_element_type=jnp.float32)
            + jnp.einsum("hqk,qhd->khd", grad_scores, inputs_h, preferred_element_type=jnp.float32)
        )
        grad_in = grad_own.astype(jnp.float32) + through.reshape(seq_len, half_width)
        return grad_in.astype(jnp.bfloat16)

    def resting(grad_full, grad_own, inputs, probs, probs_low):
        return jnp.zeros((seq_len, half_width), jnp.bfloat16)

    carried_state = jnp.zeros((seq_len, half_width), jnp.bfloat16)
    out_list = []
    grad_list = []
    total_steps = micro_count + section_count - 1
    for step_number in range(total_steps):
        micro_index = step_number - (section_count - 1 - section_index)
        active = (micro_index >= 0) & (micro_index < micro_count)
        slot_index = jnp.clip(micro_index, 0, micro_count - 1)
        from_top = lax.dynamic_index_in_dim(top_cotangent, slot_index, 0, keepdims=False)
        incoming = jnp.where(section_index == section_count - 1, from_top, carried_state)
        grad_full = lax.all_gather(incoming, "mp", axis=1, tiled=True)
        inputs_now = lax.dynamic_index_in_dim(every_layer_input, slot_index, 0, keepdims=False)
        probs_now = lax.dynamic_index_in_dim(probs_all, slot_index, 0, keepdims=False)
        low_now = lax.dynamic_index_in_dim(low_all, slot_index, 0, keepdims=False)
        grad_in = lax.cond(
            active, layer_back, resting, grad_full, incoming, inputs_now, probs_now, low_now
        )
        out_list.append(grad_in)
        grad_list.append(grad_full)
        if step_number < total_steps - 1:
            carried_state = jax.tree.map(
                lambda part, own: part.astype(own.dtype),
                passed_along(for_sending(grad_in), "section", -1),
                grad_in,
            )
    offset = section_count - 1 - section_index
    out_store = lax.dynamic_slice_in_dim(jnp.stack(out_list), offset, micro_count, 0)
    grad_store = lax.dynamic_slice_in_dim(jnp.stack(grad_list), offset, micro_count, 0)
    summed_weight = lax.psum_scatter(
        jnp.einsum(
            "mtf,mta->fa", grad_store, attend_store, preferred_element_type=jnp.float32
        ).astype(jnp.bfloat16),
        "samples",
        scatter_dimension=0,
        tiled=True,
    ).astype(jnp.float32)
    region_count = seq_len // 2
    rank_in_region = jnp.cumsum(region_mask) - 1
    select = (
        (rank_in_region[None, :] == jnp.arange(region_count)[:, None]) & (region_mask[None, :] > 0)
    ).astype(jnp.bfloat16)
    tiles = jnp.einsum("at,mtd->mad", select, out_store, preferred_element_type=jnp.float32).astype(
        jnp.bfloat16
    )
    shard_index = lax.axis_index("samples")
    my_partners = lax.dynamic_slice_in_dim(
        partner_samples, shard_index * micro_count, micro_count, 0
    )
    shard_count = lax.axis_size("samples")
    dest_shard = my_partners // micro_count
    dest_slot = my_partners % micro_count
    route = (
        (dest_shard[:, None, None] == jnp.arange(shard_count)[None, :, None])
        & (dest_slot[:, None, None] == jnp.arange(micro_count)[None, None, :])
    ).astype(jnp.bfloat16)
    outgoing = jnp.einsum("mku,mad->kuad", route, tiles, preferred_element_type=jnp.float32).astype(
        jnp.bfloat16
    )
    arrived = lax.all_to_all(outgoing, "samples", split_axis=0, concat_axis=0, tiled=True)
    ones_row = jnp.ones((shard_count,), jnp.bfloat16)
    received = jnp.einsum(
        "k,kuad->uad", ones_row, arrived, preferred_element_type=jnp.float32
    ).astype(jnp.bfloat16)
    placed = jnp.einsum("at,mad->mtd", select, received, preferred_element_type=jnp.float32)
    kept = jnp.where(region_mask[None, :, None] > 0, jnp.zeros_like(out_store), out_store)
    site_cot = (kept.astype(jnp.float32) + placed).astype(jnp.bfloat16)
    cotangents = jnp.where(section_index == 0, site_cot, out_store)
    onehot = (spins[:, :, None] == jnp.arange(SPINS)[None, None, :]).astype(jnp.bfloat16)
    embed_term = jnp.einsum("mtv,mtd->vd", onehot, site_cot, preferred_element_type=jnp.float32)
    embed_term = jnp.where(section_index == 0, embed_term, jnp.zeros_like(embed_term))
    embed_grad = lax.psum(embed_term, ("samples", "section"))
    return (summed_weight[None], cotangents[None], embed_grad)


def to_owners(value):
    return lax.all_to_all(value, "samples", split_axis=0, concat_axis=0, tiled=True)


def head_sharded(
    stored_inputs, top_cotangent, layer_weights, block_layout, region_mask, partner_samples, spins
):
    shard_count = lax.axis_size("samples")
    seq_len = stored_inputs.shape[2]
    half_width = stored_inputs.shape[3]
    shard_rows = layer_weights.shape[1]
    attention_scale = 4.0 / HEAD

    def by_head(value):
        return value.reshape(value.shape[0], shard_count, HEAD).transpose(1, 0, 2)

    inputs = to_owners(by_head(stored_inputs[0, 0]))
    weights = to_owners(by_head(layer_weights[0])).reshape(shard_count * shard_rows, HEAD)
    grad_half = lax.all_gather(top_cotangent[0], "samples", axis=0)
    grad_full = lax.all_gather(grad_half, "mp", axis=2, tiled=True)
    own_grad = to_owners(by_head(top_cotangent[0]))

    pos_block = jnp.arange(seq_len) // BLOCK
    block_onehot = (pos_block[:, None] == jnp.arange(block_layout.shape[1])[None, :]).astype(
        jnp.float32
    )
    linked = jnp.dot(jnp.dot(block_onehot, block_layout[0].astype(jnp.float32)), block_onehot.T)
    allowed = (linked > 0.5) | (pos_block[:, None] == pos_block[None, :])

    scores = (
        jnp.einsum("bqd,bkd->bqk", inputs, inputs, preferred_element_type=jnp.float32)
        * attention_scale
    )
    scores = jnp.where(allowed[None], scores, -jnp.inf)
    expo_terms = jnp.exp(scores - jnp.max(scores, axis=-1, keepdims=True))
    probs = expo_terms / jnp.sum(expo_terms, axis=-1, keepdims=True)
    probs_low = probs.astype(jnp.bfloat16)
    attended = jnp.einsum(
        "bqk,bkd->bqd", probs_low, inputs, preferred_element_type=jnp.float32
    ).astype(jnp.bfloat16)

    weight_term = jnp.einsum(
        "btf,bta->fa", grad_full, attended, preferred_element_type=jnp.float32
    ).astype(jnp.bfloat16)
    arrived = to_owners(weight_term.reshape(shard_count, shard_rows, HEAD))
    weight_grad = arrived.transpose(1, 0, 2).reshape(shard_rows, half_width).astype(jnp.float32)

    grad_attn = jnp.einsum(
        "btf,fa->bta", grad_full, weights, preferred_element_type=jnp.float32
    ).astype(jnp.bfloat16)
    grad_probs = jnp.einsum("bqd,bkd->bqk", grad_attn, inputs, preferred_element_type=jnp.float32)
    grad_scores = (
        probs * (grad_probs - jnp.sum(grad_probs * probs, axis=-1, keepdims=True))
    ).astype(jnp.bfloat16)
    through = jnp.einsum("bqk,bqd->bkd", probs_low, grad_attn, preferred_element_type=jnp.float32)
    through = through + attention_scale * (
        jnp.einsum("bqk,bkd->bqd", grad_scores, inputs, preferred_element_type=jnp.float32)
        + jnp.einsum("bqk,bqd->bkd", grad_scores, inputs, preferred_element_type=jnp.float32)
    )
    grad_in = (own_grad.astype(jnp.float32) + through).astype(jnp.bfloat16)
    swapped = jnp.take(grad_in, partner_samples, axis=0)
    site = jnp.where(region_mask[None, :, None] > 0, swapped, grad_in)
    onehot = (spins[:, :, None] == jnp.arange(SPINS)[None, None, :]).astype(jnp.bfloat16)
    spin_all = lax.all_gather(onehot, "samples", axis=0, tiled=True)
    embed = jnp.einsum("btv,btd->vd", spin_all, site, preferred_element_type=jnp.float32)
    high = embed.astype(jnp.bfloat16)
    low = (embed - high.astype(jnp.float32)).astype(jnp.bfloat16)
    extra = jnp.zeros((16 - 2 * SPINS, HEAD), jnp.bfloat16)
    tail = jnp.concatenate([high, low, extra], axis=0)
    packed = jnp.concatenate(
        [site, jnp.broadcast_to(tail[None], (shard_count, 16, HEAD))], axis=1
    )
    came = to_owners(packed).transpose(1, 0, 2).reshape(seq_len + 16, half_width)
    cotangents = came[:seq_len]
    ends = came[seq_len:].astype(jnp.float32)
    embed_grad = ends[:SPINS] + ends[SPINS : 2 * SPINS]
    return (weight_grad[None], cotangents[None, None], embed_grad)


def solution(mesh):
    in_specs = (
        P("section", ("groups", "samples"), None, "mp"),
        P(("groups", "samples"), None, "mp"),
        P("section", "samples", "mp"),
        P("section", None, None),
        P(),
        P("groups"),
        P(("groups", "samples"), None),
    )
    out_specs = (
        P(("groups", "section"), "samples", "mp"),
        P("section", ("groups", "samples"), None, "mp"),
        P("groups", "mp"),
    )
    shards = mesh.shape["samples"]

    def whole(stored_inputs, top_cotangent, *rest):
        samples, _, width = top_cotangent.shape
        layer_count = stored_inputs.shape[0]
        one_each = samples == mesh.shape["groups"] * shards and layer_count == 1
        by_heads = one_each and width == mesh.shape["mp"] * shards * HEAD
        return jax.shard_map(
            head_sharded if by_heads else local,
            mesh=mesh,
            in_specs=in_specs,
            out_specs=out_specs,
            check_vma=False,
        )(stored_inputs, top_cotangent, *rest)

    return whole
```

```python
import jax
import jax.numpy as jnp
from jax import lax
from jax.sharding import PartitionSpec as P

HEAD = 128
BLOCK = 64
SPINS = 2


def for_sending(value):

    def short(part):
        return part.astype(jnp.bfloat16) if part.dtype == jnp.float32 else part

    return jax.tree.map(short, value)


def passed_along(block, axis, distance):
    devices = range(lax.axis_size(axis))
    route = [(i - distance, i) for i in devices if i - distance in devices]
    return lax.ppermute(block, axis, route)


def softmax_parts(inputs_h, allowed, attention_scale):
    scores = (
        jnp.einsum("qhd,khd->hqk", inputs_h, inputs_h, preferred_element_type=jnp.float32)
        * attention_scale
    )
    scores = jnp.where(allowed[None], scores, -jnp.inf)
    top_score = jnp.max(scores, axis=-1, keepdims=True)
    expo_terms = jnp.exp(scores - top_score)
    probs = expo_terms / jnp.sum(expo_terms, axis=-1, keepdims=True)
    return (probs, probs.astype(jnp.bfloat16))


def local(
    stored_inputs, top_cotangent, layer_weights, block_layout, region_mask, partner_samples, spins
):
    section_index = lax.axis_index("section")
    section_count = lax.axis_size("section")
    micro_count = stored_inputs.shape[1]
    seq_len = stored_inputs.shape[2]
    half_width = stored_inputs.shape[3]
    head_count = half_width // HEAD
    attention_scale = 4.0 / HEAD
    weights = lax.all_gather(layer_weights[0], "samples", axis=0, tiled=True)
    pos_block = jnp.arange(seq_len) // BLOCK
    block_onehot = (pos_block[:, None] == jnp.arange(block_layout.shape[1])[None, :]).astype(
        jnp.float32
    )
    linked = jnp.dot(jnp.dot(block_onehot, block_layout[0].astype(jnp.float32)), block_onehot.T)
    allowed = (linked > 0.5) | (pos_block[:, None] == pos_block[None, :])
    every_layer_input = stored_inputs[0]
    inputs_h = every_layer_input[0].reshape(seq_len, head_count, HEAD)
    probs, probs_low = softmax_parts(inputs_h, allowed, attention_scale)
    attended = jnp.einsum(
        "hqk,khd->qhd", probs_low, inputs_h, preferred_element_type=jnp.float32
    ).astype(jnp.bfloat16)
    probs_list = [probs]
    low_list = [probs_low]
    attend_list = [attended.reshape(seq_len, half_width)]
    probs_all = jnp.stack(probs_list)
    low_all = jnp.stack(low_list)
    attend_store = jnp.stack(attend_list)

    def layer_back(grad_full, grad_own, inputs, probs, probs_low):
        grad_attn = jnp.dot(grad_full, weights, preferred_element_type=jnp.float32).astype(
            jnp.bfloat16
        )
        inputs_h = inputs.reshape(seq_len, head_count, HEAD)
        grad_h = grad_attn.reshape(seq_len, head_count, HEAD)
        grad_probs = jnp.einsum(
            "qhd,khd->hqk", grad_h, inputs_h, preferred_element_type=jnp.float32
        )
        grad_scores = (
            probs * (grad_probs - jnp.sum(grad_probs * probs, axis=-1, keepdims=True))
        ).astype(jnp.bfloat16)
        through = jnp.einsum("hqk,qhd->khd", probs_low, grad_h, preferred_element_type=jnp.float32)
        through = through + attention_scale * (
            jnp.einsum("hqk,khd->qhd", grad_scores, inputs_h, preferred_element_type=jnp.float32)
            + jnp.einsum("hqk,qhd->khd", grad_scores, inputs_h, preferred_element_type=jnp.float32)
        )
        grad_in = grad_own.astype(jnp.float32) + through.reshape(seq_len, half_width)
        return grad_in.astype(jnp.bfloat16)

    def resting(grad_full, grad_own, inputs, probs, probs_low):
        return jnp.zeros((seq_len, half_width), jnp.bfloat16)

    carried_state = jnp.zeros((seq_len, half_width), jnp.bfloat16)
    out_list = []
    grad_list = []
    total_steps = micro_count + section_count - 1
    for step_number in range(total_steps):
        micro_index = step_number - (section_count - 1 - section_index)
        active = (micro_index >= 0) & (micro_index < micro_count)
        slot_index = jnp.clip(micro_index, 0, micro_count - 1)
        from_top = lax.dynamic_index_in_dim(top_cotangent, slot_index, 0, keepdims=False)
        incoming = jnp.where(section_index == section_count - 1, from_top, carried_state)
        grad_full = lax.all_gather(incoming, "mp", axis=1, tiled=True)
        inputs_now = lax.dynamic_index_in_dim(every_layer_input, slot_index, 0, keepdims=False)
        probs_now = lax.dynamic_index_in_dim(probs_all, slot_index, 0, keepdims=False)
        low_now = lax.dynamic_index_in_dim(low_all, slot_index, 0, keepdims=False)
        grad_in = lax.cond(
            active, layer_back, resting, grad_full, incoming, inputs_now, probs_now, low_now
        )
        out_list.append(grad_in)
        grad_list.append(grad_full)
        if step_number < total_steps - 1:
            carried_state = jax.tree.map(
                lambda part, own: part.astype(own.dtype),
                passed_along(for_sending(grad_in), "section", -1),
                grad_in,
            )
    offset = section_count - 1 - section_index
    out_store = lax.dynamic_slice_in_dim(jnp.stack(out_list), offset, micro_count, 0)
    grad_store = lax.dynamic_slice_in_dim(jnp.stack(grad_list), offset, micro_count, 0)
    summed_weight = lax.psum_scatter(
        jnp.einsum(
            "mtf,mta->fa", grad_store, attend_store, preferred_element_type=jnp.float32
        ).astype(jnp.bfloat16),
        "samples",
        scatter_dimension=0,
        tiled=True,
    ).astype(jnp.float32)
    region_count = seq_len // 2
    rank_in_region = jnp.cumsum(region_mask) - 1
    select = (
        (rank_in_region[None, :] == jnp.arange(region_count)[:, None]) & (region_mask[None, :] > 0)
    ).astype(jnp.bfloat16)
    tiles = jnp.einsum("at,mtd->mad", select, out_store, preferred_element_type=jnp.float32).astype(
        jnp.bfloat16
    )
    shard_index = lax.axis_index("samples")
    my_partners = lax.dynamic_slice_in_dim(
        partner_samples, shard_index * micro_count, micro_count, 0
    )
    shard_count = lax.axis_size("samples")
    dest_shard = my_partners // micro_count
    dest_slot = my_partners % micro_count
    route = (
        (dest_shard[:, None, None] == jnp.arange(shard_count)[None, :, None])
        & (dest_slot[:, None, None] == jnp.arange(micro_count)[None, None, :])
    ).astype(jnp.bfloat16)
    outgoing = jnp.einsum("mku,mad->kuad", route, tiles, preferred_element_type=jnp.float32).astype(
        jnp.bfloat16
    )
    arrived = lax.all_to_all(outgoing, "samples", split_axis=0, concat_axis=0, tiled=True)
    ones_row = jnp.ones((shard_count,), jnp.bfloat16)
    received = jnp.einsum(
        "k,kuad->uad", ones_row, arrived, preferred_element_type=jnp.float32
    ).astype(jnp.bfloat16)
    placed = jnp.einsum("at,mad->mtd", select, received, preferred_element_type=jnp.float32)
    kept = jnp.where(region_mask[None, :, None] > 0, jnp.zeros_like(out_store), out_store)
    site_cot = (kept.astype(jnp.float32) + placed).astype(jnp.bfloat16)
    cotangents = jnp.where(section_index == 0, site_cot, out_store)
    onehot = (spins[:, :, None] == jnp.arange(SPINS)[None, None, :]).astype(jnp.bfloat16)
    embed_term = jnp.einsum("mtv,mtd->vd", onehot, site_cot, preferred_element_type=jnp.float32)
    embed_term = jnp.where(section_index == 0, embed_term, jnp.zeros_like(embed_term))
    embed_grad = lax.psum(embed_term, ("samples", "section"))
    return (summed_weight[None], cotangents[None], embed_grad)


def to_owners(value):
    return lax.all_to_all(value, "samples", split_axis=0, concat_axis=0, tiled=True)


def ring_order(count):
    return list(range(0, count, 2)) + list(range(1, count, 2))[::-1]


def gathered_by_ring(block):
    count = lax.axis_size("samples")
    order = ring_order(count)
    ahead = [(order[i], order[(i + 1) % count]) for i in range(count)]
    back = [(target, source) for source, target in ahead]
    rows = block.shape[0] // 2
    pieces = [block]
    forward, backward = block, block
    steps = [0]
    for step in range(1, (count + 1) // 2):
        forward = lax.ppermute(forward, "samples", ahead)
        backward = lax.ppermute(backward, "samples", back)
        pieces += [forward, backward]
        steps += [-step, step]
    if count % 2 == 0:
        pieces.append(lax.ppermute(forward[:rows], "samples", ahead))
        pieces.append(lax.ppermute(backward[rows:], "samples", back))
        steps.append(count // 2)
    place = jnp.asarray([order.index(i) for i in range(count)], jnp.int32)
    here = place[lax.axis_index("samples")]
    sample_of = jnp.asarray(order, jnp.int32)[(here + jnp.asarray(steps, jnp.int32)) % count]
    return pieces, sample_of


def head_sharded(
    stored_inputs, top_cotangent, layer_weights, block_layout, region_mask, partner_samples, spins
):
    shard_count = lax.axis_size("samples")
    seq_len = stored_inputs.shape[2]
    half_width = stored_inputs.shape[3]
    shard_rows = layer_weights.shape[1]
    attention_scale = 4.0 / HEAD

    def by_head(value):
        return value.reshape(value.shape[0], shard_count, HEAD).transpose(1, 0, 2)

    half_index = lax.axis_index("mp")
    shard_index = lax.axis_index("samples")
    pieces, sample_of = gathered_by_ring(top_cotangent[0])
    inputs = to_owners(by_head(stored_inputs[0, 0]))
    weights = to_owners(by_head(layer_weights[0])).reshape(shard_count * shard_rows, HEAD)
    other = [lax.ppermute(piece, "mp", [(0, 1), (1, 0)]) for piece in pieces]
    mine = jnp.concatenate(pieces).reshape(shard_count, seq_len, half_width)
    theirs = jnp.concatenate(other).reshape(shard_count, seq_len, half_width)
    first = jnp.where(half_index == 0, mine, theirs)
    second = jnp.where(half_index == 0, theirs, mine)
    grad_full = jnp.concatenate([first, second], axis=2)
    grad_full = jnp.take(grad_full, jnp.argsort(sample_of), axis=0)
    own_start = half_index * half_width + shard_index * HEAD
    own_grad = lax.dynamic_slice_in_dim(grad_full, own_start, HEAD, 2)

    pos_block = jnp.arange(seq_len) // BLOCK
    block_onehot = (pos_block[:, None] == jnp.arange(block_layout.shape[1])[None, :]).astype(
        jnp.float32
    )
    linked = jnp.dot(jnp.dot(block_onehot, block_layout[0].astype(jnp.float32)), block_onehot.T)
    allowed = (linked > 0.5) | (pos_block[:, None] == pos_block[None, :])

    scores = (
        jnp.einsum("bqd,bkd->bqk", inputs, inputs, preferred_element_type=jnp.float32)
        * attention_scale
    )
    scores = jnp.where(allowed[None], scores, -jnp.inf)
    expo_terms = jnp.exp(scores - jnp.max(scores, axis=-1, keepdims=True))
    probs = expo_terms / jnp.sum(expo_terms, axis=-1, keepdims=True)
    probs_low = probs.astype(jnp.bfloat16)
    attended = jnp.einsum(
        "bqk,bkd->bqd", probs_low, inputs, preferred_element_type=jnp.float32
    ).astype(jnp.bfloat16)

    weight_term = jnp.einsum(
        "btf,bta->fa", grad_full, attended, preferred_element_type=jnp.float32
    ).astype(jnp.bfloat16)
    arrived = to_owners(weight_term.reshape(shard_count, shard_rows, HEAD))
    weight_grad = arrived.transpose(1, 0, 2).reshape(shard_rows, half_width).astype(jnp.float32)

    grad_attn = jnp.einsum(
        "btf,fa->bta", grad_full, weights, preferred_element_type=jnp.float32
    ).astype(jnp.bfloat16)
    grad_probs = jnp.einsum("bqd,bkd->bqk", grad_attn, inputs, preferred_element_type=jnp.float32)
    grad_scores = (
        probs * (grad_probs - jnp.sum(grad_probs * probs, axis=-1, keepdims=True))
    ).astype(jnp.bfloat16)
    through = jnp.einsum("bqk,bqd->bkd", probs_low, grad_attn, preferred_element_type=jnp.float32)
    through = through + attention_scale * (
        jnp.einsum("bqk,bkd->bqd", grad_scores, inputs, preferred_element_type=jnp.float32)
        + jnp.einsum("bqk,bqd->bkd", grad_scores, inputs, preferred_element_type=jnp.float32)
    )
    grad_in = (own_grad.astype(jnp.float32) + through).astype(jnp.bfloat16)
    swapped = jnp.take(grad_in, partner_samples, axis=0)
    site = jnp.where(region_mask[None, :, None] > 0, swapped, grad_in)
    onehot = (spins[:, :, None] == jnp.arange(SPINS)[None, None, :]).astype(jnp.bfloat16)
    spin_all = lax.all_gather(onehot, "samples", axis=0, tiled=True)
    embed = jnp.einsum("btv,btd->vd", spin_all, site, preferred_element_type=jnp.float32)
    high = embed.astype(jnp.bfloat16)
    low = (embed - high.astype(jnp.float32)).astype(jnp.bfloat16)
    extra = jnp.zeros((16 - 2 * SPINS, HEAD), jnp.bfloat16)
    tail = jnp.concatenate([high, low, extra], axis=0)
    packed = jnp.concatenate(
        [site, jnp.broadcast_to(tail[None], (shard_count, 16, HEAD))], axis=1
    )
    came = to_owners(packed).transpose(1, 0, 2).reshape(seq_len + 16, half_width)
    cotangents = came[:seq_len]
    ends = came[seq_len:].astype(jnp.float32)
    embed_grad = ends[:SPINS] + ends[SPINS : 2 * SPINS]
    return (weight_grad[None], cotangents[None, None], embed_grad)


def solution(mesh):
    in_specs = (
        P("section", ("groups", "samples"), None, "mp"),
        P(("groups", "samples"), None, "mp"),
        P("section", "samples", "mp"),
        P("section", None, None),
        P(),
        P("groups"),
        P(("groups", "samples"), None),
    )
    out_specs = (
        P(("groups", "section"), "samples", "mp"),
        P("section", ("groups", "samples"), None, "mp"),
        P("groups", "mp"),
    )
    shards = mesh.shape["samples"]

    def whole(stored_inputs, top_cotangent, *rest):
        samples, _, width = top_cotangent.shape
        layer_count = stored_inputs.shape[0]
        one_each = samples == mesh.shape["groups"] * shards and layer_count == 1
        by_heads = one_each and width == mesh.shape["mp"] * shards * HEAD
        return jax.shard_map(
            head_sharded if by_heads else local,
            mesh=mesh,
            in_specs=in_specs,
            out_specs=out_specs,
            check_vma=False,
        )(stored_inputs, top_cotangent, *rest)

    return whole
```

```python
import functools

import jax
import jax.numpy as jnp
from jax import lax
from jax.experimental import pallas as pl
from jax.experimental.pallas import tpu as pltpu
from jax.sharding import PartitionSpec as P

HEAD = 128
BLOCK = 64
SPINS = 2
TAIL = 16


def for_sending(value):

    def short(part):
        return part.astype(jnp.bfloat16) if part.dtype == jnp.float32 else part

    return jax.tree.map(short, value)


def passed_along(block, axis, distance):
    devices = range(lax.axis_size(axis))
    route = [(i - distance, i) for i in devices if i - distance in devices]
    return lax.ppermute(block, axis, route)


def softmax_parts(inputs_h, allowed, attention_scale):
    scores = (
        jnp.einsum("qhd,khd->hqk", inputs_h, inputs_h, preferred_element_type=jnp.float32)
        * attention_scale
    )
    scores = jnp.where(allowed[None], scores, -jnp.inf)
    top_score = jnp.max(scores, axis=-1, keepdims=True)
    expo_terms = jnp.exp(scores - top_score)
    probs = expo_terms / jnp.sum(expo_terms, axis=-1, keepdims=True)
    return (probs, probs.astype(jnp.bfloat16))


def local(
    stored_inputs, top_cotangent, layer_weights, block_layout, region_mask, partner_samples, spins
):
    section_index = lax.axis_index("section")
    section_count = lax.axis_size("section")
    micro_count = stored_inputs.shape[1]
    seq_len = stored_inputs.shape[2]
    half_width = stored_inputs.shape[3]
    head_count = half_width // HEAD
    attention_scale = 4.0 / HEAD
    weights = lax.all_gather(layer_weights[0], "samples", axis=0, tiled=True)
    pos_block = jnp.arange(seq_len) // BLOCK
    block_onehot = (pos_block[:, None] == jnp.arange(block_layout.shape[1])[None, :]).astype(
        jnp.float32
    )
    linked = jnp.dot(jnp.dot(block_onehot, block_layout[0].astype(jnp.float32)), block_onehot.T)
    allowed = (linked > 0.5) | (pos_block[:, None] == pos_block[None, :])
    every_layer_input = stored_inputs[0]
    inputs_h = every_layer_input[0].reshape(seq_len, head_count, HEAD)
    probs, probs_low = softmax_parts(inputs_h, allowed, attention_scale)
    attended = jnp.einsum(
        "hqk,khd->qhd", probs_low, inputs_h, preferred_element_type=jnp.float32
    ).astype(jnp.bfloat16)
    probs_list = [probs]
    low_list = [probs_low]
    attend_list = [attended.reshape(seq_len, half_width)]
    probs_all = jnp.stack(probs_list)
    low_all = jnp.stack(low_list)
    attend_store = jnp.stack(attend_list)

    def layer_back(grad_full, grad_own, inputs, probs, probs_low):
        grad_attn = jnp.dot(grad_full, weights, preferred_element_type=jnp.float32).astype(
            jnp.bfloat16
        )
        inputs_h = inputs.reshape(seq_len, head_count, HEAD)
        grad_h = grad_attn.reshape(seq_len, head_count, HEAD)
        grad_probs = jnp.einsum(
            "qhd,khd->hqk", grad_h, inputs_h, preferred_element_type=jnp.float32
        )
        grad_scores = (
            probs * (grad_probs - jnp.sum(grad_probs * probs, axis=-1, keepdims=True))
        ).astype(jnp.bfloat16)
        through = jnp.einsum("hqk,qhd->khd", probs_low, grad_h, preferred_element_type=jnp.float32)
        through = through + attention_scale * (
            jnp.einsum("hqk,khd->qhd", grad_scores, inputs_h, preferred_element_type=jnp.float32)
            + jnp.einsum("hqk,qhd->khd", grad_scores, inputs_h, preferred_element_type=jnp.float32)
        )
        grad_in = grad_own.astype(jnp.float32) + through.reshape(seq_len, half_width)
        return grad_in.astype(jnp.bfloat16)

    def resting(grad_full, grad_own, inputs, probs, probs_low):
        return jnp.zeros((seq_len, half_width), jnp.bfloat16)

    carried_state = jnp.zeros((seq_len, half_width), jnp.bfloat16)
    out_list = []
    grad_list = []
    total_steps = micro_count + section_count - 1
    for step_number in range(total_steps):
        micro_index = step_number - (section_count - 1 - section_index)
        active = (micro_index >= 0) & (micro_index < micro_count)
        slot_index = jnp.clip(micro_index, 0, micro_count - 1)
        from_top = lax.dynamic_index_in_dim(top_cotangent, slot_index, 0, keepdims=False)
        incoming = jnp.where(section_index == section_count - 1, from_top, carried_state)
        grad_full = lax.all_gather(incoming, "mp", axis=1, tiled=True)
        inputs_now = lax.dynamic_index_in_dim(every_layer_input, slot_index, 0, keepdims=False)
        probs_now = lax.dynamic_index_in_dim(probs_all, slot_index, 0, keepdims=False)
        low_now = lax.dynamic_index_in_dim(low_all, slot_index, 0, keepdims=False)
        grad_in = lax.cond(
            active, layer_back, resting, grad_full, incoming, inputs_now, probs_now, low_now
        )
        out_list.append(grad_in)
        grad_list.append(grad_full)
        if step_number < total_steps - 1:
            carried_state = jax.tree.map(
                lambda part, own: part.astype(own.dtype),
                passed_along(for_sending(grad_in), "section", -1),
                grad_in,
            )
    offset = section_count - 1 - section_index
    out_store = lax.dynamic_slice_in_dim(jnp.stack(out_list), offset, micro_count, 0)
    grad_store = lax.dynamic_slice_in_dim(jnp.stack(grad_list), offset, micro_count, 0)
    summed_weight = lax.psum_scatter(
        jnp.einsum(
            "mtf,mta->fa", grad_store, attend_store, preferred_element_type=jnp.float32
        ).astype(jnp.bfloat16),
        "samples",
        scatter_dimension=0,
        tiled=True,
    ).astype(jnp.float32)
    region_count = seq_len // 2
    rank_in_region = jnp.cumsum(region_mask) - 1
    select = (
        (rank_in_region[None, :] == jnp.arange(region_count)[:, None]) & (region_mask[None, :] > 0)
    ).astype(jnp.bfloat16)
    tiles = jnp.einsum("at,mtd->mad", select, out_store, preferred_element_type=jnp.float32).astype(
        jnp.bfloat16
    )
    shard_index = lax.axis_index("samples")
    my_partners = lax.dynamic_slice_in_dim(
        partner_samples, shard_index * micro_count, micro_count, 0
    )
    shard_count = lax.axis_size("samples")
    dest_shard = my_partners // micro_count
    dest_slot = my_partners % micro_count
    route = (
        (dest_shard[:, None, None] == jnp.arange(shard_count)[None, :, None])
        & (dest_slot[:, None, None] == jnp.arange(micro_count)[None, None, :])
    ).astype(jnp.bfloat16)
    outgoing = jnp.einsum("mku,mad->kuad", route, tiles, preferred_element_type=jnp.float32).astype(
        jnp.bfloat16
    )
    arrived = lax.all_to_all(outgoing, "samples", split_axis=0, concat_axis=0, tiled=True)
    ones_row = jnp.ones((shard_count,), jnp.bfloat16)
    received = jnp.einsum(
        "k,kuad->uad", ones_row, arrived, preferred_element_type=jnp.float32
    ).astype(jnp.bfloat16)
    placed = jnp.einsum("at,mad->mtd", select, received, preferred_element_type=jnp.float32)
    kept = jnp.where(region_mask[None, :, None] > 0, jnp.zeros_like(out_store), out_store)
    site_cot = (kept.astype(jnp.float32) + placed).astype(jnp.bfloat16)
    cotangents = jnp.where(section_index == 0, site_cot, out_store)
    onehot = (spins[:, :, None] == jnp.arange(SPINS)[None, None, :]).astype(jnp.bfloat16)
    embed_term = jnp.einsum("mtv,mtd->vd", onehot, site_cot, preferred_element_type=jnp.float32)
    embed_term = jnp.where(section_index == 0, embed_term, jnp.zeros_like(embed_term))
    embed_grad = lax.psum(embed_term, ("samples", "section"))
    return (summed_weight[None], cotangents[None], embed_grad)


def ring_sample(place, count):
    return jnp.where(place < count // 2, 2 * place, 2 * (count - place) - 1)


def ring_place(sample, count):
    return jnp.where(lax.rem(sample, 2) == 0, sample // 2, count - 1 - sample // 2)


def ring_route(count, distance):
    order = list(range(0, count, 2)) + list(range(1, count, 2))[::-1]
    return [(order[i], order[(i - distance) % count]) for i in range(count)]


def own_place(count):
    return ring_place(lax.axis_index("samples"), count)


def peer_at(place, distance, count):
    return ring_sample(lax.rem(place + distance + count, count), count)


def columns(index, size):
    return pl.ds(pl.multiple_of(index * size, size), size)


def in_vmem(count):
    return [pl.BlockSpec(memory_space=pltpu.VMEM)] * count


def in_smem(count):
    return [pl.BlockSpec(memory_space=pltpu.SMEM)] * count


def on_core(body, out_shapes, in_specs, scratch=(), flops=0, moved=0):
    return pl.pallas_call(
        body,
        out_shape=out_shapes,
        in_specs=in_specs,
        out_specs=jax.tree.map(lambda _: pl.BlockSpec(memory_space=pltpu.VMEM), out_shapes),
        scratch_shapes=list(scratch),
        compiler_params=pltpu.CompilerParams(vmem_limit_bytes=40 * 1024 * 1024),
        cost_estimate=pl.CostEstimate(flops=flops, bytes_accessed=moved, transcendentals=0),
    )


def matmul(left, right):
    return jnp.dot(left, right, preferred_element_type=jnp.float32)


def matmul_t(left, right):
    return lax.dot_general(
        left, right, (((1,), (1,)), ((), ())), preferred_element_type=jnp.float32
    )


def pack_kernel(count, x_ref, w_ref, spins_ref, *outs):
    place = own_place(count)
    seq_len = x_ref.shape[2]
    spin_rows = jnp.broadcast_to(spins_ref[...].astype(jnp.float32), (TAIL, seq_len))
    spin_rows = spin_rows.astype(jnp.bfloat16)
    for slot in range(count):
        peer = peer_at(place, -slot, count)
        outs[slot][0:seq_len, :] = x_ref[0, 0, :, columns(peer, HEAD)]
        outs[slot][seq_len:, :] = spin_rows
        outs[count + slot][...] = w_ref[0, :, columns(peer, HEAD)]


def forward_kernel(count, scale, *refs):
    xs = refs[:count]
    layout_ref, attended_ref, probs_ref = refs[count:]
    seq_len = probs_ref.shape[1]
    blocks = layout_ref.shape[1]
    rows = lax.broadcasted_iota(jnp.int32, (seq_len, seq_len), 0) // BLOCK
    cols = lax.broadcasted_iota(jnp.int32, (seq_len, seq_len), 1) // BLOCK
    seen = rows == cols
    for q in range(blocks):
        for k in range(blocks):
            if q != k:
                seen = seen | ((rows == q) & (cols == k) & (layout_ref[0, q, k] > 0))
    for slot in range(count):
        x = xs[slot][0:seq_len, :]
        scores = jnp.where(seen, matmul_t(x, x) * scale, -jnp.inf)
        terms = jnp.exp(scores - jnp.max(scores, axis=-1, keepdims=True))
        probs = terms / jnp.sum(terms, axis=-1, keepdims=True)
        probs_ref[slot] = probs
        attended_ref[slot] = matmul(probs.astype(jnp.bfloat16), x).astype(jnp.bfloat16)


def slot_rows(pieces, slot, cols):
    return jnp.concatenate([piece[:, cols] for piece in pieces[slot]], axis=0)


def by_slot(count, refs):
    pieces = {slot: (refs[slot],) for slot in range(count) if slot != count // 2}
    pieces[count // 2] = (refs[count // 2], refs[count])
    return pieces


def weight_kernel(count, *refs):
    size = count + 1
    own, sibling = by_slot(count, refs[:size]), by_slot(count, refs[size : 2 * size])
    attended_ref = refs[2 * size]
    outs, held = refs[2 * size + 1 : -1], refs[-1]
    place = own_place(count)
    half = lax.axis_index("mp")
    shard_rows = held.shape[1]
    per_half = count // 2
    pairs = []
    for first in range(0, count, 2):
        pair = jnp.concatenate([attended_ref[first], attended_ref[first + 1]], axis=0)
        pairs.append(pair.astype(jnp.float32).T.astype(jnp.bfloat16))
    for side, pieces in ((half, own), (1 - half, sibling)):
        for part in range(per_half):
            cols = slice(part * shard_rows, (part + 1) * shard_rows)
            total = None
            for index, first in enumerate(range(0, count, 2)):
                grad = jnp.concatenate(
                    [slot_rows(pieces, first, cols), slot_rows(pieces, first + 1, cols)], axis=0
                )
                term = matmul(pairs[index], grad)
                total = term if total is None else total + term
            held[side * per_half + part] = total.T.astype(jnp.bfloat16)
    for slot in range(count):
        outs[slot][...] = held[peer_at(place, -slot, count)]


def backward_kernel(count, scale, *refs):
    size = count + 1
    own, sibling = by_slot(count, refs[:size]), by_slot(count, refs[size : 2 * size])
    ws = refs[2 * size : 2 * size + count]
    xs = refs[2 * size + count : 2 * size + 2 * count]
    probs_ref, mask_ref, partner_ref = refs[2 * size + 2 * count : 2 * size + 2 * count + 3]
    outs = refs[2 * size + 2 * count + 3 : -3]
    weights, attn, grads = refs[-3:]
    place = own_place(count)
    shard = lax.axis_index("samples")
    half = lax.axis_index("mp")
    seq_len = probs_ref.shape[1]
    shard_rows = ws[0].shape[0]
    half_width = count // 2 * shard_rows
    for slot in range(count):
        start = pl.multiple_of(peer_at(place, slot, count) * shard_rows, shard_rows)
        weights[pl.ds(start, shard_rows), :] = ws[slot][...]
    near = weights[columns(half, half_width), :]
    far = weights[columns(1 - half, half_width), :]
    every = slice(None)
    for first in range(0, count, 2):
        rows = [
            jnp.concatenate(
                [slot_rows(side, first, every), slot_rows(side, first + 1, every)], axis=0
            )
            for side in (own, sibling)
        ]
        total = matmul(rows[0], near) + matmul(rows[1], far)
        attn[first * seq_len : (first + 2) * seq_len, :] = total.astype(jnp.bfloat16)
    for slot in range(count):
        x = xs[slot][0:seq_len, :]
        probs = probs_ref[slot]
        grad_attn = attn[slot * seq_len : (slot + 1) * seq_len, :]
        grad_probs = matmul_t(grad_attn, x)
        inner = jnp.sum(grad_probs * probs, axis=-1, keepdims=True)
        grad_scores = (probs * (grad_probs - inner)).astype(jnp.bfloat16).astype(jnp.float32)
        both = jnp.concatenate([grad_scores, grad_scores.T], axis=1).astype(jnp.bfloat16)
        through = matmul(probs.astype(jnp.bfloat16).astype(jnp.float32).T.astype(jnp.bfloat16), grad_attn)
        through = through + scale * matmul(both, jnp.concatenate([x, x], axis=0))
        above = slot_rows(own, slot, columns(shard, HEAD))
        total = above.astype(jnp.float32) + through
        grads[peer_at(place, slot, count)] = total.astype(jnp.bfloat16)
    region = jnp.broadcast_to(mask_ref[...].astype(jnp.float32), (HEAD, seq_len)).T > 0.5
    which = lax.broadcasted_iota(jnp.int32, (TAIL, seq_len), 0).astype(jnp.float32)
    embed = jnp.zeros((TAIL, HEAD), jnp.float32)
    for slot in range(count):
        sample = peer_at(place, slot, count)
        swapped = grads[partner_ref[sample]].astype(jnp.float32)
        site = jnp.where(region, swapped, grads[sample].astype(jnp.float32)).astype(jnp.bfloat16)
        outs[(count - slot) % count][0:seq_len, :] = site
        onehot = (xs[slot][seq_len:, :].astype(jnp.float32) == which).astype(jnp.bfloat16)
        embed = embed + matmul(onehot, site)
    high = embed.astype(jnp.bfloat16).astype(jnp.float32)
    low = embed - high
    tail = jnp.concatenate([high[: TAIL // 2], low[: TAIL // 2]], axis=0).astype(jnp.bfloat16)
    for slot in range(count):
        outs[slot][seq_len:, :] = tail


def weight_out_kernel(count, *refs):
    place = own_place(count)
    for slot in range(count):
        peer = peer_at(place, slot, count)
        refs[-1][0, :, columns(peer, HEAD)] = refs[slot][...].astype(jnp.float32)


def site_out_kernel(count, *refs):
    place = own_place(count)
    site_ref, embed_ref = refs[-2:]
    seq_len = site_ref.shape[2]
    for slot in range(count):
        cols = columns(peer_at(place, slot, count), HEAD)
        site_ref[0, 0, :, cols] = refs[slot][0:seq_len, :]
        tail = refs[slot][seq_len:, :].astype(jnp.float32)
        embed_ref[:, cols] = (tail[: TAIL // 2] + tail[TAIL // 2 :])[:SPINS]


def gathered_by_ring(block):
    count = lax.axis_size("samples")
    rows = block.shape[0] // 2
    up, down = ring_route(count, -1), ring_route(count, 1)
    slots = {0: block}
    forward, backward = block, block
    for step in range(1, count // 2):
        forward = lax.ppermute(forward, "samples", up)
        backward = lax.ppermute(backward, "samples", down)
        slots[count - step] = forward
        slots[step] = backward
    slots[count // 2] = lax.ppermute(forward[:rows], "samples", up)
    slots[count] = lax.ppermute(backward[rows:], "samples", down)
    return [slots[slot] for slot in range(count + 1)]


def exchanged(blocks):
    count = lax.axis_size("samples")
    sent = [
        lax.ppermute(block, "samples", ring_route(count, slot))
        for slot, block in enumerate(blocks)
        if slot > 0
    ]
    return [blocks[0]] + sent


def head_sharded(
    stored_inputs, top_cotangent, layer_weights, block_layout, region_mask, partner_samples, spins
):
    count = lax.axis_size("samples")
    seq_len = stored_inputs.shape[2]
    shard_rows, half_width = layer_weights.shape[1:]
    scale = 4.0 / HEAD
    bf16, f32 = jnp.bfloat16, jnp.float32
    x_shape = jax.ShapeDtypeStruct((seq_len + TAIL, HEAD), bf16)
    w_shape = jax.ShapeDtypeStruct((shard_rows, HEAD), bf16)
    per_head = (count, seq_len, HEAD)

    own = gathered_by_ring(top_cotangent[0])
    sibling = [lax.ppermute(piece, "mp", [(0, 1), (1, 0)]) for piece in own]
    packed = on_core(
        functools.partial(pack_kernel, count),
        [x_shape] * count + [w_shape] * count,
        in_vmem(3),
        moved=3 << 19,
    )(stored_inputs, layer_weights, spins)
    inputs = exchanged(packed[:count])
    weights = exchanged(packed[count:])
    attended, probs = on_core(
        functools.partial(forward_kernel, count, scale),
        [jax.ShapeDtypeStruct(per_head, bf16), jax.ShapeDtypeStruct(per_head, f32)],
        in_vmem(count) + in_smem(1),
        flops=1 << 26,
        moved=1 << 20,
    )(*inputs, block_layout)
    weight_terms = on_core(
        functools.partial(weight_kernel, count),
        [w_shape] * count,
        in_vmem(2 * count + 3),
        [pltpu.VMEM((count, shard_rows, HEAD), bf16)],
        flops=1 << 29,
        moved=5 << 20,
    )(*own, *sibling, attended)
    weight_parts = exchanged(weight_terms)
    site_terms = on_core(
        functools.partial(backward_kernel, count, scale),
        [x_shape] * count,
        in_vmem(4 * count + 4) + in_smem(1),
        [
            pltpu.VMEM((count * shard_rows, HEAD), bf16),
            pltpu.VMEM((count * seq_len, HEAD), bf16),
            pltpu.VMEM(per_head, bf16),
        ],
        flops=1 << 29,
        moved=6 << 20,
    )(*own, *sibling, *weights, *inputs, probs, region_mask.reshape(1, seq_len), partner_samples)
    site_parts = exchanged(site_terms)
    weight_grad = on_core(
        functools.partial(weight_out_kernel, count),
        jax.ShapeDtypeStruct((1, shard_rows, half_width), f32),
        in_vmem(count),
        moved=3 << 19,
    )(*weight_parts)
    cotangents, embed_grad = on_core(
        functools.partial(site_out_kernel, count),
        [
            jax.ShapeDtypeStruct((1, 1, seq_len, half_width), bf16),
            jax.ShapeDtypeStruct((SPINS, half_width), f32),
        ],
        in_vmem(count),
        moved=1 << 19,
    )(*site_parts)
    return (weight_grad, cotangents, embed_grad)


def solution(mesh):
    in_specs = (
        P("section", ("groups", "samples"), None, "mp"),
        P(("groups", "samples"), None, "mp"),
        P("section", "samples", "mp"),
        P("section", None, None),
        P(),
        P("groups"),
        P(("groups", "samples"), None),
    )
    out_specs = (
        P(("groups", "section"), "samples", "mp"),
        P("section", ("groups", "samples"), None, "mp"),
        P("groups", "mp"),
    )
    shards = mesh.shape["samples"]

    def whole(stored_inputs, top_cotangent, *rest):
        samples, _, width = top_cotangent.shape
        layer_count = stored_inputs.shape[0]
        one_each = samples == mesh.shape["groups"] * shards and layer_count == 1
        by_heads = one_each and shards % 2 == 0 and width == mesh.shape["mp"] * shards * HEAD
        return jax.shard_map(
            head_sharded if by_heads else local,
            mesh=mesh,
            in_specs=in_specs,
            out_specs=out_specs,
            check_vma=False,
        )(stored_inputs, top_cotangent, *rest)

    return whole
```

```python
import functools

import jax
import jax.numpy as jnp
from jax import lax
from jax.experimental import pallas as pl
from jax.experimental.pallas import tpu as pltpu
from jax.sharding import PartitionSpec as P

HEAD = 128
BLOCK = 64
SPINS = 2
TAIL = 16


def for_sending(value):

    def short(part):
        return part.astype(jnp.bfloat16) if part.dtype == jnp.float32 else part

    return jax.tree.map(short, value)


def passed_along(block, axis, distance):
    devices = range(lax.axis_size(axis))
    route = [(i - distance, i) for i in devices if i - distance in devices]
    return lax.ppermute(block, axis, route)


def softmax_parts(inputs_h, allowed, attention_scale):
    scores = (
        jnp.einsum("qhd,khd->hqk", inputs_h, inputs_h, preferred_element_type=jnp.float32)
        * attention_scale
    )
    scores = jnp.where(allowed[None], scores, -jnp.inf)
    top_score = jnp.max(scores, axis=-1, keepdims=True)
    expo_terms = jnp.exp(scores - top_score)
    probs = expo_terms / jnp.sum(expo_terms, axis=-1, keepdims=True)
    return (probs, probs.astype(jnp.bfloat16))


def local(
    stored_inputs, top_cotangent, layer_weights, block_layout, region_mask, partner_samples, spins
):
    section_index = lax.axis_index("section")
    section_count = lax.axis_size("section")
    micro_count = stored_inputs.shape[1]
    seq_len = stored_inputs.shape[2]
    half_width = stored_inputs.shape[3]
    head_count = half_width // HEAD
    attention_scale = 4.0 / HEAD
    weights = lax.all_gather(layer_weights[0], "samples", axis=0, tiled=True)
    pos_block = jnp.arange(seq_len) // BLOCK
    block_onehot = (pos_block[:, None] == jnp.arange(block_layout.shape[1])[None, :]).astype(
        jnp.float32
    )
    linked = jnp.dot(jnp.dot(block_onehot, block_layout[0].astype(jnp.float32)), block_onehot.T)
    allowed = (linked > 0.5) | (pos_block[:, None] == pos_block[None, :])
    every_layer_input = stored_inputs[0]
    inputs_h = every_layer_input[0].reshape(seq_len, head_count, HEAD)
    probs, probs_low = softmax_parts(inputs_h, allowed, attention_scale)
    attended = jnp.einsum(
        "hqk,khd->qhd", probs_low, inputs_h, preferred_element_type=jnp.float32
    ).astype(jnp.bfloat16)
    probs_list = [probs]
    low_list = [probs_low]
    attend_list = [attended.reshape(seq_len, half_width)]
    probs_all = jnp.stack(probs_list)
    low_all = jnp.stack(low_list)
    attend_store = jnp.stack(attend_list)

    def layer_back(grad_full, grad_own, inputs, probs, probs_low):
        grad_attn = jnp.dot(grad_full, weights, preferred_element_type=jnp.float32).astype(
            jnp.bfloat16
        )
        inputs_h = inputs.reshape(seq_len, head_count, HEAD)
        grad_h = grad_attn.reshape(seq_len, head_count, HEAD)
        grad_probs = jnp.einsum(
            "qhd,khd->hqk", grad_h, inputs_h, preferred_element_type=jnp.float32
        )
        grad_scores = (
            probs * (grad_probs - jnp.sum(grad_probs * probs, axis=-1, keepdims=True))
        ).astype(jnp.bfloat16)
        through = jnp.einsum("hqk,qhd->khd", probs_low, grad_h, preferred_element_type=jnp.float32)
        through = through + attention_scale * (
            jnp.einsum("hqk,khd->qhd", grad_scores, inputs_h, preferred_element_type=jnp.float32)
            + jnp.einsum("hqk,qhd->khd", grad_scores, inputs_h, preferred_element_type=jnp.float32)
        )
        grad_in = grad_own.astype(jnp.float32) + through.reshape(seq_len, half_width)
        return grad_in.astype(jnp.bfloat16)

    def resting(grad_full, grad_own, inputs, probs, probs_low):
        return jnp.zeros((seq_len, half_width), jnp.bfloat16)

    carried_state = jnp.zeros((seq_len, half_width), jnp.bfloat16)
    out_list = []
    grad_list = []
    total_steps = micro_count + section_count - 1
    for step_number in range(total_steps):
        micro_index = step_number - (section_count - 1 - section_index)
        active = (micro_index >= 0) & (micro_index < micro_count)
        slot_index = jnp.clip(micro_index, 0, micro_count - 1)
        from_top = lax.dynamic_index_in_dim(top_cotangent, slot_index, 0, keepdims=False)
        incoming = jnp.where(section_index == section_count - 1, from_top, carried_state)
        grad_full = lax.all_gather(incoming, "mp", axis=1, tiled=True)
        inputs_now = lax.dynamic_index_in_dim(every_layer_input, slot_index, 0, keepdims=False)
        probs_now = lax.dynamic_index_in_dim(probs_all, slot_index, 0, keepdims=False)
        low_now = lax.dynamic_index_in_dim(low_all, slot_index, 0, keepdims=False)
        grad_in = lax.cond(
            active, layer_back, resting, grad_full, incoming, inputs_now, probs_now, low_now
        )
        out_list.append(grad_in)
        grad_list.append(grad_full)
        if step_number < total_steps - 1:
            carried_state = jax.tree.map(
                lambda part, own: part.astype(own.dtype),
                passed_along(for_sending(grad_in), "section", -1),
                grad_in,
            )
    offset = section_count - 1 - section_index
    out_store = lax.dynamic_slice_in_dim(jnp.stack(out_list), offset, micro_count, 0)
    grad_store = lax.dynamic_slice_in_dim(jnp.stack(grad_list), offset, micro_count, 0)
    summed_weight = lax.psum_scatter(
        jnp.einsum(
            "mtf,mta->fa", grad_store, attend_store, preferred_element_type=jnp.float32
        ).astype(jnp.bfloat16),
        "samples",
        scatter_dimension=0,
        tiled=True,
    ).astype(jnp.float32)
    region_count = seq_len // 2
    rank_in_region = jnp.cumsum(region_mask) - 1
    select = (
        (rank_in_region[None, :] == jnp.arange(region_count)[:, None]) & (region_mask[None, :] > 0)
    ).astype(jnp.bfloat16)
    tiles = jnp.einsum("at,mtd->mad", select, out_store, preferred_element_type=jnp.float32).astype(
        jnp.bfloat16
    )
    shard_index = lax.axis_index("samples")
    my_partners = lax.dynamic_slice_in_dim(
        partner_samples, shard_index * micro_count, micro_count, 0
    )
    shard_count = lax.axis_size("samples")
    dest_shard = my_partners // micro_count
    dest_slot = my_partners % micro_count
    route = (
        (dest_shard[:, None, None] == jnp.arange(shard_count)[None, :, None])
        & (dest_slot[:, None, None] == jnp.arange(micro_count)[None, None, :])
    ).astype(jnp.bfloat16)
    outgoing = jnp.einsum("mku,mad->kuad", route, tiles, preferred_element_type=jnp.float32).astype(
        jnp.bfloat16
    )
    arrived = lax.all_to_all(outgoing, "samples", split_axis=0, concat_axis=0, tiled=True)
    ones_row = jnp.ones((shard_count,), jnp.bfloat16)
    received = jnp.einsum(
        "k,kuad->uad", ones_row, arrived, preferred_element_type=jnp.float32
    ).astype(jnp.bfloat16)
    placed = jnp.einsum("at,mad->mtd", select, received, preferred_element_type=jnp.float32)
    kept = jnp.where(region_mask[None, :, None] > 0, jnp.zeros_like(out_store), out_store)
    site_cot = (kept.astype(jnp.float32) + placed).astype(jnp.bfloat16)
    cotangents = jnp.where(section_index == 0, site_cot, out_store)
    onehot = (spins[:, :, None] == jnp.arange(SPINS)[None, None, :]).astype(jnp.bfloat16)
    embed_term = jnp.einsum("mtv,mtd->vd", onehot, site_cot, preferred_element_type=jnp.float32)
    embed_term = jnp.where(section_index == 0, embed_term, jnp.zeros_like(embed_term))
    embed_grad = lax.psum(embed_term, ("samples", "section"))
    return (summed_weight[None], cotangents[None], embed_grad)


def ring_sample(place, count):
    return jnp.where(place < count // 2, 2 * place, 2 * (count - place) - 1)


def ring_place(sample, count):
    return jnp.where(lax.rem(sample, 2) == 0, sample // 2, count - 1 - sample // 2)


def ring_route(count, distance):
    order = list(range(0, count, 2)) + list(range(1, count, 2))[::-1]
    return [(order[i], order[(i - distance) % count]) for i in range(count)]


def own_place(count):
    return ring_place(lax.axis_index("samples"), count)


def peer_at(place, distance, count):
    return ring_sample(lax.rem(place + distance + count, count), count)


def columns(index, size):
    return pl.ds(pl.multiple_of(index * size, size), size)


def in_vmem(count):
    return [pl.BlockSpec(memory_space=pltpu.VMEM)] * count


def in_smem(count):
    return [pl.BlockSpec(memory_space=pltpu.SMEM)] * count


def on_core(body, out_shapes, in_specs, scratch=(), flops=0, moved=0):
    return pl.pallas_call(
        body,
        out_shape=out_shapes,
        in_specs=in_specs,
        out_specs=jax.tree.map(lambda _: pl.BlockSpec(memory_space=pltpu.VMEM), out_shapes),
        scratch_shapes=list(scratch),
        compiler_params=pltpu.CompilerParams(vmem_limit_bytes=40 * 1024 * 1024),
        cost_estimate=pl.CostEstimate(flops=flops, bytes_accessed=moved, transcendentals=0),
    )


def matmul(left, right):
    return jnp.dot(left, right, preferred_element_type=jnp.float32)


def matmul_t(left, right):
    return lax.dot_general(
        left, right, (((1,), (1,)), ((), ())), preferred_element_type=jnp.float32
    )


def pack_kernel(count, x_ref, w_ref, spins_ref, out_ref):
    seq_len = x_ref.shape[2]
    spin_rows = jnp.broadcast_to(spins_ref[...].astype(jnp.float32), (TAIL, seq_len))
    spin_rows = spin_rows.astype(jnp.bfloat16)
    for peer in range(count):
        cols = slice(peer * HEAD, (peer + 1) * HEAD)
        out_ref[peer, 0:seq_len, :] = x_ref[0, 0, :, cols]
        out_ref[peer, seq_len : seq_len + TAIL, :] = spin_rows
        out_ref[peer, seq_len + TAIL :, :] = w_ref[0, :, cols]


def forward_kernel(count, scale, *refs):
    heads_ref, layout_ref, attended_ref, probs_ref = refs
    seq_len = probs_ref.shape[1]
    blocks = layout_ref.shape[1]
    rows = lax.broadcasted_iota(jnp.int32, (seq_len, seq_len), 0) // BLOCK
    cols = lax.broadcasted_iota(jnp.int32, (seq_len, seq_len), 1) // BLOCK
    seen = rows == cols
    for q in range(blocks):
        for k in range(blocks):
            if q != k:
                seen = seen | ((rows == q) & (cols == k) & (layout_ref[0, q, k] > 0))
    for slot in range(count):
        x = heads_ref[slot, 0:seq_len, :]
        scores = jnp.where(seen, matmul_t(x, x) * scale, -jnp.inf)
        terms = jnp.exp(scores - jnp.max(scores, axis=-1, keepdims=True))
        probs = terms / jnp.sum(terms, axis=-1, keepdims=True)
        probs_ref[slot] = probs
        attended_ref[slot] = matmul(probs.astype(jnp.bfloat16), x).astype(jnp.bfloat16)


def slot_rows(pieces, slot, cols):
    return jnp.concatenate([piece[:, cols] for piece in pieces[slot]], axis=0)


def by_slot(count, refs):
    pieces = {slot: (refs[slot],) for slot in range(count) if slot != count // 2}
    pieces[count // 2] = (refs[count // 2], refs[count])
    return pieces


def weight_kernel(count, *refs):
    size = count + 1
    own, sibling = by_slot(count, refs[:size]), by_slot(count, refs[size : 2 * size])
    attended_ref = refs[2 * size]
    held = refs[-1]
    place = own_place(count)
    half = lax.axis_index("mp")
    shard_rows = held.shape[1]
    per_half = count // 2
    pairs = []
    for first in range(0, count, 2):
        pair = [attended_ref[peer_at(place, first + i, count)] for i in range(2)]
        pair = jnp.concatenate(pair, axis=0)
        pairs.append(pair.astype(jnp.float32).T.astype(jnp.bfloat16))
    for side, pieces in ((half, own), (1 - half, sibling)):
        for part in range(per_half):
            cols = slice(part * shard_rows, (part + 1) * shard_rows)
            total = None
            for index, first in enumerate(range(0, count, 2)):
                grad = jnp.concatenate(
                    [slot_rows(pieces, first, cols), slot_rows(pieces, first + 1, cols)], axis=0
                )
                term = matmul(pairs[index], grad)
                total = term if total is None else total + term
            held[side * per_half + part] = total.T.astype(jnp.bfloat16)


def backward_kernel(count, scale, *refs):
    size = count + 1
    own, sibling = by_slot(count, refs[:size]), by_slot(count, refs[size : 2 * size])
    heads_ref, probs_ref, mask_ref, partner_ref, out_ref = refs[2 * size : -3]
    weights, attn, grads = refs[-3:]
    place = own_place(count)
    shard = lax.axis_index("samples")
    half = lax.axis_index("mp")
    seq_len = probs_ref.shape[1]
    skipped = seq_len + TAIL
    shard_rows = heads_ref.shape[1] - skipped
    half_width = count // 2 * shard_rows
    for sample in range(count):
        weights[sample * shard_rows : (sample + 1) * shard_rows, :] = heads_ref[sample, skipped:, :]
    near = weights[columns(half, half_width), :]
    far = weights[columns(1 - half, half_width), :]
    every = slice(None)
    for first in range(0, count, 2):
        rows = [
            jnp.concatenate(
                [slot_rows(side, first, every), slot_rows(side, first + 1, every)], axis=0
            )
            for side in (own, sibling)
        ]
        total = matmul(rows[0], near) + matmul(rows[1], far)
        attn[first * seq_len : (first + 2) * seq_len, :] = total.astype(jnp.bfloat16)
    for slot in range(count):
        sample = peer_at(place, slot, count)
        x = heads_ref[sample, 0:seq_len, :]
        probs = probs_ref[sample]
        grad_attn = attn[slot * seq_len : (slot + 1) * seq_len, :]
        grad_probs = matmul_t(grad_attn, x)
        inner = jnp.sum(grad_probs * probs, axis=-1, keepdims=True)
        grad_scores = (probs * (grad_probs - inner)).astype(jnp.bfloat16).astype(jnp.float32)
        both = jnp.concatenate([grad_scores, grad_scores.T], axis=1).astype(jnp.bfloat16)
        through = matmul(probs.astype(jnp.bfloat16).astype(jnp.float32).T.astype(jnp.bfloat16), grad_attn)
        through = through + scale * matmul(both, jnp.concatenate([x, x], axis=0))
        above = slot_rows(own, slot, columns(shard, HEAD))
        total = above.astype(jnp.float32) + through
        grads[sample] = total.astype(jnp.bfloat16)
    region = jnp.broadcast_to(mask_ref[...].astype(jnp.float32), (HEAD, seq_len)).T > 0.5
    which = lax.broadcasted_iota(jnp.int32, (TAIL, seq_len), 0).astype(jnp.float32)
    embed = jnp.zeros((TAIL, HEAD), jnp.float32)
    for sample in range(count):
        swapped = grads[partner_ref[sample]].astype(jnp.float32)
        site = jnp.where(region, swapped, grads[sample].astype(jnp.float32)).astype(jnp.bfloat16)
        out_ref[sample, 0:seq_len, :] = site
        spin = heads_ref[sample, seq_len:skipped, :].astype(jnp.float32)
        embed = embed + matmul((spin == which).astype(jnp.bfloat16), site)
    high = embed.astype(jnp.bfloat16).astype(jnp.float32)
    low = embed - high
    tail = jnp.concatenate([high[: TAIL // 2], low[: TAIL // 2]], axis=0).astype(jnp.bfloat16)
    for sample in range(count):
        out_ref[sample, seq_len:, :] = tail


def weight_out_kernel(count, parts_ref, out_ref):
    for peer in range(count):
        cols = slice(peer * HEAD, (peer + 1) * HEAD)
        out_ref[0, :, cols] = parts_ref[peer].astype(jnp.float32)


def site_out_kernel(count, parts_ref, site_ref, embed_ref):
    seq_len = site_ref.shape[2]
    for peer in range(count):
        cols = slice(peer * HEAD, (peer + 1) * HEAD)
        site_ref[0, 0, :, cols] = parts_ref[peer, 0:seq_len, :]
        tail = parts_ref[peer, seq_len:, :].astype(jnp.float32)
        embed_ref[:, cols] = (tail[: TAIL // 2] + tail[TAIL // 2 :])[:SPINS]


def exchanged(blocks):
    return lax.all_to_all(blocks, "samples", split_axis=0, concat_axis=0, tiled=True)


def head_sharded(
    stored_inputs, top_cotangent, layer_weights, block_layout, region_mask, partner_samples, spins
):
    count = lax.axis_size("samples")
    seq_len = stored_inputs.shape[2]
    shard_rows, half_width = layer_weights.shape[1:]
    scale = 4.0 / HEAD
    bf16, f32 = jnp.bfloat16, jnp.float32
    per_head = (count, seq_len, HEAD)
    term_shape = (count, shard_rows, HEAD)
    lines = seq_len + TAIL

    up, down = ring_route(count, -1), ring_route(count, 1)
    block = top_cotangent[0]
    rows = seq_len // 2
    packed = on_core(
        functools.partial(pack_kernel, count),
        jax.ShapeDtypeStruct((count, lines + shard_rows, HEAD), bf16),
        in_vmem(3),
        moved=3 << 19,
    )(stored_inputs, layer_weights, spins)
    heads = exchanged(packed)
    slots = {0: block}
    forward, backward = block, block
    for step in range(1, count // 2):
        forward = lax.ppermute(forward, "samples", up)
        backward = lax.ppermute(backward, "samples", down)
        if step == 1:
            forward, backward, packed = lax.optimization_barrier((forward, backward, packed))
        slots[count - step] = forward
        slots[step] = backward
    slots[count // 2] = lax.ppermute(forward[:rows], "samples", up)
    slots[count] = lax.ppermute(backward[rows:], "samples", down)
    own = [slots[slot] for slot in range(count + 1)]
    sibling = [lax.ppermute(piece, "mp", [(0, 1), (1, 0)]) for piece in own]

    attended, probs = on_core(
        functools.partial(forward_kernel, count, scale),
        [jax.ShapeDtypeStruct(per_head, bf16), jax.ShapeDtypeStruct(per_head, f32)],
        in_vmem(1) + in_smem(1),
        flops=1 << 26,
        moved=1 << 20,
    )(heads, block_layout)
    weight_terms = on_core(
        functools.partial(weight_kernel, count),
        jax.ShapeDtypeStruct(term_shape, bf16),
        in_vmem(2 * count + 3),
        flops=1 << 29,
        moved=5 << 20,
    )(*own, *sibling, attended)
    weight_parts = exchanged(weight_terms)
    probs, weight_terms = lax.optimization_barrier((probs, weight_terms))
    site_terms = on_core(
        functools.partial(backward_kernel, count, scale),
        jax.ShapeDtypeStruct((count, lines, HEAD), bf16),
        in_vmem(2 * count + 5) + in_smem(1),
        [
            pltpu.VMEM((count * shard_rows, HEAD), bf16),
            pltpu.VMEM((count * seq_len, HEAD), bf16),
            pltpu.VMEM(per_head, bf16),
        ],
        flops=1 << 29,
        moved=6 << 20,
    )(*own, *sibling, heads, probs, region_mask.reshape(1, seq_len), partner_samples)
    site_parts = exchanged(site_terms)
    weight_grad = on_core(
        functools.partial(weight_out_kernel, count),
        jax.ShapeDtypeStruct((1, shard_rows, half_width), f32),
        in_vmem(1),
        moved=3 << 19,
    )(weight_parts)
    cotangents, embed_grad = on_core(
        functools.partial(site_out_kernel, count),
        [
            jax.ShapeDtypeStruct((1, 1, seq_len, half_width), bf16),
            jax.ShapeDtypeStruct((SPINS, half_width), f32),
        ],
        in_vmem(1),
        moved=1 << 19,
    )(site_parts)
    return (weight_grad, cotangents, embed_grad)


def solution(mesh):
    in_specs = (
        P("section", ("groups", "samples"), None, "mp"),
        P(("groups", "samples"), None, "mp"),
        P("section", "samples", "mp"),
        P("section", None, None),
        P(),
        P("groups"),
        P(("groups", "samples"), None),
    )
    out_specs = (
        P(("groups", "section"), "samples", "mp"),
        P("section", ("groups", "samples"), None, "mp"),
        P("groups", "mp"),
    )
    shards = mesh.shape["samples"]

    def whole(stored_inputs, top_cotangent, *rest):
        samples, _, width = top_cotangent.shape
        layer_count = stored_inputs.shape[0]
        one_each = samples == mesh.shape["groups"] * shards and layer_count == 1
        by_heads = one_each and shards % 2 == 0 and width == mesh.shape["mp"] * shards * HEAD
        return jax.shard_map(
            head_sharded if by_heads else local,
            mesh=mesh,
            in_specs=in_specs,
            out_specs=out_specs,
            check_vma=False,
        )(stored_inputs, top_cotangent, *rest)

    return whole
```

```python
import functools

import jax
import jax.numpy as jnp
from jax import lax
from jax.experimental import pallas as pl
from jax.experimental.pallas import tpu as pltpu
from jax.sharding import PartitionSpec as P

HEAD = 128
BLOCK = 64
SPINS = 2
TAIL = 16


def for_sending(value):

    def short(part):
        return part.astype(jnp.bfloat16) if part.dtype == jnp.float32 else part

    return jax.tree.map(short, value)


def passed_along(block, axis, distance):
    devices = range(lax.axis_size(axis))
    route = [(i - distance, i) for i in devices if i - distance in devices]
    return lax.ppermute(block, axis, route)


def softmax_parts(inputs_h, allowed, attention_scale):
    scores = (
        jnp.einsum("qhd,khd->hqk", inputs_h, inputs_h, preferred_element_type=jnp.float32)
        * attention_scale
    )
    scores = jnp.where(allowed[None], scores, -jnp.inf)
    top_score = jnp.max(scores, axis=-1, keepdims=True)
    expo_terms = jnp.exp(scores - top_score)
    probs = expo_terms / jnp.sum(expo_terms, axis=-1, keepdims=True)
    return (probs, probs.astype(jnp.bfloat16))


def local(
    stored_inputs, top_cotangent, layer_weights, block_layout, region_mask, partner_samples, spins
):
    section_index = lax.axis_index("section")
    section_count = lax.axis_size("section")
    micro_count = stored_inputs.shape[1]
    seq_len = stored_inputs.shape[2]
    half_width = stored_inputs.shape[3]
    head_count = half_width // HEAD
    attention_scale = 4.0 / HEAD
    weights = lax.all_gather(layer_weights[0], "samples", axis=0, tiled=True)
    pos_block = jnp.arange(seq_len) // BLOCK
    block_onehot = (pos_block[:, None] == jnp.arange(block_layout.shape[1])[None, :]).astype(
        jnp.float32
    )
    linked = jnp.dot(jnp.dot(block_onehot, block_layout[0].astype(jnp.float32)), block_onehot.T)
    allowed = (linked > 0.5) | (pos_block[:, None] == pos_block[None, :])
    every_layer_input = stored_inputs[0]
    inputs_h = every_layer_input[0].reshape(seq_len, head_count, HEAD)
    probs, probs_low = softmax_parts(inputs_h, allowed, attention_scale)
    attended = jnp.einsum(
        "hqk,khd->qhd", probs_low, inputs_h, preferred_element_type=jnp.float32
    ).astype(jnp.bfloat16)
    probs_list = [probs]
    low_list = [probs_low]
    attend_list = [attended.reshape(seq_len, half_width)]
    probs_all = jnp.stack(probs_list)
    low_all = jnp.stack(low_list)
    attend_store = jnp.stack(attend_list)

    def layer_back(grad_full, grad_own, inputs, probs, probs_low):
        grad_attn = jnp.dot(grad_full, weights, preferred_element_type=jnp.float32).astype(
            jnp.bfloat16
        )
        inputs_h = inputs.reshape(seq_len, head_count, HEAD)
        grad_h = grad_attn.reshape(seq_len, head_count, HEAD)
        grad_probs = jnp.einsum(
            "qhd,khd->hqk", grad_h, inputs_h, preferred_element_type=jnp.float32
        )
        grad_scores = (
            probs * (grad_probs - jnp.sum(grad_probs * probs, axis=-1, keepdims=True))
        ).astype(jnp.bfloat16)
        through = jnp.einsum("hqk,qhd->khd", probs_low, grad_h, preferred_element_type=jnp.float32)
        through = through + attention_scale * (
            jnp.einsum("hqk,khd->qhd", grad_scores, inputs_h, preferred_element_type=jnp.float32)
            + jnp.einsum("hqk,qhd->khd", grad_scores, inputs_h, preferred_element_type=jnp.float32)
        )
        grad_in = grad_own.astype(jnp.float32) + through.reshape(seq_len, half_width)
        return grad_in.astype(jnp.bfloat16)

    def resting(grad_full, grad_own, inputs, probs, probs_low):
        return jnp.zeros((seq_len, half_width), jnp.bfloat16)

    carried_state = jnp.zeros((seq_len, half_width), jnp.bfloat16)
    out_list = []
    grad_list = []
    total_steps = micro_count + section_count - 1
    for step_number in range(total_steps):
        micro_index = step_number - (section_count - 1 - section_index)
        active = (micro_index >= 0) & (micro_index < micro_count)
        slot_index = jnp.clip(micro_index, 0, micro_count - 1)
        from_top = lax.dynamic_index_in_dim(top_cotangent, slot_index, 0, keepdims=False)
        incoming = jnp.where(section_index == section_count - 1, from_top, carried_state)
        grad_full = lax.all_gather(incoming, "mp", axis=1, tiled=True)
        inputs_now = lax.dynamic_index_in_dim(every_layer_input, slot_index, 0, keepdims=False)
        probs_now = lax.dynamic_index_in_dim(probs_all, slot_index, 0, keepdims=False)
        low_now = lax.dynamic_index_in_dim(low_all, slot_index, 0, keepdims=False)
        grad_in = lax.cond(
            active, layer_back, resting, grad_full, incoming, inputs_now, probs_now, low_now
        )
        out_list.append(grad_in)
        grad_list.append(grad_full)
        if step_number < total_steps - 1:
            carried_state = jax.tree.map(
                lambda part, own: part.astype(own.dtype),
                passed_along(for_sending(grad_in), "section", -1),
                grad_in,
            )
    offset = section_count - 1 - section_index
    out_store = lax.dynamic_slice_in_dim(jnp.stack(out_list), offset, micro_count, 0)
    grad_store = lax.dynamic_slice_in_dim(jnp.stack(grad_list), offset, micro_count, 0)
    summed_weight = lax.psum_scatter(
        jnp.einsum(
            "mtf,mta->fa", grad_store, attend_store, preferred_element_type=jnp.float32
        ).astype(jnp.bfloat16),
        "samples",
        scatter_dimension=0,
        tiled=True,
    ).astype(jnp.float32)
    region_count = seq_len // 2
    rank_in_region = jnp.cumsum(region_mask) - 1
    select = (
        (rank_in_region[None, :] == jnp.arange(region_count)[:, None]) & (region_mask[None, :] > 0)
    ).astype(jnp.bfloat16)
    tiles = jnp.einsum("at,mtd->mad", select, out_store, preferred_element_type=jnp.float32).astype(
        jnp.bfloat16
    )
    shard_index = lax.axis_index("samples")
    my_partners = lax.dynamic_slice_in_dim(
        partner_samples, shard_index * micro_count, micro_count, 0
    )
    shard_count = lax.axis_size("samples")
    dest_shard = my_partners // micro_count
    dest_slot = my_partners % micro_count
    route = (
        (dest_shard[:, None, None] == jnp.arange(shard_count)[None, :, None])
        & (dest_slot[:, None, None] == jnp.arange(micro_count)[None, None, :])
    ).astype(jnp.bfloat16)
    outgoing = jnp.einsum("mku,mad->kuad", route, tiles, preferred_element_type=jnp.float32).astype(
        jnp.bfloat16
    )
    arrived = lax.all_to_all(outgoing, "samples", split_axis=0, concat_axis=0, tiled=True)
    ones_row = jnp.ones((shard_count,), jnp.bfloat16)
    received = jnp.einsum(
        "k,kuad->uad", ones_row, arrived, preferred_element_type=jnp.float32
    ).astype(jnp.bfloat16)
    placed = jnp.einsum("at,mad->mtd", select, received, preferred_element_type=jnp.float32)
    kept = jnp.where(region_mask[None, :, None] > 0, jnp.zeros_like(out_store), out_store)
    site_cot = (kept.astype(jnp.float32) + placed).astype(jnp.bfloat16)
    cotangents = jnp.where(section_index == 0, site_cot, out_store)
    onehot = (spins[:, :, None] == jnp.arange(SPINS)[None, None, :]).astype(jnp.bfloat16)
    embed_term = jnp.einsum("mtv,mtd->vd", onehot, site_cot, preferred_element_type=jnp.float32)
    embed_term = jnp.where(section_index == 0, embed_term, jnp.zeros_like(embed_term))
    embed_grad = lax.psum(embed_term, ("samples", "section"))
    return (summed_weight[None], cotangents[None], embed_grad)


def ring_sample(place, count):
    return jnp.where(place < count // 2, 2 * place, 2 * (count - place) - 1)


def ring_place(sample, count):
    return jnp.where(lax.rem(sample, 2) == 0, sample // 2, count - 1 - sample // 2)


def ring_route(count, distance):
    order = list(range(0, count, 2)) + list(range(1, count, 2))[::-1]
    return [(order[i], order[(i - distance) % count]) for i in range(count)]


def own_place(count):
    return ring_place(lax.axis_index("samples"), count)


def peer_at(place, distance, count):
    return ring_sample(lax.rem(place + distance + count, count), count)


def columns(index, size):
    return pl.ds(pl.multiple_of(index * size, size), size)


def in_vmem(count):
    return [pl.BlockSpec(memory_space=pltpu.VMEM)] * count


def in_smem(count):
    return [pl.BlockSpec(memory_space=pltpu.SMEM)] * count


def on_core(body, out_shapes, in_specs, scratch=(), flops=0, moved=0):
    return pl.pallas_call(
        body,
        out_shape=out_shapes,
        in_specs=in_specs,
        out_specs=jax.tree.map(lambda _: pl.BlockSpec(memory_space=pltpu.VMEM), out_shapes),
        scratch_shapes=list(scratch),
        compiler_params=pltpu.CompilerParams(vmem_limit_bytes=40 * 1024 * 1024),
        cost_estimate=pl.CostEstimate(flops=flops, bytes_accessed=moved, transcendentals=0),
    )


def matmul(left, right):
    return jnp.dot(left, right, preferred_element_type=jnp.float32)


def matmul_t(left, right):
    return lax.dot_general(
        left, right, (((1,), (1,)), ((), ())), preferred_element_type=jnp.float32
    )


def pack_kernel(count, share_axis, x_ref, w_ref, spins_ref, out_ref):
    seq_len = x_ref.shape[2]
    sent = out_ref.shape[1] - seq_len - TAIL
    spin_rows = jnp.broadcast_to(spins_ref[...].astype(jnp.float32), (TAIL, seq_len))
    spin_rows = spin_rows.astype(jnp.bfloat16)
    rows = columns(lax.axis_index(share_axis), sent) if share_axis else slice(None)
    for peer in range(count):
        cols = slice(peer * HEAD, (peer + 1) * HEAD)
        out_ref[peer, 0:seq_len, :] = x_ref[0, 0, :, cols]
        out_ref[peer, seq_len : seq_len + TAIL, :] = spin_rows
        out_ref[peer, seq_len + TAIL :, :] = w_ref[0, rows, cols]


def forward_kernel(count, scale, *refs):
    heads_ref, layout_ref, attended_ref, probs_ref = refs
    seq_len = probs_ref.shape[1]
    blocks = layout_ref.shape[1]
    rows = lax.broadcasted_iota(jnp.int32, (seq_len, seq_len), 0) // BLOCK
    cols = lax.broadcasted_iota(jnp.int32, (seq_len, seq_len), 1) // BLOCK
    seen = rows == cols
    for q in range(blocks):
        for k in range(blocks):
            if q != k:
                seen = seen | ((rows == q) & (cols == k) & (layout_ref[0, q, k] > 0))
    for slot in range(count):
        x = heads_ref[slot, 0:seq_len, :]
        scores = jnp.where(seen, matmul_t(x, x) * scale, -jnp.inf)
        terms = jnp.exp(scores - jnp.max(scores, axis=-1, keepdims=True))
        probs = terms / jnp.sum(terms, axis=-1, keepdims=True)
        probs_ref[slot] = probs
        attended_ref[slot] = matmul(probs.astype(jnp.bfloat16), x).astype(jnp.bfloat16)


def lay_weights(weights, heads_ref, shared, skipped, share_axis):
    count = heads_ref.shape[0]
    sent = heads_ref.shape[1] - skipped
    parts = 1 + len(shared)
    index = lax.axis_index(share_axis) if share_axis else 0
    for sample in range(count):
        for step, part in enumerate((heads_ref, *shared)):
            first = sample * parts * sent + (index if step == 0 else 1 - index) * sent
            rows = pl.ds(pl.multiple_of(first, sent), sent)
            weights[rows, :] = part[sample, skipped:, :] if step == 0 else part[sample]


def weight_product(pieces, sides, shard_rows, attended):
    for side, grads in zip(sides, pieces):
        for part in range(grads[0].shape[1] // shard_rows):
            cols = slice(part * shard_rows, (part + 1) * shard_rows)
            total = None
            for left, first in attended:
                grad = jnp.concatenate([grad[:, cols] for grad in grads[first : first + 2]], axis=0)
                term = matmul(left, grad)
                total = term if total is None else total + term
            yield side, part, total


def transposed(value):
    return value.astype(jnp.float32).T.astype(jnp.bfloat16)


def attention_back(scale, x, probs, grad_attn, above):
    grad_probs = matmul_t(grad_attn, x)
    inner = jnp.sum(grad_probs * probs, axis=-1, keepdims=True)
    grad_scores = (probs * (grad_probs - inner)).astype(jnp.bfloat16).astype(jnp.float32)
    both = jnp.concatenate([grad_scores, grad_scores.T], axis=1).astype(jnp.bfloat16)
    through = matmul(transposed(probs.astype(jnp.bfloat16)), grad_attn)
    through = through + scale * matmul(both, jnp.concatenate([x, x], axis=0))
    return (above.astype(jnp.float32) + through).astype(jnp.bfloat16)


def near_kernel(count, scale, share_axis, *refs):
    size = count - 1
    slots = [slot for slot in range(count) if slot != count // 2]
    own, sibling = refs[:size], refs[size : 2 * size]
    heads_ref, probs_ref, attended_ref = refs[2 * size : 2 * size + 3]
    shared = refs[2 * size + 3 : -4]
    partial_ref, grads_ref, weights, attn = refs[-4:]
    place = own_place(count)
    shard = lax.axis_index("samples")
    half = lax.axis_index("mp")
    seq_len, half_width = own[0].shape
    skipped = seq_len + TAIL
    shard_rows = partial_ref.shape[2]
    sample_of = [peer_at(place, slot, count) for slot in slots]
    lay_weights(weights, heads_ref, shared, skipped, share_axis)
    left = []
    for first in range(0, size, 2):
        pair = [attended_ref[sample] for sample in sample_of[first : first + 2]]
        left.append((transposed(jnp.concatenate(pair, axis=0)), first))
    sides = (half, 1 - half)
    per_half = count // 2
    for side, part, total in weight_product((own, sibling), sides, shard_rows, left):
        partial_ref[side * per_half + part] = total
    near = weights[columns(half, half_width), :]
    far = weights[columns(1 - half, half_width), :]
    for first in range(0, size, 2):
        rows = [
            jnp.concatenate([grad[...] for grad in grads[first : first + 2]], axis=0)
            for grads in (own, sibling)
        ]
        total = matmul(rows[0], near) + matmul(rows[1], far)
        attn[first * seq_len : first * seq_len + total.shape[0], :] = total.astype(jnp.bfloat16)
    for index, sample in enumerate(sample_of):
        grads_ref[index] = attention_back(
            scale,
            heads_ref[sample, 0:seq_len, :],
            probs_ref[sample],
            attn[index * seq_len : (index + 1) * seq_len, :],
            own[index][:, columns(shard, HEAD)],
        )


def far_kernel(count, scale, share_axis, *refs):
    own, sibling = refs[:2], refs[2:4]
    heads_ref, probs_ref, attended_ref, partial_ref, near_ref, mask_ref, partner_ref = refs[4:11]
    shared = refs[11:-3]
    out_ref, weights, grads = refs[-3:]
    place = own_place(count)
    shard = lax.axis_index("samples")
    half = lax.axis_index("mp")
    rows, half_width = own[0].shape
    seq_len = 2 * rows
    skipped = seq_len + TAIL
    shard_rows = partial_ref.shape[2]
    slots = [slot for slot in range(count) if slot != count // 2]
    for index, slot in enumerate(slots):
        grads[peer_at(place, slot, count)] = near_ref[index]
    lay_weights(weights, heads_ref, shared, skipped, share_axis)
    sample = peer_at(place, count // 2, count)
    sides = (half, 1 - half)
    per_half = count // 2
    left = [(transposed(attended_ref[sample]), 0)]
    for side, part, total in weight_product((own, sibling), sides, shard_rows, left):
        peer = side * per_half + part
        total = total + partial_ref[peer]
        out_ref[peer, skipped:, :] = total.T.astype(jnp.bfloat16)
    near = weights[columns(half, half_width), :]
    far = weights[columns(1 - half, half_width), :]
    whole = [jnp.concatenate([grad[...] for grad in side], axis=0) for side in (own, sibling)]
    grad_attn = (matmul(whole[0], near) + matmul(whole[1], far)).astype(jnp.bfloat16)
    cols = columns(shard, HEAD)
    grads[sample] = attention_back(
        scale,
        heads_ref[sample, 0:seq_len, :],
        probs_ref[sample],
        grad_attn,
        jnp.concatenate([grad[:, cols] for grad in own], axis=0),
    )
    region = jnp.broadcast_to(mask_ref[...].astype(jnp.float32), (HEAD, seq_len)).T > 0.5
    which = lax.broadcasted_iota(jnp.int32, (TAIL, seq_len), 0).astype(jnp.float32)
    embed = jnp.zeros((TAIL, HEAD), jnp.float32)
    for sample in range(count):
        swapped = grads[partner_ref[sample]].astype(jnp.float32)
        site = jnp.where(region, swapped, grads[sample].astype(jnp.float32)).astype(jnp.bfloat16)
        out_ref[sample, 0:seq_len, :] = site
        spin = heads_ref[sample, seq_len:skipped, :].astype(jnp.float32)
        embed = embed + matmul((spin == which).astype(jnp.bfloat16), site)
    high = embed.astype(jnp.bfloat16).astype(jnp.float32)
    low = embed - high
    tail = jnp.concatenate([high[: TAIL // 2], low[: TAIL // 2]], axis=0).astype(jnp.bfloat16)
    for sample in range(count):
        out_ref[sample, seq_len:skipped, :] = tail


def unpack_kernel(count, parts_ref, weight_ref, site_ref, embed_ref):
    seq_len = site_ref.shape[2]
    skipped = seq_len + TAIL
    for peer in range(count):
        cols = slice(peer * HEAD, (peer + 1) * HEAD)
        weight_ref[0, :, cols] = parts_ref[peer, skipped:, :].astype(jnp.float32)
        site_ref[0, 0, :, cols] = parts_ref[peer, 0:seq_len, :]
        tail = parts_ref[peer, seq_len:skipped, :].astype(jnp.float32)
        embed_ref[:, cols] = (tail[: TAIL // 2] + tail[TAIL // 2 :])[:SPINS]


def exchanged(blocks):
    return lax.all_to_all(blocks, "samples", split_axis=0, concat_axis=0, tiled=True)


def head_sharded(
    stored_inputs, top_cotangent, layer_weights, block_layout, region_mask, partner_samples, spins
):
    count = lax.axis_size("samples")
    seq_len = stored_inputs.shape[2]
    shard_rows, half_width = layer_weights.shape[1:]
    scale = 4.0 / HEAD
    bf16, f32 = jnp.bfloat16, jnp.float32
    per_head = (count, seq_len, HEAD)
    lines = seq_len + TAIL
    share_axis = "groups" if lax.axis_size("groups") == 2 else None
    sent = shard_rows // 2 if share_axis else shard_rows
    laid = pltpu.VMEM((count * shard_rows, HEAD), bf16)

    up, down = ring_route(count, -1), ring_route(count, 1)
    block = top_cotangent[0]
    rows = seq_len // 2
    packed = on_core(
        functools.partial(pack_kernel, count, share_axis),
        jax.ShapeDtypeStruct((count, lines + sent, HEAD), bf16),
        in_vmem(3),
        moved=3 << 19,
    )(stored_inputs, layer_weights, spins)
    slots = {0: block}
    forward, backward = block, block
    for step in range(1, count // 2):
        forward = lax.ppermute(forward, "samples", up)
        backward = lax.ppermute(backward, "samples", down)
        if step == 1:
            forward, backward, packed = lax.optimization_barrier((forward, backward, packed))
        slots[count - step] = forward
        slots[step] = backward
    heads = exchanged(packed)
    shared = []
    if share_axis:
        shared = [lax.ppermute(heads[:, lines:], share_axis, [(0, 1), (1, 0)])]
    far = [
        lax.ppermute(forward[:rows], "samples", up),
        lax.ppermute(backward[rows:], "samples", down),
    ]
    near = [slots[slot] for slot in range(count) if slot != count // 2]
    swap = [(0, 1), (1, 0)]
    near_sibling = [lax.ppermute(piece, "mp", swap) for piece in near]
    far_sibling = [lax.ppermute(piece, "mp", swap) for piece in far]

    attended, probs = on_core(
        functools.partial(forward_kernel, count, scale),
        [jax.ShapeDtypeStruct(per_head, bf16), jax.ShapeDtypeStruct(per_head, f32)],
        in_vmem(1) + in_smem(1),
        flops=1 << 26,
        moved=1 << 20,
    )(heads, block_layout)
    partial, near_grads = on_core(
        functools.partial(near_kernel, count, scale, share_axis),
        [
            jax.ShapeDtypeStruct((count, HEAD, shard_rows), f32),
            jax.ShapeDtypeStruct((count - 1, seq_len, HEAD), bf16),
        ],
        in_vmem(2 * count + 1 + len(shared)),
        [laid, pltpu.VMEM((count * seq_len, HEAD), bf16)],
        flops=1 << 30,
        moved=6 << 20,
    )(*near, *near_sibling, heads, probs, attended, *shared)
    terms = on_core(
        functools.partial(far_kernel, count, scale, share_axis),
        jax.ShapeDtypeStruct((count, lines + shard_rows, HEAD), bf16),
        in_vmem(10) + in_smem(1) + in_vmem(len(shared)),
        [laid, pltpu.VMEM(per_head, bf16)],
        flops=1 << 27,
        moved=3 << 20,
    )(
        *far,
        *far_sibling,
        heads,
        probs,
        attended,
        partial,
        near_grads,
        region_mask.reshape(1, seq_len),
        partner_samples,
        *shared,
    )
    return on_core(
        functools.partial(unpack_kernel, count),
        [
            jax.ShapeDtypeStruct((1, shard_rows, half_width), f32),
            jax.ShapeDtypeStruct((1, 1, seq_len, half_width), bf16),
            jax.ShapeDtypeStruct((SPINS, half_width), f32),
        ],
        in_vmem(1),
        moved=2 << 20,
    )(exchanged(terms))


def solution(mesh):
    in_specs = (
        P("section", ("groups", "samples"), None, "mp"),
        P(("groups", "samples"), None, "mp"),
        P("section", "samples", "mp"),
        P("section", None, None),
        P(),
        P("groups"),
        P(("groups", "samples"), None),
    )
    out_specs = (
        P(("groups", "section"), "samples", "mp"),
        P("section", ("groups", "samples"), None, "mp"),
        P("groups", "mp"),
    )
    shards = mesh.shape["samples"]

    def whole(stored_inputs, top_cotangent, *rest):
        samples, _, width = top_cotangent.shape
        layer_count = stored_inputs.shape[0]
        one_each = samples == mesh.shape["groups"] * shards and layer_count == 1
        by_heads = one_each and shards % 2 == 0 and width == mesh.shape["mp"] * shards * HEAD
        return jax.shard_map(
            head_sharded if by_heads else local,
            mesh=mesh,
            in_specs=in_specs,
            out_specs=out_specs,
            check_vma=False,
        )(stored_inputs, top_cotangent, *rest)

    return whole
```

```python
import functools

import jax
import jax.numpy as jnp
from jax import lax
from jax.experimental import pallas as pl
from jax.experimental.pallas import tpu as pltpu
from jax.sharding import PartitionSpec as P

HEAD = 128
BLOCK = 64
SPINS = 2
TAIL = 16
FLOPS_PER_MICRO = 1.15e9


def for_sending(value):

    def short(part):
        return part.astype(jnp.bfloat16) if part.dtype == jnp.float32 else part

    return jax.tree.map(short, value)


def passed_along(block, axis, distance):
    devices = range(lax.axis_size(axis))
    route = [(i - distance, i) for i in devices if i - distance in devices]
    return lax.ppermute(block, axis, route)


def softmax_parts(inputs_h, allowed, attention_scale):
    scores = (
        jnp.einsum("qhd,khd->hqk", inputs_h, inputs_h, preferred_element_type=jnp.float32)
        * attention_scale
    )
    scores = jnp.where(allowed[None], scores, -jnp.inf)
    top_score = jnp.max(scores, axis=-1, keepdims=True)
    expo_terms = jnp.exp(scores - top_score)
    probs = expo_terms / jnp.sum(expo_terms, axis=-1, keepdims=True)
    return (probs, probs.astype(jnp.bfloat16))


def local(
    stored_inputs, top_cotangent, layer_weights, block_layout, region_mask, partner_samples, spins
):
    section_index = lax.axis_index("section")
    section_count = lax.axis_size("section")
    micro_count = stored_inputs.shape[1]
    seq_len = stored_inputs.shape[2]
    half_width = stored_inputs.shape[3]
    head_count = half_width // HEAD
    attention_scale = 4.0 / HEAD
    weights = lax.all_gather(layer_weights[0], "samples", axis=0, tiled=True)
    pos_block = jnp.arange(seq_len) // BLOCK
    block_onehot = (pos_block[:, None] == jnp.arange(block_layout.shape[1])[None, :]).astype(
        jnp.float32
    )
    linked = jnp.dot(jnp.dot(block_onehot, block_layout[0].astype(jnp.float32)), block_onehot.T)
    allowed = (linked > 0.5) | (pos_block[:, None] == pos_block[None, :])
    every_layer_input = stored_inputs[0]
    inputs_h = every_layer_input[0].reshape(seq_len, head_count, HEAD)
    probs, probs_low = softmax_parts(inputs_h, allowed, attention_scale)
    attended = jnp.einsum(
        "hqk,khd->qhd", probs_low, inputs_h, preferred_element_type=jnp.float32
    ).astype(jnp.bfloat16)
    probs_list = [probs]
    low_list = [probs_low]
    attend_list = [attended.reshape(seq_len, half_width)]
    probs_all = jnp.stack(probs_list)
    low_all = jnp.stack(low_list)
    attend_store = jnp.stack(attend_list)

    def layer_back(grad_full, grad_own, inputs, probs, probs_low):
        grad_attn = jnp.dot(grad_full, weights, preferred_element_type=jnp.float32).astype(
            jnp.bfloat16
        )
        inputs_h = inputs.reshape(seq_len, head_count, HEAD)
        grad_h = grad_attn.reshape(seq_len, head_count, HEAD)
        grad_probs = jnp.einsum(
            "qhd,khd->hqk", grad_h, inputs_h, preferred_element_type=jnp.float32
        )
        grad_scores = (
            probs * (grad_probs - jnp.sum(grad_probs * probs, axis=-1, keepdims=True))
        ).astype(jnp.bfloat16)
        through = jnp.einsum("hqk,qhd->khd", probs_low, grad_h, preferred_element_type=jnp.float32)
        through = through + attention_scale * (
            jnp.einsum("hqk,khd->qhd", grad_scores, inputs_h, preferred_element_type=jnp.float32)
            + jnp.einsum("hqk,qhd->khd", grad_scores, inputs_h, preferred_element_type=jnp.float32)
        )
        grad_in = grad_own.astype(jnp.float32) + through.reshape(seq_len, half_width)
        return grad_in.astype(jnp.bfloat16)

    def resting(grad_full, grad_own, inputs, probs, probs_low):
        return jnp.zeros((seq_len, half_width), jnp.bfloat16)

    carried_state = jnp.zeros((seq_len, half_width), jnp.bfloat16)
    out_list = []
    grad_list = []
    total_steps = micro_count + section_count - 1
    for step_number in range(total_steps):
        micro_index = step_number - (section_count - 1 - section_index)
        active = (micro_index >= 0) & (micro_index < micro_count)
        slot_index = jnp.clip(micro_index, 0, micro_count - 1)
        from_top = lax.dynamic_index_in_dim(top_cotangent, slot_index, 0, keepdims=False)
        incoming = jnp.where(section_index == section_count - 1, from_top, carried_state)
        grad_full = lax.all_gather(incoming, "mp", axis=1, tiled=True)
        inputs_now = lax.dynamic_index_in_dim(every_layer_input, slot_index, 0, keepdims=False)
        probs_now = lax.dynamic_index_in_dim(probs_all, slot_index, 0, keepdims=False)
        low_now = lax.dynamic_index_in_dim(low_all, slot_index, 0, keepdims=False)
        grad_in = lax.cond(
            active, layer_back, resting, grad_full, incoming, inputs_now, probs_now, low_now
        )
        out_list.append(grad_in)
        grad_list.append(grad_full)
        if step_number < total_steps - 1:
            carried_state = jax.tree.map(
                lambda part, own: part.astype(own.dtype),
                passed_along(for_sending(grad_in), "section", -1),
                grad_in,
            )
    offset = section_count - 1 - section_index
    out_store = lax.dynamic_slice_in_dim(jnp.stack(out_list), offset, micro_count, 0)
    grad_store = lax.dynamic_slice_in_dim(jnp.stack(grad_list), offset, micro_count, 0)
    summed_weight = lax.psum_scatter(
        jnp.einsum(
            "mtf,mta->fa", grad_store, attend_store, preferred_element_type=jnp.float32
        ).astype(jnp.bfloat16),
        "samples",
        scatter_dimension=0,
        tiled=True,
    ).astype(jnp.float32)
    region_count = seq_len // 2
    rank_in_region = jnp.cumsum(region_mask) - 1
    select = (
        (rank_in_region[None, :] == jnp.arange(region_count)[:, None]) & (region_mask[None, :] > 0)
    ).astype(jnp.bfloat16)
    tiles = jnp.einsum("at,mtd->mad", select, out_store, preferred_element_type=jnp.float32).astype(
        jnp.bfloat16
    )
    shard_index = lax.axis_index("samples")
    my_partners = lax.dynamic_slice_in_dim(
        partner_samples, shard_index * micro_count, micro_count, 0
    )
    shard_count = lax.axis_size("samples")
    dest_shard = my_partners // micro_count
    dest_slot = my_partners % micro_count
    route = (
        (dest_shard[:, None, None] == jnp.arange(shard_count)[None, :, None])
        & (dest_slot[:, None, None] == jnp.arange(micro_count)[None, None, :])
    ).astype(jnp.bfloat16)
    outgoing = jnp.einsum("mku,mad->kuad", route, tiles, preferred_element_type=jnp.float32).astype(
        jnp.bfloat16
    )
    arrived = lax.all_to_all(outgoing, "samples", split_axis=0, concat_axis=0, tiled=True)
    ones_row = jnp.ones((shard_count,), jnp.bfloat16)
    received = jnp.einsum(
        "k,kuad->uad", ones_row, arrived, preferred_element_type=jnp.float32
    ).astype(jnp.bfloat16)
    placed = jnp.einsum("at,mad->mtd", select, received, preferred_element_type=jnp.float32)
    kept = jnp.where(region_mask[None, :, None] > 0, jnp.zeros_like(out_store), out_store)
    site_cot = (kept.astype(jnp.float32) + placed).astype(jnp.bfloat16)
    cotangents = jnp.where(section_index == 0, site_cot, out_store)
    onehot = (spins[:, :, None] == jnp.arange(SPINS)[None, None, :]).astype(jnp.bfloat16)
    embed_term = jnp.einsum("mtv,mtd->vd", onehot, site_cot, preferred_element_type=jnp.float32)
    embed_term = jnp.where(section_index == 0, embed_term, jnp.zeros_like(embed_term))
    embed_grad = lax.psum(embed_term, ("samples", "section"))
    return (summed_weight[None], cotangents[None], embed_grad)


def ring_sample(place, count):
    return jnp.where(place < count // 2, 2 * place, 2 * (count - place) - 1)


def ring_place(sample, count):
    return jnp.where(lax.rem(sample, 2) == 0, sample // 2, count - 1 - sample // 2)


def ring_route(count, distance):
    order = list(range(0, count, 2)) + list(range(1, count, 2))[::-1]
    return [(order[i], order[(i - distance) % count]) for i in range(count)]


def own_place(count):
    return ring_place(lax.axis_index("samples"), count)


def peer_at(place, distance, count):
    return ring_sample(lax.rem(place + distance + count, count), count)


def columns(index, size):
    return pl.ds(pl.multiple_of(index * size, size), size)


def in_vmem(count):
    return [pl.BlockSpec(memory_space=pltpu.VMEM)] * count


def in_smem(count):
    return [pl.BlockSpec(memory_space=pltpu.SMEM)] * count


def on_core(body, out_shapes, in_specs, scratch=(), micros=1):
    return pl.pallas_call(
        body,
        out_shape=out_shapes,
        in_specs=in_specs,
        out_specs=jax.tree.map(lambda _: pl.BlockSpec(memory_space=pltpu.VMEM), out_shapes),
        scratch_shapes=list(scratch),
        compiler_params=pltpu.CompilerParams(vmem_limit_bytes=40 * 1024 * 1024),
        cost_estimate=pl.CostEstimate(
            flops=int(micros * FLOPS_PER_MICRO), bytes_accessed=1 << 16, transcendentals=0
        ),
    )


def matmul(left, right):
    return jnp.dot(left, right, preferred_element_type=jnp.float32)


def matmul_t(left, right):
    return lax.dot_general(
        left, right, (((1,), (1,)), ((), ())), preferred_element_type=jnp.float32
    )


def pack_kernel(count, share_axis, x_ref, w_ref, spins_ref, out_ref, sems):
    seq_len = x_ref.shape[2]
    skipped = seq_len + TAIL
    sent = out_ref.shape[1] - skipped
    rows = columns(lax.axis_index(share_axis), sent) if share_axis else slice(None)
    copies = []
    for peer in range(count):
        cols = slice(peer * HEAD, (peer + 1) * HEAD)
        head, weight = out_ref.at[peer, 0:seq_len, :], out_ref.at[peer, skipped:, :]
        copies.append(pltpu.make_async_copy(x_ref.at[0, 0, :, cols], head, sems.at[0, peer]))
        copies.append(pltpu.make_async_copy(w_ref.at[0, rows, cols], weight, sems.at[1, peer]))
    for copy in copies:
        copy.start()
    spin_rows = jnp.broadcast_to(spins_ref[...].astype(jnp.float32), (TAIL, seq_len))
    for peer in range(count):
        out_ref[peer, seq_len:skipped, :] = spin_rows.astype(jnp.bfloat16)
    for copy in copies:
        copy.wait()


def forward_kernel(count, scale, *refs):
    heads_ref, layout_ref, attended_ref, probs_ref = refs[0], refs[-3], refs[-2], refs[-1]
    seq_len = probs_ref.shape[1]
    blocks = layout_ref.shape[1]
    rows = lax.broadcasted_iota(jnp.int32, (seq_len, seq_len), 0) // BLOCK
    cols = lax.broadcasted_iota(jnp.int32, (seq_len, seq_len), 1) // BLOCK
    seen = rows == cols
    for q in range(blocks):
        for k in range(blocks):
            if q != k:
                seen = seen | ((rows == q) & (cols == k) & (layout_ref[0, q, k] > 0))
    for slot in range(count):
        x = heads_ref[slot, 0:seq_len, :]
        scores = jnp.where(seen, matmul_t(x, x) * scale, -jnp.inf)
        terms = jnp.exp(scores - jnp.max(scores, axis=-1, keepdims=True))
        probs = terms / jnp.sum(terms, axis=-1, keepdims=True)
        probs_ref[slot] = probs
        attended_ref[slot] = matmul(probs.astype(jnp.bfloat16), x).astype(jnp.bfloat16)


def lay_weights(weights, heads_ref, shared, skipped, share_axis):
    count = heads_ref.shape[0]
    sent = heads_ref.shape[1] - skipped
    parts = 1 + len(shared)
    index = lax.axis_index(share_axis) if share_axis else 0
    for sample in range(count):
        for step, part in enumerate((heads_ref, *shared)):
            first = sample * parts * sent + (index if step == 0 else 1 - index) * sent
            rows = pl.ds(pl.multiple_of(first, sent), sent)
            weights[rows, :] = part[sample, skipped:, :] if step == 0 else part[sample]


def weight_product(pieces, sides, shard_rows, attended):
    for side, grads in zip(sides, pieces):
        for part in range(grads[0].shape[1] // shard_rows):
            cols = slice(part * shard_rows, (part + 1) * shard_rows)
            total = None
            for left, first in attended:
                grad = jnp.concatenate([grad[:, cols] for grad in grads[first : first + 2]], axis=0)
                term = matmul(left, grad)
                total = term if total is None else total + term
            yield side, part, total


def transposed(value):
    return value.astype(jnp.float32).T.astype(jnp.bfloat16)


def attention_back(scale, x, probs, grad_attn, above):
    grad_probs = matmul_t(grad_attn, x)
    inner = jnp.sum(grad_probs * probs, axis=-1, keepdims=True)
    grad_scores = (probs * (grad_probs - inner)).astype(jnp.bfloat16).astype(jnp.float32)
    both = jnp.concatenate([grad_scores, grad_scores.T], axis=1).astype(jnp.bfloat16)
    through = matmul(transposed(probs.astype(jnp.bfloat16)), grad_attn)
    through = through + scale * matmul(both, jnp.concatenate([x, x], axis=0))
    return (above.astype(jnp.float32) + through).astype(jnp.bfloat16)


def near_products_kernel(count, share_axis, *refs):
    size = count - 1
    slots = [slot for slot in range(count) if slot != count // 2]
    own, sibling = refs[:size], refs[size : 2 * size]
    heads_ref, attended_ref = refs[2 * size : 2 * size + 2]
    shared = refs[2 * size + 2 : -3]
    partial_ref, attn_ref, weights = refs[-3:]
    place = own_place(count)
    half = lax.axis_index("mp")
    seq_len, half_width = own[0].shape
    shard_rows = partial_ref.shape[2]
    sample_of = [peer_at(place, slot, count) for slot in slots]
    lay_weights(weights, heads_ref, shared, seq_len + TAIL, share_axis)
    left = []
    for first in range(0, size, 2):
        pair = [attended_ref[sample] for sample in sample_of[first : first + 2]]
        left.append((transposed(jnp.concatenate(pair, axis=0)), first))
    sides = (half, 1 - half)
    per_half = count // 2
    for side, part, total in weight_product((own, sibling), sides, shard_rows, left):
        partial_ref[side * per_half + part] = total
    near = weights[columns(half, half_width), :]
    far = weights[columns(1 - half, half_width), :]
    for first in range(0, size, 2):
        rows = [
            jnp.concatenate([grad[...] for grad in grads[first : first + 2]], axis=0)
            for grads in (own, sibling)
        ]
        total = matmul(rows[0], near) + matmul(rows[1], far)
        attn_ref[first * seq_len : first * seq_len + total.shape[0], :] = total.astype(jnp.bfloat16)


def near_back_kernel(count, scale, *refs):
    size = count - 1
    own = refs[:size]
    heads_ref, probs_ref, attn_ref, _, _, grads_ref = refs[size:]
    place = own_place(count)
    shard = lax.axis_index("samples")
    seq_len = own[0].shape[0]
    slots = [slot for slot in range(count) if slot != count // 2]
    for index, slot in enumerate(slots):
        sample = peer_at(place, slot, count)
        grads_ref[index] = attention_back(
            scale,
            heads_ref[sample, 0:seq_len, :],
            probs_ref[sample],
            attn_ref[index * seq_len : (index + 1) * seq_len, :],
            own[index][:, columns(shard, HEAD)],
        )


def far_kernel(count, scale, share_axis, *refs):
    own, sibling = refs[:2], refs[2:4]
    heads_ref, probs_ref, attended_ref, partial_ref, near_ref, mask_ref, partner_ref = refs[4:11]
    shared = refs[11:-3]
    out_ref, weights, grads = refs[-3:]
    place = own_place(count)
    shard = lax.axis_index("samples")
    half = lax.axis_index("mp")
    rows, half_width = own[0].shape
    seq_len = 2 * rows
    skipped = seq_len + TAIL
    shard_rows = partial_ref.shape[2]
    slots = [slot for slot in range(count) if slot != count // 2]
    for index, slot in enumerate(slots):
        grads[peer_at(place, slot, count)] = near_ref[index]
    lay_weights(weights, heads_ref, shared, skipped, share_axis)
    sample = peer_at(place, count // 2, count)
    sides = (half, 1 - half)
    per_half = count // 2
    left = [(transposed(attended_ref[sample]), 0)]
    for side, part, total in weight_product((own, sibling), sides, shard_rows, left):
        peer = side * per_half + part
        total = total + partial_ref[peer]
        out_ref[peer, skipped:, :] = total.T.astype(jnp.bfloat16)
    near = weights[columns(half, half_width), :]
    far = weights[columns(1 - half, half_width), :]
    whole = [jnp.concatenate([grad[...] for grad in side], axis=0) for side in (own, sibling)]
    grad_attn = (matmul(whole[0], near) + matmul(whole[1], far)).astype(jnp.bfloat16)
    cols = columns(shard, HEAD)
    grads[sample] = attention_back(
        scale,
        heads_ref[sample, 0:seq_len, :],
        probs_ref[sample],
        grad_attn,
        jnp.concatenate([grad[:, cols] for grad in own], axis=0),
    )
    region = jnp.broadcast_to(mask_ref[...].astype(jnp.float32), (HEAD, seq_len)).T > 0.5
    which = lax.broadcasted_iota(jnp.int32, (TAIL, seq_len), 0).astype(jnp.float32)
    embed = jnp.zeros((TAIL, HEAD), jnp.float32)
    for sample in range(count):
        swapped = grads[partner_ref[sample]].astype(jnp.float32)
        site = jnp.where(region, swapped, grads[sample].astype(jnp.float32)).astype(jnp.bfloat16)
        out_ref[sample, 0:seq_len, :] = site
        spin = heads_ref[sample, seq_len:skipped, :].astype(jnp.float32)
        embed = embed + matmul((spin == which).astype(jnp.bfloat16), site)
    high = embed.astype(jnp.bfloat16).astype(jnp.float32)
    low = embed - high
    tail = jnp.concatenate([high[: TAIL // 2], low[: TAIL // 2]], axis=0).astype(jnp.bfloat16)
    for sample in range(count):
        out_ref[sample, seq_len:skipped, :] = tail


def unpack_kernel(count, parts_ref, weight_ref, site_ref, embed_ref):
    seq_len = site_ref.shape[2]
    skipped = seq_len + TAIL
    for peer in range(count):
        cols = slice(peer * HEAD, (peer + 1) * HEAD)
        weight_ref[0, :, cols] = parts_ref[peer, skipped:, :].astype(jnp.float32)
        site_ref[0, 0, :, cols] = parts_ref[peer, 0:seq_len, :]
        tail = parts_ref[peer, seq_len:skipped, :].astype(jnp.float32)
        embed_ref[:, cols] = (tail[: TAIL // 2] + tail[TAIL // 2 :])[:SPINS]


def exchanged(blocks):
    return lax.all_to_all(blocks, "samples", split_axis=0, concat_axis=0, tiled=True)


def head_sharded(
    stored_inputs, top_cotangent, layer_weights, block_layout, region_mask, partner_samples, spins
):
    count = lax.axis_size("samples")
    seq_len = stored_inputs.shape[2]
    shard_rows, half_width = layer_weights.shape[1:]
    scale = 4.0 / HEAD
    bf16, f32 = jnp.bfloat16, jnp.float32
    per_head = (count, seq_len, HEAD)
    lines = seq_len + TAIL
    share_axis = "groups" if lax.axis_size("groups") == 2 else None
    sent = shard_rows // 2 if share_axis else shard_rows
    laid = pltpu.VMEM((count * shard_rows, HEAD), bf16)

    up, down = ring_route(count, -1), ring_route(count, 1)
    block = top_cotangent[0]
    rows = seq_len // 2
    packed = on_core(
        functools.partial(pack_kernel, count, share_axis),
        jax.ShapeDtypeStruct((count, lines + sent, HEAD), bf16),
        [pl.BlockSpec(memory_space=pltpu.HBM)] * 2 + in_vmem(1),
        [pltpu.SemaphoreType.DMA((2, count))],
        micros=1,
    )(stored_inputs, layer_weights, spins)
    slots = {0: block}
    forward, backward = block, block
    for step in range(1, count // 2):
        forward = lax.ppermute(forward, "samples", up)
        backward = lax.ppermute(backward, "samples", down)
        slots[count - step] = forward
        slots[step] = backward
    heads = exchanged(packed)
    shared = []
    if share_axis:
        shared = [lax.ppermute(heads[:, lines:], share_axis, [(0, 1), (1, 0)])]
    small = (region_mask.reshape(1, seq_len), partner_samples)
    attended, probs = on_core(
        functools.partial(forward_kernel, count, scale),
        [jax.ShapeDtypeStruct(per_head, bf16), jax.ShapeDtypeStruct(per_head, f32)],
        in_vmem(2) + in_smem(2),
        micros=3.3,
    )(heads, *small, block_layout)
    forward, backward, attended = lax.optimization_barrier((forward, backward, attended))
    far = [
        lax.ppermute(forward[:rows], "samples", up),
        lax.ppermute(backward[rows:], "samples", down),
    ]
    near = [slots[slot] for slot in range(count) if slot != count // 2]
    swap = [(0, 1), (1, 0)]
    near_sibling = [lax.ppermute(piece, "mp", swap) for piece in near]
    partial, near_attn = on_core(
        functools.partial(near_products_kernel, count, share_axis),
        [
            jax.ShapeDtypeStruct((count, HEAD, shard_rows), f32),
            jax.ShapeDtypeStruct(((count - 1) * seq_len, HEAD), bf16),
        ],
        in_vmem(2 * count + len(shared)),
        [laid],
        micros=2.5,
    )(*near, *near_sibling, heads, attended, *shared)
    far[0], far[1], partial, near_attn = lax.optimization_barrier((*far, partial, near_attn))
    far_sibling = [lax.ppermute(piece, "mp", swap) for piece in far]
    near_grads = on_core(
        functools.partial(near_back_kernel, count, scale),
        jax.ShapeDtypeStruct((count - 1, seq_len, HEAD), bf16),
        in_vmem(count + 3) + in_smem(1),
        micros=2.5,
    )(*near, heads, probs, near_attn, *small)
    terms = on_core(
        functools.partial(far_kernel, count, scale, share_axis),
        jax.ShapeDtypeStruct((count, lines + shard_rows, HEAD), bf16),
        in_vmem(10) + in_smem(1) + in_vmem(len(shared)),
        [laid, pltpu.VMEM(per_head, bf16)],
        micros=1.9,
    )(*far, *far_sibling, heads, probs, attended, partial, near_grads, *small, *shared)
    return on_core(
        functools.partial(unpack_kernel, count),
        [
            jax.ShapeDtypeStruct((1, shard_rows, half_width), f32),
            jax.ShapeDtypeStruct((1, 1, seq_len, half_width), bf16),
            jax.ShapeDtypeStruct((SPINS, half_width), f32),
        ],
        in_vmem(1),
        micros=1.2,
    )(exchanged(terms))


def solution(mesh):
    in_specs = (
        P("section", ("groups", "samples"), None, "mp"),
        P(("groups", "samples"), None, "mp"),
        P("section", "samples", "mp"),
        P("section", None, None),
        P(),
        P("groups"),
        P(("groups", "samples"), None),
    )
    out_specs = (
        P(("groups", "section"), "samples", "mp"),
        P("section", ("groups", "samples"), None, "mp"),
        P("groups", "mp"),
    )
    shards = mesh.shape["samples"]

    def whole(stored_inputs, top_cotangent, *rest):
        samples, _, width = top_cotangent.shape
        layer_count = stored_inputs.shape[0]
        one_each = samples == mesh.shape["groups"] * shards and layer_count == 1
        by_heads = one_each and shards % 2 == 0 and width == mesh.shape["mp"] * shards * HEAD
        return jax.shard_map(
            head_sharded if by_heads else local,
            mesh=mesh,
            in_specs=in_specs,
            out_specs=out_specs,
            check_vma=False,
        )(stored_inputs, top_cotangent, *rest)

    return whole
```

```python
import functools

import jax
import jax.numpy as jnp
from jax import lax
from jax.experimental import pallas as pl
from jax.experimental.pallas import tpu as pltpu
from jax.sharding import PartitionSpec as P

HEAD = 128
BLOCK = 64
SPINS = 2
TAIL = 16
FLOPS_PER_MICRO = 1.15e9


def for_sending(value):

    def short(part):
        return part.astype(jnp.bfloat16) if part.dtype == jnp.float32 else part

    return jax.tree.map(short, value)


def passed_along(block, axis, distance):
    devices = range(lax.axis_size(axis))
    route = [(i - distance, i) for i in devices if i - distance in devices]
    return lax.ppermute(block, axis, route)


def softmax_parts(inputs_h, allowed, attention_scale):
    scores = (
        jnp.einsum("qhd,khd->hqk", inputs_h, inputs_h, preferred_element_type=jnp.float32)
        * attention_scale
    )
    scores = jnp.where(allowed[None], scores, -jnp.inf)
    top_score = jnp.max(scores, axis=-1, keepdims=True)
    expo_terms = jnp.exp(scores - top_score)
    probs = expo_terms / jnp.sum(expo_terms, axis=-1, keepdims=True)
    return (probs, probs.astype(jnp.bfloat16))


def local(
    stored_inputs, top_cotangent, layer_weights, block_layout, region_mask, partner_samples, spins
):
    section_index = lax.axis_index("section")
    section_count = lax.axis_size("section")
    micro_count = stored_inputs.shape[1]
    seq_len = stored_inputs.shape[2]
    half_width = stored_inputs.shape[3]
    head_count = half_width // HEAD
    attention_scale = 4.0 / HEAD
    weights = lax.all_gather(layer_weights[0], "samples", axis=0, tiled=True)
    pos_block = jnp.arange(seq_len) // BLOCK
    block_onehot = (pos_block[:, None] == jnp.arange(block_layout.shape[1])[None, :]).astype(
        jnp.float32
    )
    linked = jnp.dot(jnp.dot(block_onehot, block_layout[0].astype(jnp.float32)), block_onehot.T)
    allowed = (linked > 0.5) | (pos_block[:, None] == pos_block[None, :])
    every_layer_input = stored_inputs[0]
    inputs_h = every_layer_input[0].reshape(seq_len, head_count, HEAD)
    probs, probs_low = softmax_parts(inputs_h, allowed, attention_scale)
    attended = jnp.einsum(
        "hqk,khd->qhd", probs_low, inputs_h, preferred_element_type=jnp.float32
    ).astype(jnp.bfloat16)
    probs_list = [probs]
    low_list = [probs_low]
    attend_list = [attended.reshape(seq_len, half_width)]
    probs_all = jnp.stack(probs_list)
    low_all = jnp.stack(low_list)
    attend_store = jnp.stack(attend_list)

    def layer_back(grad_full, grad_own, inputs, probs, probs_low):
        grad_attn = jnp.dot(grad_full, weights, preferred_element_type=jnp.float32).astype(
            jnp.bfloat16
        )
        inputs_h = inputs.reshape(seq_len, head_count, HEAD)
        grad_h = grad_attn.reshape(seq_len, head_count, HEAD)
        grad_probs = jnp.einsum(
            "qhd,khd->hqk", grad_h, inputs_h, preferred_element_type=jnp.float32
        )
        grad_scores = (
            probs * (grad_probs - jnp.sum(grad_probs * probs, axis=-1, keepdims=True))
        ).astype(jnp.bfloat16)
        through = jnp.einsum("hqk,qhd->khd", probs_low, grad_h, preferred_element_type=jnp.float32)
        through = through + attention_scale * (
            jnp.einsum("hqk,khd->qhd", grad_scores, inputs_h, preferred_element_type=jnp.float32)
            + jnp.einsum("hqk,qhd->khd", grad_scores, inputs_h, preferred_element_type=jnp.float32)
        )
        grad_in = grad_own.astype(jnp.float32) + through.reshape(seq_len, half_width)
        return grad_in.astype(jnp.bfloat16)

    def resting(grad_full, grad_own, inputs, probs, probs_low):
        return jnp.zeros((seq_len, half_width), jnp.bfloat16)

    carried_state = jnp.zeros((seq_len, half_width), jnp.bfloat16)
    out_list = []
    grad_list = []
    total_steps = micro_count + section_count - 1
    for step_number in range(total_steps):
        micro_index = step_number - (section_count - 1 - section_index)
        active = (micro_index >= 0) & (micro_index < micro_count)
        slot_index = jnp.clip(micro_index, 0, micro_count - 1)
        from_top = lax.dynamic_index_in_dim(top_cotangent, slot_index, 0, keepdims=False)
        incoming = jnp.where(section_index == section_count - 1, from_top, carried_state)
        grad_full = lax.all_gather(incoming, "mp", axis=1, tiled=True)
        inputs_now = lax.dynamic_index_in_dim(every_layer_input, slot_index, 0, keepdims=False)
        probs_now = lax.dynamic_index_in_dim(probs_all, slot_index, 0, keepdims=False)
        low_now = lax.dynamic_index_in_dim(low_all, slot_index, 0, keepdims=False)
        grad_in = lax.cond(
            active, layer_back, resting, grad_full, incoming, inputs_now, probs_now, low_now
        )
        out_list.append(grad_in)
        grad_list.append(grad_full)
        if step_number < total_steps - 1:
            carried_state = jax.tree.map(
                lambda part, own: part.astype(own.dtype),
                passed_along(for_sending(grad_in), "section", -1),
                grad_in,
            )
    offset = section_count - 1 - section_index
    out_store = lax.dynamic_slice_in_dim(jnp.stack(out_list), offset, micro_count, 0)
    grad_store = lax.dynamic_slice_in_dim(jnp.stack(grad_list), offset, micro_count, 0)
    summed_weight = lax.psum_scatter(
        jnp.einsum(
            "mtf,mta->fa", grad_store, attend_store, preferred_element_type=jnp.float32
        ).astype(jnp.bfloat16),
        "samples",
        scatter_dimension=0,
        tiled=True,
    ).astype(jnp.float32)
    region_count = seq_len // 2
    rank_in_region = jnp.cumsum(region_mask) - 1
    select = (
        (rank_in_region[None, :] == jnp.arange(region_count)[:, None]) & (region_mask[None, :] > 0)
    ).astype(jnp.bfloat16)
    tiles = jnp.einsum("at,mtd->mad", select, out_store, preferred_element_type=jnp.float32).astype(
        jnp.bfloat16
    )
    shard_index = lax.axis_index("samples")
    my_partners = lax.dynamic_slice_in_dim(
        partner_samples, shard_index * micro_count, micro_count, 0
    )
    shard_count = lax.axis_size("samples")
    dest_shard = my_partners // micro_count
    dest_slot = my_partners % micro_count
    route = (
        (dest_shard[:, None, None] == jnp.arange(shard_count)[None, :, None])
        & (dest_slot[:, None, None] == jnp.arange(micro_count)[None, None, :])
    ).astype(jnp.bfloat16)
    outgoing = jnp.einsum("mku,mad->kuad", route, tiles, preferred_element_type=jnp.float32).astype(
        jnp.bfloat16
    )
    arrived = lax.all_to_all(outgoing, "samples", split_axis=0, concat_axis=0, tiled=True)
    ones_row = jnp.ones((shard_count,), jnp.bfloat16)
    received = jnp.einsum(
        "k,kuad->uad", ones_row, arrived, preferred_element_type=jnp.float32
    ).astype(jnp.bfloat16)
    placed = jnp.einsum("at,mad->mtd", select, received, preferred_element_type=jnp.float32)
    kept = jnp.where(region_mask[None, :, None] > 0, jnp.zeros_like(out_store), out_store)
    site_cot = (kept.astype(jnp.float32) + placed).astype(jnp.bfloat16)
    cotangents = jnp.where(section_index == 0, site_cot, out_store)
    onehot = (spins[:, :, None] == jnp.arange(SPINS)[None, None, :]).astype(jnp.bfloat16)
    embed_term = jnp.einsum("mtv,mtd->vd", onehot, site_cot, preferred_element_type=jnp.float32)
    embed_term = jnp.where(section_index == 0, embed_term, jnp.zeros_like(embed_term))
    embed_grad = lax.psum(embed_term, ("samples", "section"))
    return (summed_weight[None], cotangents[None], embed_grad)


def ring_sample(place, count):
    return jnp.where(place < count // 2, 2 * place, 2 * (count - place) - 1)


def ring_place(sample, count):
    return jnp.where(lax.rem(sample, 2) == 0, sample // 2, count - 1 - sample // 2)


def ring_route(count, distance):
    order = list(range(0, count, 2)) + list(range(1, count, 2))[::-1]
    return [(order[i], order[(i - distance) % count]) for i in range(count)]


def own_place(count):
    return ring_place(lax.axis_index("samples"), count)


def peer_at(place, distance, count):
    return ring_sample(lax.rem(place + distance + count, count), count)


def columns(index, size):
    return pl.ds(pl.multiple_of(index * size, size), size)


def in_vmem(count):
    return [pl.BlockSpec(memory_space=pltpu.VMEM)] * count


def in_smem(count):
    return [pl.BlockSpec(memory_space=pltpu.SMEM)] * count


def on_core(body, out_shapes, in_specs, scratch=(), micros=1, vmem=40):
    return pl.pallas_call(
        body,
        out_shape=out_shapes,
        in_specs=in_specs,
        out_specs=jax.tree.map(lambda _: pl.BlockSpec(memory_space=pltpu.VMEM), out_shapes),
        scratch_shapes=list(scratch),
        compiler_params=pltpu.CompilerParams(vmem_limit_bytes=vmem << 20),
        cost_estimate=pl.CostEstimate(
            flops=int(micros * FLOPS_PER_MICRO), bytes_accessed=1 << 16, transcendentals=0
        ),
    )


def matmul(left, right):
    return jnp.dot(left, right, preferred_element_type=jnp.float32)


def matmul_t(left, right):
    return lax.dot_general(
        left, right, (((1,), (1,)), ((), ())), preferred_element_type=jnp.float32
    )


def pack_kernel(count, share_axis, x_ref, w_ref, spins_ref, out_ref, sems):
    seq_len = x_ref.shape[2]
    skipped = seq_len + TAIL
    sent = out_ref.shape[1] - skipped
    rows = columns(lax.axis_index(share_axis), sent) if share_axis else slice(None)
    copies = []
    for peer in range(count):
        cols = slice(peer * HEAD, (peer + 1) * HEAD)
        head, weight = out_ref.at[peer, 0:seq_len, :], out_ref.at[peer, skipped:, :]
        copies.append(pltpu.make_async_copy(x_ref.at[0, 0, :, cols], head, sems.at[0, peer]))
        copies.append(pltpu.make_async_copy(w_ref.at[0, rows, cols], weight, sems.at[1, peer]))
    for copy in copies:
        copy.start()
    spin_rows = jnp.broadcast_to(spins_ref[...].astype(jnp.float32), (TAIL, seq_len))
    for peer in range(count):
        out_ref[peer, seq_len:skipped, :] = spin_rows.astype(jnp.bfloat16)
    for copy in copies:
        copy.wait()


def forward_kernel(count, scale, *refs):
    heads_ref, layout_ref = refs[0], refs[-5]
    attended_ref, probs_ref, keep_ref, send_ref = refs[-4:]
    seq_len = probs_ref.shape[1]
    half = lax.axis_index("mp")
    per_half = count // 2
    for part in range(per_half):
        keep_ref[part] = heads_ref[half * per_half + part, seq_len + TAIL :, :]
        send_ref[part] = heads_ref[(1 - half) * per_half + part, seq_len + TAIL :, :]
    blocks = layout_ref.shape[1]
    rows = lax.broadcasted_iota(jnp.int32, (seq_len, seq_len), 0) // BLOCK
    cols = lax.broadcasted_iota(jnp.int32, (seq_len, seq_len), 1) // BLOCK
    seen = rows == cols
    for q in range(blocks):
        for k in range(blocks):
            if q != k:
                seen = seen | ((rows == q) & (cols == k) & (layout_ref[0, q, k] > 0))
    for slot in range(count):
        x = heads_ref[slot, 0:seq_len, :]
        scores = jnp.where(seen, matmul_t(x, x) * scale, -jnp.inf)
        terms = jnp.exp(scores - jnp.max(scores, axis=-1, keepdims=True))
        probs = terms / jnp.sum(terms, axis=-1, keepdims=True)
        probs_ref[slot] = probs
        attended_ref[slot] = matmul(probs.astype(jnp.bfloat16), x).astype(jnp.bfloat16)


def lay_weights(weights, shares, share_axis):
    index = lax.axis_index(share_axis) if share_axis else 0
    parts, sent = shares[0].shape[:2]
    pieces = len(shares) // 2
    for number, share in enumerate(shares):
        head, piece = number % 2, number // 2
        place = index if piece == 0 else 1 - index
        for part in range(parts):
            rows = pl.ds(pl.multiple_of((part * pieces + place) * sent, sent), sent)
            weights[rows, head * HEAD : (head + 1) * HEAD] = share[part]


def weight_term(pieces, left, cols):
    total = None
    for index, first in enumerate(range(0, len(pieces), 2)):
        rows = [piece[:, cols] for slot in pieces[first : first + 2] for piece in slot]
        term = matmul(left[index], jnp.concatenate(rows, axis=0))
        total = term if total is None else total + term
    return total


def both_heads(own_ref, sibling_ref, samples):
    rows = [jnp.concatenate([own_ref[i], sibling_ref[i]], axis=1) for i in samples]
    return transposed(jnp.concatenate(rows, axis=0))


def transposed(value):
    return value.astype(jnp.float32).T.astype(jnp.bfloat16)


def attention_back(scale, x, probs, grad_attn, above):
    grad_probs = matmul_t(grad_attn, x)
    inner = jnp.sum(grad_probs * probs, axis=-1, keepdims=True)
    grad_scores = (probs * (grad_probs - inner)).astype(jnp.bfloat16).astype(jnp.float32)
    both = jnp.concatenate([grad_scores, grad_scores.T], axis=1).astype(jnp.bfloat16)
    through = matmul(transposed(probs.astype(jnp.bfloat16)), grad_attn)
    through = through + scale * matmul(both, jnp.concatenate([x, x], axis=0))
    return (above.astype(jnp.float32) + through).astype(jnp.bfloat16)


def near_slots(count):
    return [slot for slot in range(count) if slot != count // 2]


def by_slot(refs, sizes):
    pieces, first = [], 0
    for size in sizes:
        pieces.append(refs[first : first + size])
        first += size
    return pieces, refs[first:]


def near_products_kernel(count, sizes, share_axis, *refs):
    pieces, refs = by_slot(refs, sizes)
    attended_ref, sibling_ref = refs[:2]
    shares = refs[2:-5]
    partial_ref, own_ref, other_ref, above_ref, weights = refs[-5:]
    place = own_place(count)
    shard = lax.axis_index("samples")
    parts, _, shard_rows = partial_ref.shape
    seq_len = attended_ref.shape[1]
    sample_of = [peer_at(place, slot, count) for slot in near_slots(count)]
    lay_weights(weights, shares, share_axis)
    left = [
        both_heads(attended_ref, sibling_ref, sample_of[first : first + 2])
        for first in range(0, count - 1, 2)
    ]
    for part in range(parts):
        cols = slice(part * shard_rows, (part + 1) * shard_rows)
        partial_ref[part] = weight_term(pieces, left, cols)
    for first in range(0, count - 1, 2):
        rows = [piece[...] for slot in pieces[first : first + 2] for piece in slot]
        total = matmul(jnp.concatenate(rows, axis=0), weights[...])
        lines = slice(first * seq_len, first * seq_len + total.shape[0])
        own_ref[lines, :] = total[:, :HEAD]
        other_ref[lines, :] = total[:, HEAD:].astype(jnp.bfloat16)
    for index, slot in enumerate(pieces):
        rows = [piece[:, columns(shard, HEAD)] for piece in slot]
        above_ref[index * seq_len : (index + 1) * seq_len, :] = jnp.concatenate(rows, axis=0)


def near_back_kernel(count, scale, *refs):
    heads_ref, probs_ref, own_ref, other_ref, above_ref, _, _, grads_ref = refs
    place = own_place(count)
    seq_len = probs_ref.shape[1]
    for index, slot in enumerate(near_slots(count)):
        sample = peer_at(place, slot, count)
        lines = slice(index * seq_len, (index + 1) * seq_len)
        grads_ref[index] = attention_back(
            scale,
            heads_ref[sample, 0:seq_len, :],
            probs_ref[sample],
            (own_ref[lines, :] + other_ref[lines, :].astype(jnp.float32)).astype(jnp.bfloat16),
            above_ref[lines, :],
        )


def far_products_kernel(count, *refs):
    piece, refs = refs[:2], refs[2:]
    attended_ref, sibling_ref, partial_ref, weights_ref = refs[:4]
    send_ref, keep_ref, own_ref, above_ref = refs[4:]
    sample = peer_at(own_place(count), count // 2, count)
    shard = lax.axis_index("samples")
    parts, _, shard_rows = partial_ref.shape
    left = [both_heads(attended_ref, sibling_ref, [sample])]
    for part in range(parts):
        cols = slice(part * shard_rows, (part + 1) * shard_rows)
        total = transposed(partial_ref[part] + weight_term([piece], left, cols))
        keep_ref[part] = total[:, :HEAD]
        send_ref[cols, :] = total[:, HEAD:]
    total = matmul(jnp.concatenate([rows[...] for rows in piece], axis=0), weights_ref[...])
    own_ref[...] = total[:, :HEAD]
    send_ref[parts * shard_rows :, :] = total[:, HEAD:].astype(jnp.bfloat16)
    cols = columns(shard, HEAD)
    above_ref[...] = jnp.concatenate([rows[:, cols] for rows in piece], axis=0)


def far_kernel(count, scale, *refs):
    came_ref, keep_ref, own_ref, above_ref, heads_ref, probs_ref = refs[:6]
    near_ref, mask_ref, partner_ref, out_ref, grads = refs[6:]
    place = own_place(count)
    half = lax.axis_index("mp")
    seq_len = probs_ref.shape[1]
    skipped = seq_len + TAIL
    parts, shard_rows = keep_ref.shape[:2]
    for part in range(parts):
        out_ref[half * parts + part, skipped:, :] = keep_ref[part]
        lines = slice(part * shard_rows, (part + 1) * shard_rows)
        out_ref[(1 - half) * parts + part, skipped:, :] = came_ref[lines, :]
    for index, slot in enumerate(near_slots(count)):
        grads[peer_at(place, slot, count)] = near_ref[index]
    sample = peer_at(place, count // 2, count)
    other = came_ref[parts * shard_rows :, :].astype(jnp.float32)
    grads[sample] = attention_back(
        scale,
        heads_ref[sample, 0:seq_len, :],
        probs_ref[sample],
        (own_ref[...] + other).astype(jnp.bfloat16),
        above_ref[...],
    )
    region = jnp.broadcast_to(mask_ref[...].astype(jnp.float32), (HEAD, seq_len)).T > 0.5
    which = lax.broadcasted_iota(jnp.int32, (TAIL, seq_len), 0).astype(jnp.float32)
    embed = jnp.zeros((TAIL, HEAD), jnp.float32)
    for sample in range(count):
        swapped = grads[partner_ref[sample]].astype(jnp.float32)
        site = jnp.where(region, swapped, grads[sample].astype(jnp.float32)).astype(jnp.bfloat16)
        out_ref[sample, 0:seq_len, :] = site
        spin = heads_ref[sample, seq_len:skipped, :].astype(jnp.float32)
        embed = embed + matmul((spin == which).astype(jnp.bfloat16), site)
    high = embed.astype(jnp.bfloat16).astype(jnp.float32)
    low = embed - high
    tail = jnp.concatenate([high[: TAIL // 2], low[: TAIL // 2]], axis=0).astype(jnp.bfloat16)
    for sample in range(count):
        out_ref[sample, seq_len:skipped, :] = tail


def unpack_kernel(count, parts_ref, weight_ref, site_ref, embed_ref):
    seq_len = site_ref.shape[2]
    skipped = seq_len + TAIL
    for peer in range(count):
        cols = slice(peer * HEAD, (peer + 1) * HEAD)
        weight_ref[0, :, cols] = parts_ref[peer, skipped:, :].astype(jnp.float32)
        site_ref[0, 0, :, cols] = parts_ref[peer, 0:seq_len, :]
        tail = parts_ref[peer, seq_len:skipped, :].astype(jnp.float32)
        embed_ref[:, cols] = (tail[: TAIL // 2] + tail[TAIL // 2 :])[:SPINS]


def exchanged(blocks):
    return lax.all_to_all(blocks, "samples", split_axis=0, concat_axis=0, tiled=True)


def head_sharded(
    stored_inputs, top_cotangent, layer_weights, block_layout, region_mask, partner_samples, spins
):
    count = lax.axis_size("samples")
    seq_len = stored_inputs.shape[2]
    shard_rows, half_width = layer_weights.shape[1:]
    scale = 4.0 / HEAD
    bf16, f32 = jnp.bfloat16, jnp.float32
    per_head = (count, seq_len, HEAD)
    lines = seq_len + TAIL
    share_axis = "groups" if lax.axis_size("groups") == 2 else None
    sent = shard_rows // 2 if share_axis else shard_rows
    parts = count // 2
    swap = [(0, 1), (1, 0)]

    up, down = ring_route(count, -1), ring_route(count, 1)
    block = top_cotangent[0]
    rows = seq_len // 2
    packed = on_core(
        functools.partial(pack_kernel, count, share_axis),
        jax.ShapeDtypeStruct((count, lines + sent, HEAD), bf16),
        [pl.BlockSpec(memory_space=pltpu.HBM)] * 2 + in_vmem(1),
        [pltpu.SemaphoreType.DMA((2, count))],
        micros=1,
        vmem=60,
    )(stored_inputs, layer_weights, spins)
    moving = {(route, chunk): block[chunk * rows : (chunk + 1) * rows] for route in (0, 1) for chunk in (0, 1)}
    slots = {0: (block,)}
    for step in range(1, count // 2 + 1):
        for route, chunk in ((0, 0), (1, 1), (0, 1), (1, 0)):
            if step < count // 2 or route == chunk:
                moving[route, chunk] = lax.ppermute(
                    moving[route, chunk], "samples", (up, down)[route]
                )
        if step == 1:
            moving[0, 0], moving[1, 1], packed = lax.optimization_barrier(
                (moving[0, 0], moving[1, 1], packed)
            )
        if step < count // 2:
            slots[count - step] = (moving[0, 0], moving[0, 1])
            slots[step] = (moving[1, 0], moving[1, 1])
        else:
            slots[step] = (moving[0, 0], moving[1, 1])
    heads = exchanged(packed)
    small = (region_mask.reshape(1, seq_len), partner_samples)
    share_shape = jax.ShapeDtypeStruct((parts, sent, HEAD), bf16)
    attended, probs, keep, send = on_core(
        functools.partial(forward_kernel, count, scale),
        [
            jax.ShapeDtypeStruct(per_head, bf16),
            jax.ShapeDtypeStruct(per_head, f32),
            share_shape,
            share_shape,
        ],
        in_vmem(2) + in_smem(2),
        micros=3.3,
    )(heads, *small, block_layout)
    shares = [keep, lax.ppermute(send, "mp", swap)]
    if share_axis:
        shares.append(lax.ppermute(keep, share_axis, swap))
        shares.append(
            lax.ppermute(send, (share_axis, "mp"), [(0, 3), (1, 2), (2, 1), (3, 0)])
        )
    attended_sibling = lax.ppermute(attended, "mp", swap)

    near = [piece for slot in near_slots(count) for piece in slots[slot]]
    sizes = [len(slots[slot]) for slot in near_slots(count)]
    near_lines = (count - 1) * seq_len
    partial, near_own, near_other, near_above, weights = on_core(
        functools.partial(near_products_kernel, count, sizes, share_axis),
        [
            jax.ShapeDtypeStruct((parts, 2 * HEAD, shard_rows), f32),
            jax.ShapeDtypeStruct((near_lines, HEAD), f32),
            jax.ShapeDtypeStruct((near_lines, HEAD), bf16),
            jax.ShapeDtypeStruct((near_lines, HEAD), bf16),
            jax.ShapeDtypeStruct((half_width, 2 * HEAD), bf16),
        ],
        in_vmem(len(near) + 2 + len(shares)),
        micros=2,
    )(*near, attended, attended_sibling, *shares)
    near_other = lax.ppermute(near_other, "mp", swap)
    near_grads = on_core(
        functools.partial(near_back_kernel, count, scale),
        jax.ShapeDtypeStruct((count - 1, seq_len, HEAD), bf16),
        in_vmem(6) + in_smem(1),
        micros=2.9,
    )(heads, probs, near_own, near_other, near_above, *small)
    far_send, far_keep, far_own, far_above = on_core(
        functools.partial(far_products_kernel, count),
        [
            jax.ShapeDtypeStruct((half_width + seq_len, HEAD), bf16),
            jax.ShapeDtypeStruct((parts, shard_rows, HEAD), bf16),
            jax.ShapeDtypeStruct((seq_len, HEAD), f32),
            jax.ShapeDtypeStruct((seq_len, HEAD), bf16),
        ],
        in_vmem(6),
        micros=1,
    )(*slots[count // 2], attended, attended_sibling, partial, weights)
    far_came = lax.ppermute(far_send, "mp", swap)
    terms = on_core(
        functools.partial(far_kernel, count, scale),
        jax.ShapeDtypeStruct((count, lines + shard_rows, HEAD), bf16),
        in_vmem(8) + in_smem(1),
        [pltpu.VMEM(per_head, bf16)],
        micros=1.5,
    )(far_came, far_keep, far_own, far_above, heads, probs, near_grads, *small)
    return on_core(
        functools.partial(unpack_kernel, count),
        [
            jax.ShapeDtypeStruct((1, shard_rows, half_width), f32),
            jax.ShapeDtypeStruct((1, 1, seq_len, half_width), bf16),
            jax.ShapeDtypeStruct((SPINS, half_width), f32),
        ],
        in_vmem(1),
        micros=1.2,
    )(exchanged(terms))


def solution(mesh):
    in_specs = (
        P("section", ("groups", "samples"), None, "mp"),
        P(("groups", "samples"), None, "mp"),
        P("section", "samples", "mp"),
        P("section", None, None),
        P(),
        P("groups"),
        P(("groups", "samples"), None),
    )
    out_specs = (
        P(("groups", "section"), "samples", "mp"),
        P("section", ("groups", "samples"), None, "mp"),
        P("groups", "mp"),
    )
    shards = mesh.shape["samples"]

    def whole(stored_inputs, top_cotangent, *rest):
        samples, _, width = top_cotangent.shape
        layer_count = stored_inputs.shape[0]
        one_each = samples == mesh.shape["groups"] * shards and layer_count == 1
        by_heads = one_each and shards % 2 == 0 and width == mesh.shape["mp"] * shards * HEAD
        return jax.shard_map(
            head_sharded if by_heads else local,
            mesh=mesh,
            in_specs=in_specs,
            out_specs=out_specs,
            check_vma=False,
        )(stored_inputs, top_cotangent, *rest)

    return whole
```

```python
import functools

import jax
import jax.numpy as jnp
from jax import lax
from jax.experimental import pallas as pl
from jax.experimental.pallas import tpu as pltpu
from jax.sharding import PartitionSpec as P

HEAD = 128
BLOCK = 64
SPINS = 2
TAIL = 16
FLOPS_PER_MICRO = 1.15e9


def for_sending(value):

    def short(part):
        return part.astype(jnp.bfloat16) if part.dtype == jnp.float32 else part

    return jax.tree.map(short, value)


def passed_along(block, axis, distance):
    devices = range(lax.axis_size(axis))
    route = [(i - distance, i) for i in devices if i - distance in devices]
    return lax.ppermute(block, axis, route)


def softmax_parts(inputs_h, allowed, attention_scale):
    scores = (
        jnp.einsum("qhd,khd->hqk", inputs_h, inputs_h, preferred_element_type=jnp.float32)
        * attention_scale
    )
    scores = jnp.where(allowed[None], scores, -jnp.inf)
    top_score = jnp.max(scores, axis=-1, keepdims=True)
    expo_terms = jnp.exp(scores - top_score)
    probs = expo_terms / jnp.sum(expo_terms, axis=-1, keepdims=True)
    return (probs, probs.astype(jnp.bfloat16))


def local(
    stored_inputs, top_cotangent, layer_weights, block_layout, region_mask, partner_samples, spins
):
    section_index = lax.axis_index("section")
    section_count = lax.axis_size("section")
    micro_count = stored_inputs.shape[1]
    seq_len = stored_inputs.shape[2]
    half_width = stored_inputs.shape[3]
    head_count = half_width // HEAD
    attention_scale = 4.0 / HEAD
    weights = lax.all_gather(layer_weights[0], "samples", axis=0, tiled=True)
    pos_block = jnp.arange(seq_len) // BLOCK
    block_onehot = (pos_block[:, None] == jnp.arange(block_layout.shape[1])[None, :]).astype(
        jnp.float32
    )
    linked = jnp.dot(jnp.dot(block_onehot, block_layout[0].astype(jnp.float32)), block_onehot.T)
    allowed = (linked > 0.5) | (pos_block[:, None] == pos_block[None, :])
    every_layer_input = stored_inputs[0]
    inputs_h = every_layer_input[0].reshape(seq_len, head_count, HEAD)
    probs, probs_low = softmax_parts(inputs_h, allowed, attention_scale)
    attended = jnp.einsum(
        "hqk,khd->qhd", probs_low, inputs_h, preferred_element_type=jnp.float32
    ).astype(jnp.bfloat16)
    probs_list = [probs]
    low_list = [probs_low]
    attend_list = [attended.reshape(seq_len, half_width)]
    probs_all = jnp.stack(probs_list)
    low_all = jnp.stack(low_list)
    attend_store = jnp.stack(attend_list)

    def layer_back(grad_full, grad_own, inputs, probs, probs_low):
        grad_attn = jnp.dot(grad_full, weights, preferred_element_type=jnp.float32).astype(
            jnp.bfloat16
        )
        inputs_h = inputs.reshape(seq_len, head_count, HEAD)
        grad_h = grad_attn.reshape(seq_len, head_count, HEAD)
        grad_probs = jnp.einsum(
            "qhd,khd->hqk", grad_h, inputs_h, preferred_element_type=jnp.float32
        )
        grad_scores = (
            probs * (grad_probs - jnp.sum(grad_probs * probs, axis=-1, keepdims=True))
        ).astype(jnp.bfloat16)
        through = jnp.einsum("hqk,qhd->khd", probs_low, grad_h, preferred_element_type=jnp.float32)
        through = through + attention_scale * (
            jnp.einsum("hqk,khd->qhd", grad_scores, inputs_h, preferred_element_type=jnp.float32)
            + jnp.einsum("hqk,qhd->khd", grad_scores, inputs_h, preferred_element_type=jnp.float32)
        )
        grad_in = grad_own.astype(jnp.float32) + through.reshape(seq_len, half_width)
        return grad_in.astype(jnp.bfloat16)

    def resting(grad_full, grad_own, inputs, probs, probs_low):
        return jnp.zeros((seq_len, half_width), jnp.bfloat16)

    carried_state = jnp.zeros((seq_len, half_width), jnp.bfloat16)
    out_list = []
    grad_list = []
    total_steps = micro_count + section_count - 1
    for step_number in range(total_steps):
        micro_index = step_number - (section_count - 1 - section_index)
        active = (micro_index >= 0) & (micro_index < micro_count)
        slot_index = jnp.clip(micro_index, 0, micro_count - 1)
        from_top = lax.dynamic_index_in_dim(top_cotangent, slot_index, 0, keepdims=False)
        incoming = jnp.where(section_index == section_count - 1, from_top, carried_state)
        grad_full = lax.all_gather(incoming, "mp", axis=1, tiled=True)
        inputs_now = lax.dynamic_index_in_dim(every_layer_input, slot_index, 0, keepdims=False)
        probs_now = lax.dynamic_index_in_dim(probs_all, slot_index, 0, keepdims=False)
        low_now = lax.dynamic_index_in_dim(low_all, slot_index, 0, keepdims=False)
        grad_in = lax.cond(
            active, layer_back, resting, grad_full, incoming, inputs_now, probs_now, low_now
        )
        out_list.append(grad_in)
        grad_list.append(grad_full)
        if step_number < total_steps - 1:
            carried_state = jax.tree.map(
                lambda part, own: part.astype(own.dtype),
                passed_along(for_sending(grad_in), "section", -1),
                grad_in,
            )
    offset = section_count - 1 - section_index
    out_store = lax.dynamic_slice_in_dim(jnp.stack(out_list), offset, micro_count, 0)
    grad_store = lax.dynamic_slice_in_dim(jnp.stack(grad_list), offset, micro_count, 0)
    summed_weight = lax.psum_scatter(
        jnp.einsum(
            "mtf,mta->fa", grad_store, attend_store, preferred_element_type=jnp.float32
        ).astype(jnp.bfloat16),
        "samples",
        scatter_dimension=0,
        tiled=True,
    ).astype(jnp.float32)
    region_count = seq_len // 2
    rank_in_region = jnp.cumsum(region_mask) - 1
    select = (
        (rank_in_region[None, :] == jnp.arange(region_count)[:, None]) & (region_mask[None, :] > 0)
    ).astype(jnp.bfloat16)
    tiles = jnp.einsum("at,mtd->mad", select, out_store, preferred_element_type=jnp.float32).astype(
        jnp.bfloat16
    )
    shard_index = lax.axis_index("samples")
    my_partners = lax.dynamic_slice_in_dim(
        partner_samples, shard_index * micro_count, micro_count, 0
    )
    shard_count = lax.axis_size("samples")
    dest_shard = my_partners // micro_count
    dest_slot = my_partners % micro_count
    route = (
        (dest_shard[:, None, None] == jnp.arange(shard_count)[None, :, None])
        & (dest_slot[:, None, None] == jnp.arange(micro_count)[None, None, :])
    ).astype(jnp.bfloat16)
    outgoing = jnp.einsum("mku,mad->kuad", route, tiles, preferred_element_type=jnp.float32).astype(
        jnp.bfloat16
    )
    arrived = lax.all_to_all(outgoing, "samples", split_axis=0, concat_axis=0, tiled=True)
    ones_row = jnp.ones((shard_count,), jnp.bfloat16)
    received = jnp.einsum(
        "k,kuad->uad", ones_row, arrived, preferred_element_type=jnp.float32
    ).astype(jnp.bfloat16)
    placed = jnp.einsum("at,mad->mtd", select, received, preferred_element_type=jnp.float32)
    kept = jnp.where(region_mask[None, :, None] > 0, jnp.zeros_like(out_store), out_store)
    site_cot = (kept.astype(jnp.float32) + placed).astype(jnp.bfloat16)
    cotangents = jnp.where(section_index == 0, site_cot, out_store)
    onehot = (spins[:, :, None] == jnp.arange(SPINS)[None, None, :]).astype(jnp.bfloat16)
    embed_term = jnp.einsum("mtv,mtd->vd", onehot, site_cot, preferred_element_type=jnp.float32)
    embed_term = jnp.where(section_index == 0, embed_term, jnp.zeros_like(embed_term))
    embed_grad = lax.psum(embed_term, ("samples", "section"))
    return (summed_weight[None], cotangents[None], embed_grad)


def ring_sample(place, count):
    return jnp.where(place < count // 2, 2 * place, 2 * (count - place) - 1)


def ring_place(sample, count):
    return jnp.where(lax.rem(sample, 2) == 0, sample // 2, count - 1 - sample // 2)


def ring_route(count, distance):
    order = list(range(0, count, 2)) + list(range(1, count, 2))[::-1]
    return [(order[i], order[(i - distance) % count]) for i in range(count)]


def own_place(count):
    return ring_place(lax.axis_index("samples"), count)


def peer_at(place, distance, count):
    return ring_sample(lax.rem(place + distance + count, count), count)


def columns(index, size):
    return pl.ds(pl.multiple_of(index * size, size), size)


def in_vmem(count):
    return [pl.BlockSpec(memory_space=pltpu.VMEM)] * count


def in_smem(count):
    return [pl.BlockSpec(memory_space=pltpu.SMEM)] * count


def on_core(body, out_shapes, in_specs, scratch=(), micros=1, vmem=40):
    return pl.pallas_call(
        body,
        out_shape=out_shapes,
        in_specs=in_specs,
        out_specs=jax.tree.map(lambda _: pl.BlockSpec(memory_space=pltpu.VMEM), out_shapes),
        scratch_shapes=list(scratch),
        compiler_params=pltpu.CompilerParams(vmem_limit_bytes=vmem << 20),
        cost_estimate=pl.CostEstimate(
            flops=int(micros * FLOPS_PER_MICRO), bytes_accessed=1 << 16, transcendentals=0
        ),
    )


def matmul(left, right):
    return jnp.dot(left, right, preferred_element_type=jnp.float32)


def matmul_t(left, right):
    return lax.dot_general(
        left, right, (((1,), (1,)), ((), ())), preferred_element_type=jnp.float32
    )


def pack_kernel(count, share_axis, x_ref, w_ref, spins_ref, out_ref, sems):
    seq_len = x_ref.shape[2]
    skipped = seq_len + TAIL
    sent = out_ref.shape[1] - skipped
    rows = columns(lax.axis_index(share_axis), sent) if share_axis else slice(None)
    copies = []
    for peer in range(count):
        cols = slice(peer * HEAD, (peer + 1) * HEAD)
        head, weight = out_ref.at[peer, 0:seq_len, :], out_ref.at[peer, skipped:, :]
        copies.append(pltpu.make_async_copy(x_ref.at[0, 0, :, cols], head, sems.at[0, peer]))
        copies.append(pltpu.make_async_copy(w_ref.at[0, rows, cols], weight, sems.at[1, peer]))
    for copy in copies:
        copy.start()
    spin_rows = jnp.broadcast_to(spins_ref[...].astype(jnp.float32), (TAIL, seq_len))
    for peer in range(count):
        out_ref[peer, seq_len:skipped, :] = spin_rows.astype(jnp.bfloat16)
    for copy in copies:
        copy.wait()


def split_kernel(grad_ref, early_ref, late_ref, sems):
    parts = sems.shape[1]
    size = early_ref.shape[1] // parts
    copies = []
    for part in range(parts):
        cols = slice(part * size, (part + 1) * size)
        for chunk, out in enumerate((early_ref, late_ref)):
            first = (2 * part + chunk) * size
            source = grad_ref.at[0, :, first : first + size]
            copies.append(pltpu.make_async_copy(source, out.at[:, cols], sems.at[chunk, part]))
    for copy in copies:
        copy.start()
    for copy in copies:
        copy.wait()


def forward_kernel(count, scale, *refs):
    heads_ref, layout_ref = refs[0], refs[-6]
    attended_ref, probs_ref, turned_ref, keep_ref, send_ref = refs[-5:]
    seq_len = probs_ref.shape[1]
    half = lax.axis_index("mp")
    per_half = count // 2
    for part in range(per_half):
        keep_ref[part] = heads_ref[half * per_half + part, seq_len + TAIL :, :]
        send_ref[part] = heads_ref[(1 - half) * per_half + part, seq_len + TAIL :, :]
    blocks = layout_ref.shape[1]
    rows = lax.broadcasted_iota(jnp.int32, (seq_len, seq_len), 0) // BLOCK
    cols = lax.broadcasted_iota(jnp.int32, (seq_len, seq_len), 1) // BLOCK
    seen = rows == cols
    for q in range(blocks):
        for k in range(blocks):
            if q != k:
                seen = seen | ((rows == q) & (cols == k) & (layout_ref[0, q, k] > 0))
    xs = [heads_ref[slot, 0:seq_len, :] for slot in range(count)]
    scores = [jnp.where(seen, matmul_t(x, x) * scale, -jnp.inf) for x in xs]
    tops = [jnp.max(score, axis=-1, keepdims=True) for score in scores]
    terms = [jnp.exp(score - top) for score, top in zip(scores, tops)]
    sums = [jnp.sum(term, axis=-1, keepdims=True) for term in terms]
    for slot in range(count):
        probs = terms[slot] / sums[slot]
        low = probs.astype(jnp.bfloat16)
        probs_ref[slot] = probs
        attended_ref[slot] = matmul(low, xs[slot]).astype(jnp.bfloat16)
        turned_ref[slot] = transposed(low)


def lay_weights(weights, keep_ref, send_ref):
    for head, share in enumerate((keep_ref, send_ref)):
        parts, sent = share.shape[:2]
        for part in range(parts):
            weights[part * sent : (part + 1) * sent, head * HEAD : (head + 1) * HEAD] = share[part]


def weight_term(pieces, left, cols):
    total = None
    for index, first in enumerate(range(0, len(pieces), 2)):
        rows = [piece[:, cols] for slot in pieces[first : first + 2] for piece in slot]
        term = matmul(left[index], jnp.concatenate(rows, axis=0))
        total = term if total is None else total + term
    return total


def both_heads(own_ref, sibling_ref, samples):
    rows = [jnp.concatenate([own_ref[i], sibling_ref[i]], axis=1) for i in samples]
    return transposed(jnp.concatenate(rows, axis=0))


def transposed(value):
    return value.astype(jnp.float32).T.astype(jnp.bfloat16)


def by_slot(refs, count):
    far = count // 2
    pieces = [refs[slot : slot + 1] for slot in range(count)]
    pieces[far] = (refs[far], refs[count])
    return pieces, refs[count + 1 :]


def products(count, pieces, attended_ref, sibling_ref, parts, weights):
    place = own_place(count)
    sample_of = [peer_at(place, slot, count) for slot in range(count)]
    firsts = range(0, count, 2)
    left = [both_heads(attended_ref, sibling_ref, sample_of[first : first + 2]) for first in firsts]
    size = pieces[0][0].shape[1] // parts
    terms = []
    for part in range(parts):
        cols = slice(part * size, (part + 1) * size)
        terms.append(transposed(weight_term(pieces, left, cols)))
    sums = []
    for first in firsts:
        rows = [piece[...] for slot in pieces[first : first + 2] for piece in slot]
        sums.append(matmul(jnp.concatenate(rows, axis=0), weights[...]))
    return terms, sums


def early_kernel(count, *refs):
    pieces, refs = by_slot(refs, count)
    attended_ref, sibling_ref, w_keep_ref, w_send_ref = refs[:4]
    keep_ref, send_ref, total_ref, weights = refs[4:]
    lay_weights(weights, w_keep_ref, w_send_ref)
    parts = keep_ref.shape[0]
    terms, sums = products(count, pieces, attended_ref, sibling_ref, parts, weights)
    for part, term in enumerate(terms):
        keep_ref[part] = term[:, :HEAD]
        send_ref[part] = term[:, HEAD:]
    for index, value in enumerate(sums):
        total_ref[index] = value


def join_kernel(keep_ref, came_ref, out_ref):
    parts = keep_ref.shape[0]
    half = lax.axis_index("mp")
    for part in range(parts):
        out_ref[half * parts + part] = keep_ref[part]
        out_ref[(1 - half) * parts + part] = came_ref[part]


def late_kernel(count, *refs):
    pieces, refs = by_slot(refs, count)
    attended_ref, sibling_ref, w_keep_ref, w_send_ref, total_ref = refs[:5]
    keep_ref, send_ref, own_ref, weights = refs[5:]
    lay_weights(weights, w_keep_ref, w_send_ref)
    parts, size = keep_ref.shape[:2]
    terms, sums = products(count, pieces, attended_ref, sibling_ref, parts, weights)
    for part, term in enumerate(terms):
        keep_ref[part] = term[:, :HEAD]
        send_ref[part * size : (part + 1) * size, :] = term[:, HEAD:]
    for index, value in enumerate(sums):
        total = total_ref[index] + value
        lines = slice(index * total.shape[0], (index + 1) * total.shape[0])
        own_ref[lines, :] = total[:, :HEAD]
        below = slice(parts * size + lines.start, parts * size + lines.stop)
        send_ref[below, :] = total[:, HEAD:].astype(jnp.bfloat16)


def back_kernel(count, scale, *refs):
    blocks = refs[:-10]
    came_ref, keep_ref, own_ref, heads_ref, probs_ref, turned_ref = refs[-10:-4]
    mask_ref, partner_ref, out_ref, grads = refs[-4:]
    place = own_place(count)
    half = lax.axis_index("mp")
    shard = lax.axis_index("samples")
    seq_len = probs_ref.shape[1]
    skipped = seq_len + TAIL
    parts, size = keep_ref.shape[:2]
    for part in range(parts):
        out_ref[half * parts + part, skipped:, :] = keep_ref[part]
        lines = slice(part * size, (part + 1) * size)
        out_ref[(1 - half) * parts + part, skipped:, :] = came_ref[lines, :]
    sample_of = [peer_at(place, slot, count) for slot in range(count)]
    xs = [heads_ref[sample, 0:seq_len, :] for sample in sample_of]
    attn = []
    for slot in range(count):
        lines = slice(slot * seq_len, (slot + 1) * seq_len)
        below = slice(parts * size + lines.start, parts * size + lines.stop)
        total = own_ref[lines, :] + came_ref[below, :].astype(jnp.float32)
        attn.append(total.astype(jnp.bfloat16))
    grad_probs = [matmul_t(grad, x) for grad, x in zip(attn, xs)]
    inner = [
        jnp.sum(grad * probs_ref[sample], axis=-1, keepdims=True)
        for grad, sample in zip(grad_probs, sample_of)
    ]
    grad_scores = [
        (probs_ref[sample] * (grad - total)).astype(jnp.bfloat16)
        for grad, total, sample in zip(grad_probs, inner, sample_of)
    ]
    both = [jnp.concatenate([grad, transposed(grad)], axis=1) for grad in grad_scores]
    which = lax.rem(shard, 2)
    cols = columns(shard // 2, HEAD)
    chunks = [by_slot(blocks[: count + 1], count)[0], by_slot(blocks[count + 1 :], count)[0]]
    for slot, sample in enumerate(sample_of):
        through = matmul(turned_ref[sample], attn[slot])
        through = through + scale * matmul(
            both[slot], jnp.concatenate([xs[slot], xs[slot]], axis=0)
        )
        first, second = [
            jnp.concatenate([piece[:, cols] for piece in chunk[slot]], axis=0).astype(jnp.float32)
            for chunk in chunks
        ]
        above = jnp.where(which == 0, first, second)
        grads[sample] = (above + through).astype(jnp.bfloat16)
    region = jnp.broadcast_to(mask_ref[...].astype(jnp.float32), (HEAD, seq_len)).T > 0.5
    which = lax.broadcasted_iota(jnp.int32, (TAIL, seq_len), 0).astype(jnp.float32)
    embed = jnp.zeros((TAIL, HEAD), jnp.float32)
    for sample in range(count):
        swapped = grads[partner_ref[sample]].astype(jnp.float32)
        site = jnp.where(region, swapped, grads[sample].astype(jnp.float32)).astype(jnp.bfloat16)
        out_ref[sample, 0:seq_len, :] = site
        spin = heads_ref[sample, seq_len:skipped, :].astype(jnp.float32)
        embed = embed + matmul((spin == which).astype(jnp.bfloat16), site)
    high = embed.astype(jnp.bfloat16).astype(jnp.float32)
    low = embed - high
    tail = jnp.concatenate([high[: TAIL // 2], low[: TAIL // 2]], axis=0).astype(jnp.bfloat16)
    for sample in range(count):
        out_ref[sample, seq_len:skipped, :] = tail


def unpack_kernel(count, early_ref, parts_ref, weight_ref, site_ref, embed_ref):
    seq_len = site_ref.shape[2]
    skipped = seq_len + TAIL
    size = early_ref.shape[1]
    for peer in range(count):
        cols = slice(peer * HEAD, (peer + 1) * HEAD)
        weight_ref[0, 0:size, cols] = early_ref[peer].astype(jnp.float32)
        weight_ref[0, size:, cols] = parts_ref[peer, skipped:, :].astype(jnp.float32)
        site_ref[0, 0, :, cols] = parts_ref[peer, 0:seq_len, :]
        tail = parts_ref[peer, seq_len:skipped, :].astype(jnp.float32)
        embed_ref[:, cols] = (tail[: TAIL // 2] + tail[TAIL // 2 :])[:SPINS]


def exchanged(blocks):
    return lax.all_to_all(blocks, "samples", split_axis=0, concat_axis=0, tiled=True)


def head_sharded(
    stored_inputs, top_cotangent, layer_weights, block_layout, region_mask, partner_samples, spins
):
    count = lax.axis_size("samples")
    seq_len = stored_inputs.shape[2]
    shard_rows, half_width = layer_weights.shape[1:]
    scale = 4.0 / HEAD
    bf16, f32 = jnp.bfloat16, jnp.float32
    per_head = (count, seq_len, HEAD)
    lines = seq_len + TAIL
    share_axis = "groups" if lax.axis_size("groups") == 2 else None
    chunk_rows = shard_rows // 2
    sent = chunk_rows if share_axis else shard_rows
    parts = count // 2
    swap = [(0, 1), (1, 0)]
    up, down = ring_route(count, -1), ring_route(count, 1)

    rows = seq_len // 2
    packed = on_core(
        functools.partial(pack_kernel, count, share_axis),
        jax.ShapeDtypeStruct((count, lines + sent, HEAD), bf16),
        [pl.BlockSpec(memory_space=pltpu.HBM)] * 2 + in_vmem(1),
        [pltpu.SemaphoreType.DMA((2, count))],
        micros=1,
        vmem=60,
    )(stored_inputs, layer_weights, spins)
    chunk_shape = jax.ShapeDtypeStruct((seq_len, parts * chunk_rows), bf16)
    early, late = on_core(
        split_kernel,
        [chunk_shape, chunk_shape],
        [pl.BlockSpec(memory_space=pltpu.HBM)],
        [pltpu.SemaphoreType.DMA((2, parts))],
        micros=1,
    )(top_cotangent)

    def step_on(moving):
        ahead, back = moving
        return lax.ppermute(ahead, "samples", up), lax.ppermute(back, "samples", down)

    def last_step(moving):
        ahead, back = moving
        return step_on((ahead[:rows], back[rows:]))

    early_slots, late_slots = {0: early}, {0: late}
    moving, late_moving = (early, early), (late, late)
    for step in range(1, count // 2):
        moving = step_on(moving)
        if step == 1:
            *moving, packed = lax.optimization_barrier((*moving, packed))
            late_moving = step_on(late_moving)
            late_slots[count - 1], late_slots[1] = late_moving
        early_slots[count - step], early_slots[step] = moving
    tied = lax.optimization_barrier((*late_moving, *moving))
    late_moving, moving = tied[:2], tied[2:]
    early_slots[count // 2], early_slots[count] = last_step(moving)
    for step in range(2, count // 2):
        late_moving = step_on(late_moving)
        late_slots[count - step], late_slots[step] = late_moving
    late_slots[count // 2], late_slots[count] = last_step(late_moving)
    early_pieces = [early_slots[slot] for slot in range(count + 1)]
    late_pieces = [late_slots[slot] for slot in range(count + 1)]

    heads = exchanged(packed)
    small = (region_mask.reshape(1, seq_len), partner_samples)
    share_shape = jax.ShapeDtypeStruct((parts, sent, HEAD), bf16)
    attended, probs, turned, keep, send = on_core(
        functools.partial(forward_kernel, count, scale),
        [
            jax.ShapeDtypeStruct(per_head, bf16),
            jax.ShapeDtypeStruct(per_head, f32),
            jax.ShapeDtypeStruct(per_head, bf16),
            share_shape,
            share_shape,
        ],
        in_vmem(2) + in_smem(2),
        micros=2,
    )(heads, *small, block_layout)
    came = lax.ppermute(send, "mp", swap)
    attended_sibling = lax.ppermute(attended, "mp", swap)
    if share_axis:
        keep_other = lax.ppermute(keep, share_axis, swap)
        came_other = lax.ppermute(
            send, (share_axis, "mp"), [(0, 3), (1, 2), (2, 1), (3, 0)]
        )
        first = lax.axis_index(share_axis) == 0
        early_shares = jnp.where(first, keep, keep_other), jnp.where(first, came, came_other)
        late_shares = jnp.where(first, keep_other, keep), jnp.where(first, came_other, came)
    else:
        early_shares = keep[:, :chunk_rows], came[:, :chunk_rows]
        late_shares = keep[:, chunk_rows:], came[:, chunk_rows:]

    laid = pltpu.VMEM((parts * chunk_rows, 2 * HEAD), bf16)
    term_shape = jax.ShapeDtypeStruct((parts, chunk_rows, HEAD), bf16)
    early_keep, early_send, early_total = on_core(
        functools.partial(early_kernel, count),
        [
            term_shape,
            term_shape,
            jax.ShapeDtypeStruct((parts, 2 * seq_len, 2 * HEAD), f32),
        ],
        in_vmem(count + 5),
        [laid],
        micros=1.2,
    )(*early_pieces, attended, attended_sibling, *early_shares)
    early_came = lax.ppermute(early_send, "mp", swap)
    early_terms = on_core(
        join_kernel,
        jax.ShapeDtypeStruct((count, chunk_rows, HEAD), bf16),
        in_vmem(2),
        micros=0.2,
    )(early_keep, early_came)
    early_grad = exchanged(early_terms)
    late_keep, late_send, late_own = on_core(
        functools.partial(late_kernel, count),
        [
            term_shape,
            jax.ShapeDtypeStruct((parts * chunk_rows + count * seq_len, HEAD), bf16),
            jax.ShapeDtypeStruct((count * seq_len, HEAD), f32),
        ],
        in_vmem(count + 6),
        [laid],
        micros=1.2,
    )(*late_pieces, attended, attended_sibling, *late_shares, early_total)
    late_came = lax.ppermute(late_send, "mp", swap)
    late_came, early_grad = lax.optimization_barrier((late_came, early_grad))
    terms = on_core(
        functools.partial(back_kernel, count, scale),
        jax.ShapeDtypeStruct((count, lines + chunk_rows, HEAD), bf16),
        in_vmem(2 * count + 9) + in_smem(1),
        [pltpu.VMEM(per_head, bf16)],
        micros=4,
    )(
        *early_pieces,
        *late_pieces,
        late_came,
        late_keep,
        late_own,
        heads,
        probs,
        turned,
        *small,
    )
    return on_core(
        functools.partial(unpack_kernel, count),
        [
            jax.ShapeDtypeStruct((1, shard_rows, half_width), f32),
            jax.ShapeDtypeStruct((1, 1, seq_len, half_width), bf16),
            jax.ShapeDtypeStruct((SPINS, half_width), f32),
        ],
        in_vmem(2),
        micros=1.2,
    )(early_grad, exchanged(terms))


def solution(mesh):
    in_specs = (
        P("section", ("groups", "samples"), None, "mp"),
        P(("groups", "samples"), None, "mp"),
        P("section", "samples", "mp"),
        P("section", None, None),
        P(),
        P("groups"),
        P(("groups", "samples"), None),
    )
    out_specs = (
        P(("groups", "section"), "samples", "mp"),
        P("section", ("groups", "samples"), None, "mp"),
        P("groups", "mp"),
    )
    shards = mesh.shape["samples"]

    def whole(stored_inputs, top_cotangent, *rest):
        samples, _, width = top_cotangent.shape
        layer_count = stored_inputs.shape[0]
        one_each = samples == mesh.shape["groups"] * shards and layer_count == 1
        by_heads = one_each and shards % 2 == 0 and width == mesh.shape["mp"] * shards * HEAD
        return jax.shard_map(
            head_sharded if by_heads else local,
            mesh=mesh,
            in_specs=in_specs,
            out_specs=out_specs,
            check_vma=False,
        )(stored_inputs, top_cotangent, *rest)

    return whole
```

```python
import functools

import jax
import jax.numpy as jnp
from jax import lax
from jax.experimental import pallas as pl
from jax.experimental.pallas import tpu as pltpu
from jax.sharding import PartitionSpec as P

HEAD = 128
BLOCK = 64
SPINS = 2
TAIL = 16
FLOPS_PER_MICRO = 1.15e9


def for_sending(value):

    def short(part):
        return part.astype(jnp.bfloat16) if part.dtype == jnp.float32 else part

    return jax.tree.map(short, value)


def passed_along(block, axis, distance):
    devices = range(lax.axis_size(axis))
    route = [(i - distance, i) for i in devices if i - distance in devices]
    return lax.ppermute(block, axis, route)


def softmax_parts(inputs_h, allowed, attention_scale):
    scores = (
        jnp.einsum("qhd,khd->hqk", inputs_h, inputs_h, preferred_element_type=jnp.float32)
        * attention_scale
    )
    scores = jnp.where(allowed[None], scores, -jnp.inf)
    top_score = jnp.max(scores, axis=-1, keepdims=True)
    expo_terms = jnp.exp(scores - top_score)
    probs = expo_terms / jnp.sum(expo_terms, axis=-1, keepdims=True)
    return (probs, probs.astype(jnp.bfloat16))


def local(
    stored_inputs, top_cotangent, layer_weights, block_layout, region_mask, partner_samples, spins
):
    section_index = lax.axis_index("section")
    section_count = lax.axis_size("section")
    micro_count = stored_inputs.shape[1]
    seq_len = stored_inputs.shape[2]
    half_width = stored_inputs.shape[3]
    head_count = half_width // HEAD
    attention_scale = 4.0 / HEAD
    weights = lax.all_gather(layer_weights[0], "samples", axis=0, tiled=True)
    pos_block = jnp.arange(seq_len) // BLOCK
    block_onehot = (pos_block[:, None] == jnp.arange(block_layout.shape[1])[None, :]).astype(
        jnp.float32
    )
    linked = jnp.dot(jnp.dot(block_onehot, block_layout[0].astype(jnp.float32)), block_onehot.T)
    allowed = (linked > 0.5) | (pos_block[:, None] == pos_block[None, :])
    every_layer_input = stored_inputs[0]
    inputs_h = every_layer_input[0].reshape(seq_len, head_count, HEAD)
    probs, probs_low = softmax_parts(inputs_h, allowed, attention_scale)
    attended = jnp.einsum(
        "hqk,khd->qhd", probs_low, inputs_h, preferred_element_type=jnp.float32
    ).astype(jnp.bfloat16)
    probs_list = [probs]
    low_list = [probs_low]
    attend_list = [attended.reshape(seq_len, half_width)]
    probs_all = jnp.stack(probs_list)
    low_all = jnp.stack(low_list)
    attend_store = jnp.stack(attend_list)

    def layer_back(grad_full, grad_own, inputs, probs, probs_low):
        grad_attn = jnp.dot(grad_full, weights, preferred_element_type=jnp.float32).astype(
            jnp.bfloat16
        )
        inputs_h = inputs.reshape(seq_len, head_count, HEAD)
        grad_h = grad_attn.reshape(seq_len, head_count, HEAD)
        grad_probs = jnp.einsum(
            "qhd,khd->hqk", grad_h, inputs_h, preferred_element_type=jnp.float32
        )
        grad_scores = (
            probs * (grad_probs - jnp.sum(grad_probs * probs, axis=-1, keepdims=True))
        ).astype(jnp.bfloat16)
        through = jnp.einsum("hqk,qhd->khd", probs_low, grad_h, preferred_element_type=jnp.float32)
        through = through + attention_scale * (
            jnp.einsum("hqk,khd->qhd", grad_scores, inputs_h, preferred_element_type=jnp.float32)
            + jnp.einsum("hqk,qhd->khd", grad_scores, inputs_h, preferred_element_type=jnp.float32)
        )
        grad_in = grad_own.astype(jnp.float32) + through.reshape(seq_len, half_width)
        return grad_in.astype(jnp.bfloat16)

    def resting(grad_full, grad_own, inputs, probs, probs_low):
        return jnp.zeros((seq_len, half_width), jnp.bfloat16)

    carried_state = jnp.zeros((seq_len, half_width), jnp.bfloat16)
    out_list = []
    grad_list = []
    total_steps = micro_count + section_count - 1
    for step_number in range(total_steps):
        micro_index = step_number - (section_count - 1 - section_index)
        active = (micro_index >= 0) & (micro_index < micro_count)
        slot_index = jnp.clip(micro_index, 0, micro_count - 1)
        from_top = lax.dynamic_index_in_dim(top_cotangent, slot_index, 0, keepdims=False)
        incoming = jnp.where(section_index == section_count - 1, from_top, carried_state)
        grad_full = lax.all_gather(incoming, "mp", axis=1, tiled=True)
        inputs_now = lax.dynamic_index_in_dim(every_layer_input, slot_index, 0, keepdims=False)
        probs_now = lax.dynamic_index_in_dim(probs_all, slot_index, 0, keepdims=False)
        low_now = lax.dynamic_index_in_dim(low_all, slot_index, 0, keepdims=False)
        grad_in = lax.cond(
            active, layer_back, resting, grad_full, incoming, inputs_now, probs_now, low_now
        )
        out_list.append(grad_in)
        grad_list.append(grad_full)
        if step_number < total_steps - 1:
            carried_state = jax.tree.map(
                lambda part, own: part.astype(own.dtype),
                passed_along(for_sending(grad_in), "section", -1),
                grad_in,
            )
    offset = section_count - 1 - section_index
    out_store = lax.dynamic_slice_in_dim(jnp.stack(out_list), offset, micro_count, 0)
    grad_store = lax.dynamic_slice_in_dim(jnp.stack(grad_list), offset, micro_count, 0)
    summed_weight = lax.psum_scatter(
        jnp.einsum(
            "mtf,mta->fa", grad_store, attend_store, preferred_element_type=jnp.float32
        ).astype(jnp.bfloat16),
        "samples",
        scatter_dimension=0,
        tiled=True,
    ).astype(jnp.float32)
    region_count = seq_len // 2
    rank_in_region = jnp.cumsum(region_mask) - 1
    select = (
        (rank_in_region[None, :] == jnp.arange(region_count)[:, None]) & (region_mask[None, :] > 0)
    ).astype(jnp.bfloat16)
    tiles = jnp.einsum("at,mtd->mad", select, out_store, preferred_element_type=jnp.float32).astype(
        jnp.bfloat16
    )
    shard_index = lax.axis_index("samples")
    my_partners = lax.dynamic_slice_in_dim(
        partner_samples, shard_index * micro_count, micro_count, 0
    )
    shard_count = lax.axis_size("samples")
    dest_shard = my_partners // micro_count
    dest_slot = my_partners % micro_count
    route = (
        (dest_shard[:, None, None] == jnp.arange(shard_count)[None, :, None])
        & (dest_slot[:, None, None] == jnp.arange(micro_count)[None, None, :])
    ).astype(jnp.bfloat16)
    outgoing = jnp.einsum("mku,mad->kuad", route, tiles, preferred_element_type=jnp.float32).astype(
        jnp.bfloat16
    )
    arrived = lax.all_to_all(outgoing, "samples", split_axis=0, concat_axis=0, tiled=True)
    ones_row = jnp.ones((shard_count,), jnp.bfloat16)
    received = jnp.einsum(
        "k,kuad->uad", ones_row, arrived, preferred_element_type=jnp.float32
    ).astype(jnp.bfloat16)
    placed = jnp.einsum("at,mad->mtd", select, received, preferred_element_type=jnp.float32)
    kept = jnp.where(region_mask[None, :, None] > 0, jnp.zeros_like(out_store), out_store)
    site_cot = (kept.astype(jnp.float32) + placed).astype(jnp.bfloat16)
    cotangents = jnp.where(section_index == 0, site_cot, out_store)
    onehot = (spins[:, :, None] == jnp.arange(SPINS)[None, None, :]).astype(jnp.bfloat16)
    embed_term = jnp.einsum("mtv,mtd->vd", onehot, site_cot, preferred_element_type=jnp.float32)
    embed_term = jnp.where(section_index == 0, embed_term, jnp.zeros_like(embed_term))
    embed_grad = lax.psum(embed_term, ("samples", "section"))
    return (summed_weight[None], cotangents[None], embed_grad)


def ring_sample(place, count):
    return jnp.where(place < count // 2, 2 * place, 2 * (count - place) - 1)


def ring_place(sample, count):
    return jnp.where(lax.rem(sample, 2) == 0, sample // 2, count - 1 - sample // 2)


def ring_route(count, distance):
    order = list(range(0, count, 2)) + list(range(1, count, 2))[::-1]
    return [(order[i], order[(i - distance) % count]) for i in range(count)]


def own_place(count):
    return ring_place(lax.axis_index("samples"), count)


def peer_at(place, distance, count):
    return ring_sample(lax.rem(place + distance + count, count), count)


def columns(index, size):
    return pl.ds(pl.multiple_of(index * size, size), size)


def in_vmem(count):
    return [pl.BlockSpec(memory_space=pltpu.VMEM)] * count


def in_smem(count):
    return [pl.BlockSpec(memory_space=pltpu.SMEM)] * count


def on_core(body, out_shapes, in_specs, scratch=(), micros=1, vmem=16):
    return pl.pallas_call(
        body,
        out_shape=out_shapes,
        in_specs=in_specs,
        out_specs=jax.tree.map(lambda _: pl.BlockSpec(memory_space=pltpu.VMEM), out_shapes),
        scratch_shapes=list(scratch),
        compiler_params=pltpu.CompilerParams(vmem_limit_bytes=vmem << 20),
        cost_estimate=pl.CostEstimate(
            flops=int(micros * FLOPS_PER_MICRO), bytes_accessed=1 << 16, transcendentals=0
        ),
    )


def matmul(left, right):
    return jnp.dot(left, right, preferred_element_type=jnp.float32)


def matmul_t(left, right):
    return lax.dot_general(
        left, right, (((1,), (1,)), ((), ())), preferred_element_type=jnp.float32
    )


def pack_kernel(count, share_axis, x_ref, w_ref, spins_ref, out_ref, sems):
    seq_len = x_ref.shape[2]
    skipped = seq_len + TAIL
    sent = out_ref.shape[1] - skipped
    rows = columns(lax.axis_index(share_axis), sent) if share_axis else slice(None)
    copies = []
    for peer in range(count):
        cols = slice(peer * HEAD, (peer + 1) * HEAD)
        head, weight = out_ref.at[peer, 0:seq_len, :], out_ref.at[peer, skipped:, :]
        copies.append(pltpu.make_async_copy(x_ref.at[0, 0, :, cols], head, sems.at[0, peer]))
        copies.append(pltpu.make_async_copy(w_ref.at[0, rows, cols], weight, sems.at[1, peer]))
    for copy in copies:
        copy.start()
    spin_rows = jnp.broadcast_to(spins_ref[...].astype(jnp.float32), (TAIL, seq_len))
    for peer in range(count):
        out_ref[peer, seq_len:skipped, :] = spin_rows.astype(jnp.bfloat16)
    for copy in copies:
        copy.wait()


def forward_kernel(count, scale, *refs):
    heads_ref, layout_ref = refs[0], refs[-6]
    probs_ref, turned_ref, bundle_ref, keep_ref, send_ref = refs[-5:]
    seq_len = probs_ref.shape[1]
    half = lax.axis_index("mp")
    parts, sent = keep_ref.shape[:2]
    for part in range(parts):
        keep_ref[part] = heads_ref[half * parts + part, seq_len + TAIL :, :]
        send = heads_ref[(1 - half) * parts + part, seq_len + TAIL :, :]
        send_ref[part] = send
        first = count * seq_len + part * sent
        bundle_ref[first : first + sent, :] = send
    blocks = layout_ref.shape[1]
    rows = lax.broadcasted_iota(jnp.int32, (seq_len, seq_len), 0) // BLOCK
    cols = lax.broadcasted_iota(jnp.int32, (seq_len, seq_len), 1) // BLOCK
    seen = rows == cols
    for q in range(blocks):
        for k in range(blocks):
            if q != k:
                seen = seen | ((rows == q) & (cols == k) & (layout_ref[0, q, k] > 0))
    xs = [heads_ref[slot, 0:seq_len, :] for slot in range(count)]
    scores = [jnp.where(seen, matmul_t(x, x) * scale, -jnp.inf) for x in xs]
    tops = [jnp.max(score, axis=-1, keepdims=True) for score in scores]
    terms = [jnp.exp(score - top) for score, top in zip(scores, tops)]
    sums = [jnp.sum(term, axis=-1, keepdims=True) for term in terms]
    for slot in range(count):
        probs = terms[slot] / sums[slot]
        low = probs.astype(jnp.bfloat16)
        probs_ref[slot] = probs
        attended = matmul(low, xs[slot]).astype(jnp.bfloat16)
        bundle_ref[slot * seq_len : (slot + 1) * seq_len, :] = attended
        turned_ref[slot] = transposed(low)


def lay_weights(weights, shares, share_axis):
    index = lax.axis_index(share_axis) if share_axis else 0
    pieces = len(shares) // 2
    parts = len(shares[0])
    for number, share in enumerate(shares):
        head, piece = number % 2, number // 2
        place = index if piece == 0 else 1 - index
        for part, value in enumerate(share):
            sent = value.shape[0]
            rows = pl.ds(pl.multiple_of((part * pieces + place) * sent, sent), sent)
            weights[rows, head * HEAD : (head + 1) * HEAD] = value


def weight_term(pieces, left, cols):
    total = None
    for index, first in enumerate(range(0, len(pieces), 2)):
        rows = [piece[:, cols] for slot in pieces[first : first + 2] for piece in slot]
        term = matmul(left[index], jnp.concatenate(rows, axis=0))
        total = term if total is None else total + term
    return total


def both_heads(own_ref, sibling_ref, samples, seq_len):
    rows = [
        jnp.concatenate(
            [ref[columns(sample, seq_len), :] for ref in (own_ref, sibling_ref)], axis=1
        )
        for sample in samples
    ]
    return transposed(jnp.concatenate(rows, axis=0))


def transposed(value):
    return value.astype(jnp.float32).T.astype(jnp.bfloat16)


def attention_back(scale, xs, probs, turned, grads, above):
    grad_probs = [matmul_t(grad, x) for grad, x in zip(grads, xs)]
    inner = [jnp.sum(grad * prob, axis=-1, keepdims=True) for grad, prob in zip(grad_probs, probs)]
    grad_scores = [
        (prob * (grad - total)).astype(jnp.bfloat16)
        for prob, grad, total in zip(probs, grad_probs, inner)
    ]
    both = [jnp.concatenate([grad, transposed(grad)], axis=1) for grad in grad_scores]
    results = []
    for index, x in enumerate(xs):
        through = matmul(turned[index], grads[index])
        through = through + scale * matmul(both[index], jnp.concatenate([x, x], axis=0))
        results.append((above[index].astype(jnp.float32) + through).astype(jnp.bfloat16))
    return results


def near_slots(count):
    return [slot for slot in range(count) if slot != count // 2]


def near_products_kernel(count, share_axis, *refs):
    pieces = [refs[index : index + 1] for index in range(count - 1)]
    bundle_ref, sibling_ref, keep_ref = refs[count - 1 : count + 2]
    others = refs[count + 2 : -5]
    partial_ref, own_ref, other_ref, above_ref, weights = refs[-5:]
    place = own_place(count)
    shard = lax.axis_index("samples")
    parts, _, shard_rows = partial_ref.shape
    sent = keep_ref.shape[1]
    seq_len = pieces[0][0].shape[0]
    sample_of = [peer_at(place, slot, count) for slot in near_slots(count)]
    firsts = [count * seq_len + part * sent for part in range(parts)]
    shares = [
        [keep_ref[part] for part in range(parts)],
        [sibling_ref[first : first + sent, :] for first in firsts],
    ]
    shares += [[ref[part] for part in range(parts)] for ref in others]
    lay_weights(weights, shares, share_axis)
    left = [
        both_heads(bundle_ref, sibling_ref, sample_of[first : first + 2], seq_len)
        for first in range(0, count - 1, 2)
    ]
    for part in range(parts):
        cols = slice(part * shard_rows, (part + 1) * shard_rows)
        partial_ref[part] = weight_term(pieces, left, cols)
    for first in range(0, count - 1, 2):
        rows = [piece[...] for slot in pieces[first : first + 2] for piece in slot]
        total = matmul(jnp.concatenate(rows, axis=0), weights[...])
        lines = slice(first * seq_len, first * seq_len + total.shape[0])
        own_ref[lines, :] = total[:, :HEAD]
        other_ref[lines, :] = total[:, HEAD:].astype(jnp.bfloat16)
    for index, slot in enumerate(pieces):
        above_ref[index * seq_len : (index + 1) * seq_len, :] = slot[0][:, columns(shard, HEAD)]


def near_back_kernel(count, scale, *refs):
    heads_ref, probs_ref, turned_ref, own_ref, other_ref, above_ref = refs[:6]
    grads_ref = refs[-1]
    place = own_place(count)
    seq_len = probs_ref.shape[1]
    sample_of = [peer_at(place, slot, count) for slot in near_slots(count)]
    lines = [slice(index * seq_len, (index + 1) * seq_len) for index in range(count - 1)]
    results = attention_back(
        scale,
        [heads_ref[sample, 0:seq_len, :] for sample in sample_of],
        [probs_ref[sample] for sample in sample_of],
        [turned_ref[sample] for sample in sample_of],
        [
            (own_ref[line, :] + other_ref[line, :].astype(jnp.float32)).astype(jnp.bfloat16)
            for line in lines
        ],
        [above_ref[line, :] for line in lines],
    )
    for index, result in enumerate(results):
        grads_ref[index] = result


def far_products_kernel(count, *refs):
    piece, refs = refs[:2], refs[2:]
    bundle_ref, sibling_ref, partial_ref, weights_ref = refs[:4]
    send_ref, keep_ref, own_ref, above_ref = refs[4:]
    sample = peer_at(own_place(count), count // 2, count)
    shard = lax.axis_index("samples")
    parts, _, shard_rows = partial_ref.shape
    left = [both_heads(bundle_ref, sibling_ref, [sample], 2 * piece[0].shape[0])]
    for part in range(parts):
        cols = slice(part * shard_rows, (part + 1) * shard_rows)
        total = transposed(partial_ref[part] + weight_term([piece], left, cols))
        keep_ref[part] = total[:, :HEAD]
        send_ref[cols, :] = total[:, HEAD:]
    total = matmul(jnp.concatenate([rows[...] for rows in piece], axis=0), weights_ref[...])
    own_ref[...] = total[:, :HEAD]
    send_ref[parts * shard_rows :, :] = total[:, HEAD:].astype(jnp.bfloat16)
    cols = columns(shard, HEAD)
    above_ref[...] = jnp.concatenate([rows[:, cols] for rows in piece], axis=0)


def far_kernel(count, scale, *refs):
    came_ref, keep_ref, own_ref, above_ref, heads_ref, probs_ref, turned_ref = refs[:7]
    near_ref, mask_ref, partner_ref, out_ref, grads = refs[7:]
    place = own_place(count)
    half = lax.axis_index("mp")
    seq_len = probs_ref.shape[1]
    skipped = seq_len + TAIL
    parts, shard_rows = keep_ref.shape[:2]
    for part in range(parts):
        out_ref[half * parts + part, skipped:, :] = keep_ref[part]
        lines = slice(part * shard_rows, (part + 1) * shard_rows)
        out_ref[(1 - half) * parts + part, skipped:, :] = came_ref[lines, :]
    for index, slot in enumerate(near_slots(count)):
        grads[peer_at(place, slot, count)] = near_ref[index]
    sample = peer_at(place, count // 2, count)
    other = came_ref[parts * shard_rows :, :].astype(jnp.float32)
    (grads[sample],) = attention_back(
        scale,
        [heads_ref[sample, 0:seq_len, :]],
        [probs_ref[sample]],
        [turned_ref[sample]],
        [(own_ref[...] + other).astype(jnp.bfloat16)],
        [above_ref[...]],
    )
    region = jnp.broadcast_to(mask_ref[...].astype(jnp.float32), (HEAD, seq_len)).T > 0.5
    which = lax.broadcasted_iota(jnp.int32, (TAIL, seq_len), 0).astype(jnp.float32)
    embed = jnp.zeros((TAIL, HEAD), jnp.float32)
    for sample in range(count):
        swapped = grads[partner_ref[sample]].astype(jnp.float32)
        site = jnp.where(region, swapped, grads[sample].astype(jnp.float32)).astype(jnp.bfloat16)
        out_ref[sample, 0:seq_len, :] = site
        spin = heads_ref[sample, seq_len:skipped, :].astype(jnp.float32)
        embed = embed + matmul((spin == which).astype(jnp.bfloat16), site)
    high = embed.astype(jnp.bfloat16).astype(jnp.float32)
    low = embed - high
    tail = jnp.concatenate([high[: TAIL // 2], low[: TAIL // 2]], axis=0).astype(jnp.bfloat16)
    for sample in range(count):
        out_ref[sample, seq_len:skipped, :] = tail


def unpack_kernel(count, parts_ref, weight_ref, site_ref, embed_ref):
    seq_len = site_ref.shape[2]
    skipped = seq_len + TAIL
    for peer in range(count):
        cols = slice(peer * HEAD, (peer + 1) * HEAD)
        weight_ref[0, :, cols] = parts_ref[peer, skipped:, :].astype(jnp.float32)
        site_ref[0, 0, :, cols] = parts_ref[peer, 0:seq_len, :]
        tail = parts_ref[peer, seq_len:skipped, :].astype(jnp.float32)
        embed_ref[:, cols] = (tail[: TAIL // 2] + tail[TAIL // 2 :])[:SPINS]


def exchanged(blocks):
    return lax.all_to_all(blocks, "samples", split_axis=0, concat_axis=0, tiled=True)


def head_sharded(
    stored_inputs, top_cotangent, layer_weights, block_layout, region_mask, partner_samples, spins
):
    count = lax.axis_size("samples")
    seq_len = stored_inputs.shape[2]
    shard_rows, half_width = layer_weights.shape[1:]
    scale = 4.0 / HEAD
    bf16, f32 = jnp.bfloat16, jnp.float32
    per_head = (count, seq_len, HEAD)
    lines = seq_len + TAIL
    share_axis = "groups" if lax.axis_size("groups") == 2 else None
    sent = shard_rows // 2 if share_axis else shard_rows
    parts = count // 2
    swap = [(0, 1), (1, 0)]

    up, down = ring_route(count, -1), ring_route(count, 1)
    block = top_cotangent[0]
    rows = seq_len // 2
    packed = on_core(
        functools.partial(pack_kernel, count, share_axis),
        jax.ShapeDtypeStruct((count, lines + sent, HEAD), bf16),
        [pl.BlockSpec(memory_space=pltpu.HBM)] * 2 + in_vmem(1),
        [pltpu.SemaphoreType.DMA((2, count))],
        micros=1,
        vmem=60,
    )(stored_inputs, layer_weights, spins)
    heads = exchanged(packed)
    slots = {0: block}
    ahead, back = block, block
    for step in range(1, count // 2):
        ahead = lax.ppermute(ahead, "samples", up)
        back = lax.ppermute(back, "samples", down)
        slots[count - step], slots[step] = ahead, back
    far = (
        lax.ppermute(ahead[:rows], "samples", up),
        lax.ppermute(back[rows:], "samples", down),
    )
    near = [slots[slot] for slot in near_slots(count)]
    small = (region_mask.reshape(1, seq_len), partner_samples)
    share_shape = jax.ShapeDtypeStruct((parts, sent, HEAD), bf16)
    probs, turned, bundle, keep, send = on_core(
        functools.partial(forward_kernel, count, scale),
        [
            jax.ShapeDtypeStruct(per_head, f32),
            jax.ShapeDtypeStruct(per_head, bf16),
            jax.ShapeDtypeStruct((count * seq_len + parts * sent, HEAD), bf16),
            share_shape,
            share_shape,
        ],
        in_vmem(2) + in_smem(2),
        micros=1.2,
    )(heads, *small, block_layout)
    sibling = lax.ppermute(bundle, "mp", swap)
    others = []
    if share_axis:
        others = [
            lax.ppermute(keep, share_axis, swap),
            lax.ppermute(send, (share_axis, "mp"), [(0, 3), (1, 2), (2, 1), (3, 0)]),
        ]
    near_lines = (count - 1) * seq_len
    partial, near_own, near_other, near_above, weights = on_core(
        functools.partial(near_products_kernel, count, share_axis),
        [
            jax.ShapeDtypeStruct((parts, 2 * HEAD, shard_rows), f32),
            jax.ShapeDtypeStruct((near_lines, HEAD), f32),
            jax.ShapeDtypeStruct((near_lines, HEAD), bf16),
            jax.ShapeDtypeStruct((near_lines, HEAD), bf16),
            jax.ShapeDtypeStruct((half_width, 2 * HEAD), bf16),
        ],
        in_vmem(count + 2 + len(others)),
        micros=1.4,
    )(*near, bundle, sibling, keep, *others)
    near_other = lax.ppermute(near_other, "mp", swap)
    near_grads = on_core(
        functools.partial(near_back_kernel, count, scale),
        jax.ShapeDtypeStruct((count - 1, seq_len, HEAD), bf16),
        in_vmem(7) + in_smem(1),
        micros=1.8,
    )(heads, probs, turned, near_own, near_other, near_above, *small)
    far_send, far_keep, far_own, far_above = on_core(
        functools.partial(far_products_kernel, count),
        [
            jax.ShapeDtypeStruct((half_width + seq_len, HEAD), bf16),
            jax.ShapeDtypeStruct((parts, shard_rows, HEAD), bf16),
            jax.ShapeDtypeStruct((seq_len, HEAD), f32),
            jax.ShapeDtypeStruct((seq_len, HEAD), bf16),
        ],
        in_vmem(6),
        micros=0.5,
    )(*far, bundle, sibling, partial, weights)
    far_came = lax.ppermute(far_send, "mp", swap)
    terms = on_core(
        functools.partial(far_kernel, count, scale),
        jax.ShapeDtypeStruct((count, lines + shard_rows, HEAD), bf16),
        in_vmem(9) + in_smem(1),
        [pltpu.VMEM(per_head, bf16)],
        micros=1.2,
    )(far_came, far_keep, far_own, far_above, heads, probs, turned, near_grads, *small)
    return on_core(
        functools.partial(unpack_kernel, count),
        [
            jax.ShapeDtypeStruct((1, shard_rows, half_width), f32),
            jax.ShapeDtypeStruct((1, 1, seq_len, half_width), bf16),
            jax.ShapeDtypeStruct((SPINS, half_width), f32),
        ],
        in_vmem(1),
        micros=1.2,
    )(exchanged(terms))


def solution(mesh):
    in_specs = (
        P("section", ("groups", "samples"), None, "mp"),
        P(("groups", "samples"), None, "mp"),
        P("section", "samples", "mp"),
        P("section", None, None),
        P(),
        P("groups"),
        P(("groups", "samples"), None),
    )
    out_specs = (
        P(("groups", "section"), "samples", "mp"),
        P("section", ("groups", "samples"), None, "mp"),
        P("groups", "mp"),
    )
    shards = mesh.shape["samples"]

    def whole(stored_inputs, top_cotangent, *rest):
        samples, _, width = top_cotangent.shape
        layer_count = stored_inputs.shape[0]
        one_each = samples == mesh.shape["groups"] * shards and layer_count == 1
        by_heads = one_each and shards % 2 == 0 and width == mesh.shape["mp"] * shards * HEAD
        return jax.shard_map(
            head_sharded if by_heads else local,
            mesh=mesh,
            in_specs=in_specs,
            out_specs=out_specs,
            check_vma=False,
        )(stored_inputs, top_cotangent, *rest)

    return whole
```

```python
import functools

import jax
import jax.numpy as jnp
from jax import lax
from jax.experimental import pallas as pl
from jax.experimental.pallas import tpu as pltpu
from jax.sharding import PartitionSpec as P

HEAD = 128
BLOCK = 64
SPINS = 2
TAIL = 16
FLOPS_PER_MICRO = 1.15e9


def for_sending(value):

    def short(part):
        return part.astype(jnp.bfloat16) if part.dtype == jnp.float32 else part

    return jax.tree.map(short, value)


def passed_along(block, axis, distance):
    devices = range(lax.axis_size(axis))
    route = [(i - distance, i) for i in devices if i - distance in devices]
    return lax.ppermute(block, axis, route)


def softmax_parts(inputs_h, allowed, attention_scale):
    scores = (
        jnp.einsum("qhd,khd->hqk", inputs_h, inputs_h, preferred_element_type=jnp.float32)
        * attention_scale
    )
    scores = jnp.where(allowed[None], scores, -jnp.inf)
    top_score = jnp.max(scores, axis=-1, keepdims=True)
    expo_terms = jnp.exp(scores - top_score)
    probs = expo_terms / jnp.sum(expo_terms, axis=-1, keepdims=True)
    return (probs, probs.astype(jnp.bfloat16))


def local(
    stored_inputs, top_cotangent, layer_weights, block_layout, region_mask, partner_samples, spins
):
    section_index = lax.axis_index("section")
    section_count = lax.axis_size("section")
    micro_count = stored_inputs.shape[1]
    seq_len = stored_inputs.shape[2]
    half_width = stored_inputs.shape[3]
    head_count = half_width // HEAD
    attention_scale = 4.0 / HEAD
    weights = lax.all_gather(layer_weights[0], "samples", axis=0, tiled=True)
    pos_block = jnp.arange(seq_len) // BLOCK
    block_onehot = (pos_block[:, None] == jnp.arange(block_layout.shape[1])[None, :]).astype(
        jnp.float32
    )
    linked = jnp.dot(jnp.dot(block_onehot, block_layout[0].astype(jnp.float32)), block_onehot.T)
    allowed = (linked > 0.5) | (pos_block[:, None] == pos_block[None, :])
    every_layer_input = stored_inputs[0]
    inputs_h = every_layer_input[0].reshape(seq_len, head_count, HEAD)
    probs, probs_low = softmax_parts(inputs_h, allowed, attention_scale)
    attended = jnp.einsum(
        "hqk,khd->qhd", probs_low, inputs_h, preferred_element_type=jnp.float32
    ).astype(jnp.bfloat16)
    probs_list = [probs]
    low_list = [probs_low]
    attend_list = [attended.reshape(seq_len, half_width)]
    probs_all = jnp.stack(probs_list)
    low_all = jnp.stack(low_list)
    attend_store = jnp.stack(attend_list)

    def layer_back(grad_full, grad_own, inputs, probs, probs_low):
        grad_attn = jnp.dot(grad_full, weights, preferred_element_type=jnp.float32).astype(
            jnp.bfloat16
        )
        inputs_h = inputs.reshape(seq_len, head_count, HEAD)
        grad_h = grad_attn.reshape(seq_len, head_count, HEAD)
        grad_probs = jnp.einsum(
            "qhd,khd->hqk", grad_h, inputs_h, preferred_element_type=jnp.float32
        )
        grad_scores = (
            probs * (grad_probs - jnp.sum(grad_probs * probs, axis=-1, keepdims=True))
        ).astype(jnp.bfloat16)
        through = jnp.einsum("hqk,qhd->khd", probs_low, grad_h, preferred_element_type=jnp.float32)
        through = through + attention_scale * (
            jnp.einsum("hqk,khd->qhd", grad_scores, inputs_h, preferred_element_type=jnp.float32)
            + jnp.einsum("hqk,qhd->khd", grad_scores, inputs_h, preferred_element_type=jnp.float32)
        )
        grad_in = grad_own.astype(jnp.float32) + through.reshape(seq_len, half_width)
        return grad_in.astype(jnp.bfloat16)

    def resting(grad_full, grad_own, inputs, probs, probs_low):
        return jnp.zeros((seq_len, half_width), jnp.bfloat16)

    carried_state = jnp.zeros((seq_len, half_width), jnp.bfloat16)
    out_list = []
    grad_list = []
    total_steps = micro_count + section_count - 1
    for step_number in range(total_steps):
        micro_index = step_number - (section_count - 1 - section_index)
        active = (micro_index >= 0) & (micro_index < micro_count)
        slot_index = jnp.clip(micro_index, 0, micro_count - 1)
        from_top = lax.dynamic_index_in_dim(top_cotangent, slot_index, 0, keepdims=False)
        incoming = jnp.where(section_index == section_count - 1, from_top, carried_state)
        grad_full = lax.all_gather(incoming, "mp", axis=1, tiled=True)
        inputs_now = lax.dynamic_index_in_dim(every_layer_input, slot_index, 0, keepdims=False)
        probs_now = lax.dynamic_index_in_dim(probs_all, slot_index, 0, keepdims=False)
        low_now = lax.dynamic_index_in_dim(low_all, slot_index, 0, keepdims=False)
        grad_in = lax.cond(
            active, layer_back, resting, grad_full, incoming, inputs_now, probs_now, low_now
        )
        out_list.append(grad_in)
        grad_list.append(grad_full)
        if step_number < total_steps - 1:
            carried_state = jax.tree.map(
                lambda part, own: part.astype(own.dtype),
                passed_along(for_sending(grad_in), "section", -1),
                grad_in,
            )
    offset = section_count - 1 - section_index
    out_store = lax.dynamic_slice_in_dim(jnp.stack(out_list), offset, micro_count, 0)
    grad_store = lax.dynamic_slice_in_dim(jnp.stack(grad_list), offset, micro_count, 0)
    summed_weight = lax.psum_scatter(
        jnp.einsum(
            "mtf,mta->fa", grad_store, attend_store, preferred_element_type=jnp.float32
        ).astype(jnp.bfloat16),
        "samples",
        scatter_dimension=0,
        tiled=True,
    ).astype(jnp.float32)
    region_count = seq_len // 2
    rank_in_region = jnp.cumsum(region_mask) - 1
    select = (
        (rank_in_region[None, :] == jnp.arange(region_count)[:, None]) & (region_mask[None, :] > 0)
    ).astype(jnp.bfloat16)
    tiles = jnp.einsum("at,mtd->mad", select, out_store, preferred_element_type=jnp.float32).astype(
        jnp.bfloat16
    )
    shard_index = lax.axis_index("samples")
    my_partners = lax.dynamic_slice_in_dim(
        partner_samples, shard_index * micro_count, micro_count, 0
    )
    shard_count = lax.axis_size("samples")
    dest_shard = my_partners // micro_count
    dest_slot = my_partners % micro_count
    route = (
        (dest_shard[:, None, None] == jnp.arange(shard_count)[None, :, None])
        & (dest_slot[:, None, None] == jnp.arange(micro_count)[None, None, :])
    ).astype(jnp.bfloat16)
    outgoing = jnp.einsum("mku,mad->kuad", route, tiles, preferred_element_type=jnp.float32).astype(
        jnp.bfloat16
    )
    arrived = lax.all_to_all(outgoing, "samples", split_axis=0, concat_axis=0, tiled=True)
    ones_row = jnp.ones((shard_count,), jnp.bfloat16)
    received = jnp.einsum(
        "k,kuad->uad", ones_row, arrived, preferred_element_type=jnp.float32
    ).astype(jnp.bfloat16)
    placed = jnp.einsum("at,mad->mtd", select, received, preferred_element_type=jnp.float32)
    kept = jnp.where(region_mask[None, :, None] > 0, jnp.zeros_like(out_store), out_store)
    site_cot = (kept.astype(jnp.float32) + placed).astype(jnp.bfloat16)
    cotangents = jnp.where(section_index == 0, site_cot, out_store)
    onehot = (spins[:, :, None] == jnp.arange(SPINS)[None, None, :]).astype(jnp.bfloat16)
    embed_term = jnp.einsum("mtv,mtd->vd", onehot, site_cot, preferred_element_type=jnp.float32)
    embed_term = jnp.where(section_index == 0, embed_term, jnp.zeros_like(embed_term))
    embed_grad = lax.psum(embed_term, ("samples", "section"))
    return (summed_weight[None], cotangents[None], embed_grad)


def ring_sample(place, count):
    return jnp.where(place < count // 2, 2 * place, 2 * (count - place) - 1)


def ring_place(sample, count):
    return jnp.where(lax.rem(sample, 2) == 0, sample // 2, count - 1 - sample // 2)


def ring_route(count, distance):
    order = list(range(0, count, 2)) + list(range(1, count, 2))[::-1]
    return [(order[i], order[(i - distance) % count]) for i in range(count)]


def own_place(count):
    return ring_place(lax.axis_index("samples"), count)


def peer_at(place, distance, count):
    return ring_sample(lax.rem(place + distance + count, count), count)


def columns(index, size):
    return pl.ds(pl.multiple_of(index * size, size), size)


def in_vmem(count):
    return [pl.BlockSpec(memory_space=pltpu.VMEM)] * count


def in_smem(count):
    return [pl.BlockSpec(memory_space=pltpu.SMEM)] * count


def on_core(body, out_shapes, in_specs, scratch=(), micros=1, vmem=16):
    return pl.pallas_call(
        body,
        out_shape=out_shapes,
        in_specs=in_specs,
        out_specs=jax.tree.map(lambda _: pl.BlockSpec(memory_space=pltpu.VMEM), out_shapes),
        scratch_shapes=list(scratch),
        compiler_params=pltpu.CompilerParams(vmem_limit_bytes=vmem << 20),
        cost_estimate=pl.CostEstimate(
            flops=int(micros * FLOPS_PER_MICRO), bytes_accessed=1 << 16, transcendentals=0
        ),
    )


def matmul(left, right):
    return jnp.dot(left, right, preferred_element_type=jnp.float32)


def matmul_t(left, right):
    return lax.dot_general(
        left, right, (((1,), (1,)), ((), ())), preferred_element_type=jnp.float32
    )


def pack_kernel(count, share_axis, x_ref, w_ref, spins_ref, out_ref, sems):
    seq_len = x_ref.shape[2]
    skipped = seq_len + TAIL
    sent = out_ref.shape[1] - skipped
    rows = columns(lax.axis_index(share_axis), sent) if share_axis else slice(None)
    copies = []
    for peer in range(count):
        cols = slice(peer * HEAD, (peer + 1) * HEAD)
        head, weight = out_ref.at[peer, 0:seq_len, :], out_ref.at[peer, skipped:, :]
        copies.append(pltpu.make_async_copy(x_ref.at[0, 0, :, cols], head, sems.at[0, peer]))
        copies.append(pltpu.make_async_copy(w_ref.at[0, rows, cols], weight, sems.at[1, peer]))
    for copy in copies:
        copy.start()
    spin_rows = jnp.broadcast_to(spins_ref[...].astype(jnp.float32), (TAIL, seq_len))
    for peer in range(count):
        out_ref[peer, seq_len:skipped, :] = spin_rows.astype(jnp.bfloat16)
    for copy in copies:
        copy.wait()


def forward_kernel(count, scale, *refs):
    heads_ref, layout_ref = refs[0], refs[-5]
    probs_ref, turned_ref, bundle_ref, keep_ref = refs[-4:]
    seq_len = probs_ref.shape[1]
    half = lax.axis_index("mp")
    parts, sent = keep_ref.shape[:2]
    for part in range(parts):
        keep_ref[part] = heads_ref[half * parts + part, seq_len + TAIL :, :]
        first = count * seq_len + part * sent
        send = heads_ref[(1 - half) * parts + part, seq_len + TAIL :, :]
        bundle_ref[first : first + sent, :] = send
    blocks = layout_ref.shape[1]
    rows = lax.broadcasted_iota(jnp.int32, (seq_len, seq_len), 0) // BLOCK
    cols = lax.broadcasted_iota(jnp.int32, (seq_len, seq_len), 1) // BLOCK
    seen = rows == cols
    for q in range(blocks):
        for k in range(blocks):
            if q != k:
                seen = seen | ((rows == q) & (cols == k) & (layout_ref[0, q, k] > 0))
    xs = [heads_ref[slot, 0:seq_len, :] for slot in range(count)]
    scores = [jnp.where(seen, matmul_t(x, x) * scale, -jnp.inf) for x in xs]
    tops = [jnp.max(score, axis=-1, keepdims=True) for score in scores]
    terms = [jnp.exp(score - top) for score, top in zip(scores, tops)]
    sums = [jnp.sum(term, axis=-1, keepdims=True) for term in terms]
    for slot in range(count):
        probs = terms[slot] / sums[slot]
        low = probs.astype(jnp.bfloat16)
        probs_ref[slot] = probs
        attended = matmul(low, xs[slot]).astype(jnp.bfloat16)
        bundle_ref[slot * seq_len : (slot + 1) * seq_len, :] = attended
        turned_ref[slot] = transposed(low)


def lay_weights(weights, shares, share_axis):
    index = lax.axis_index(share_axis) if share_axis else 0
    pieces = len(shares) // 2
    parts = len(shares[0])
    for number, share in enumerate(shares):
        head, piece = number % 2, number // 2
        place = index if piece == 0 else 1 - index
        for part, value in enumerate(share):
            sent = value.shape[0]
            rows = pl.ds(pl.multiple_of((part * pieces + place) * sent, sent), sent)
            weights[rows, head * HEAD : (head + 1) * HEAD] = value


def weight_term(pieces, left, cols):
    total = None
    for index, first in enumerate(range(0, len(pieces), 2)):
        rows = [piece[:, cols] for slot in pieces[first : first + 2] for piece in slot]
        term = matmul(left[index], jnp.concatenate(rows, axis=0))
        total = term if total is None else total + term
    return total


def both_heads(own_ref, sibling_ref, samples, seq_len):
    rows = [
        jnp.concatenate(
            [ref[columns(sample, seq_len), :] for ref in (own_ref, sibling_ref)], axis=1
        )
        for sample in samples
    ]
    return transposed(jnp.concatenate(rows, axis=0))


def transposed(value):
    return value.astype(jnp.float32).T.astype(jnp.bfloat16)


def attention_back(scale, xs, probs, turned, grads, above):
    grad_probs = [matmul_t(grad, x) for grad, x in zip(grads, xs)]
    inner = [jnp.sum(grad * prob, axis=-1, keepdims=True) for grad, prob in zip(grad_probs, probs)]
    grad_scores = [
        (prob * (grad - total)).astype(jnp.bfloat16)
        for prob, grad, total in zip(probs, grad_probs, inner)
    ]
    both = [jnp.concatenate([grad, transposed(grad)], axis=1) for grad in grad_scores]
    results = []
    for index, x in enumerate(xs):
        through = matmul(turned[index], grads[index])
        through = through + scale * matmul(both[index], jnp.concatenate([x, x], axis=0))
        results.append((above[index].astype(jnp.float32) + through).astype(jnp.bfloat16))
    return results


def near_slots(count):
    return [slot for slot in range(count) if slot != count // 2]


def near_products_kernel(count, share_axis, *refs):
    pieces = [refs[index : index + 1] for index in range(count - 1)]
    bundle_ref, sibling_ref, keep_ref = refs[count - 1 : count + 2]
    others = refs[count + 2 : -5]
    partial_ref, own_ref, other_ref, above_ref, weights = refs[-5:]
    place = own_place(count)
    shard = lax.axis_index("samples")
    parts, _, shard_rows = partial_ref.shape
    sent = keep_ref.shape[1]
    seq_len = pieces[0][0].shape[0]
    sample_of = [peer_at(place, slot, count) for slot in near_slots(count)]
    firsts = [count * seq_len + part * sent for part in range(parts)]
    shares = [
        [keep_ref[part] for part in range(parts)],
        [sibling_ref[first : first + sent, :] for first in firsts],
    ]
    shares += [[ref[part] for part in range(parts)] for ref in others]
    lay_weights(weights, shares, share_axis)
    left = [
        both_heads(bundle_ref, sibling_ref, sample_of[first : first + 2], seq_len)
        for first in range(0, count - 1, 2)
    ]
    for part in range(parts):
        cols = slice(part * shard_rows, (part + 1) * shard_rows)
        partial_ref[part] = weight_term(pieces, left, cols)
    for first in range(0, count - 1, 2):
        rows = [piece[...] for slot in pieces[first : first + 2] for piece in slot]
        total = matmul(jnp.concatenate(rows, axis=0), weights[...])
        lines = slice(first * seq_len, first * seq_len + total.shape[0])
        own_ref[lines, :] = total[:, :HEAD]
        other_ref[lines, :] = total[:, HEAD:].astype(jnp.bfloat16)
    for index, slot in enumerate(pieces):
        above_ref[index * seq_len : (index + 1) * seq_len, :] = slot[0][:, columns(shard, HEAD)]


def near_back_kernel(count, scale, *refs):
    heads_ref, probs_ref, turned_ref, own_ref, other_ref, above_ref = refs[:6]
    grads_ref = refs[-1]
    place = own_place(count)
    seq_len = probs_ref.shape[1]
    sample_of = [peer_at(place, slot, count) for slot in near_slots(count)]
    lines = [slice(index * seq_len, (index + 1) * seq_len) for index in range(count - 1)]
    results = attention_back(
        scale,
        [heads_ref[sample, 0:seq_len, :] for sample in sample_of],
        [probs_ref[sample] for sample in sample_of],
        [turned_ref[sample] for sample in sample_of],
        [
            (own_ref[line, :] + other_ref[line, :].astype(jnp.float32)).astype(jnp.bfloat16)
            for line in lines
        ],
        [above_ref[line, :] for line in lines],
    )
    for index, result in enumerate(results):
        grads_ref[index] = result


def far_products_kernel(count, *refs):
    piece, refs = refs[:2], refs[2:]
    bundle_ref, sibling_ref, partial_ref, weights_ref = refs[:4]
    send_ref, keep_ref, own_ref, above_ref = refs[4:]
    sample = peer_at(own_place(count), count // 2, count)
    shard = lax.axis_index("samples")
    parts, _, shard_rows = partial_ref.shape
    left = [both_heads(bundle_ref, sibling_ref, [sample], 2 * piece[0].shape[0])]
    for part in range(parts):
        cols = slice(part * shard_rows, (part + 1) * shard_rows)
        total = transposed(partial_ref[part] + weight_term([piece], left, cols))
        keep_ref[part] = total[:, :HEAD]
        send_ref[cols, :] = total[:, HEAD:]
    total = matmul(jnp.concatenate([rows[...] for rows in piece], axis=0), weights_ref[...])
    own_ref[...] = total[:, :HEAD]
    send_ref[parts * shard_rows :, :] = total[:, HEAD:].astype(jnp.bfloat16)
    cols = columns(shard, HEAD)
    above_ref[...] = jnp.concatenate([rows[:, cols] for rows in piece], axis=0)


def far_kernel(count, scale, *refs):
    came_ref, keep_ref, own_ref, above_ref, heads_ref, probs_ref, turned_ref = refs[:7]
    near_ref, mask_ref, partner_ref, out_ref, grads = refs[7:]
    place = own_place(count)
    half = lax.axis_index("mp")
    seq_len = probs_ref.shape[1]
    skipped = seq_len + TAIL
    parts, shard_rows = keep_ref.shape[:2]
    for part in range(parts):
        out_ref[half * parts + part, skipped:, :] = keep_ref[part]
        lines = slice(part * shard_rows, (part + 1) * shard_rows)
        out_ref[(1 - half) * parts + part, skipped:, :] = came_ref[lines, :]
    for index, slot in enumerate(near_slots(count)):
        grads[peer_at(place, slot, count)] = near_ref[index]
    sample = peer_at(place, count // 2, count)
    other = came_ref[parts * shard_rows :, :].astype(jnp.float32)
    (grads[sample],) = attention_back(
        scale,
        [heads_ref[sample, 0:seq_len, :]],
        [probs_ref[sample]],
        [turned_ref[sample]],
        [(own_ref[...] + other).astype(jnp.bfloat16)],
        [above_ref[...]],
    )
    region = jnp.broadcast_to(mask_ref[...].astype(jnp.float32), (HEAD, seq_len)).T > 0.5
    which = lax.broadcasted_iota(jnp.int32, (TAIL, seq_len), 0).astype(jnp.float32)
    embed = jnp.zeros((TAIL, HEAD), jnp.float32)
    for sample in range(count):
        swapped = grads[partner_ref[sample]].astype(jnp.float32)
        site = jnp.where(region, swapped, grads[sample].astype(jnp.float32)).astype(jnp.bfloat16)
        out_ref[sample, 0:seq_len, :] = site
        spin = heads_ref[sample, seq_len:skipped, :].astype(jnp.float32)
        embed = embed + matmul((spin == which).astype(jnp.bfloat16), site)
    high = embed.astype(jnp.bfloat16).astype(jnp.float32)
    low = embed - high
    tail = jnp.concatenate([high[: TAIL // 2], low[: TAIL // 2]], axis=0).astype(jnp.bfloat16)
    for sample in range(count):
        out_ref[sample, seq_len:skipped, :] = tail


def unpack_kernel(count, parts_ref, weight_ref, site_ref, embed_ref):
    seq_len = site_ref.shape[2]
    skipped = seq_len + TAIL
    for peer in range(count):
        cols = slice(peer * HEAD, (peer + 1) * HEAD)
        weight_ref[0, :, cols] = parts_ref[peer, skipped:, :].astype(jnp.float32)
        site_ref[0, 0, :, cols] = parts_ref[peer, 0:seq_len, :]
        tail = parts_ref[peer, seq_len:skipped, :].astype(jnp.float32)
        embed_ref[:, cols] = (tail[: TAIL // 2] + tail[TAIL // 2 :])[:SPINS]


def exchanged(blocks):
    return lax.all_to_all(blocks, "samples", split_axis=0, concat_axis=0, tiled=True)


def head_sharded(
    stored_inputs, top_cotangent, layer_weights, block_layout, region_mask, partner_samples, spins
):
    count = lax.axis_size("samples")
    seq_len = stored_inputs.shape[2]
    shard_rows, half_width = layer_weights.shape[1:]
    scale = 4.0 / HEAD
    bf16, f32 = jnp.bfloat16, jnp.float32
    per_head = (count, seq_len, HEAD)
    lines = seq_len + TAIL
    share_axis = "groups" if lax.axis_size("groups") == 2 else None
    sent = shard_rows // 2 if share_axis else shard_rows
    parts = count // 2
    swap = [(0, 1), (1, 0)]

    up, down = ring_route(count, -1), ring_route(count, 1)
    block = top_cotangent[0]
    rows = seq_len // 2
    packed = on_core(
        functools.partial(pack_kernel, count, share_axis),
        jax.ShapeDtypeStruct((count, lines + sent, HEAD), bf16),
        [pl.BlockSpec(memory_space=pltpu.HBM)] * 2 + in_vmem(1),
        [pltpu.SemaphoreType.DMA((2, count))],
        micros=1,
        vmem=60,
    )(stored_inputs, layer_weights, spins)
    heads = exchanged(packed)
    slots = {0: block}
    ahead, back = block, block
    for step in range(1, count // 2):
        ahead = lax.ppermute(ahead, "samples", up)
        back = lax.ppermute(back, "samples", down)
        if step == 2:
            ahead, back, heads = lax.optimization_barrier((ahead, back, heads))
        slots[count - step], slots[step] = ahead, back
    far = (
        lax.ppermute(ahead[:rows], "samples", up),
        lax.ppermute(back[rows:], "samples", down),
    )
    near = [slots[slot] for slot in near_slots(count)]
    small = (region_mask.reshape(1, seq_len), partner_samples)
    share_shape = jax.ShapeDtypeStruct((parts, sent, HEAD), bf16)
    others = []
    if share_axis:
        came = lax.ppermute(heads[:, lines:], share_axis, swap)
        half = lax.axis_index("mp")
        kept, given = [
            lax.dynamic_slice_in_dim(came, start * parts, parts) for start in (half, 1 - half)
        ]
        others = [kept, lax.ppermute(given, "mp", swap)]
    probs, turned, bundle, keep = on_core(
        functools.partial(forward_kernel, count, scale),
        [
            jax.ShapeDtypeStruct(per_head, f32),
            jax.ShapeDtypeStruct(per_head, bf16),
            jax.ShapeDtypeStruct((count * seq_len + parts * sent, HEAD), bf16),
            share_shape,
        ],
        in_vmem(2) + in_smem(2),
        micros=1.2,
    )(heads, *small, block_layout)
    sibling = lax.ppermute(bundle, "mp", swap)
    near_lines = (count - 1) * seq_len
    partial, near_own, near_other, near_above, weights = on_core(
        functools.partial(near_products_kernel, count, share_axis),
        [
            jax.ShapeDtypeStruct((parts, 2 * HEAD, shard_rows), f32),
            jax.ShapeDtypeStruct((near_lines, HEAD), f32),
            jax.ShapeDtypeStruct((near_lines, HEAD), bf16),
            jax.ShapeDtypeStruct((near_lines, HEAD), bf16),
            jax.ShapeDtypeStruct((half_width, 2 * HEAD), bf16),
        ],
        in_vmem(count + 2 + len(others)),
        micros=1.4,
    )(*near, bundle, sibling, keep, *others)
    near_other = lax.ppermute(near_other, "mp", swap)
    near_grads = on_core(
        functools.partial(near_back_kernel, count, scale),
        jax.ShapeDtypeStruct((count - 1, seq_len, HEAD), bf16),
        in_vmem(7) + in_smem(1),
        micros=1.8,
    )(heads, probs, turned, near_own, near_other, near_above, *small)
    far_send, far_keep, far_own, far_above = on_core(
        functools.partial(far_products_kernel, count),
        [
            jax.ShapeDtypeStruct((half_width + seq_len, HEAD), bf16),
            jax.ShapeDtypeStruct((parts, shard_rows, HEAD), bf16),
            jax.ShapeDtypeStruct((seq_len, HEAD), f32),
            jax.ShapeDtypeStruct((seq_len, HEAD), bf16),
        ],
        in_vmem(6),
        micros=0.5,
    )(*far, bundle, sibling, partial, weights)
    far_came = lax.ppermute(far_send, "mp", swap)
    terms = on_core(
        functools.partial(far_kernel, count, scale),
        jax.ShapeDtypeStruct((count, lines + shard_rows, HEAD), bf16),
        in_vmem(9) + in_smem(1),
        [pltpu.VMEM(per_head, bf16)],
        micros=1.2,
    )(far_came, far_keep, far_own, far_above, heads, probs, turned, near_grads, *small)
    return on_core(
        functools.partial(unpack_kernel, count),
        [
            jax.ShapeDtypeStruct((1, shard_rows, half_width), f32),
            jax.ShapeDtypeStruct((1, 1, seq_len, half_width), bf16),
            jax.ShapeDtypeStruct((SPINS, half_width), f32),
        ],
        in_vmem(1),
        micros=1.2,
    )(exchanged(terms))


def solution(mesh):
    in_specs = (
        P("section", ("groups", "samples"), None, "mp"),
        P(("groups", "samples"), None, "mp"),
        P("section", "samples", "mp"),
        P("section", None, None),
        P(),
        P("groups"),
        P(("groups", "samples"), None),
    )
    out_specs = (
        P(("groups", "section"), "samples", "mp"),
        P("section", ("groups", "samples"), None, "mp"),
        P("groups", "mp"),
    )
    shards = mesh.shape["samples"]

    def whole(stored_inputs, top_cotangent, *rest):
        samples, _, width = top_cotangent.shape
        layer_count = stored_inputs.shape[0]
        one_each = samples == mesh.shape["groups"] * shards and layer_count == 1
        by_heads = one_each and shards % 2 == 0 and width == mesh.shape["mp"] * shards * HEAD
        return jax.shard_map(
            head_sharded if by_heads else local,
            mesh=mesh,
            in_specs=in_specs,
            out_specs=out_specs,
            check_vma=False,
        )(stored_inputs, top_cotangent, *rest)

    return whole
```

```python
import functools

import jax
import jax.numpy as jnp
from jax import lax
from jax.experimental import pallas as pl
from jax.experimental.pallas import tpu as pltpu
from jax.sharding import PartitionSpec as P

HEAD = 128
BLOCK = 64
SPINS = 2
TAIL = 16
FLOPS_PER_MICRO = 1.15e9


def for_sending(value):

    def short(part):
        return part.astype(jnp.bfloat16) if part.dtype == jnp.float32 else part

    return jax.tree.map(short, value)


def passed_along(block, axis, distance):
    devices = range(lax.axis_size(axis))
    route = [(i - distance, i) for i in devices if i - distance in devices]
    return lax.ppermute(block, axis, route)


def softmax_parts(inputs_h, allowed, attention_scale):
    scores = (
        jnp.einsum("qhd,khd->hqk", inputs_h, inputs_h, preferred_element_type=jnp.float32)
        * attention_scale
    )
    scores = jnp.where(allowed[None], scores, -jnp.inf)
    top_score = jnp.max(scores, axis=-1, keepdims=True)
    expo_terms = jnp.exp(scores - top_score)
    probs = expo_terms / jnp.sum(expo_terms, axis=-1, keepdims=True)
    return (probs, probs.astype(jnp.bfloat16))


def local(
    stored_inputs, top_cotangent, layer_weights, block_layout, region_mask, partner_samples, spins
):
    section_index = lax.axis_index("section")
    section_count = lax.axis_size("section")
    micro_count = stored_inputs.shape[1]
    seq_len = stored_inputs.shape[2]
    half_width = stored_inputs.shape[3]
    head_count = half_width // HEAD
    attention_scale = 4.0 / HEAD
    weights = lax.all_gather(layer_weights[0], "samples", axis=0, tiled=True)
    pos_block = jnp.arange(seq_len) // BLOCK
    block_onehot = (pos_block[:, None] == jnp.arange(block_layout.shape[1])[None, :]).astype(
        jnp.float32
    )
    linked = jnp.dot(jnp.dot(block_onehot, block_layout[0].astype(jnp.float32)), block_onehot.T)
    allowed = (linked > 0.5) | (pos_block[:, None] == pos_block[None, :])
    every_layer_input = stored_inputs[0]
    inputs_h = every_layer_input[0].reshape(seq_len, head_count, HEAD)
    probs, probs_low = softmax_parts(inputs_h, allowed, attention_scale)
    attended = jnp.einsum(
        "hqk,khd->qhd", probs_low, inputs_h, preferred_element_type=jnp.float32
    ).astype(jnp.bfloat16)
    probs_list = [probs]
    low_list = [probs_low]
    attend_list = [attended.reshape(seq_len, half_width)]
    probs_all = jnp.stack(probs_list)
    low_all = jnp.stack(low_list)
    attend_store = jnp.stack(attend_list)

    def layer_back(grad_full, grad_own, inputs, probs, probs_low):
        grad_attn = jnp.dot(grad_full, weights, preferred_element_type=jnp.float32).astype(
            jnp.bfloat16
        )
        inputs_h = inputs.reshape(seq_len, head_count, HEAD)
        grad_h = grad_attn.reshape(seq_len, head_count, HEAD)
        grad_probs = jnp.einsum(
            "qhd,khd->hqk", grad_h, inputs_h, preferred_element_type=jnp.float32
        )
        grad_scores = (
            probs * (grad_probs - jnp.sum(grad_probs * probs, axis=-1, keepdims=True))
        ).astype(jnp.bfloat16)
        through = jnp.einsum("hqk,qhd->khd", probs_low, grad_h, preferred_element_type=jnp.float32)
        through = through + attention_scale * (
            jnp.einsum("hqk,khd->qhd", grad_scores, inputs_h, preferred_element_type=jnp.float32)
            + jnp.einsum("hqk,qhd->khd", grad_scores, inputs_h, preferred_element_type=jnp.float32)
        )
        grad_in = grad_own.astype(jnp.float32) + through.reshape(seq_len, half_width)
        return grad_in.astype(jnp.bfloat16)

    def resting(grad_full, grad_own, inputs, probs, probs_low):
        return jnp.zeros((seq_len, half_width), jnp.bfloat16)

    carried_state = jnp.zeros((seq_len, half_width), jnp.bfloat16)
    out_list = []
    grad_list = []
    total_steps = micro_count + section_count - 1
    for step_number in range(total_steps):
        micro_index = step_number - (section_count - 1 - section_index)
        active = (micro_index >= 0) & (micro_index < micro_count)
        slot_index = jnp.clip(micro_index, 0, micro_count - 1)
        from_top = lax.dynamic_index_in_dim(top_cotangent, slot_index, 0, keepdims=False)
        incoming = jnp.where(section_index == section_count - 1, from_top, carried_state)
        grad_full = lax.all_gather(incoming, "mp", axis=1, tiled=True)
        inputs_now = lax.dynamic_index_in_dim(every_layer_input, slot_index, 0, keepdims=False)
        probs_now = lax.dynamic_index_in_dim(probs_all, slot_index, 0, keepdims=False)
        low_now = lax.dynamic_index_in_dim(low_all, slot_index, 0, keepdims=False)
        grad_in = lax.cond(
            active, layer_back, resting, grad_full, incoming, inputs_now, probs_now, low_now
        )
        out_list.append(grad_in)
        grad_list.append(grad_full)
        if step_number < total_steps - 1:
            carried_state = jax.tree.map(
                lambda part, own: part.astype(own.dtype),
                passed_along(for_sending(grad_in), "section", -1),
                grad_in,
            )
    offset = section_count - 1 - section_index
    out_store = lax.dynamic_slice_in_dim(jnp.stack(out_list), offset, micro_count, 0)
    grad_store = lax.dynamic_slice_in_dim(jnp.stack(grad_list), offset, micro_count, 0)
    summed_weight = lax.psum_scatter(
        jnp.einsum(
            "mtf,mta->fa", grad_store, attend_store, preferred_element_type=jnp.float32
        ).astype(jnp.bfloat16),
        "samples",
        scatter_dimension=0,
        tiled=True,
    ).astype(jnp.float32)
    region_count = seq_len // 2
    rank_in_region = jnp.cumsum(region_mask) - 1
    select = (
        (rank_in_region[None, :] == jnp.arange(region_count)[:, None]) & (region_mask[None, :] > 0)
    ).astype(jnp.bfloat16)
    tiles = jnp.einsum("at,mtd->mad", select, out_store, preferred_element_type=jnp.float32).astype(
        jnp.bfloat16
    )
    shard_index = lax.axis_index("samples")
    my_partners = lax.dynamic_slice_in_dim(
        partner_samples, shard_index * micro_count, micro_count, 0
    )
    shard_count = lax.axis_size("samples")
    dest_shard = my_partners // micro_count
    dest_slot = my_partners % micro_count
    route = (
        (dest_shard[:, None, None] == jnp.arange(shard_count)[None, :, None])
        & (dest_slot[:, None, None] == jnp.arange(micro_count)[None, None, :])
    ).astype(jnp.bfloat16)
    outgoing = jnp.einsum("mku,mad->kuad", route, tiles, preferred_element_type=jnp.float32).astype(
        jnp.bfloat16
    )
    arrived = lax.all_to_all(outgoing, "samples", split_axis=0, concat_axis=0, tiled=True)
    ones_row = jnp.ones((shard_count,), jnp.bfloat16)
    received = jnp.einsum(
        "k,kuad->uad", ones_row, arrived, preferred_element_type=jnp.float32
    ).astype(jnp.bfloat16)
    placed = jnp.einsum("at,mad->mtd", select, received, preferred_element_type=jnp.float32)
    kept = jnp.where(region_mask[None, :, None] > 0, jnp.zeros_like(out_store), out_store)
    site_cot = (kept.astype(jnp.float32) + placed).astype(jnp.bfloat16)
    cotangents = jnp.where(section_index == 0, site_cot, out_store)
    onehot = (spins[:, :, None] == jnp.arange(SPINS)[None, None, :]).astype(jnp.bfloat16)
    embed_term = jnp.einsum("mtv,mtd->vd", onehot, site_cot, preferred_element_type=jnp.float32)
    embed_term = jnp.where(section_index == 0, embed_term, jnp.zeros_like(embed_term))
    embed_grad = lax.psum(embed_term, ("samples", "section"))
    return (summed_weight[None], cotangents[None], embed_grad)


def ring_sample(place, count):
    return jnp.where(place < count // 2, 2 * place, 2 * (count - place) - 1)


def ring_place(sample, count):
    return jnp.where(lax.rem(sample, 2) == 0, sample // 2, count - 1 - sample // 2)


def ring_route(count, distance):
    order = list(range(0, count, 2)) + list(range(1, count, 2))[::-1]
    return [(order[i], order[(i - distance) % count]) for i in range(count)]


def own_place(count):
    return ring_place(lax.axis_index("samples"), count)


def peer_at(place, distance, count):
    return ring_sample(lax.rem(place + distance + count, count), count)


def columns(index, size):
    return pl.ds(pl.multiple_of(index * size, size), size)


def in_vmem(count):
    return [pl.BlockSpec(memory_space=pltpu.VMEM)] * count


def in_smem(count):
    return [pl.BlockSpec(memory_space=pltpu.SMEM)] * count


def on_core(body, out_shapes, in_specs, scratch=(), micros=1, vmem=16):
    return pl.pallas_call(
        body,
        out_shape=out_shapes,
        in_specs=in_specs,
        out_specs=jax.tree.map(lambda _: pl.BlockSpec(memory_space=pltpu.VMEM), out_shapes),
        scratch_shapes=list(scratch),
        compiler_params=pltpu.CompilerParams(vmem_limit_bytes=vmem << 20),
        cost_estimate=pl.CostEstimate(
            flops=int(micros * FLOPS_PER_MICRO), bytes_accessed=1 << 16, transcendentals=0
        ),
    )


def matmul(left, right):
    return jnp.dot(left, right, preferred_element_type=jnp.float32)


def matmul_t(left, right):
    return lax.dot_general(
        left, right, (((1,), (1,)), ((), ())), preferred_element_type=jnp.float32
    )


def pack_kernel(count, share_axis, x_ref, w_ref, spins_ref, out_ref, sems):
    seq_len = x_ref.shape[2]
    skipped = seq_len + TAIL
    sent = out_ref.shape[1] - skipped
    rows = columns(lax.axis_index(share_axis), sent) if share_axis else slice(None)
    copies = []
    for peer in range(count):
        cols = slice(peer * HEAD, (peer + 1) * HEAD)
        head, weight = out_ref.at[peer, 0:seq_len, :], out_ref.at[peer, skipped:, :]
        copies.append(pltpu.make_async_copy(x_ref.at[0, 0, :, cols], head, sems.at[0, peer]))
        copies.append(pltpu.make_async_copy(w_ref.at[0, rows, cols], weight, sems.at[1, peer]))
    for copy in copies:
        copy.start()
    spin_rows = jnp.broadcast_to(spins_ref[...].astype(jnp.float32), (TAIL, seq_len))
    for peer in range(count):
        out_ref[peer, seq_len:skipped, :] = spin_rows.astype(jnp.bfloat16)
    for copy in copies:
        copy.wait()


def forward_kernel(count, scale, *refs):
    heads_ref, shared, layout_ref = refs[0], refs[1:-6], refs[-4]
    probs_ref, turned_ref, bundle_ref = refs[-3:]
    seq_len = probs_ref.shape[1]
    lines = seq_len + TAIL
    half = lax.axis_index("mp")
    parts = count // 2
    sent = heads_ref.shape[1] - lines
    for part in range(parts):
        shard = (1 - half) * parts + part
        for piece, value in enumerate((heads_ref[shard, lines:, :], *(ref[shard] for ref in shared))):
            first = count * seq_len + (piece * parts + part) * sent
            bundle_ref[first : first + sent, :] = value
    blocks = layout_ref.shape[1]
    rows = lax.broadcasted_iota(jnp.int32, (seq_len, seq_len), 0) // BLOCK
    cols = lax.broadcasted_iota(jnp.int32, (seq_len, seq_len), 1) // BLOCK
    seen = rows == cols
    for q in range(blocks):
        for k in range(blocks):
            if q != k:
                seen = seen | ((rows == q) & (cols == k) & (layout_ref[0, q, k] > 0))
    xs = [heads_ref[slot, 0:seq_len, :] for slot in range(count)]
    scores = [jnp.where(seen, matmul_t(x, x) * scale, -jnp.inf) for x in xs]
    tops = [jnp.max(score, axis=-1, keepdims=True) for score in scores]
    terms = [jnp.exp(score - top) for score, top in zip(scores, tops)]
    sums = [jnp.sum(term, axis=-1, keepdims=True) for term in terms]
    for slot in range(count):
        probs = terms[slot] / sums[slot]
        low = probs.astype(jnp.bfloat16)
        probs_ref[slot] = probs
        attended = matmul(low, xs[slot]).astype(jnp.bfloat16)
        bundle_ref[slot * seq_len : (slot + 1) * seq_len, :] = attended
        turned_ref[slot] = transposed(low)


def lay_weights(weights, shares, share_axis):
    index = lax.axis_index(share_axis) if share_axis else 0
    pieces = len(shares) // 2
    parts = len(shares[0])
    for number, share in enumerate(shares):
        head, piece = number % 2, number // 2
        place = index if piece == 0 else 1 - index
        for part, value in enumerate(share):
            sent = value.shape[0]
            rows = pl.ds(pl.multiple_of((part * pieces + place) * sent, sent), sent)
            weights[rows, head * HEAD : (head + 1) * HEAD] = value


def weight_term(pieces, left, cols):
    total = None
    for index, first in enumerate(range(0, len(pieces), 2)):
        rows = [piece[:, cols] for slot in pieces[first : first + 2] for piece in slot]
        term = matmul(left[index], jnp.concatenate(rows, axis=0))
        total = term if total is None else total + term
    return total


def both_heads(own_ref, sibling_ref, samples, seq_len):
    rows = [
        jnp.concatenate(
            [ref[columns(sample, seq_len), :] for ref in (own_ref, sibling_ref)], axis=1
        )
        for sample in samples
    ]
    return transposed(jnp.concatenate(rows, axis=0))


def transposed(value):
    return value.astype(jnp.float32).T.astype(jnp.bfloat16)


def attention_back(scale, xs, probs, turned, grads, above):
    grad_probs = [matmul_t(grad, x) for grad, x in zip(grads, xs)]
    inner = [jnp.sum(grad * prob, axis=-1, keepdims=True) for grad, prob in zip(grad_probs, probs)]
    grad_scores = [
        (prob * (grad - total)).astype(jnp.bfloat16)
        for prob, grad, total in zip(probs, grad_probs, inner)
    ]
    both = [jnp.concatenate([grad, transposed(grad)], axis=1) for grad in grad_scores]
    results = []
    for index, x in enumerate(xs):
        through = matmul(turned[index], grads[index])
        through = through + scale * matmul(both[index], jnp.concatenate([x, x], axis=0))
        results.append((above[index].astype(jnp.float32) + through).astype(jnp.bfloat16))
    return results


def near_slots(count):
    return [slot for slot in range(count) if slot != count // 2]


def near_products_kernel(count, share_axis, *refs):
    pieces = [refs[index : index + 1] for index in range(count - 1)]
    bundle_ref, sibling_ref, heads_ref = refs[count - 1 : count + 2]
    shared = refs[count + 2 : -5]
    partial_ref, own_ref, other_ref, above_ref, weights = refs[-5:]
    place = own_place(count)
    shard = lax.axis_index("samples")
    parts, _, shard_rows = partial_ref.shape
    seq_len = pieces[0][0].shape[0]
    lines = seq_len + TAIL
    sent = heads_ref.shape[1] - lines
    half = lax.axis_index("mp")
    sample_of = [peer_at(place, slot, count) for slot in near_slots(count)]
    shares = []
    for piece, ref in enumerate((heads_ref, *shared)):
        skipped = lines if piece == 0 else 0
        shares.append([ref[half * parts + part, skipped:, :] for part in range(parts)])
        firsts = [count * seq_len + (piece * parts + part) * sent for part in range(parts)]
        shares.append([sibling_ref[first : first + sent, :] for first in firsts])
    lay_weights(weights, shares, share_axis)
    left = [
        both_heads(bundle_ref, sibling_ref, sample_of[first : first + 2], seq_len)
        for first in range(0, count - 1, 2)
    ]
    for part in range(parts):
        cols = slice(part * shard_rows, (part + 1) * shard_rows)
        partial_ref[part] = weight_term(pieces, left, cols)
    for first in range(0, count - 1, 2):
        rows = [piece[...] for slot in pieces[first : first + 2] for piece in slot]
        total = matmul(jnp.concatenate(rows, axis=0), weights[...])
        lines = slice(first * seq_len, first * seq_len + total.shape[0])
        own_ref[lines, :] = total[:, :HEAD]
        other_ref[lines, :] = total[:, HEAD:].astype(jnp.bfloat16)
    for index, slot in enumerate(pieces):
        above_ref[index * seq_len : (index + 1) * seq_len, :] = slot[0][:, columns(shard, HEAD)]


def near_back_kernel(count, scale, *refs):
    heads_ref, probs_ref, turned_ref, own_ref, other_ref, above_ref = refs[:6]
    grads_ref = refs[-1]
    place = own_place(count)
    seq_len = probs_ref.shape[1]
    sample_of = [peer_at(place, slot, count) for slot in near_slots(count)]
    lines = [slice(index * seq_len, (index + 1) * seq_len) for index in range(count - 1)]
    results = attention_back(
        scale,
        [heads_ref[sample, 0:seq_len, :] for sample in sample_of],
        [probs_ref[sample] for sample in sample_of],
        [turned_ref[sample] for sample in sample_of],
        [
            (own_ref[line, :] + other_ref[line, :].astype(jnp.float32)).astype(jnp.bfloat16)
            for line in lines
        ],
        [above_ref[line, :] for line in lines],
    )
    for index, result in enumerate(results):
        grads_ref[index] = result


def far_products_kernel(count, *refs):
    piece, refs = refs[:2], refs[2:]
    bundle_ref, sibling_ref, partial_ref, weights_ref = refs[:4]
    send_ref, keep_ref, own_ref, above_ref = refs[4:]
    sample = peer_at(own_place(count), count // 2, count)
    shard = lax.axis_index("samples")
    parts, _, shard_rows = partial_ref.shape
    left = [both_heads(bundle_ref, sibling_ref, [sample], 2 * piece[0].shape[0])]
    for part in range(parts):
        cols = slice(part * shard_rows, (part + 1) * shard_rows)
        total = transposed(partial_ref[part] + weight_term([piece], left, cols))
        keep_ref[part] = total[:, :HEAD]
        send_ref[cols, :] = total[:, HEAD:]
    total = matmul(jnp.concatenate([rows[...] for rows in piece], axis=0), weights_ref[...])
    own_ref[...] = total[:, :HEAD]
    send_ref[parts * shard_rows :, :] = total[:, HEAD:].astype(jnp.bfloat16)
    cols = columns(shard, HEAD)
    above_ref[...] = jnp.concatenate([rows[:, cols] for rows in piece], axis=0)


def far_kernel(count, scale, *refs):
    came_ref, keep_ref, own_ref, above_ref, heads_ref, probs_ref, turned_ref = refs[:7]
    near_ref, mask_ref, partner_ref = refs[7:10]
    outs, (grads, terms) = refs[10:-2], refs[-2:]
    place = own_place(count)
    half = lax.axis_index("mp")
    seq_len = probs_ref.shape[1]
    skipped = seq_len + TAIL
    parts, shard_rows = keep_ref.shape[:2]
    for part in range(parts):
        terms[half * parts + part] = keep_ref[part]
        lines = slice(part * shard_rows, (part + 1) * shard_rows)
        terms[(1 - half) * parts + part] = came_ref[lines, :]
    for index, slot in enumerate(near_slots(count)):
        grads[peer_at(place, slot, count)] = near_ref[index]
    sample = peer_at(place, count // 2, count)
    other = came_ref[parts * shard_rows :, :].astype(jnp.float32)
    (grads[sample],) = attention_back(
        scale,
        [heads_ref[sample, 0:seq_len, :]],
        [probs_ref[sample]],
        [turned_ref[sample]],
        [(own_ref[...] + other).astype(jnp.bfloat16)],
        [above_ref[...]],
    )
    region = jnp.broadcast_to(mask_ref[...].astype(jnp.float32), (HEAD, seq_len)).T > 0.5
    which = lax.broadcasted_iota(jnp.int32, (TAIL, seq_len), 0).astype(jnp.float32)
    embed = jnp.zeros((TAIL, HEAD), jnp.float32)
    for slot in range(count):
        sample = peer_at(place, -slot, count)
        swapped = grads[partner_ref[sample]].astype(jnp.float32)
        site = jnp.where(region, swapped, grads[sample].astype(jnp.float32)).astype(jnp.bfloat16)
        outs[slot][0:seq_len, :] = site
        outs[slot][skipped:, :] = terms[sample]
        spin = heads_ref[sample, seq_len:skipped, :].astype(jnp.float32)
        embed = embed + matmul((spin == which).astype(jnp.bfloat16), site)
    high = embed.astype(jnp.bfloat16).astype(jnp.float32)
    low = embed - high
    tail = jnp.concatenate([high[: TAIL // 2], low[: TAIL // 2]], axis=0).astype(jnp.bfloat16)
    for slot in range(count):
        outs[slot][seq_len:skipped, :] = tail


def unpack_kernel(count, *refs):
    weight_ref, site_ref, embed_ref = refs[count:]
    place = own_place(count)
    seq_len = site_ref.shape[2]
    skipped = seq_len + TAIL
    for slot in range(count):
        cols = columns(peer_at(place, slot, count), HEAD)
        weight_ref[0, :, cols] = refs[slot][skipped:, :].astype(jnp.float32)
        site_ref[0, 0, :, cols] = refs[slot][0:seq_len, :]
        tail = refs[slot][seq_len:skipped, :].astype(jnp.float32)
        embed_ref[:, cols] = (tail[: TAIL // 2] + tail[TAIL // 2 :])[:SPINS]


def exchanged(blocks):
    return lax.all_to_all(blocks, "samples", split_axis=0, concat_axis=0, tiled=True)


def spread(blocks):
    count = len(blocks)
    sent = {
        slot: lax.ppermute(blocks[slot], "samples", ring_route(count, slot))
        for slot in sorted(range(1, count), key=lambda slot: abs(slot - count // 2))
    }
    return [blocks[0]] + [sent[slot] for slot in range(1, count)]


def head_sharded(
    stored_inputs, top_cotangent, layer_weights, block_layout, region_mask, partner_samples, spins
):
    count = lax.axis_size("samples")
    seq_len = stored_inputs.shape[2]
    shard_rows, half_width = layer_weights.shape[1:]
    scale = 4.0 / HEAD
    bf16, f32 = jnp.bfloat16, jnp.float32
    per_head = (count, seq_len, HEAD)
    lines = seq_len + TAIL
    share_axis = "groups" if lax.axis_size("groups") == 2 else None
    sent = shard_rows // 2 if share_axis else shard_rows
    parts = count // 2
    swap = [(0, 1), (1, 0)]

    up, down = ring_route(count, -1), ring_route(count, 1)
    block = top_cotangent[0]
    rows = seq_len // 2
    packed = on_core(
        functools.partial(pack_kernel, count, share_axis),
        jax.ShapeDtypeStruct((count, lines + sent, HEAD), bf16),
        [pl.BlockSpec(memory_space=pltpu.HBM)] * 2 + in_vmem(1),
        [pltpu.SemaphoreType.DMA((2, count))],
        micros=1,
        vmem=60,
    )(stored_inputs, layer_weights, spins)
    heads = exchanged(packed)
    slots = {0: block}
    ahead, back = block, block
    for step in range(1, count // 2):
        ahead = lax.ppermute(ahead, "samples", up)
        back = lax.ppermute(back, "samples", down)
        slots[count - step], slots[step] = ahead, back
    far = (
        lax.ppermute(ahead[:rows], "samples", up),
        lax.ppermute(back[rows:], "samples", down),
    )
    near = [slots[slot] for slot in near_slots(count)]
    small = (region_mask.reshape(1, seq_len), partner_samples)
    shared = []
    if share_axis:
        shared = [lax.ppermute(heads[:, lines:], share_axis, swap)]
    probs, turned, bundle = on_core(
        functools.partial(forward_kernel, count, scale),
        [
            jax.ShapeDtypeStruct(per_head, f32),
            jax.ShapeDtypeStruct(per_head, bf16),
            jax.ShapeDtypeStruct((count * seq_len + half_width, HEAD), bf16),
        ],
        in_vmem(2 + len(shared)) + in_smem(2),
        micros=1.2,
    )(heads, *shared, *small, block_layout)
    sibling = lax.ppermute(bundle, "mp", swap)
    near_lines = (count - 1) * seq_len
    partial, near_own, near_other, near_above, weights = on_core(
        functools.partial(near_products_kernel, count, share_axis),
        [
            jax.ShapeDtypeStruct((parts, 2 * HEAD, shard_rows), f32),
            jax.ShapeDtypeStruct((near_lines, HEAD), f32),
            jax.ShapeDtypeStruct((near_lines, HEAD), bf16),
            jax.ShapeDtypeStruct((near_lines, HEAD), bf16),
            jax.ShapeDtypeStruct((half_width, 2 * HEAD), bf16),
        ],
        in_vmem(count + 2 + len(shared)),
        micros=1.4,
    )(*near, bundle, sibling, heads, *shared)
    near_other = lax.ppermute(near_other, "mp", swap)
    near_grads = on_core(
        functools.partial(near_back_kernel, count, scale),
        jax.ShapeDtypeStruct((count - 1, seq_len, HEAD), bf16),
        in_vmem(7) + in_smem(1),
        micros=1.8,
    )(heads, probs, turned, near_own, near_other, near_above, *small)
    far_send, far_keep, far_own, far_above = on_core(
        functools.partial(far_products_kernel, count),
        [
            jax.ShapeDtypeStruct((half_width + seq_len, HEAD), bf16),
            jax.ShapeDtypeStruct((parts, shard_rows, HEAD), bf16),
            jax.ShapeDtypeStruct((seq_len, HEAD), f32),
            jax.ShapeDtypeStruct((seq_len, HEAD), bf16),
        ],
        in_vmem(6),
        micros=0.5,
    )(*far, bundle, sibling, partial, weights)
    far_came = lax.ppermute(far_send, "mp", swap)
    terms = on_core(
        functools.partial(far_kernel, count, scale),
        [jax.ShapeDtypeStruct((lines + shard_rows, HEAD), bf16)] * count,
        in_vmem(9) + in_smem(1),
        [pltpu.VMEM(per_head, bf16), pltpu.VMEM((count, shard_rows, HEAD), bf16)],
        micros=1.2,
    )(far_came, far_keep, far_own, far_above, heads, probs, turned, near_grads, *small)
    return on_core(
        functools.partial(unpack_kernel, count),
        [
            jax.ShapeDtypeStruct((1, shard_rows, half_width), f32),
            jax.ShapeDtypeStruct((1, 1, seq_len, half_width), bf16),
            jax.ShapeDtypeStruct((SPINS, half_width), f32),
        ],
        in_vmem(count),
        micros=1.2,
    )(*spread(terms))


def solution(mesh):
    in_specs = (
        P("section", ("groups", "samples"), None, "mp"),
        P(("groups", "samples"), None, "mp"),
        P("section", "samples", "mp"),
        P("section", None, None),
        P(),
        P("groups"),
        P(("groups", "samples"), None),
    )
    out_specs = (
        P(("groups", "section"), "samples", "mp"),
        P("section", ("groups", "samples"), None, "mp"),
        P("groups", "mp"),
    )
    shards = mesh.shape["samples"]

    def whole(stored_inputs, top_cotangent, *rest):
        samples, _, width = top_cotangent.shape
        layer_count = stored_inputs.shape[0]
        one_each = samples == mesh.shape["groups"] * shards and layer_count == 1
        by_heads = one_each and shards % 2 == 0 and width == mesh.shape["mp"] * shards * HEAD
        return jax.shard_map(
            head_sharded if by_heads else local,
            mesh=mesh,
            in_specs=in_specs,
            out_specs=out_specs,
            check_vma=False,
        )(stored_inputs, top_cotangent, *rest)

    return whole
```

```python
import functools

import jax
import jax.numpy as jnp
from jax import lax
from jax.experimental import pallas as pl
from jax.experimental.pallas import tpu as pltpu
from jax.sharding import PartitionSpec as P

HEAD = 128
BLOCK = 64
SPINS = 2
TAIL = 16
FLOPS_PER_MICRO = 1.15e9


def for_sending(value):

    def short(part):
        return part.astype(jnp.bfloat16) if part.dtype == jnp.float32 else part

    return jax.tree.map(short, value)


def passed_along(block, axis, distance):
    devices = range(lax.axis_size(axis))
    route = [(i - distance, i) for i in devices if i - distance in devices]
    return lax.ppermute(block, axis, route)


def softmax_parts(inputs_h, allowed, attention_scale):
    scores = (
        jnp.einsum("qhd,khd->hqk", inputs_h, inputs_h, preferred_element_type=jnp.float32)
        * attention_scale
    )
    scores = jnp.where(allowed[None], scores, -jnp.inf)
    top_score = jnp.max(scores, axis=-1, keepdims=True)
    expo_terms = jnp.exp(scores - top_score)
    probs = expo_terms / jnp.sum(expo_terms, axis=-1, keepdims=True)
    return (probs, probs.astype(jnp.bfloat16))


def local(
    stored_inputs, top_cotangent, layer_weights, block_layout, region_mask, partner_samples, spins
):
    section_index = lax.axis_index("section")
    section_count = lax.axis_size("section")
    micro_count = stored_inputs.shape[1]
    seq_len = stored_inputs.shape[2]
    half_width = stored_inputs.shape[3]
    head_count = half_width // HEAD
    attention_scale = 4.0 / HEAD
    weights = lax.all_gather(layer_weights[0], "samples", axis=0, tiled=True)
    pos_block = jnp.arange(seq_len) // BLOCK
    block_onehot = (pos_block[:, None] == jnp.arange(block_layout.shape[1])[None, :]).astype(
        jnp.float32
    )
    linked = jnp.dot(jnp.dot(block_onehot, block_layout[0].astype(jnp.float32)), block_onehot.T)
    allowed = (linked > 0.5) | (pos_block[:, None] == pos_block[None, :])
    every_layer_input = stored_inputs[0]
    inputs_h = every_layer_input[0].reshape(seq_len, head_count, HEAD)
    probs, probs_low = softmax_parts(inputs_h, allowed, attention_scale)
    attended = jnp.einsum(
        "hqk,khd->qhd", probs_low, inputs_h, preferred_element_type=jnp.float32
    ).astype(jnp.bfloat16)
    probs_list = [probs]
    low_list = [probs_low]
    attend_list = [attended.reshape(seq_len, half_width)]
    probs_all = jnp.stack(probs_list)
    low_all = jnp.stack(low_list)
    attend_store = jnp.stack(attend_list)

    def layer_back(grad_full, grad_own, inputs, probs, probs_low):
        grad_attn = jnp.dot(grad_full, weights, preferred_element_type=jnp.float32).astype(
            jnp.bfloat16
        )
        inputs_h = inputs.reshape(seq_len, head_count, HEAD)
        grad_h = grad_attn.reshape(seq_len, head_count, HEAD)
        grad_probs = jnp.einsum(
            "qhd,khd->hqk", grad_h, inputs_h, preferred_element_type=jnp.float32
        )
        grad_scores = (
            probs * (grad_probs - jnp.sum(grad_probs * probs, axis=-1, keepdims=True))
        ).astype(jnp.bfloat16)
        through = jnp.einsum("hqk,qhd->khd", probs_low, grad_h, preferred_element_type=jnp.float32)
        through = through + attention_scale * (
            jnp.einsum("hqk,khd->qhd", grad_scores, inputs_h, preferred_element_type=jnp.float32)
            + jnp.einsum("hqk,qhd->khd", grad_scores, inputs_h, preferred_element_type=jnp.float32)
        )
        grad_in = grad_own.astype(jnp.float32) + through.reshape(seq_len, half_width)
        return grad_in.astype(jnp.bfloat16)

    def resting(grad_full, grad_own, inputs, probs, probs_low):
        return jnp.zeros((seq_len, half_width), jnp.bfloat16)

    carried_state = jnp.zeros((seq_len, half_width), jnp.bfloat16)
    out_list = []
    grad_list = []
    total_steps = micro_count + section_count - 1
    for step_number in range(total_steps):
        micro_index = step_number - (section_count - 1 - section_index)
        active = (micro_index >= 0) & (micro_index < micro_count)
        slot_index = jnp.clip(micro_index, 0, micro_count - 1)
        from_top = lax.dynamic_index_in_dim(top_cotangent, slot_index, 0, keepdims=False)
        incoming = jnp.where(section_index == section_count - 1, from_top, carried_state)
        grad_full = lax.all_gather(incoming, "mp", axis=1, tiled=True)
        inputs_now = lax.dynamic_index_in_dim(every_layer_input, slot_index, 0, keepdims=False)
        probs_now = lax.dynamic_index_in_dim(probs_all, slot_index, 0, keepdims=False)
        low_now = lax.dynamic_index_in_dim(low_all, slot_index, 0, keepdims=False)
        grad_in = lax.cond(
            active, layer_back, resting, grad_full, incoming, inputs_now, probs_now, low_now
        )
        out_list.append(grad_in)
        grad_list.append(grad_full)
        if step_number < total_steps - 1:
            carried_state = jax.tree.map(
                lambda part, own: part.astype(own.dtype),
                passed_along(for_sending(grad_in), "section", -1),
                grad_in,
            )
    offset = section_count - 1 - section_index
    out_store = lax.dynamic_slice_in_dim(jnp.stack(out_list), offset, micro_count, 0)
    grad_store = lax.dynamic_slice_in_dim(jnp.stack(grad_list), offset, micro_count, 0)
    summed_weight = lax.psum_scatter(
        jnp.einsum(
            "mtf,mta->fa", grad_store, attend_store, preferred_element_type=jnp.float32
        ).astype(jnp.bfloat16),
        "samples",
        scatter_dimension=0,
        tiled=True,
    ).astype(jnp.float32)
    region_count = seq_len // 2
    rank_in_region = jnp.cumsum(region_mask) - 1
    select = (
        (rank_in_region[None, :] == jnp.arange(region_count)[:, None]) & (region_mask[None, :] > 0)
    ).astype(jnp.bfloat16)
    tiles = jnp.einsum("at,mtd->mad", select, out_store, preferred_element_type=jnp.float32).astype(
        jnp.bfloat16
    )
    shard_index = lax.axis_index("samples")
    my_partners = lax.dynamic_slice_in_dim(
        partner_samples, shard_index * micro_count, micro_count, 0
    )
    shard_count = lax.axis_size("samples")
    dest_shard = my_partners // micro_count
    dest_slot = my_partners % micro_count
    route = (
        (dest_shard[:, None, None] == jnp.arange(shard_count)[None, :, None])
        & (dest_slot[:, None, None] == jnp.arange(micro_count)[None, None, :])
    ).astype(jnp.bfloat16)
    outgoing = jnp.einsum("mku,mad->kuad", route, tiles, preferred_element_type=jnp.float32).astype(
        jnp.bfloat16
    )
    arrived = lax.all_to_all(outgoing, "samples", split_axis=0, concat_axis=0, tiled=True)
    ones_row = jnp.ones((shard_count,), jnp.bfloat16)
    received = jnp.einsum(
        "k,kuad->uad", ones_row, arrived, preferred_element_type=jnp.float32
    ).astype(jnp.bfloat16)
    placed = jnp.einsum("at,mad->mtd", select, received, preferred_element_type=jnp.float32)
    kept = jnp.where(region_mask[None, :, None] > 0, jnp.zeros_like(out_store), out_store)
    site_cot = (kept.astype(jnp.float32) + placed).astype(jnp.bfloat16)
    cotangents = jnp.where(section_index == 0, site_cot, out_store)
    onehot = (spins[:, :, None] == jnp.arange(SPINS)[None, None, :]).astype(jnp.bfloat16)
    embed_term = jnp.einsum("mtv,mtd->vd", onehot, site_cot, preferred_element_type=jnp.float32)
    embed_term = jnp.where(section_index == 0, embed_term, jnp.zeros_like(embed_term))
    embed_grad = lax.psum(embed_term, ("samples", "section"))
    return (summed_weight[None], cotangents[None], embed_grad)


def ring_sample(place, count):
    return jnp.where(place < count // 2, 2 * place, 2 * (count - place) - 1)


def ring_place(sample, count):
    return jnp.where(lax.rem(sample, 2) == 0, sample // 2, count - 1 - sample // 2)


def ring_route(count, distance):
    order = list(range(0, count, 2)) + list(range(1, count, 2))[::-1]
    return [(order[i], order[(i - distance) % count]) for i in range(count)]


def own_place(count):
    return ring_place(lax.axis_index("samples"), count)


def peer_at(place, distance, count):
    return ring_sample(lax.rem(place + distance + count, count), count)


def columns(index, size):
    return pl.ds(pl.multiple_of(index * size, size), size)


def in_vmem(count):
    return [pl.BlockSpec(memory_space=pltpu.VMEM)] * count


def in_smem(count):
    return [pl.BlockSpec(memory_space=pltpu.SMEM)] * count


def on_core(body, out_shapes, in_specs, scratch=(), micros=1, vmem=16):
    return pl.pallas_call(
        body,
        out_shape=out_shapes,
        in_specs=in_specs,
        out_specs=jax.tree.map(lambda _: pl.BlockSpec(memory_space=pltpu.VMEM), out_shapes),
        scratch_shapes=list(scratch),
        compiler_params=pltpu.CompilerParams(vmem_limit_bytes=vmem << 20),
        cost_estimate=pl.CostEstimate(
            flops=int(micros * FLOPS_PER_MICRO), bytes_accessed=1 << 16, transcendentals=0
        ),
    )


def matmul(left, right):
    return jnp.dot(left, right, preferred_element_type=jnp.float32)


def matmul_t(left, right):
    return lax.dot_general(
        left, right, (((1,), (1,)), ((), ())), preferred_element_type=jnp.float32
    )


def pack_kernel(count, share_axis, x_ref, w_ref, spins_ref, *refs):
    outs, sems = refs[:-1], refs[-1]
    place = own_place(count)
    seq_len = x_ref.shape[2]
    skipped = seq_len + TAIL
    sent = outs[0].shape[0] - skipped
    rows = columns(lax.axis_index(share_axis), sent) if share_axis else slice(None)
    copies = []
    for slot in range(count):
        cols = columns(peer_at(place, -slot, count), HEAD)
        head, weight = outs[slot].at[0:seq_len, :], outs[slot].at[skipped:, :]
        copies.append(pltpu.make_async_copy(x_ref.at[0, 0, :, cols], head, sems.at[0, slot]))
        copies.append(pltpu.make_async_copy(w_ref.at[0, rows, cols], weight, sems.at[1, slot]))
    for copy in copies:
        copy.start()
    spin_rows = jnp.broadcast_to(spins_ref[...].astype(jnp.float32), (TAIL, seq_len))
    for slot in range(count):
        outs[slot][seq_len:skipped, :] = spin_rows.astype(jnp.bfloat16)
    for copy in copies:
        copy.wait()


def collect_kernel(count, *refs):
    heads_ref, rows_ref = refs[count:]
    place = own_place(count)
    sent = rows_ref.shape[1]
    for slot in range(count):
        peer = peer_at(place, slot, count)
        heads_ref[peer] = refs[slot][...]
        rows_ref[peer] = refs[slot][-sent:, :]


def forward_kernel(count, scale, *refs):
    heads_ref, shared, layout_ref = refs[0], refs[1:-6], refs[-4]
    probs_ref, turned_ref, bundle_ref = refs[-3:]
    seq_len = probs_ref.shape[1]
    lines = seq_len + TAIL
    half = lax.axis_index("mp")
    parts = count // 2
    sent = heads_ref.shape[1] - lines
    for part in range(parts):
        shard = (1 - half) * parts + part
        for piece, value in enumerate((heads_ref[shard, lines:, :], *(ref[shard] for ref in shared))):
            first = count * seq_len + (piece * parts + part) * sent
            bundle_ref[first : first + sent, :] = value
    blocks = layout_ref.shape[1]
    rows = lax.broadcasted_iota(jnp.int32, (seq_len, seq_len), 0) // BLOCK
    cols = lax.broadcasted_iota(jnp.int32, (seq_len, seq_len), 1) // BLOCK
    seen = rows == cols
    for q in range(blocks):
        for k in range(blocks):
            if q != k:
                seen = seen | ((rows == q) & (cols == k) & (layout_ref[0, q, k] > 0))
    xs = [heads_ref[slot, 0:seq_len, :] for slot in range(count)]
    scores = [jnp.where(seen, matmul_t(x, x) * scale, -jnp.inf) for x in xs]
    tops = [jnp.max(score, axis=-1, keepdims=True) for score in scores]
    terms = [jnp.exp(score - top) for score, top in zip(scores, tops)]
    sums = [jnp.sum(term, axis=-1, keepdims=True) for term in terms]
    for slot in range(count):
        probs = terms[slot] / sums[slot]
        low = probs.astype(jnp.bfloat16)
        probs_ref[slot] = probs
        attended = matmul(low, xs[slot]).astype(jnp.bfloat16)
        bundle_ref[slot * seq_len : (slot + 1) * seq_len, :] = attended
        turned_ref[slot] = transposed(low)


def lay_weights(weights, shares, share_axis):
    index = lax.axis_index(share_axis) if share_axis else 0
    pieces = len(shares) // 2
    parts = len(shares[0])
    for number, share in enumerate(shares):
        head, piece = number % 2, number // 2
        place = index if piece == 0 else 1 - index
        for part, value in enumerate(share):
            sent = value.shape[0]
            rows = pl.ds(pl.multiple_of((part * pieces + place) * sent, sent), sent)
            weights[rows, head * HEAD : (head + 1) * HEAD] = value


def weight_term(pieces, left, cols):
    total = None
    for index, first in enumerate(range(0, len(pieces), 2)):
        rows = [piece[:, cols] for slot in pieces[first : first + 2] for piece in slot]
        term = matmul(left[index], jnp.concatenate(rows, axis=0))
        total = term if total is None else total + term
    return total


def both_heads(own_ref, sibling_ref, samples, seq_len):
    rows = [
        jnp.concatenate(
            [ref[columns(sample, seq_len), :] for ref in (own_ref, sibling_ref)], axis=1
        )
        for sample in samples
    ]
    return transposed(jnp.concatenate(rows, axis=0))


def transposed(value):
    return value.astype(jnp.float32).T.astype(jnp.bfloat16)


def attention_back(scale, xs, probs, turned, grads, above):
    grad_probs = [matmul_t(grad, x) for grad, x in zip(grads, xs)]
    inner = [jnp.sum(grad * prob, axis=-1, keepdims=True) for grad, prob in zip(grad_probs, probs)]
    grad_scores = [
        (prob * (grad - total)).astype(jnp.bfloat16)
        for prob, grad, total in zip(probs, grad_probs, inner)
    ]
    both = [jnp.concatenate([grad, transposed(grad)], axis=1) for grad in grad_scores]
    results = []
    for index, x in enumerate(xs):
        through = matmul(turned[index], grads[index])
        through = through + scale * matmul(both[index], jnp.concatenate([x, x], axis=0))
        results.append((above[index].astype(jnp.float32) + through).astype(jnp.bfloat16))
    return results


def near_slots(count):
    return [slot for slot in range(count) if slot != count // 2]


def near_products_kernel(count, share_axis, *refs):
    pieces = [refs[index : index + 1] for index in range(count - 1)]
    bundle_ref, sibling_ref, heads_ref = refs[count - 1 : count + 2]
    shared = refs[count + 2 : -5]
    partial_ref, own_ref, other_ref, above_ref, weights = refs[-5:]
    place = own_place(count)
    shard = lax.axis_index("samples")
    parts, _, shard_rows = partial_ref.shape
    seq_len = pieces[0][0].shape[0]
    lines = seq_len + TAIL
    sent = heads_ref.shape[1] - lines
    half = lax.axis_index("mp")
    sample_of = [peer_at(place, slot, count) for slot in near_slots(count)]
    shares = []
    for piece, ref in enumerate((heads_ref, *shared)):
        skipped = lines if piece == 0 else 0
        shares.append([ref[half * parts + part, skipped:, :] for part in range(parts)])
        firsts = [count * seq_len + (piece * parts + part) * sent for part in range(parts)]
        shares.append([sibling_ref[first : first + sent, :] for first in firsts])
    lay_weights(weights, shares, share_axis)
    left = [
        both_heads(bundle_ref, sibling_ref, sample_of[first : first + 2], seq_len)
        for first in range(0, count - 1, 2)
    ]
    for part in range(parts):
        cols = slice(part * shard_rows, (part + 1) * shard_rows)
        partial_ref[part] = weight_term(pieces, left, cols)
    for first in range(0, count - 1, 2):
        rows = [piece[...] for slot in pieces[first : first + 2] for piece in slot]
        total = matmul(jnp.concatenate(rows, axis=0), weights[...])
        lines = slice(first * seq_len, first * seq_len + total.shape[0])
        own_ref[lines, :] = total[:, :HEAD]
        other_ref[lines, :] = total[:, HEAD:].astype(jnp.bfloat16)
    for index, slot in enumerate(pieces):
        above_ref[index * seq_len : (index + 1) * seq_len, :] = slot[0][:, columns(shard, HEAD)]


def near_back_kernel(count, scale, *refs):
    heads_ref, probs_ref, turned_ref, own_ref, other_ref, above_ref = refs[:6]
    grads_ref = refs[-1]
    place = own_place(count)
    seq_len = probs_ref.shape[1]
    sample_of = [peer_at(place, slot, count) for slot in near_slots(count)]
    lines = [slice(index * seq_len, (index + 1) * seq_len) for index in range(count - 1)]
    results = attention_back(
        scale,
        [heads_ref[sample, 0:seq_len, :] for sample in sample_of],
        [probs_ref[sample] for sample in sample_of],
        [turned_ref[sample] for sample in sample_of],
        [
            (own_ref[line, :] + other_ref[line, :].astype(jnp.float32)).astype(jnp.bfloat16)
            for line in lines
        ],
        [above_ref[line, :] for line in lines],
    )
    for index, result in enumerate(results):
        grads_ref[index] = result


def far_products_kernel(count, *refs):
    piece, refs = refs[:2], refs[2:]
    bundle_ref, sibling_ref, partial_ref, weights_ref = refs[:4]
    send_ref, keep_ref, own_ref, above_ref = refs[4:]
    sample = peer_at(own_place(count), count // 2, count)
    shard = lax.axis_index("samples")
    parts, _, shard_rows = partial_ref.shape
    left = [both_heads(bundle_ref, sibling_ref, [sample], 2 * piece[0].shape[0])]
    for part in range(parts):
        cols = slice(part * shard_rows, (part + 1) * shard_rows)
        total = transposed(partial_ref[part] + weight_term([piece], left, cols))
        keep_ref[part] = total[:, :HEAD]
        send_ref[cols, :] = total[:, HEAD:]
    total = matmul(jnp.concatenate([rows[...] for rows in piece], axis=0), weights_ref[...])
    own_ref[...] = total[:, :HEAD]
    send_ref[parts * shard_rows :, :] = total[:, HEAD:].astype(jnp.bfloat16)
    cols = columns(shard, HEAD)
    above_ref[...] = jnp.concatenate([rows[:, cols] for rows in piece], axis=0)


def far_kernel(count, scale, *refs):
    came_ref, keep_ref, own_ref, above_ref, heads_ref, probs_ref, turned_ref = refs[:7]
    near_ref, mask_ref, partner_ref = refs[7:10]
    outs, (grads, terms) = refs[10:-2], refs[-2:]
    place = own_place(count)
    half = lax.axis_index("mp")
    seq_len = probs_ref.shape[1]
    skipped = seq_len + TAIL
    parts, shard_rows = keep_ref.shape[:2]
    for part in range(parts):
        terms[half * parts + part] = keep_ref[part]
        lines = slice(part * shard_rows, (part + 1) * shard_rows)
        terms[(1 - half) * parts + part] = came_ref[lines, :]
    for index, slot in enumerate(near_slots(count)):
        grads[peer_at(place, slot, count)] = near_ref[index]
    sample = peer_at(place, count // 2, count)
    other = came_ref[parts * shard_rows :, :].astype(jnp.float32)
    (grads[sample],) = attention_back(
        scale,
        [heads_ref[sample, 0:seq_len, :]],
        [probs_ref[sample]],
        [turned_ref[sample]],
        [(own_ref[...] + other).astype(jnp.bfloat16)],
        [above_ref[...]],
    )
    region = jnp.broadcast_to(mask_ref[...].astype(jnp.float32), (HEAD, seq_len)).T > 0.5
    which = lax.broadcasted_iota(jnp.int32, (TAIL, seq_len), 0).astype(jnp.float32)
    embed = jnp.zeros((TAIL, HEAD), jnp.float32)
    for slot in range(count):
        sample = peer_at(place, -slot, count)
        swapped = grads[partner_ref[sample]].astype(jnp.float32)
        site = jnp.where(region, swapped, grads[sample].astype(jnp.float32)).astype(jnp.bfloat16)
        outs[slot][0:seq_len, :] = site
        outs[slot][skipped:, :] = terms[sample]
        spin = heads_ref[sample, seq_len:skipped, :].astype(jnp.float32)
        embed = embed + matmul((spin == which).astype(jnp.bfloat16), site)
    high = embed.astype(jnp.bfloat16).astype(jnp.float32)
    low = embed - high
    tail = jnp.concatenate([high[: TAIL // 2], low[: TAIL // 2]], axis=0).astype(jnp.bfloat16)
    for slot in range(count):
        outs[slot][seq_len:skipped, :] = tail


def unpack_kernel(count, *refs):
    weight_ref, site_ref, embed_ref = refs[count:]
    place = own_place(count)
    seq_len = site_ref.shape[2]
    skipped = seq_len + TAIL
    for slot in range(count):
        cols = columns(peer_at(place, slot, count), HEAD)
        weight_ref[0, :, cols] = refs[slot][skipped:, :].astype(jnp.float32)
        site_ref[0, 0, :, cols] = refs[slot][0:seq_len, :]
        tail = refs[slot][seq_len:skipped, :].astype(jnp.float32)
        embed_ref[:, cols] = (tail[: TAIL // 2] + tail[TAIL // 2 :])[:SPINS]


def spread(blocks):
    count = len(blocks)
    sent = {
        slot: lax.ppermute(blocks[slot], "samples", ring_route(count, slot))
        for slot in sorted(range(1, count), key=lambda slot: abs(slot - count // 2))
    }
    return [blocks[0]] + [sent[slot] for slot in range(1, count)]


def head_sharded(
    stored_inputs, top_cotangent, layer_weights, block_layout, region_mask, partner_samples, spins
):
    count = lax.axis_size("samples")
    seq_len = stored_inputs.shape[2]
    shard_rows, half_width = layer_weights.shape[1:]
    scale = 4.0 / HEAD
    bf16, f32 = jnp.bfloat16, jnp.float32
    per_head = (count, seq_len, HEAD)
    lines = seq_len + TAIL
    share_axis = "groups" if lax.axis_size("groups") == 2 else None
    sent = shard_rows // 2 if share_axis else shard_rows
    parts = count // 2
    swap = [(0, 1), (1, 0)]

    up, down = ring_route(count, -1), ring_route(count, 1)
    block = top_cotangent[0]
    rows = seq_len // 2
    packed = on_core(
        functools.partial(pack_kernel, count, share_axis),
        [jax.ShapeDtypeStruct((lines + sent, HEAD), bf16)] * count,
        [pl.BlockSpec(memory_space=pltpu.HBM)] * 2 + in_vmem(1),
        [pltpu.SemaphoreType.DMA((2, count))],
        micros=1,
        vmem=60,
    )(stored_inputs, layer_weights, spins)
    heads, weight_rows = on_core(
        functools.partial(collect_kernel, count),
        [
            jax.ShapeDtypeStruct((count, lines + sent, HEAD), bf16),
            jax.ShapeDtypeStruct((count, sent, HEAD), bf16),
        ],
        in_vmem(count),
        micros=0.4,
    )(*spread(packed))
    slots = {0: block}
    ahead, back = block, block
    for step in range(1, count // 2):
        ahead = lax.ppermute(ahead, "samples", up)
        back = lax.ppermute(back, "samples", down)
        slots[count - step], slots[step] = ahead, back
    far = (
        lax.ppermute(ahead[:rows], "samples", up),
        lax.ppermute(back[rows:], "samples", down),
    )
    near = [slots[slot] for slot in near_slots(count)]
    small = (region_mask.reshape(1, seq_len), partner_samples)
    shared = []
    if share_axis:
        shared = [lax.ppermute(weight_rows, share_axis, swap)]
    probs, turned, bundle = on_core(
        functools.partial(forward_kernel, count, scale),
        [
            jax.ShapeDtypeStruct(per_head, f32),
            jax.ShapeDtypeStruct(per_head, bf16),
            jax.ShapeDtypeStruct((count * seq_len + half_width, HEAD), bf16),
        ],
        in_vmem(2 + len(shared)) + in_smem(2),
        micros=1.2,
    )(heads, *shared, *small, block_layout)
    sibling = lax.ppermute(bundle, "mp", swap)
    near_lines = (count - 1) * seq_len
    partial, near_own, near_other, near_above, weights = on_core(
        functools.partial(near_products_kernel, count, share_axis),
        [
            jax.ShapeDtypeStruct((parts, 2 * HEAD, shard_rows), f32),
            jax.ShapeDtypeStruct((near_lines, HEAD), f32),
            jax.ShapeDtypeStruct((near_lines, HEAD), bf16),
            jax.ShapeDtypeStruct((near_lines, HEAD), bf16),
            jax.ShapeDtypeStruct((half_width, 2 * HEAD), bf16),
        ],
        in_vmem(count + 2 + len(shared)),
        micros=1.4,
    )(*near, bundle, sibling, heads, *shared)
    near_other = lax.ppermute(near_other, "mp", swap)
    near_grads = on_core(
        functools.partial(near_back_kernel, count, scale),
        jax.ShapeDtypeStruct((count - 1, seq_len, HEAD), bf16),
        in_vmem(7) + in_smem(1),
        micros=1.8,
    )(heads, probs, turned, near_own, near_other, near_above, *small)
    far_send, far_keep, far_own, far_above = on_core(
        functools.partial(far_products_kernel, count),
        [
            jax.ShapeDtypeStruct((half_width + seq_len, HEAD), bf16),
            jax.ShapeDtypeStruct((parts, shard_rows, HEAD), bf16),
            jax.ShapeDtypeStruct((seq_len, HEAD), f32),
            jax.ShapeDtypeStruct((seq_len, HEAD), bf16),
        ],
        in_vmem(6),
        micros=0.5,
    )(*far, bundle, sibling, partial, weights)
    far_came = lax.ppermute(far_send, "mp", swap)
    terms = on_core(
        functools.partial(far_kernel, count, scale),
        [jax.ShapeDtypeStruct((lines + shard_rows, HEAD), bf16)] * count,
        in_vmem(9) + in_smem(1),
        [pltpu.VMEM(per_head, bf16), pltpu.VMEM((count, shard_rows, HEAD), bf16)],
        micros=1.2,
    )(far_came, far_keep, far_own, far_above, heads, probs, turned, near_grads, *small)
    return on_core(
        functools.partial(unpack_kernel, count),
        [
            jax.ShapeDtypeStruct((1, shard_rows, half_width), f32),
            jax.ShapeDtypeStruct((1, 1, seq_len, half_width), bf16),
            jax.ShapeDtypeStruct((SPINS, half_width), f32),
        ],
        in_vmem(count),
        micros=1.2,
    )(*spread(terms))


def solution(mesh):
    in_specs = (
        P("section", ("groups", "samples"), None, "mp"),
        P(("groups", "samples"), None, "mp"),
        P("section", "samples", "mp"),
        P("section", None, None),
        P(),
        P("groups"),
        P(("groups", "samples"), None),
    )
    out_specs = (
        P(("groups", "section"), "samples", "mp"),
        P("section", ("groups", "samples"), None, "mp"),
        P("groups", "mp"),
    )
    shards = mesh.shape["samples"]

    def whole(stored_inputs, top_cotangent, *rest):
        samples, _, width = top_cotangent.shape
        layer_count = stored_inputs.shape[0]
        one_each = samples == mesh.shape["groups"] * shards and layer_count == 1
        by_heads = one_each and shards % 2 == 0 and width == mesh.shape["mp"] * shards * HEAD
        return jax.shard_map(
            head_sharded if by_heads else local,
            mesh=mesh,
            in_specs=in_specs,
            out_specs=out_specs,
            check_vma=False,
        )(stored_inputs, top_cotangent, *rest)

    return whole
```

```python
import functools

import jax
import jax.numpy as jnp
from jax import lax
from jax.experimental import pallas as pl
from jax.experimental.pallas import tpu as pltpu
from jax.sharding import PartitionSpec as P

HEAD = 128
BLOCK = 64
SPINS = 2
TAIL = 16
FLOPS_PER_MICRO = 1.15e9


def for_sending(value):

    def short(part):
        return part.astype(jnp.bfloat16) if part.dtype == jnp.float32 else part

    return jax.tree.map(short, value)


def passed_along(block, axis, distance):
    devices = range(lax.axis_size(axis))
    route = [(i - distance, i) for i in devices if i - distance in devices]
    return lax.ppermute(block, axis, route)


def softmax_parts(inputs_h, allowed, attention_scale):
    scores = (
        jnp.einsum("qhd,khd->hqk", inputs_h, inputs_h, preferred_element_type=jnp.float32)
        * attention_scale
    )
    scores = jnp.where(allowed[None], scores, -jnp.inf)
    top_score = jnp.max(scores, axis=-1, keepdims=True)
    expo_terms = jnp.exp(scores - top_score)
    probs = expo_terms / jnp.sum(expo_terms, axis=-1, keepdims=True)
    return (probs, probs.astype(jnp.bfloat16))


def local(
    stored_inputs, top_cotangent, layer_weights, block_layout, region_mask, partner_samples, spins
):
    section_index = lax.axis_index("section")
    section_count = lax.axis_size("section")
    micro_count = stored_inputs.shape[1]
    seq_len = stored_inputs.shape[2]
    half_width = stored_inputs.shape[3]
    head_count = half_width // HEAD
    attention_scale = 4.0 / HEAD
    weights = lax.all_gather(layer_weights[0], "samples", axis=0, tiled=True)
    pos_block = jnp.arange(seq_len) // BLOCK
    block_onehot = (pos_block[:, None] == jnp.arange(block_layout.shape[1])[None, :]).astype(
        jnp.float32
    )
    linked = jnp.dot(jnp.dot(block_onehot, block_layout[0].astype(jnp.float32)), block_onehot.T)
    allowed = (linked > 0.5) | (pos_block[:, None] == pos_block[None, :])
    every_layer_input = stored_inputs[0]
    inputs_h = every_layer_input[0].reshape(seq_len, head_count, HEAD)
    probs, probs_low = softmax_parts(inputs_h, allowed, attention_scale)
    attended = jnp.einsum(
        "hqk,khd->qhd", probs_low, inputs_h, preferred_element_type=jnp.float32
    ).astype(jnp.bfloat16)
    probs_list = [probs]
    low_list = [probs_low]
    attend_list = [attended.reshape(seq_len, half_width)]
    probs_all = jnp.stack(probs_list)
    low_all = jnp.stack(low_list)
    attend_store = jnp.stack(attend_list)

    def layer_back(grad_full, grad_own, inputs, probs, probs_low):
        grad_attn = jnp.dot(grad_full, weights, preferred_element_type=jnp.float32).astype(
            jnp.bfloat16
        )
        inputs_h = inputs.reshape(seq_len, head_count, HEAD)
        grad_h = grad_attn.reshape(seq_len, head_count, HEAD)
        grad_probs = jnp.einsum(
            "qhd,khd->hqk", grad_h, inputs_h, preferred_element_type=jnp.float32
        )
        grad_scores = (
            probs * (grad_probs - jnp.sum(grad_probs * probs, axis=-1, keepdims=True))
        ).astype(jnp.bfloat16)
        through = jnp.einsum("hqk,qhd->khd", probs_low, grad_h, preferred_element_type=jnp.float32)
        through = through + attention_scale * (
            jnp.einsum("hqk,khd->qhd", grad_scores, inputs_h, preferred_element_type=jnp.float32)
            + jnp.einsum("hqk,qhd->khd", grad_scores, inputs_h, preferred_element_type=jnp.float32)
        )
        grad_in = grad_own.astype(jnp.float32) + through.reshape(seq_len, half_width)
        return grad_in.astype(jnp.bfloat16)

    def resting(grad_full, grad_own, inputs, probs, probs_low):
        return jnp.zeros((seq_len, half_width), jnp.bfloat16)

    carried_state = jnp.zeros((seq_len, half_width), jnp.bfloat16)
    out_list = []
    grad_list = []
    total_steps = micro_count + section_count - 1
    for step_number in range(total_steps):
        micro_index = step_number - (section_count - 1 - section_index)
        active = (micro_index >= 0) & (micro_index < micro_count)
        slot_index = jnp.clip(micro_index, 0, micro_count - 1)
        from_top = lax.dynamic_index_in_dim(top_cotangent, slot_index, 0, keepdims=False)
        incoming = jnp.where(section_index == section_count - 1, from_top, carried_state)
        grad_full = lax.all_gather(incoming, "mp", axis=1, tiled=True)
        inputs_now = lax.dynamic_index_in_dim(every_layer_input, slot_index, 0, keepdims=False)
        probs_now = lax.dynamic_index_in_dim(probs_all, slot_index, 0, keepdims=False)
        low_now = lax.dynamic_index_in_dim(low_all, slot_index, 0, keepdims=False)
        grad_in = lax.cond(
            active, layer_back, resting, grad_full, incoming, inputs_now, probs_now, low_now
        )
        out_list.append(grad_in)
        grad_list.append(grad_full)
        if step_number < total_steps - 1:
            carried_state = jax.tree.map(
                lambda part, own: part.astype(own.dtype),
                passed_along(for_sending(grad_in), "section", -1),
                grad_in,
            )
    offset = section_count - 1 - section_index
    out_store = lax.dynamic_slice_in_dim(jnp.stack(out_list), offset, micro_count, 0)
    grad_store = lax.dynamic_slice_in_dim(jnp.stack(grad_list), offset, micro_count, 0)
    summed_weight = lax.psum_scatter(
        jnp.einsum(
            "mtf,mta->fa", grad_store, attend_store, preferred_element_type=jnp.float32
        ).astype(jnp.bfloat16),
        "samples",
        scatter_dimension=0,
        tiled=True,
    ).astype(jnp.float32)
    region_count = seq_len // 2
    rank_in_region = jnp.cumsum(region_mask) - 1
    select = (
        (rank_in_region[None, :] == jnp.arange(region_count)[:, None]) & (region_mask[None, :] > 0)
    ).astype(jnp.bfloat16)
    tiles = jnp.einsum("at,mtd->mad", select, out_store, preferred_element_type=jnp.float32).astype(
        jnp.bfloat16
    )
    shard_index = lax.axis_index("samples")
    my_partners = lax.dynamic_slice_in_dim(
        partner_samples, shard_index * micro_count, micro_count, 0
    )
    shard_count = lax.axis_size("samples")
    dest_shard = my_partners // micro_count
    dest_slot = my_partners % micro_count
    route = (
        (dest_shard[:, None, None] == jnp.arange(shard_count)[None, :, None])
        & (dest_slot[:, None, None] == jnp.arange(micro_count)[None, None, :])
    ).astype(jnp.bfloat16)
    outgoing = jnp.einsum("mku,mad->kuad", route, tiles, preferred_element_type=jnp.float32).astype(
        jnp.bfloat16
    )
    arrived = lax.all_to_all(outgoing, "samples", split_axis=0, concat_axis=0, tiled=True)
    ones_row = jnp.ones((shard_count,), jnp.bfloat16)
    received = jnp.einsum(
        "k,kuad->uad", ones_row, arrived, preferred_element_type=jnp.float32
    ).astype(jnp.bfloat16)
    placed = jnp.einsum("at,mad->mtd", select, received, preferred_element_type=jnp.float32)
    kept = jnp.where(region_mask[None, :, None] > 0, jnp.zeros_like(out_store), out_store)
    site_cot = (kept.astype(jnp.float32) + placed).astype(jnp.bfloat16)
    cotangents = jnp.where(section_index == 0, site_cot, out_store)
    onehot = (spins[:, :, None] == jnp.arange(SPINS)[None, None, :]).astype(jnp.bfloat16)
    embed_term = jnp.einsum("mtv,mtd->vd", onehot, site_cot, preferred_element_type=jnp.float32)
    embed_term = jnp.where(section_index == 0, embed_term, jnp.zeros_like(embed_term))
    embed_grad = lax.psum(embed_term, ("samples", "section"))
    return (summed_weight[None], cotangents[None], embed_grad)


def ring_sample(place, count):
    return jnp.where(place < count // 2, 2 * place, 2 * (count - place) - 1)


def ring_place(sample, count):
    return jnp.where(lax.rem(sample, 2) == 0, sample // 2, count - 1 - sample // 2)


def ring_route(count, distance):
    order = list(range(0, count, 2)) + list(range(1, count, 2))[::-1]
    return [(order[i], order[(i - distance) % count]) for i in range(count)]


def own_place(count):
    return ring_place(lax.axis_index("samples"), count)


def peer_at(place, distance, count):
    return ring_sample(lax.rem(place + distance + count, count), count)


def columns(index, size):
    return pl.ds(pl.multiple_of(index * size, size), size)


def in_vmem(count):
    return [pl.BlockSpec(memory_space=pltpu.VMEM)] * count


def in_smem(count):
    return [pl.BlockSpec(memory_space=pltpu.SMEM)] * count


def on_core(body, out_shapes, in_specs, scratch=(), micros=1, vmem=16):
    return pl.pallas_call(
        body,
        out_shape=out_shapes,
        in_specs=in_specs,
        out_specs=jax.tree.map(lambda _: pl.BlockSpec(memory_space=pltpu.VMEM), out_shapes),
        scratch_shapes=list(scratch),
        compiler_params=pltpu.CompilerParams(vmem_limit_bytes=vmem << 20),
        cost_estimate=pl.CostEstimate(
            flops=int(micros * FLOPS_PER_MICRO), bytes_accessed=1 << 16, transcendentals=0
        ),
    )


def matmul(left, right):
    return jnp.dot(left, right, preferred_element_type=jnp.float32)


def matmul_t(left, right):
    return lax.dot_general(
        left, right, (((1,), (1,)), ((), ())), preferred_element_type=jnp.float32
    )


def pack_kernel(count, share_axis, x_ref, w_ref, spins_ref, *refs):
    outs, sems = refs[:-1], refs[-1]
    place = own_place(count)
    seq_len = x_ref.shape[2]
    skipped = seq_len + TAIL
    sent = outs[0].shape[0] - skipped
    rows = columns(lax.axis_index(share_axis), sent) if share_axis else slice(None)
    copies = []
    for slot in range(count):
        cols = columns(peer_at(place, -slot, count), HEAD)
        head, weight = outs[slot].at[0:seq_len, :], outs[slot].at[skipped:, :]
        copies.append(pltpu.make_async_copy(x_ref.at[0, 0, :, cols], head, sems.at[0, slot]))
        copies.append(pltpu.make_async_copy(w_ref.at[0, rows, cols], weight, sems.at[1, slot]))
    for copy in copies:
        copy.start()
    spin_rows = jnp.broadcast_to(spins_ref[...].astype(jnp.float32), (TAIL, seq_len))
    for slot in range(count):
        outs[slot][seq_len:skipped, :] = spin_rows.astype(jnp.bfloat16)
    for copy in copies:
        copy.wait()


def collect_kernel(count, *refs):
    heads_ref, rows_ref = refs[count:]
    place = own_place(count)
    sent = rows_ref.shape[1]
    for slot in range(count):
        peer = peer_at(place, slot, count)
        heads_ref[peer] = refs[slot][...]
        rows_ref[peer] = refs[slot][-sent:, :]


def forward_kernel(count, scale, *refs):
    heads_ref, shared, layout_ref = refs[0], refs[1:-6], refs[-4]
    probs_ref, turned_ref, bundle_ref = refs[-3:]
    seq_len = probs_ref.shape[1]
    lines = seq_len + TAIL
    half = lax.axis_index("mp")
    parts = count // 2
    sent = heads_ref.shape[1] - lines
    for part in range(parts):
        shard = (1 - half) * parts + part
        for piece, value in enumerate((heads_ref[shard, lines:, :], *(ref[shard] for ref in shared))):
            first = count * seq_len + (piece * parts + part) * sent
            bundle_ref[first : first + sent, :] = value
    blocks = layout_ref.shape[1]
    rows = lax.broadcasted_iota(jnp.int32, (seq_len, seq_len), 0) // BLOCK
    cols = lax.broadcasted_iota(jnp.int32, (seq_len, seq_len), 1) // BLOCK
    seen = rows == cols
    for q in range(blocks):
        for k in range(blocks):
            if q != k:
                seen = seen | ((rows == q) & (cols == k) & (layout_ref[0, q, k] > 0))
    xs = [heads_ref[slot, 0:seq_len, :] for slot in range(count)]
    scores = [jnp.where(seen, matmul_t(x, x) * scale, -jnp.inf) for x in xs]
    tops = [jnp.max(score, axis=-1, keepdims=True) for score in scores]
    terms = [jnp.exp(score - top) for score, top in zip(scores, tops)]
    sums = [jnp.sum(term, axis=-1, keepdims=True) for term in terms]
    for slot in range(count):
        probs = terms[slot] / sums[slot]
        low = probs.astype(jnp.bfloat16)
        probs_ref[slot] = probs
        attended = matmul(low, xs[slot]).astype(jnp.bfloat16)
        bundle_ref[slot * seq_len : (slot + 1) * seq_len, :] = attended
        turned_ref[slot] = transposed(low)


def lay_weights(weights, shares, share_axis):
    index = lax.axis_index(share_axis) if share_axis else 0
    pieces = len(shares) // 2
    parts = len(shares[0])
    for number, share in enumerate(shares):
        head, piece = number % 2, number // 2
        place = index if piece == 0 else 1 - index
        for part, value in enumerate(share):
            sent = value.shape[0]
            rows = pl.ds(pl.multiple_of((part * pieces + place) * sent, sent), sent)
            weights[rows, head * HEAD : (head + 1) * HEAD] = value


def weight_term(pieces, left, cols):
    total = None
    for index, first in enumerate(range(0, len(pieces), 2)):
        rows = [piece[:, cols] for slot in pieces[first : first + 2] for piece in slot]
        term = matmul(left[index], jnp.concatenate(rows, axis=0))
        total = term if total is None else total + term
    return total


def both_heads(own_ref, sibling_ref, samples, seq_len):
    rows = [
        jnp.concatenate(
            [ref[columns(sample, seq_len), :] for ref in (own_ref, sibling_ref)], axis=1
        )
        for sample in samples
    ]
    return transposed(jnp.concatenate(rows, axis=0))


def transposed(value):
    return value.astype(jnp.float32).T.astype(jnp.bfloat16)


def attention_back(scale, xs, probs, turned, grads, above):
    grad_probs = [matmul_t(grad, x) for grad, x in zip(grads, xs)]
    inner = [jnp.sum(grad * prob, axis=-1, keepdims=True) for grad, prob in zip(grad_probs, probs)]
    grad_scores = [
        (prob * (grad - total)).astype(jnp.bfloat16)
        for prob, grad, total in zip(probs, grad_probs, inner)
    ]
    both = [jnp.concatenate([grad, transposed(grad)], axis=1) for grad in grad_scores]
    results = []
    for index, x in enumerate(xs):
        through = matmul(turned[index], grads[index])
        through = through + scale * matmul(both[index], jnp.concatenate([x, x], axis=0))
        results.append((above[index].astype(jnp.float32) + through).astype(jnp.bfloat16))
    return results


def near_slots(count):
    return [slot for slot in range(count) if slot != count // 2]


def near_products_kernel(count, share_axis, *refs):
    pieces = [refs[index : index + 1] for index in range(count - 1)]
    bundle_ref, sibling_ref, heads_ref = refs[count - 1 : count + 2]
    shared = refs[count + 2 : -5]
    partial_ref, own_ref, other_ref, above_ref, weights = refs[-5:]
    place = own_place(count)
    shard = lax.axis_index("samples")
    parts, _, shard_rows = partial_ref.shape
    seq_len = pieces[0][0].shape[0]
    lines = seq_len + TAIL
    sent = heads_ref.shape[1] - lines
    half = lax.axis_index("mp")
    sample_of = [peer_at(place, slot, count) for slot in near_slots(count)]
    shares = []
    for piece, ref in enumerate((heads_ref, *shared)):
        skipped = lines if piece == 0 else 0
        shares.append([ref[half * parts + part, skipped:, :] for part in range(parts)])
        firsts = [count * seq_len + (piece * parts + part) * sent for part in range(parts)]
        shares.append([sibling_ref[first : first + sent, :] for first in firsts])
    lay_weights(weights, shares, share_axis)
    left = [
        both_heads(bundle_ref, sibling_ref, sample_of[first : first + 2], seq_len)
        for first in range(0, count - 1, 2)
    ]
    for part in range(parts):
        cols = slice(part * shard_rows, (part + 1) * shard_rows)
        partial_ref[part] = weight_term(pieces, left, cols)
    for first in range(0, count - 1, 2):
        rows = [piece[...] for slot in pieces[first : first + 2] for piece in slot]
        total = matmul(jnp.concatenate(rows, axis=0), weights[...])
        lines = slice(first * seq_len, first * seq_len + total.shape[0])
        own_ref[lines, :] = total[:, :HEAD]
        other_ref[lines, :] = total[:, HEAD:].astype(jnp.bfloat16)
    for index, slot in enumerate(pieces):
        above_ref[index * seq_len : (index + 1) * seq_len, :] = slot[0][:, columns(shard, HEAD)]


def near_back_kernel(count, scale, *refs):
    heads_ref, probs_ref, turned_ref, own_ref, other_ref, above_ref = refs[:6]
    grads_ref = refs[-1]
    place = own_place(count)
    seq_len = probs_ref.shape[1]
    sample_of = [peer_at(place, slot, count) for slot in near_slots(count)]
    lines = [slice(index * seq_len, (index + 1) * seq_len) for index in range(count - 1)]
    results = attention_back(
        scale,
        [heads_ref[sample, 0:seq_len, :] for sample in sample_of],
        [probs_ref[sample] for sample in sample_of],
        [turned_ref[sample] for sample in sample_of],
        [
            (own_ref[line, :] + other_ref[line, :].astype(jnp.float32)).astype(jnp.bfloat16)
            for line in lines
        ],
        [above_ref[line, :] for line in lines],
    )
    for index, result in enumerate(results):
        grads_ref[index] = result


def far_products_kernel(count, *refs):
    piece, refs = refs[:2], refs[2:]
    bundle_ref, sibling_ref, partial_ref, weights_ref = refs[:4]
    send_ref, keep_ref, own_ref, above_ref = refs[4:]
    sample = peer_at(own_place(count), count // 2, count)
    shard = lax.axis_index("samples")
    parts, _, shard_rows = partial_ref.shape
    left = [both_heads(bundle_ref, sibling_ref, [sample], 2 * piece[0].shape[0])]
    for part in range(parts):
        cols = slice(part * shard_rows, (part + 1) * shard_rows)
        total = transposed(partial_ref[part] + weight_term([piece], left, cols))
        keep_ref[part] = total[:, :HEAD]
        send_ref[cols, :] = total[:, HEAD:]
    total = matmul(jnp.concatenate([rows[...] for rows in piece], axis=0), weights_ref[...])
    own_ref[...] = total[:, :HEAD]
    send_ref[parts * shard_rows :, :] = total[:, HEAD:].astype(jnp.bfloat16)
    cols = columns(shard, HEAD)
    above_ref[...] = jnp.concatenate([rows[:, cols] for rows in piece], axis=0)


def far_kernel(count, scale, *refs):
    came_ref, keep_ref, own_ref, above_ref, heads_ref, probs_ref, turned_ref = refs[:7]
    near_ref, mask_ref, partner_ref = refs[7:10]
    outs, (grads, terms) = refs[10:-2], refs[-2:]
    place = own_place(count)
    half = lax.axis_index("mp")
    seq_len = probs_ref.shape[1]
    skipped = seq_len + TAIL
    parts, shard_rows = keep_ref.shape[:2]
    for part in range(parts):
        terms[half * parts + part] = keep_ref[part]
        lines = slice(part * shard_rows, (part + 1) * shard_rows)
        terms[(1 - half) * parts + part] = came_ref[lines, :]
    for index, slot in enumerate(near_slots(count)):
        grads[peer_at(place, slot, count)] = near_ref[index]
    sample = peer_at(place, count // 2, count)
    other = came_ref[parts * shard_rows :, :].astype(jnp.float32)
    (grads[sample],) = attention_back(
        scale,
        [heads_ref[sample, 0:seq_len, :]],
        [probs_ref[sample]],
        [turned_ref[sample]],
        [(own_ref[...] + other).astype(jnp.bfloat16)],
        [above_ref[...]],
    )
    region = jnp.broadcast_to(mask_ref[...].astype(jnp.float32), (HEAD, seq_len)).T > 0.5
    which = lax.broadcasted_iota(jnp.int32, (TAIL, seq_len), 0).astype(jnp.float32)
    embed = jnp.zeros((TAIL, HEAD), jnp.float32)
    for slot in range(count):
        sample = peer_at(place, -slot, count)
        swapped = grads[partner_ref[sample]].astype(jnp.float32)
        site = jnp.where(region, swapped, grads[sample].astype(jnp.float32)).astype(jnp.bfloat16)
        outs[slot][0:seq_len, :] = site
        outs[slot][skipped:, :] = terms[sample]
        spin = heads_ref[sample, seq_len:skipped, :].astype(jnp.float32)
        embed = embed + matmul((spin == which).astype(jnp.bfloat16), site)
    high = embed.astype(jnp.bfloat16).astype(jnp.float32)
    low = embed - high
    tail = jnp.concatenate([high[: TAIL // 2], low[: TAIL // 2]], axis=0).astype(jnp.bfloat16)
    for slot in range(count):
        outs[slot][seq_len:skipped, :] = tail


def unpack_kernel(count, *refs):
    weight_ref, site_ref, embed_ref = refs[count:]
    place = own_place(count)
    seq_len = site_ref.shape[2]
    skipped = seq_len + TAIL
    for slot in range(count):
        cols = columns(peer_at(place, slot, count), HEAD)
        weight_ref[0, :, cols] = refs[slot][skipped:, :].astype(jnp.float32)
        site_ref[0, 0, :, cols] = refs[slot][0:seq_len, :]
        tail = refs[slot][seq_len:skipped, :].astype(jnp.float32)
        embed_ref[:, cols] = (tail[: TAIL // 2] + tail[TAIL // 2 :])[:SPINS]


def spread(blocks):
    count = len(blocks)
    sent = {
        slot: lax.ppermute(blocks[slot], "samples", ring_route(count, slot))
        for slot in sorted(range(1, count), key=lambda slot: abs(slot - count // 2))
    }
    return [blocks[0]] + [sent[slot] for slot in range(1, count)]


def head_sharded(
    stored_inputs, top_cotangent, layer_weights, block_layout, region_mask, partner_samples, spins
):
    count = lax.axis_size("samples")
    seq_len = stored_inputs.shape[2]
    shard_rows, half_width = layer_weights.shape[1:]
    scale = 4.0 / HEAD
    bf16, f32 = jnp.bfloat16, jnp.float32
    per_head = (count, seq_len, HEAD)
    lines = seq_len + TAIL
    share_axis = "groups" if lax.axis_size("groups") == 2 else None
    sent = shard_rows // 2 if share_axis else shard_rows
    parts = count // 2
    swap = [(0, 1), (1, 0)]

    up, down = ring_route(count, -1), ring_route(count, 1)
    block = top_cotangent[0]
    rows = seq_len // 2
    packed = on_core(
        functools.partial(pack_kernel, count, share_axis),
        [jax.ShapeDtypeStruct((lines + sent, HEAD), bf16)] * count,
        [pl.BlockSpec(memory_space=pltpu.HBM)] * 2 + in_vmem(1),
        [pltpu.SemaphoreType.DMA((2, count))],
        micros=1,
        vmem=60,
    )(stored_inputs, layer_weights, spins)
    slots = {0: block}
    ahead, back = block, block
    for step in range(1, count // 2):
        ahead = lax.ppermute(ahead, "samples", up)
        back = lax.ppermute(back, "samples", down)
        if step == 1:
            ahead, back, *packed = lax.optimization_barrier((ahead, back, *packed))
        slots[count - step], slots[step] = ahead, back
    far = (
        lax.ppermute(ahead[:rows], "samples", up),
        lax.ppermute(back[rows:], "samples", down),
    )
    heads, weight_rows = on_core(
        functools.partial(collect_kernel, count),
        [
            jax.ShapeDtypeStruct((count, lines + sent, HEAD), bf16),
            jax.ShapeDtypeStruct((count, sent, HEAD), bf16),
        ],
        in_vmem(count),
        micros=0.4,
    )(*spread(packed))
    near = [slots[slot] for slot in near_slots(count)]
    small = (region_mask.reshape(1, seq_len), partner_samples)
    shared = []
    if share_axis:
        shared = [lax.ppermute(weight_rows, share_axis, swap)]
    probs, turned, bundle = on_core(
        functools.partial(forward_kernel, count, scale),
        [
            jax.ShapeDtypeStruct(per_head, f32),
            jax.ShapeDtypeStruct(per_head, bf16),
            jax.ShapeDtypeStruct((count * seq_len + half_width, HEAD), bf16),
        ],
        in_vmem(2 + len(shared)) + in_smem(2),
        micros=1.2,
    )(heads, *shared, *small, block_layout)
    sibling = lax.ppermute(bundle, "mp", swap)
    near_lines = (count - 1) * seq_len
    partial, near_own, near_other, near_above, weights = on_core(
        functools.partial(near_products_kernel, count, share_axis),
        [
            jax.ShapeDtypeStruct((parts, 2 * HEAD, shard_rows), f32),
            jax.ShapeDtypeStruct((near_lines, HEAD), f32),
            jax.ShapeDtypeStruct((near_lines, HEAD), bf16),
            jax.ShapeDtypeStruct((near_lines, HEAD), bf16),
            jax.ShapeDtypeStruct((half_width, 2 * HEAD), bf16),
        ],
        in_vmem(count + 2 + len(shared)),
        micros=1.4,
    )(*near, bundle, sibling, heads, *shared)
    near_other = lax.ppermute(near_other, "mp", swap)
    near_grads = on_core(
        functools.partial(near_back_kernel, count, scale),
        jax.ShapeDtypeStruct((count - 1, seq_len, HEAD), bf16),
        in_vmem(7) + in_smem(1),
        micros=1.8,
    )(heads, probs, turned, near_own, near_other, near_above, *small)
    far_send, far_keep, far_own, far_above = on_core(
        functools.partial(far_products_kernel, count),
        [
            jax.ShapeDtypeStruct((half_width + seq_len, HEAD), bf16),
            jax.ShapeDtypeStruct((parts, shard_rows, HEAD), bf16),
            jax.ShapeDtypeStruct((seq_len, HEAD), f32),
            jax.ShapeDtypeStruct((seq_len, HEAD), bf16),
        ],
        in_vmem(6),
        micros=0.5,
    )(*far, bundle, sibling, partial, weights)
    far_came = lax.ppermute(far_send, "mp", swap)
    terms = on_core(
        functools.partial(far_kernel, count, scale),
        [jax.ShapeDtypeStruct((lines + shard_rows, HEAD), bf16)] * count,
        in_vmem(9) + in_smem(1),
        [pltpu.VMEM(per_head, bf16), pltpu.VMEM((count, shard_rows, HEAD), bf16)],
        micros=1.2,
    )(far_came, far_keep, far_own, far_above, heads, probs, turned, near_grads, *small)
    return on_core(
        functools.partial(unpack_kernel, count),
        [
            jax.ShapeDtypeStruct((1, shard_rows, half_width), f32),
            jax.ShapeDtypeStruct((1, 1, seq_len, half_width), bf16),
            jax.ShapeDtypeStruct((SPINS, half_width), f32),
        ],
        in_vmem(count),
        micros=1.2,
    )(*spread(terms))


def solution(mesh):
    in_specs = (
        P("section", ("groups", "samples"), None, "mp"),
        P(("groups", "samples"), None, "mp"),
        P("section", "samples", "mp"),
        P("section", None, None),
        P(),
        P("groups"),
        P(("groups", "samples"), None),
    )
    out_specs = (
        P(("groups", "section"), "samples", "mp"),
        P("section", ("groups", "samples"), None, "mp"),
        P("groups", "mp"),
    )
    shards = mesh.shape["samples"]

    def whole(stored_inputs, top_cotangent, *rest):
        samples, _, width = top_cotangent.shape
        layer_count = stored_inputs.shape[0]
        one_each = samples == mesh.shape["groups"] * shards and layer_count == 1
        by_heads = one_each and shards % 2 == 0 and width == mesh.shape["mp"] * shards * HEAD
        return jax.shard_map(
            head_sharded if by_heads else local,
            mesh=mesh,
            in_specs=in_specs,
            out_specs=out_specs,
            check_vma=False,
        )(stored_inputs, top_cotangent, *rest)

    return whole
```

```python
import functools

import jax
import jax.numpy as jnp
from jax import lax
from jax.experimental import pallas as pl
from jax.experimental.pallas import tpu as pltpu
from jax.sharding import PartitionSpec as P

HEAD = 128
BLOCK = 64
SPINS = 2
TAIL = 16
FLOPS_PER_MICRO = 1.15e9


def for_sending(value):

    def short(part):
        return part.astype(jnp.bfloat16) if part.dtype == jnp.float32 else part

    return jax.tree.map(short, value)


def passed_along(block, axis, distance):
    devices = range(lax.axis_size(axis))
    route = [(i - distance, i) for i in devices if i - distance in devices]
    return lax.ppermute(block, axis, route)


def softmax_parts(inputs_h, allowed, attention_scale):
    scores = (
        jnp.einsum("qhd,khd->hqk", inputs_h, inputs_h, preferred_element_type=jnp.float32)
        * attention_scale
    )
    scores = jnp.where(allowed[None], scores, -jnp.inf)
    top_score = jnp.max(scores, axis=-1, keepdims=True)
    expo_terms = jnp.exp(scores - top_score)
    probs = expo_terms / jnp.sum(expo_terms, axis=-1, keepdims=True)
    return (probs, probs.astype(jnp.bfloat16))


def local(
    stored_inputs, top_cotangent, layer_weights, block_layout, region_mask, partner_samples, spins
):
    section_index = lax.axis_index("section")
    section_count = lax.axis_size("section")
    micro_count = stored_inputs.shape[1]
    seq_len = stored_inputs.shape[2]
    half_width = stored_inputs.shape[3]
    head_count = half_width // HEAD
    attention_scale = 4.0 / HEAD
    weights = lax.all_gather(layer_weights[0], "samples", axis=0, tiled=True)
    pos_block = jnp.arange(seq_len) // BLOCK
    block_onehot = (pos_block[:, None] == jnp.arange(block_layout.shape[1])[None, :]).astype(
        jnp.float32
    )
    linked = jnp.dot(jnp.dot(block_onehot, block_layout[0].astype(jnp.float32)), block_onehot.T)
    allowed = (linked > 0.5) | (pos_block[:, None] == pos_block[None, :])
    every_layer_input = stored_inputs[0]
    inputs_h = every_layer_input[0].reshape(seq_len, head_count, HEAD)
    probs, probs_low = softmax_parts(inputs_h, allowed, attention_scale)
    attended = jnp.einsum(
        "hqk,khd->qhd", probs_low, inputs_h, preferred_element_type=jnp.float32
    ).astype(jnp.bfloat16)
    probs_list = [probs]
    low_list = [probs_low]
    attend_list = [attended.reshape(seq_len, half_width)]
    probs_all = jnp.stack(probs_list)
    low_all = jnp.stack(low_list)
    attend_store = jnp.stack(attend_list)

    def layer_back(grad_full, grad_own, inputs, probs, probs_low):
        grad_attn = jnp.dot(grad_full, weights, preferred_element_type=jnp.float32).astype(
            jnp.bfloat16
        )
        inputs_h = inputs.reshape(seq_len, head_count, HEAD)
        grad_h = grad_attn.reshape(seq_len, head_count, HEAD)
        grad_probs = jnp.einsum(
            "qhd,khd->hqk", grad_h, inputs_h, preferred_element_type=jnp.float32
        )
        grad_scores = (
            probs * (grad_probs - jnp.sum(grad_probs * probs, axis=-1, keepdims=True))
        ).astype(jnp.bfloat16)
        through = jnp.einsum("hqk,qhd->khd", probs_low, grad_h, preferred_element_type=jnp.float32)
        through = through + attention_scale * (
            jnp.einsum("hqk,khd->qhd", grad_scores, inputs_h, preferred_element_type=jnp.float32)
            + jnp.einsum("hqk,qhd->khd", grad_scores, inputs_h, preferred_element_type=jnp.float32)
        )
        grad_in = grad_own.astype(jnp.float32) + through.reshape(seq_len, half_width)
        return grad_in.astype(jnp.bfloat16)

    def resting(grad_full, grad_own, inputs, probs, probs_low):
        return jnp.zeros((seq_len, half_width), jnp.bfloat16)

    carried_state = jnp.zeros((seq_len, half_width), jnp.bfloat16)
    out_list = []
    grad_list = []
    total_steps = micro_count + section_count - 1
    for step_number in range(total_steps):
        micro_index = step_number - (section_count - 1 - section_index)
        active = (micro_index >= 0) & (micro_index < micro_count)
        slot_index = jnp.clip(micro_index, 0, micro_count - 1)
        from_top = lax.dynamic_index_in_dim(top_cotangent, slot_index, 0, keepdims=False)
        incoming = jnp.where(section_index == section_count - 1, from_top, carried_state)
        grad_full = lax.all_gather(incoming, "mp", axis=1, tiled=True)
        inputs_now = lax.dynamic_index_in_dim(every_layer_input, slot_index, 0, keepdims=False)
        probs_now = lax.dynamic_index_in_dim(probs_all, slot_index, 0, keepdims=False)
        low_now = lax.dynamic_index_in_dim(low_all, slot_index, 0, keepdims=False)
        grad_in = lax.cond(
            active, layer_back, resting, grad_full, incoming, inputs_now, probs_now, low_now
        )
        out_list.append(grad_in)
        grad_list.append(grad_full)
        if step_number < total_steps - 1:
            carried_state = jax.tree.map(
                lambda part, own: part.astype(own.dtype),
                passed_along(for_sending(grad_in), "section", -1),
                grad_in,
            )
    offset = section_count - 1 - section_index
    out_store = lax.dynamic_slice_in_dim(jnp.stack(out_list), offset, micro_count, 0)
    grad_store = lax.dynamic_slice_in_dim(jnp.stack(grad_list), offset, micro_count, 0)
    summed_weight = lax.psum_scatter(
        jnp.einsum(
            "mtf,mta->fa", grad_store, attend_store, preferred_element_type=jnp.float32
        ).astype(jnp.bfloat16),
        "samples",
        scatter_dimension=0,
        tiled=True,
    ).astype(jnp.float32)
    region_count = seq_len // 2
    rank_in_region = jnp.cumsum(region_mask) - 1
    select = (
        (rank_in_region[None, :] == jnp.arange(region_count)[:, None]) & (region_mask[None, :] > 0)
    ).astype(jnp.bfloat16)
    tiles = jnp.einsum("at,mtd->mad", select, out_store, preferred_element_type=jnp.float32).astype(
        jnp.bfloat16
    )
    shard_index = lax.axis_index("samples")
    my_partners = lax.dynamic_slice_in_dim(
        partner_samples, shard_index * micro_count, micro_count, 0
    )
    shard_count = lax.axis_size("samples")
    dest_shard = my_partners // micro_count
    dest_slot = my_partners % micro_count
    route = (
        (dest_shard[:, None, None] == jnp.arange(shard_count)[None, :, None])
        & (dest_slot[:, None, None] == jnp.arange(micro_count)[None, None, :])
    ).astype(jnp.bfloat16)
    outgoing = jnp.einsum("mku,mad->kuad", route, tiles, preferred_element_type=jnp.float32).astype(
        jnp.bfloat16
    )
    arrived = lax.all_to_all(outgoing, "samples", split_axis=0, concat_axis=0, tiled=True)
    ones_row = jnp.ones((shard_count,), jnp.bfloat16)
    received = jnp.einsum(
        "k,kuad->uad", ones_row, arrived, preferred_element_type=jnp.float32
    ).astype(jnp.bfloat16)
    placed = jnp.einsum("at,mad->mtd", select, received, preferred_element_type=jnp.float32)
    kept = jnp.where(region_mask[None, :, None] > 0, jnp.zeros_like(out_store), out_store)
    site_cot = (kept.astype(jnp.float32) + placed).astype(jnp.bfloat16)
    cotangents = jnp.where(section_index == 0, site_cot, out_store)
    onehot = (spins[:, :, None] == jnp.arange(SPINS)[None, None, :]).astype(jnp.bfloat16)
    embed_term = jnp.einsum("mtv,mtd->vd", onehot, site_cot, preferred_element_type=jnp.float32)
    embed_term = jnp.where(section_index == 0, embed_term, jnp.zeros_like(embed_term))
    embed_grad = lax.psum(embed_term, ("samples", "section"))
    return (summed_weight[None], cotangents[None], embed_grad)


def ring_sample(place, count):
    return jnp.where(place < count // 2, 2 * place, 2 * (count - place) - 1)


def ring_place(sample, count):
    return jnp.where(lax.rem(sample, 2) == 0, sample // 2, count - 1 - sample // 2)


def ring_route(count, distance):
    order = list(range(0, count, 2)) + list(range(1, count, 2))[::-1]
    return [(order[i], order[(i - distance) % count]) for i in range(count)]


def own_place(count):
    return ring_place(lax.axis_index("samples"), count)


def peer_at(place, distance, count):
    return ring_sample(lax.rem(place + distance + count, count), count)


def columns(index, size):
    return pl.ds(pl.multiple_of(index * size, size), size)


def in_vmem(count):
    return [pl.BlockSpec(memory_space=pltpu.VMEM)] * count


def in_smem(count):
    return [pl.BlockSpec(memory_space=pltpu.SMEM)] * count


def on_core(body, out_shapes, in_specs, scratch=(), micros=1, vmem=16):
    return pl.pallas_call(
        body,
        out_shape=out_shapes,
        in_specs=in_specs,
        out_specs=jax.tree.map(lambda _: pl.BlockSpec(memory_space=pltpu.VMEM), out_shapes),
        scratch_shapes=list(scratch),
        compiler_params=pltpu.CompilerParams(vmem_limit_bytes=vmem << 20),
        cost_estimate=pl.CostEstimate(
            flops=int(micros * FLOPS_PER_MICRO), bytes_accessed=1 << 16, transcendentals=0
        ),
    )


def matmul(left, right):
    return jnp.dot(left, right, preferred_element_type=jnp.float32)


def matmul_t(left, right):
    return lax.dot_general(
        left, right, (((1,), (1,)), ((), ())), preferred_element_type=jnp.float32
    )


def pack_kernel(count, share_axis, x_ref, w_ref, spins_ref, *refs):
    outs, sems = refs[:-1], refs[-1]
    place = own_place(count)
    seq_len = x_ref.shape[2]
    skipped = seq_len + TAIL
    sent = outs[0].shape[0] - skipped
    rows = columns(lax.axis_index(share_axis), sent) if share_axis else slice(None)
    copies = []
    for slot in range(count):
        cols = columns(peer_at(place, -slot, count), HEAD)
        head, weight = outs[slot].at[0:seq_len, :], outs[slot].at[skipped:, :]
        copies.append(pltpu.make_async_copy(x_ref.at[0, 0, :, cols], head, sems.at[0, slot]))
        copies.append(pltpu.make_async_copy(w_ref.at[0, rows, cols], weight, sems.at[1, slot]))
    for copy in copies:
        copy.start()
    spin_rows = jnp.broadcast_to(spins_ref[...].astype(jnp.float32), (TAIL, seq_len))
    for slot in range(count):
        outs[slot][seq_len:skipped, :] = spin_rows.astype(jnp.bfloat16)
    for copy in copies:
        copy.wait()


def collect_kernel(count, *refs):
    heads_ref, rows_ref = refs[count:]
    place = own_place(count)
    sent = rows_ref.shape[1]
    for slot in range(count):
        peer = peer_at(place, slot, count)
        heads_ref[peer] = refs[slot][...]
        rows_ref[peer] = refs[slot][-sent:, :]


def forward_kernel(count, scale, *refs):
    heads_ref, shared, layout_ref = refs[0], refs[1:-6], refs[-4]
    probs_ref, turned_ref, bundle_ref = refs[-3:]
    seq_len = probs_ref.shape[1]
    lines = seq_len + TAIL
    half = lax.axis_index("mp")
    parts = count // 2
    sent = heads_ref.shape[1] - lines
    for part in range(parts):
        shard = (1 - half) * parts + part
        for piece, value in enumerate((heads_ref[shard, lines:, :], *(ref[shard] for ref in shared))):
            first = count * seq_len + (piece * parts + part) * sent
            bundle_ref[first : first + sent, :] = value
    blocks = layout_ref.shape[1]
    rows = lax.broadcasted_iota(jnp.int32, (seq_len, seq_len), 0) // BLOCK
    cols = lax.broadcasted_iota(jnp.int32, (seq_len, seq_len), 1) // BLOCK
    seen = rows == cols
    for q in range(blocks):
        for k in range(blocks):
            if q != k:
                seen = seen | ((rows == q) & (cols == k) & (layout_ref[0, q, k] > 0))
    xs = [heads_ref[slot, 0:seq_len, :] for slot in range(count)]
    scores = [jnp.where(seen, matmul_t(x, x) * scale, -jnp.inf) for x in xs]
    tops = [jnp.max(score, axis=-1, keepdims=True) for score in scores]
    terms = [jnp.exp(score - top) for score, top in zip(scores, tops)]
    sums = [jnp.sum(term, axis=-1, keepdims=True) for term in terms]
    for slot in range(count):
        probs = terms[slot] / sums[slot]
        low = probs.astype(jnp.bfloat16)
        probs_ref[slot] = probs
        attended = matmul(low, xs[slot]).astype(jnp.bfloat16)
        bundle_ref[slot * seq_len : (slot + 1) * seq_len, :] = attended
        turned_ref[slot] = transposed(low)


def lay_weights(weights, shares, share_axis):
    index = lax.axis_index(share_axis) if share_axis else 0
    pieces = len(shares) // 2
    parts = len(shares[0])
    for number, share in enumerate(shares):
        head, piece = number % 2, number // 2
        place = index if piece == 0 else 1 - index
        for part, value in enumerate(share):
            sent = value.shape[0]
            rows = pl.ds(pl.multiple_of((part * pieces + place) * sent, sent), sent)
            weights[rows, head * HEAD : (head + 1) * HEAD] = value


def weight_term(pieces, left, cols):
    total = None
    for index, first in enumerate(range(0, len(pieces), 2)):
        rows = [piece[:, cols] for slot in pieces[first : first + 2] for piece in slot]
        term = matmul(left[index], jnp.concatenate(rows, axis=0))
        total = term if total is None else total + term
    return total


def both_heads(own_ref, sibling_ref, samples, seq_len):
    rows = [
        jnp.concatenate(
            [ref[columns(sample, seq_len), :] for ref in (own_ref, sibling_ref)], axis=1
        )
        for sample in samples
    ]
    return transposed(jnp.concatenate(rows, axis=0))


def transposed(value):
    return value.astype(jnp.float32).T.astype(jnp.bfloat16)


def attention_back(scale, xs, probs, turned, grads, above):
    grad_probs = [matmul_t(grad, x) for grad, x in zip(grads, xs)]
    inner = [jnp.sum(grad * prob, axis=-1, keepdims=True) for grad, prob in zip(grad_probs, probs)]
    grad_scores = [
        (prob * (grad - total)).astype(jnp.bfloat16)
        for prob, grad, total in zip(probs, grad_probs, inner)
    ]
    both = [jnp.concatenate([grad, transposed(grad)], axis=1) for grad in grad_scores]
    results = []
    for index, x in enumerate(xs):
        through = matmul(turned[index], grads[index])
        through = through + scale * matmul(both[index], jnp.concatenate([x, x], axis=0))
        results.append((above[index].astype(jnp.float32) + through).astype(jnp.bfloat16))
    return results


def near_slots(count):
    return [slot for slot in range(count) if slot != count // 2]


def near_products_kernel(count, share_axis, *refs):
    pieces = [refs[index : index + 1] for index in range(count - 1)]
    bundle_ref, sibling_ref, heads_ref = refs[count - 1 : count + 2]
    shared = refs[count + 2 : -5]
    partial_ref, own_ref, other_ref, above_ref, weights = refs[-5:]
    place = own_place(count)
    shard = lax.axis_index("samples")
    parts, _, shard_rows = partial_ref.shape
    seq_len = pieces[0][0].shape[0]
    lines = seq_len + TAIL
    sent = heads_ref.shape[1] - lines
    half = lax.axis_index("mp")
    sample_of = [peer_at(place, slot, count) for slot in near_slots(count)]
    shares = []
    for piece, ref in enumerate((heads_ref, *shared)):
        skipped = lines if piece == 0 else 0
        shares.append([ref[half * parts + part, skipped:, :] for part in range(parts)])
        firsts = [count * seq_len + (piece * parts + part) * sent for part in range(parts)]
        shares.append([sibling_ref[first : first + sent, :] for first in firsts])
    lay_weights(weights, shares, share_axis)
    left = [
        both_heads(bundle_ref, sibling_ref, sample_of[first : first + 2], seq_len)
        for first in range(0, count - 1, 2)
    ]
    for part in range(parts):
        cols = slice(part * shard_rows, (part + 1) * shard_rows)
        partial_ref[part] = weight_term(pieces, left, cols)
    for first in range(0, count - 1, 2):
        rows = [piece[...] for slot in pieces[first : first + 2] for piece in slot]
        total = matmul(jnp.concatenate(rows, axis=0), weights[...])
        lines = slice(first * seq_len, first * seq_len + total.shape[0])
        own_ref[lines, :] = total[:, :HEAD]
        other_ref[lines, :] = total[:, HEAD:].astype(jnp.bfloat16)
    for index, slot in enumerate(pieces):
        above_ref[index * seq_len : (index + 1) * seq_len, :] = slot[0][:, columns(shard, HEAD)]


def near_back_kernel(count, scale, *refs):
    heads_ref, probs_ref, turned_ref, own_ref, other_ref, above_ref = refs[:6]
    grads_ref = refs[-1]
    place = own_place(count)
    seq_len = probs_ref.shape[1]
    sample_of = [peer_at(place, slot, count) for slot in near_slots(count)]
    lines = [slice(index * seq_len, (index + 1) * seq_len) for index in range(count - 1)]
    results = attention_back(
        scale,
        [heads_ref[sample, 0:seq_len, :] for sample in sample_of],
        [probs_ref[sample] for sample in sample_of],
        [turned_ref[sample] for sample in sample_of],
        [
            (own_ref[line, :] + other_ref[line, :].astype(jnp.float32)).astype(jnp.bfloat16)
            for line in lines
        ],
        [above_ref[line, :] for line in lines],
    )
    for index, result in enumerate(results):
        grads_ref[index] = result


def far_products_kernel(count, *refs):
    piece, refs = refs[:2], refs[2:]
    bundle_ref, sibling_ref, partial_ref, weights_ref = refs[:4]
    send_ref, keep_ref, own_ref, above_ref = refs[4:]
    sample = peer_at(own_place(count), count // 2, count)
    shard = lax.axis_index("samples")
    parts, _, shard_rows = partial_ref.shape
    left = [both_heads(bundle_ref, sibling_ref, [sample], 2 * piece[0].shape[0])]
    for part in range(parts):
        cols = slice(part * shard_rows, (part + 1) * shard_rows)
        total = transposed(partial_ref[part] + weight_term([piece], left, cols))
        keep_ref[part] = total[:, :HEAD]
        send_ref[cols, :] = total[:, HEAD:]
    total = matmul(jnp.concatenate([rows[...] for rows in piece], axis=0), weights_ref[...])
    own_ref[...] = total[:, :HEAD]
    send_ref[parts * shard_rows :, :] = total[:, HEAD:].astype(jnp.bfloat16)
    cols = columns(shard, HEAD)
    above_ref[...] = jnp.concatenate([rows[:, cols] for rows in piece], axis=0)


def far_kernel(count, scale, *refs):
    came_ref, keep_ref, own_ref, above_ref, heads_ref, probs_ref, turned_ref = refs[:7]
    near_ref, mask_ref, partner_ref = refs[7:10]
    outs, (grads, terms) = refs[10:-2], refs[-2:]
    place = own_place(count)
    half = lax.axis_index("mp")
    seq_len = probs_ref.shape[1]
    skipped = seq_len + TAIL
    parts, shard_rows = keep_ref.shape[:2]
    for part in range(parts):
        terms[half * parts + part] = keep_ref[part]
        lines = slice(part * shard_rows, (part + 1) * shard_rows)
        terms[(1 - half) * parts + part] = came_ref[lines, :]
    for index, slot in enumerate(near_slots(count)):
        grads[peer_at(place, slot, count)] = near_ref[index]
    sample = peer_at(place, count // 2, count)
    other = came_ref[parts * shard_rows :, :].astype(jnp.float32)
    (grads[sample],) = attention_back(
        scale,
        [heads_ref[sample, 0:seq_len, :]],
        [probs_ref[sample]],
        [turned_ref[sample]],
        [(own_ref[...] + other).astype(jnp.bfloat16)],
        [above_ref[...]],
    )
    region = jnp.broadcast_to(mask_ref[...].astype(jnp.float32), (HEAD, seq_len)).T > 0.5
    which = lax.broadcasted_iota(jnp.int32, (TAIL, seq_len), 0).astype(jnp.float32)
    embed = jnp.zeros((TAIL, HEAD), jnp.float32)
    for slot in range(count):
        sample = peer_at(place, -slot, count)
        swapped = grads[partner_ref[sample]].astype(jnp.float32)
        site = jnp.where(region, swapped, grads[sample].astype(jnp.float32)).astype(jnp.bfloat16)
        outs[slot][0:seq_len, :] = site
        outs[slot][skipped:, :] = terms[sample]
        spin = heads_ref[sample, seq_len:skipped, :].astype(jnp.float32)
        embed = embed + matmul((spin == which).astype(jnp.bfloat16), site)
    high = embed.astype(jnp.bfloat16).astype(jnp.float32)
    low = embed - high
    tail = jnp.concatenate([high[: TAIL // 2], low[: TAIL // 2]], axis=0).astype(jnp.bfloat16)
    for slot in range(count):
        outs[slot][seq_len:skipped, :] = tail


def unpack_kernel(count, *refs):
    weight_ref, site_ref, embed_ref = refs[count:]
    place = own_place(count)
    seq_len = site_ref.shape[2]
    skipped = seq_len + TAIL
    for slot in range(count):
        cols = columns(peer_at(place, slot, count), HEAD)
        weight_ref[0, :, cols] = refs[slot][skipped:, :].astype(jnp.float32)
        site_ref[0, 0, :, cols] = refs[slot][0:seq_len, :]
        tail = refs[slot][seq_len:skipped, :].astype(jnp.float32)
        embed_ref[:, cols] = (tail[: TAIL // 2] + tail[TAIL // 2 :])[:SPINS]


def spread(blocks):
    count = len(blocks)
    sent = {
        slot: lax.ppermute(blocks[slot], "samples", ring_route(count, slot))
        for slot in sorted(range(1, count), key=lambda slot: abs(slot - count // 2))
    }
    return [blocks[0]] + [sent[slot] for slot in range(1, count)]


def head_sharded(
    stored_inputs, top_cotangent, layer_weights, block_layout, region_mask, partner_samples, spins
):
    count = lax.axis_size("samples")
    seq_len = stored_inputs.shape[2]
    shard_rows, half_width = layer_weights.shape[1:]
    scale = 4.0 / HEAD
    bf16, f32 = jnp.bfloat16, jnp.float32
    per_head = (count, seq_len, HEAD)
    lines = seq_len + TAIL
    share_axis = "groups" if lax.axis_size("groups") == 2 else None
    sent = shard_rows // 2 if share_axis else shard_rows
    parts = count // 2
    swap = [(0, 1), (1, 0)]

    up, down = ring_route(count, -1), ring_route(count, 1)
    block = top_cotangent[0]
    rows = seq_len // 2
    packed = on_core(
        functools.partial(pack_kernel, count, share_axis),
        [jax.ShapeDtypeStruct((lines + sent, HEAD), bf16)] * count,
        [pl.BlockSpec(memory_space=pltpu.HBM)] * 2 + in_vmem(1),
        [pltpu.SemaphoreType.DMA((2, count))],
        micros=1,
        vmem=60,
    )(stored_inputs, layer_weights, spins)
    def step_on(ahead, back):
        return lax.ppermute(ahead, "samples", up), lax.ppermute(back, "samples", down)

    def together(moving, others):
        tied = lax.optimization_barrier((*moving, *others))
        return tied[:2], list(tied[2:])

    slots = {0: block}
    moving = (block, block)
    shared, small = [], (region_mask.reshape(1, seq_len), partner_samples)
    for step in range(1, count // 2):
        moving = step_on(*moving)
        if step == 1:
            moving, packed = together(moving, packed)
        if step == 2:
            moving, came = together(moving, spread(packed))
            heads, weight_rows = on_core(
                functools.partial(collect_kernel, count),
                [
                    jax.ShapeDtypeStruct((count, lines + sent, HEAD), bf16),
                    jax.ShapeDtypeStruct((count, sent, HEAD), bf16),
                ],
                in_vmem(count),
                micros=0.4,
            )(*came)
            if share_axis:
                shared = [lax.ppermute(weight_rows, share_axis, swap)]
        if step == 3:
            moving, (heads, *shared) = together(moving, [heads, *shared])
        slots[count - step], slots[step] = moving
    ahead, back = moving
    far = step_on(ahead[:rows], back[rows:])
    near = [slots[slot] for slot in near_slots(count)]
    probs, turned, bundle = on_core(
        functools.partial(forward_kernel, count, scale),
        [
            jax.ShapeDtypeStruct(per_head, f32),
            jax.ShapeDtypeStruct(per_head, bf16),
            jax.ShapeDtypeStruct((count * seq_len + half_width, HEAD), bf16),
        ],
        in_vmem(2 + len(shared)) + in_smem(2),
        micros=1.2,
    )(heads, *shared, *small, block_layout)
    sibling = lax.ppermute(bundle, "mp", swap)
    near_lines = (count - 1) * seq_len
    partial, near_own, near_other, near_above, weights = on_core(
        functools.partial(near_products_kernel, count, share_axis),
        [
            jax.ShapeDtypeStruct((parts, 2 * HEAD, shard_rows), f32),
            jax.ShapeDtypeStruct((near_lines, HEAD), f32),
            jax.ShapeDtypeStruct((near_lines, HEAD), bf16),
            jax.ShapeDtypeStruct((near_lines, HEAD), bf16),
            jax.ShapeDtypeStruct((half_width, 2 * HEAD), bf16),
        ],
        in_vmem(count + 2 + len(shared)),
        micros=1.4,
    )(*near, bundle, sibling, heads, *shared)
    near_other = lax.ppermute(near_other, "mp", swap)
    near_grads = on_core(
        functools.partial(near_back_kernel, count, scale),
        jax.ShapeDtypeStruct((count - 1, seq_len, HEAD), bf16),
        in_vmem(7) + in_smem(1),
        micros=1.8,
    )(heads, probs, turned, near_own, near_other, near_above, *small)
    far_send, far_keep, far_own, far_above = on_core(
        functools.partial(far_products_kernel, count),
        [
            jax.ShapeDtypeStruct((half_width + seq_len, HEAD), bf16),
            jax.ShapeDtypeStruct((parts, shard_rows, HEAD), bf16),
            jax.ShapeDtypeStruct((seq_len, HEAD), f32),
            jax.ShapeDtypeStruct((seq_len, HEAD), bf16),
        ],
        in_vmem(6),
        micros=0.5,
    )(*far, bundle, sibling, partial, weights)
    far_came = lax.ppermute(far_send, "mp", swap)
    terms = on_core(
        functools.partial(far_kernel, count, scale),
        [jax.ShapeDtypeStruct((lines + shard_rows, HEAD), bf16)] * count,
        in_vmem(9) + in_smem(1),
        [pltpu.VMEM(per_head, bf16), pltpu.VMEM((count, shard_rows, HEAD), bf16)],
        micros=1.2,
    )(far_came, far_keep, far_own, far_above, heads, probs, turned, near_grads, *small)
    return on_core(
        functools.partial(unpack_kernel, count),
        [
            jax.ShapeDtypeStruct((1, shard_rows, half_width), f32),
            jax.ShapeDtypeStruct((1, 1, seq_len, half_width), bf16),
            jax.ShapeDtypeStruct((SPINS, half_width), f32),
        ],
        in_vmem(count),
        micros=1.2,
    )(*spread(terms))


def solution(mesh):
    in_specs = (
        P("section", ("groups", "samples"), None, "mp"),
        P(("groups", "samples"), None, "mp"),
        P("section", "samples", "mp"),
        P("section", None, None),
        P(),
        P("groups"),
        P(("groups", "samples"), None),
    )
    out_specs = (
        P(("groups", "section"), "samples", "mp"),
        P("section", ("groups", "samples"), None, "mp"),
        P("groups", "mp"),
    )
    shards = mesh.shape["samples"]

    def whole(stored_inputs, top_cotangent, *rest):
        samples, _, width = top_cotangent.shape
        layer_count = stored_inputs.shape[0]
        one_each = samples == mesh.shape["groups"] * shards and layer_count == 1
        by_heads = one_each and shards % 2 == 0 and shards > 4 and width == mesh.shape["mp"] * shards * HEAD
        return jax.shard_map(
            head_sharded if by_heads else local,
            mesh=mesh,
            in_specs=in_specs,
            out_specs=out_specs,
            check_vma=False,
        )(stored_inputs, top_cotangent, *rest)

    return whole
```

```python
import functools

import jax
import jax.numpy as jnp
from jax import lax
from jax.experimental import pallas as pl
from jax.experimental.pallas import tpu as pltpu
from jax.sharding import PartitionSpec as P

HEAD = 128
BLOCK = 64
SPINS = 2
TAIL = 16
FLOPS_PER_MICRO = 1.15e9


def for_sending(value):

    def short(part):
        return part.astype(jnp.bfloat16) if part.dtype == jnp.float32 else part

    return jax.tree.map(short, value)


def passed_along(block, axis, distance):
    devices = range(lax.axis_size(axis))
    route = [(i - distance, i) for i in devices if i - distance in devices]
    return lax.ppermute(block, axis, route)


def softmax_parts(inputs_h, allowed, attention_scale):
    scores = (
        jnp.einsum("qhd,khd->hqk", inputs_h, inputs_h, preferred_element_type=jnp.float32)
        * attention_scale
    )
    scores = jnp.where(allowed[None], scores, -jnp.inf)
    top_score = jnp.max(scores, axis=-1, keepdims=True)
    expo_terms = jnp.exp(scores - top_score)
    probs = expo_terms / jnp.sum(expo_terms, axis=-1, keepdims=True)
    return (probs, probs.astype(jnp.bfloat16))


def local(
    stored_inputs, top_cotangent, layer_weights, block_layout, region_mask, partner_samples, spins
):
    section_index = lax.axis_index("section")
    section_count = lax.axis_size("section")
    micro_count = stored_inputs.shape[1]
    seq_len = stored_inputs.shape[2]
    half_width = stored_inputs.shape[3]
    head_count = half_width // HEAD
    attention_scale = 4.0 / HEAD
    weights = lax.all_gather(layer_weights[0], "samples", axis=0, tiled=True)
    pos_block = jnp.arange(seq_len) // BLOCK
    block_onehot = (pos_block[:, None] == jnp.arange(block_layout.shape[1])[None, :]).astype(
        jnp.float32
    )
    linked = jnp.dot(jnp.dot(block_onehot, block_layout[0].astype(jnp.float32)), block_onehot.T)
    allowed = (linked > 0.5) | (pos_block[:, None] == pos_block[None, :])
    every_layer_input = stored_inputs[0]
    inputs_h = every_layer_input[0].reshape(seq_len, head_count, HEAD)
    probs, probs_low = softmax_parts(inputs_h, allowed, attention_scale)
    attended = jnp.einsum(
        "hqk,khd->qhd", probs_low, inputs_h, preferred_element_type=jnp.float32
    ).astype(jnp.bfloat16)
    probs_list = [probs]
    low_list = [probs_low]
    attend_list = [attended.reshape(seq_len, half_width)]
    probs_all = jnp.stack(probs_list)
    low_all = jnp.stack(low_list)
    attend_store = jnp.stack(attend_list)

    def layer_back(grad_full, grad_own, inputs, probs, probs_low):
        grad_attn = jnp.dot(grad_full, weights, preferred_element_type=jnp.float32).astype(
            jnp.bfloat16
        )
        inputs_h = inputs.reshape(seq_len, head_count, HEAD)
        grad_h = grad_attn.reshape(seq_len, head_count, HEAD)
        grad_probs = jnp.einsum(
            "qhd,khd->hqk", grad_h, inputs_h, preferred_element_type=jnp.float32
        )
        grad_scores = (
            probs * (grad_probs - jnp.sum(grad_probs * probs, axis=-1, keepdims=True))
        ).astype(jnp.bfloat16)
        through = jnp.einsum("hqk,qhd->khd", probs_low, grad_h, preferred_element_type=jnp.float32)
        through = through + attention_scale * (
            jnp.einsum("hqk,khd->qhd", grad_scores, inputs_h, preferred_element_type=jnp.float32)
            + jnp.einsum("hqk,qhd->khd", grad_scores, inputs_h, preferred_element_type=jnp.float32)
        )
        grad_in = grad_own.astype(jnp.float32) + through.reshape(seq_len, half_width)
        return grad_in.astype(jnp.bfloat16)

    def resting(grad_full, grad_own, inputs, probs, probs_low):
        return jnp.zeros((seq_len, half_width), jnp.bfloat16)

    carried_state = jnp.zeros((seq_len, half_width), jnp.bfloat16)
    out_list = []
    grad_list = []
    total_steps = micro_count + section_count - 1
    for step_number in range(total_steps):
        micro_index = step_number - (section_count - 1 - section_index)
        active = (micro_index >= 0) & (micro_index < micro_count)
        slot_index = jnp.clip(micro_index, 0, micro_count - 1)
        from_top = lax.dynamic_index_in_dim(top_cotangent, slot_index, 0, keepdims=False)
        incoming = jnp.where(section_index == section_count - 1, from_top, carried_state)
        grad_full = lax.all_gather(incoming, "mp", axis=1, tiled=True)
        inputs_now = lax.dynamic_index_in_dim(every_layer_input, slot_index, 0, keepdims=False)
        probs_now = lax.dynamic_index_in_dim(probs_all, slot_index, 0, keepdims=False)
        low_now = lax.dynamic_index_in_dim(low_all, slot_index, 0, keepdims=False)
        grad_in = lax.cond(
            active, layer_back, resting, grad_full, incoming, inputs_now, probs_now, low_now
        )
        out_list.append(grad_in)
        grad_list.append(grad_full)
        if step_number < total_steps - 1:
            carried_state = jax.tree.map(
                lambda part, own: part.astype(own.dtype),
                passed_along(for_sending(grad_in), "section", -1),
                grad_in,
            )
    offset = section_count - 1 - section_index
    out_store = lax.dynamic_slice_in_dim(jnp.stack(out_list), offset, micro_count, 0)
    grad_store = lax.dynamic_slice_in_dim(jnp.stack(grad_list), offset, micro_count, 0)
    summed_weight = lax.psum_scatter(
        jnp.einsum(
            "mtf,mta->fa", grad_store, attend_store, preferred_element_type=jnp.float32
        ).astype(jnp.bfloat16),
        "samples",
        scatter_dimension=0,
        tiled=True,
    ).astype(jnp.float32)
    region_count = seq_len // 2
    rank_in_region = jnp.cumsum(region_mask) - 1
    select = (
        (rank_in_region[None, :] == jnp.arange(region_count)[:, None]) & (region_mask[None, :] > 0)
    ).astype(jnp.bfloat16)
    tiles = jnp.einsum("at,mtd->mad", select, out_store, preferred_element_type=jnp.float32).astype(
        jnp.bfloat16
    )
    shard_index = lax.axis_index("samples")
    my_partners = lax.dynamic_slice_in_dim(
        partner_samples, shard_index * micro_count, micro_count, 0
    )
    shard_count = lax.axis_size("samples")
    dest_shard = my_partners // micro_count
    dest_slot = my_partners % micro_count
    route = (
        (dest_shard[:, None, None] == jnp.arange(shard_count)[None, :, None])
        & (dest_slot[:, None, None] == jnp.arange(micro_count)[None, None, :])
    ).astype(jnp.bfloat16)
    outgoing = jnp.einsum("mku,mad->kuad", route, tiles, preferred_element_type=jnp.float32).astype(
        jnp.bfloat16
    )
    arrived = lax.all_to_all(outgoing, "samples", split_axis=0, concat_axis=0, tiled=True)
    ones_row = jnp.ones((shard_count,), jnp.bfloat16)
    received = jnp.einsum(
        "k,kuad->uad", ones_row, arrived, preferred_element_type=jnp.float32
    ).astype(jnp.bfloat16)
    placed = jnp.einsum("at,mad->mtd", select, received, preferred_element_type=jnp.float32)
    kept = jnp.where(region_mask[None, :, None] > 0, jnp.zeros_like(out_store), out_store)
    site_cot = (kept.astype(jnp.float32) + placed).astype(jnp.bfloat16)
    cotangents = jnp.where(section_index == 0, site_cot, out_store)
    onehot = (spins[:, :, None] == jnp.arange(SPINS)[None, None, :]).astype(jnp.bfloat16)
    embed_term = jnp.einsum("mtv,mtd->vd", onehot, site_cot, preferred_element_type=jnp.float32)
    embed_term = jnp.where(section_index == 0, embed_term, jnp.zeros_like(embed_term))
    embed_grad = lax.psum(embed_term, ("samples", "section"))
    return (summed_weight[None], cotangents[None], embed_grad)


def ring_sample(place, count):
    return jnp.where(place < count // 2, 2 * place, 2 * (count - place) - 1)


def ring_place(sample, count):
    return jnp.where(lax.rem(sample, 2) == 0, sample // 2, count - 1 - sample // 2)


def ring_route(count, distance):
    order = list(range(0, count, 2)) + list(range(1, count, 2))[::-1]
    return [(order[i], order[(i - distance) % count]) for i in range(count)]


def own_place(count):
    return ring_place(lax.axis_index("samples"), count)


def peer_at(place, distance, count):
    return ring_sample(lax.rem(place + distance + count, count), count)


def partner_of(slot):
    return jnp.bitwise_xor(lax.axis_index("samples"), slot)


def columns(index, size):
    return pl.ds(pl.multiple_of(index * size, size), size)


def in_vmem(count):
    return [pl.BlockSpec(memory_space=pltpu.VMEM)] * count


def in_smem(count):
    return [pl.BlockSpec(memory_space=pltpu.SMEM)] * count


def on_core(body, out_shapes, in_specs, scratch=(), micros=1, vmem=16):
    return pl.pallas_call(
        body,
        out_shape=out_shapes,
        in_specs=in_specs,
        out_specs=jax.tree.map(lambda _: pl.BlockSpec(memory_space=pltpu.VMEM), out_shapes),
        scratch_shapes=list(scratch),
        compiler_params=pltpu.CompilerParams(vmem_limit_bytes=vmem << 20),
        cost_estimate=pl.CostEstimate(
            flops=int(micros * FLOPS_PER_MICRO), bytes_accessed=1 << 16, transcendentals=0
        ),
    )


def matmul(left, right):
    return jnp.dot(left, right, preferred_element_type=jnp.float32)


def matmul_t(left, right):
    return lax.dot_general(
        left, right, (((1,), (1,)), ((), ())), preferred_element_type=jnp.float32
    )


def pack_kernel(count, share_axis, x_ref, w_ref, spins_ref, *refs):
    outs, sems = refs[:-1], refs[-1]
    seq_len = x_ref.shape[2]
    skipped = seq_len + TAIL
    sent = outs[0].shape[0] - skipped
    rows = columns(lax.axis_index(share_axis), sent) if share_axis else slice(None)
    copies = []
    for slot in range(count):
        cols = columns(partner_of(slot), HEAD)
        head, weight = outs[slot].at[0:seq_len, :], outs[slot].at[skipped:, :]
        copies.append(pltpu.make_async_copy(x_ref.at[0, 0, :, cols], head, sems.at[0, slot]))
        copies.append(pltpu.make_async_copy(w_ref.at[0, rows, cols], weight, sems.at[1, slot]))
    for copy in copies:
        copy.start()
    spin_rows = jnp.broadcast_to(spins_ref[...].astype(jnp.float32), (TAIL, seq_len))
    for slot in range(count):
        outs[slot][seq_len:skipped, :] = spin_rows.astype(jnp.bfloat16)
    for copy in copies:
        copy.wait()


def collect_kernel(count, *refs):
    heads_ref, rows_ref = refs[count:]
    sent = rows_ref.shape[1]
    for slot in range(count):
        peer = partner_of(slot)
        heads_ref[peer] = refs[slot][...]
        rows_ref[peer] = refs[slot][-sent:, :]


def forward_kernel(count, scale, *refs):
    heads_ref, shared, layout_ref = refs[0], refs[1:-6], refs[-4]
    probs_ref, turned_ref, bundle_ref = refs[-3:]
    seq_len = probs_ref.shape[1]
    lines = seq_len + TAIL
    half = lax.axis_index("mp")
    parts = count // 2
    sent = heads_ref.shape[1] - lines
    for part in range(parts):
        shard = (1 - half) * parts + part
        for piece, value in enumerate((heads_ref[shard, lines:, :], *(ref[shard] for ref in shared))):
            first = count * seq_len + (piece * parts + part) * sent
            bundle_ref[first : first + sent, :] = value
    blocks = layout_ref.shape[1]
    rows = lax.broadcasted_iota(jnp.int32, (seq_len, seq_len), 0) // BLOCK
    cols = lax.broadcasted_iota(jnp.int32, (seq_len, seq_len), 1) // BLOCK
    seen = rows == cols
    for q in range(blocks):
        for k in range(blocks):
            if q != k:
                seen = seen | ((rows == q) & (cols == k) & (layout_ref[0, q, k] > 0))
    xs = [heads_ref[slot, 0:seq_len, :] for slot in range(count)]
    scores = [jnp.where(seen, matmul_t(x, x) * scale, -jnp.inf) for x in xs]
    tops = [jnp.max(score, axis=-1, keepdims=True) for score in scores]
    terms = [jnp.exp(score - top) for score, top in zip(scores, tops)]
    sums = [jnp.sum(term, axis=-1, keepdims=True) for term in terms]
    for slot in range(count):
        probs = terms[slot] / sums[slot]
        low = probs.astype(jnp.bfloat16)
        probs_ref[slot] = probs
        attended = matmul(low, xs[slot]).astype(jnp.bfloat16)
        bundle_ref[slot * seq_len : (slot + 1) * seq_len, :] = attended
        turned_ref[slot] = transposed(low)


def lay_weights(weights, shares, share_axis):
    index = lax.axis_index(share_axis) if share_axis else 0
    pieces = len(shares) // 2
    parts = len(shares[0])
    for number, share in enumerate(shares):
        head, piece = number % 2, number // 2
        place = index if piece == 0 else 1 - index
        for part, value in enumerate(share):
            sent = value.shape[0]
            rows = pl.ds(pl.multiple_of((part * pieces + place) * sent, sent), sent)
            weights[rows, head * HEAD : (head + 1) * HEAD] = value


def weight_term(pieces, left, cols):
    total = None
    for index, first in enumerate(range(0, len(pieces), 2)):
        rows = [piece[:, cols] for slot in pieces[first : first + 2] for piece in slot]
        term = matmul(left[index], jnp.concatenate(rows, axis=0))
        total = term if total is None else total + term
    return total


def both_heads(own_ref, sibling_ref, samples, seq_len):
    rows = [
        jnp.concatenate(
            [ref[columns(sample, seq_len), :] for ref in (own_ref, sibling_ref)], axis=1
        )
        for sample in samples
    ]
    return transposed(jnp.concatenate(rows, axis=0))


def transposed(value):
    return value.astype(jnp.float32).T.astype(jnp.bfloat16)


def attention_back(scale, xs, probs, turned, grads, above):
    grad_probs = [matmul_t(grad, x) for grad, x in zip(grads, xs)]
    inner = [jnp.sum(grad * prob, axis=-1, keepdims=True) for grad, prob in zip(grad_probs, probs)]
    grad_scores = [
        (prob * (grad - total)).astype(jnp.bfloat16)
        for prob, grad, total in zip(probs, grad_probs, inner)
    ]
    both = [jnp.concatenate([grad, transposed(grad)], axis=1) for grad in grad_scores]
    results = []
    for index, x in enumerate(xs):
        through = matmul(turned[index], grads[index])
        through = through + scale * matmul(both[index], jnp.concatenate([x, x], axis=0))
        results.append((above[index].astype(jnp.float32) + through).astype(jnp.bfloat16))
    return results


def near_slots(count):
    return [slot for slot in range(count) if slot != count // 2]


def near_products_kernel(count, share_axis, *refs):
    pieces = [refs[index : index + 1] for index in range(count - 1)]
    bundle_ref, sibling_ref, heads_ref = refs[count - 1 : count + 2]
    shared = refs[count + 2 : -5]
    partial_ref, own_ref, other_ref, above_ref, weights = refs[-5:]
    place = own_place(count)
    shard = lax.axis_index("samples")
    parts, _, shard_rows = partial_ref.shape
    seq_len = pieces[0][0].shape[0]
    lines = seq_len + TAIL
    sent = heads_ref.shape[1] - lines
    half = lax.axis_index("mp")
    sample_of = [peer_at(place, slot, count) for slot in near_slots(count)]
    shares = []
    for piece, ref in enumerate((heads_ref, *shared)):
        skipped = lines if piece == 0 else 0
        shares.append([ref[half * parts + part, skipped:, :] for part in range(parts)])
        firsts = [count * seq_len + (piece * parts + part) * sent for part in range(parts)]
        shares.append([sibling_ref[first : first + sent, :] for first in firsts])
    lay_weights(weights, shares, share_axis)
    left = [
        both_heads(bundle_ref, sibling_ref, sample_of[first : first + 2], seq_len)
        for first in range(0, count - 1, 2)
    ]
    for part in range(parts):
        cols = slice(part * shard_rows, (part + 1) * shard_rows)
        partial_ref[part] = weight_term(pieces, left, cols)
    for first in range(0, count - 1, 2):
        rows = [piece[...] for slot in pieces[first : first + 2] for piece in slot]
        total = matmul(jnp.concatenate(rows, axis=0), weights[...])
        lines = slice(first * seq_len, first * seq_len + total.shape[0])
        own_ref[lines, :] = total[:, :HEAD]
        other_ref[lines, :] = total[:, HEAD:].astype(jnp.bfloat16)
    for index, slot in enumerate(pieces):
        above_ref[index * seq_len : (index + 1) * seq_len, :] = slot[0][:, columns(shard, HEAD)]


def near_back_kernel(count, scale, *refs):
    heads_ref, probs_ref, turned_ref, own_ref, other_ref, above_ref = refs[:6]
    grads_ref = refs[-1]
    place = own_place(count)
    seq_len = probs_ref.shape[1]
    sample_of = [peer_at(place, slot, count) for slot in near_slots(count)]
    lines = [slice(index * seq_len, (index + 1) * seq_len) for index in range(count - 1)]
    results = attention_back(
        scale,
        [heads_ref[sample, 0:seq_len, :] for sample in sample_of],
        [probs_ref[sample] for sample in sample_of],
        [turned_ref[sample] for sample in sample_of],
        [
            (own_ref[line, :] + other_ref[line, :].astype(jnp.float32)).astype(jnp.bfloat16)
            for line in lines
        ],
        [above_ref[line, :] for line in lines],
    )
    for index, result in enumerate(results):
        grads_ref[index] = result


def far_products_kernel(count, *refs):
    piece, refs = refs[:2], refs[2:]
    bundle_ref, sibling_ref, partial_ref, weights_ref = refs[:4]
    send_ref, keep_ref, own_ref, above_ref = refs[4:]
    sample = peer_at(own_place(count), count // 2, count)
    shard = lax.axis_index("samples")
    parts, _, shard_rows = partial_ref.shape
    left = [both_heads(bundle_ref, sibling_ref, [sample], 2 * piece[0].shape[0])]
    for part in range(parts):
        cols = slice(part * shard_rows, (part + 1) * shard_rows)
        total = transposed(partial_ref[part] + weight_term([piece], left, cols))
        keep_ref[part] = total[:, :HEAD]
        send_ref[cols, :] = total[:, HEAD:]
    total = matmul(jnp.concatenate([rows[...] for rows in piece], axis=0), weights_ref[...])
    own_ref[...] = total[:, :HEAD]
    send_ref[parts * shard_rows :, :] = total[:, HEAD:].astype(jnp.bfloat16)
    cols = columns(shard, HEAD)
    above_ref[...] = jnp.concatenate([rows[:, cols] for rows in piece], axis=0)


def far_kernel(count, scale, *refs):
    came_ref, keep_ref, own_ref, above_ref, heads_ref, probs_ref, turned_ref = refs[:7]
    near_ref, mask_ref, partner_ref = refs[7:10]
    outs, (grads, terms) = refs[10:-2], refs[-2:]
    place = own_place(count)
    half = lax.axis_index("mp")
    seq_len = probs_ref.shape[1]
    skipped = seq_len + TAIL
    parts, shard_rows = keep_ref.shape[:2]
    for part in range(parts):
        terms[half * parts + part] = keep_ref[part]
        lines = slice(part * shard_rows, (part + 1) * shard_rows)
        terms[(1 - half) * parts + part] = came_ref[lines, :]
    for index, slot in enumerate(near_slots(count)):
        grads[peer_at(place, slot, count)] = near_ref[index]
    sample = peer_at(place, count // 2, count)
    other = came_ref[parts * shard_rows :, :].astype(jnp.float32)
    (grads[sample],) = attention_back(
        scale,
        [heads_ref[sample, 0:seq_len, :]],
        [probs_ref[sample]],
        [turned_ref[sample]],
        [(own_ref[...] + other).astype(jnp.bfloat16)],
        [above_ref[...]],
    )
    region = jnp.broadcast_to(mask_ref[...].astype(jnp.float32), (HEAD, seq_len)).T > 0.5
    which = lax.broadcasted_iota(jnp.int32, (TAIL, seq_len), 0).astype(jnp.float32)
    embed = jnp.zeros((TAIL, HEAD), jnp.float32)
    for slot in range(count):
        sample = partner_of(slot)
        swapped = grads[partner_ref[sample]].astype(jnp.float32)
        site = jnp.where(region, swapped, grads[sample].astype(jnp.float32)).astype(jnp.bfloat16)
        outs[slot][0:seq_len, :] = site
        outs[slot][skipped:, :] = terms[sample]
        spin = heads_ref[sample, seq_len:skipped, :].astype(jnp.float32)
        embed = embed + matmul((spin == which).astype(jnp.bfloat16), site)
    high = embed.astype(jnp.bfloat16).astype(jnp.float32)
    low = embed - high
    tail = jnp.concatenate([high[: TAIL // 2], low[: TAIL // 2]], axis=0).astype(jnp.bfloat16)
    for slot in range(count):
        outs[slot][seq_len:skipped, :] = tail


def unpack_kernel(count, *refs):
    weight_ref, site_ref, embed_ref = refs[count:]
    seq_len = site_ref.shape[2]
    skipped = seq_len + TAIL
    for slot in range(count):
        cols = columns(partner_of(slot), HEAD)
        weight_ref[0, :, cols] = refs[slot][skipped:, :].astype(jnp.float32)
        site_ref[0, 0, :, cols] = refs[slot][0:seq_len, :]
        tail = refs[slot][seq_len:skipped, :].astype(jnp.float32)
        embed_ref[:, cols] = (tail[: TAIL // 2] + tail[TAIL // 2 :])[:SPINS]


def spread(blocks):
    count = len(blocks)
    came = [blocks[0]]
    for slot in range(1, count):
        route = [(shard, shard ^ slot) for shard in range(count)]
        came.append(lax.ppermute(blocks[slot], "samples", route))
    return came


def head_sharded(
    stored_inputs, top_cotangent, layer_weights, block_layout, region_mask, partner_samples, spins
):
    count = lax.axis_size("samples")
    seq_len = stored_inputs.shape[2]
    shard_rows, half_width = layer_weights.shape[1:]
    scale = 4.0 / HEAD
    bf16, f32 = jnp.bfloat16, jnp.float32
    per_head = (count, seq_len, HEAD)
    lines = seq_len + TAIL
    share_axis = "groups" if lax.axis_size("groups") == 2 else None
    sent = shard_rows // 2 if share_axis else shard_rows
    parts = count // 2
    swap = [(0, 1), (1, 0)]

    up, down = ring_route(count, -1), ring_route(count, 1)
    block = top_cotangent[0]
    rows = seq_len // 2
    packed = on_core(
        functools.partial(pack_kernel, count, share_axis),
        [jax.ShapeDtypeStruct((lines + sent, HEAD), bf16)] * count,
        [pl.BlockSpec(memory_space=pltpu.HBM)] * 2 + in_vmem(1),
        [pltpu.SemaphoreType.DMA((2, count))],
        micros=1,
        vmem=60,
    )(stored_inputs, layer_weights, spins)
    heads, weight_rows = on_core(
        functools.partial(collect_kernel, count),
        [
            jax.ShapeDtypeStruct((count, lines + sent, HEAD), bf16),
            jax.ShapeDtypeStruct((count, sent, HEAD), bf16),
        ],
        in_vmem(count),
        micros=0.4,
    )(*spread(packed))
    slots = {0: block}
    ahead, back = block, block
    for step in range(1, count // 2):
        ahead = lax.ppermute(ahead, "samples", up)
        back = lax.ppermute(back, "samples", down)
        slots[count - step], slots[step] = ahead, back
    far = (
        lax.ppermute(ahead[:rows], "samples", up),
        lax.ppermute(back[rows:], "samples", down),
    )
    near = [slots[slot] for slot in near_slots(count)]
    small = (region_mask.reshape(1, seq_len), partner_samples)
    shared = []
    if share_axis:
        shared = [lax.ppermute(weight_rows, share_axis, swap)]
    probs, turned, bundle = on_core(
        functools.partial(forward_kernel, count, scale),
        [
            jax.ShapeDtypeStruct(per_head, f32),
            jax.ShapeDtypeStruct(per_head, bf16),
            jax.ShapeDtypeStruct((count * seq_len + half_width, HEAD), bf16),
        ],
        in_vmem(2 + len(shared)) + in_smem(2),
        micros=1.2,
    )(heads, *shared, *small, block_layout)
    sibling = lax.ppermute(bundle, "mp", swap)
    near_lines = (count - 1) * seq_len
    partial, near_own, near_other, near_above, weights = on_core(
        functools.partial(near_products_kernel, count, share_axis),
        [
            jax.ShapeDtypeStruct((parts, 2 * HEAD, shard_rows), f32),
            jax.ShapeDtypeStruct((near_lines, HEAD), f32),
            jax.ShapeDtypeStruct((near_lines, HEAD), bf16),
            jax.ShapeDtypeStruct((near_lines, HEAD), bf16),
            jax.ShapeDtypeStruct((half_width, 2 * HEAD), bf16),
        ],
        in_vmem(count + 2 + len(shared)),
        micros=1.4,
    )(*near, bundle, sibling, heads, *shared)
    near_other = lax.ppermute(near_other, "mp", swap)
    near_grads = on_core(
        functools.partial(near_back_kernel, count, scale),
        jax.ShapeDtypeStruct((count - 1, seq_len, HEAD), bf16),
        in_vmem(7) + in_smem(1),
        micros=1.8,
    )(heads, probs, turned, near_own, near_other, near_above, *small)
    far_send, far_keep, far_own, far_above = on_core(
        functools.partial(far_products_kernel, count),
        [
            jax.ShapeDtypeStruct((half_width + seq_len, HEAD), bf16),
            jax.ShapeDtypeStruct((parts, shard_rows, HEAD), bf16),
            jax.ShapeDtypeStruct((seq_len, HEAD), f32),
            jax.ShapeDtypeStruct((seq_len, HEAD), bf16),
        ],
        in_vmem(6),
        micros=0.5,
    )(*far, bundle, sibling, partial, weights)
    far_came = lax.ppermute(far_send, "mp", swap)
    terms = on_core(
        functools.partial(far_kernel, count, scale),
        [jax.ShapeDtypeStruct((lines + shard_rows, HEAD), bf16)] * count,
        in_vmem(9) + in_smem(1),
        [pltpu.VMEM(per_head, bf16), pltpu.VMEM((count, shard_rows, HEAD), bf16)],
        micros=1.2,
    )(far_came, far_keep, far_own, far_above, heads, probs, turned, near_grads, *small)
    return on_core(
        functools.partial(unpack_kernel, count),
        [
            jax.ShapeDtypeStruct((1, shard_rows, half_width), f32),
            jax.ShapeDtypeStruct((1, 1, seq_len, half_width), bf16),
            jax.ShapeDtypeStruct((SPINS, half_width), f32),
        ],
        in_vmem(count),
        micros=1.2,
    )(*spread(terms))


def solution(mesh):
    in_specs = (
        P("section", ("groups", "samples"), None, "mp"),
        P(("groups", "samples"), None, "mp"),
        P("section", "samples", "mp"),
        P("section", None, None),
        P(),
        P("groups"),
        P(("groups", "samples"), None),
    )
    out_specs = (
        P(("groups", "section"), "samples", "mp"),
        P("section", ("groups", "samples"), None, "mp"),
        P("groups", "mp"),
    )
    shards = mesh.shape["samples"]

    def whole(stored_inputs, top_cotangent, *rest):
        samples, _, width = top_cotangent.shape
        layer_count = stored_inputs.shape[0]
        one_each = samples == mesh.shape["groups"] * shards and layer_count == 1
        by_heads = one_each and shards > 1 and shards & (shards - 1) == 0 and width == mesh.shape["mp"] * shards * HEAD
        return jax.shard_map(
            head_sharded if by_heads else local,
            mesh=mesh,
            in_specs=in_specs,
            out_specs=out_specs,
            check_vma=False,
        )(stored_inputs, top_cotangent, *rest)

    return whole
```

```python
import functools

import jax
import jax.numpy as jnp
from jax import lax
from jax.experimental import pallas as pl
from jax.experimental.pallas import tpu as pltpu
from jax.sharding import PartitionSpec as P

HEAD = 128
BLOCK = 64
SPINS = 2
TAIL = 16
FLOPS_PER_MICRO = 1.15e9


def for_sending(value):

    def short(part):
        return part.astype(jnp.bfloat16) if part.dtype == jnp.float32 else part

    return jax.tree.map(short, value)


def passed_along(block, axis, distance):
    devices = range(lax.axis_size(axis))
    route = [(i - distance, i) for i in devices if i - distance in devices]
    return lax.ppermute(block, axis, route)


def softmax_parts(inputs_h, allowed, attention_scale):
    scores = (
        jnp.einsum("qhd,khd->hqk", inputs_h, inputs_h, preferred_element_type=jnp.float32)
        * attention_scale
    )
    scores = jnp.where(allowed[None], scores, -jnp.inf)
    top_score = jnp.max(scores, axis=-1, keepdims=True)
    expo_terms = jnp.exp(scores - top_score)
    probs = expo_terms / jnp.sum(expo_terms, axis=-1, keepdims=True)
    return (probs, probs.astype(jnp.bfloat16))


def local(
    stored_inputs, top_cotangent, layer_weights, block_layout, region_mask, partner_samples, spins
):
    section_index = lax.axis_index("section")
    section_count = lax.axis_size("section")
    micro_count = stored_inputs.shape[1]
    seq_len = stored_inputs.shape[2]
    half_width = stored_inputs.shape[3]
    head_count = half_width // HEAD
    attention_scale = 4.0 / HEAD
    weights = lax.all_gather(layer_weights[0], "samples", axis=0, tiled=True)
    pos_block = jnp.arange(seq_len) // BLOCK
    block_onehot = (pos_block[:, None] == jnp.arange(block_layout.shape[1])[None, :]).astype(
        jnp.float32
    )
    linked = jnp.dot(jnp.dot(block_onehot, block_layout[0].astype(jnp.float32)), block_onehot.T)
    allowed = (linked > 0.5) | (pos_block[:, None] == pos_block[None, :])
    every_layer_input = stored_inputs[0]
    inputs_h = every_layer_input[0].reshape(seq_len, head_count, HEAD)
    probs, probs_low = softmax_parts(inputs_h, allowed, attention_scale)
    attended = jnp.einsum(
        "hqk,khd->qhd", probs_low, inputs_h, preferred_element_type=jnp.float32
    ).astype(jnp.bfloat16)
    probs_list = [probs]
    low_list = [probs_low]
    attend_list = [attended.reshape(seq_len, half_width)]
    probs_all = jnp.stack(probs_list)
    low_all = jnp.stack(low_list)
    attend_store = jnp.stack(attend_list)

    def layer_back(grad_full, grad_own, inputs, probs, probs_low):
        grad_attn = jnp.dot(grad_full, weights, preferred_element_type=jnp.float32).astype(
            jnp.bfloat16
        )
        inputs_h = inputs.reshape(seq_len, head_count, HEAD)
        grad_h = grad_attn.reshape(seq_len, head_count, HEAD)
        grad_probs = jnp.einsum(
            "qhd,khd->hqk", grad_h, inputs_h, preferred_element_type=jnp.float32
        )
        grad_scores = (
            probs * (grad_probs - jnp.sum(grad_probs * probs, axis=-1, keepdims=True))
        ).astype(jnp.bfloat16)
        through = jnp.einsum("hqk,qhd->khd", probs_low, grad_h, preferred_element_type=jnp.float32)
        through = through + attention_scale * (
            jnp.einsum("hqk,khd->qhd", grad_scores, inputs_h, preferred_element_type=jnp.float32)
            + jnp.einsum("hqk,qhd->khd", grad_scores, inputs_h, preferred_element_type=jnp.float32)
        )
        grad_in = grad_own.astype(jnp.float32) + through.reshape(seq_len, half_width)
        return grad_in.astype(jnp.bfloat16)

    def resting(grad_full, grad_own, inputs, probs, probs_low):
        return jnp.zeros((seq_len, half_width), jnp.bfloat16)

    carried_state = jnp.zeros((seq_len, half_width), jnp.bfloat16)
    out_list = []
    grad_list = []
    total_steps = micro_count + section_count - 1
    for step_number in range(total_steps):
        micro_index = step_number - (section_count - 1 - section_index)
        active = (micro_index >= 0) & (micro_index < micro_count)
        slot_index = jnp.clip(micro_index, 0, micro_count - 1)
        from_top = lax.dynamic_index_in_dim(top_cotangent, slot_index, 0, keepdims=False)
        incoming = jnp.where(section_index == section_count - 1, from_top, carried_state)
        grad_full = lax.all_gather(incoming, "mp", axis=1, tiled=True)
        inputs_now = lax.dynamic_index_in_dim(every_layer_input, slot_index, 0, keepdims=False)
        probs_now = lax.dynamic_index_in_dim(probs_all, slot_index, 0, keepdims=False)
        low_now = lax.dynamic_index_in_dim(low_all, slot_index, 0, keepdims=False)
        grad_in = lax.cond(
            active, layer_back, resting, grad_full, incoming, inputs_now, probs_now, low_now
        )
        out_list.append(grad_in)
        grad_list.append(grad_full)
        if step_number < total_steps - 1:
            carried_state = jax.tree.map(
                lambda part, own: part.astype(own.dtype),
                passed_along(for_sending(grad_in), "section", -1),
                grad_in,
            )
    offset = section_count - 1 - section_index
    out_store = lax.dynamic_slice_in_dim(jnp.stack(out_list), offset, micro_count, 0)
    grad_store = lax.dynamic_slice_in_dim(jnp.stack(grad_list), offset, micro_count, 0)
    summed_weight = lax.psum_scatter(
        jnp.einsum(
            "mtf,mta->fa", grad_store, attend_store, preferred_element_type=jnp.float32
        ).astype(jnp.bfloat16),
        "samples",
        scatter_dimension=0,
        tiled=True,
    ).astype(jnp.float32)
    region_count = seq_len // 2
    rank_in_region = jnp.cumsum(region_mask) - 1
    select = (
        (rank_in_region[None, :] == jnp.arange(region_count)[:, None]) & (region_mask[None, :] > 0)
    ).astype(jnp.bfloat16)
    tiles = jnp.einsum("at,mtd->mad", select, out_store, preferred_element_type=jnp.float32).astype(
        jnp.bfloat16
    )
    shard_index = lax.axis_index("samples")
    my_partners = lax.dynamic_slice_in_dim(
        partner_samples, shard_index * micro_count, micro_count, 0
    )
    shard_count = lax.axis_size("samples")
    dest_shard = my_partners // micro_count
    dest_slot = my_partners % micro_count
    route = (
        (dest_shard[:, None, None] == jnp.arange(shard_count)[None, :, None])
        & (dest_slot[:, None, None] == jnp.arange(micro_count)[None, None, :])
    ).astype(jnp.bfloat16)
    outgoing = jnp.einsum("mku,mad->kuad", route, tiles, preferred_element_type=jnp.float32).astype(
        jnp.bfloat16
    )
    arrived = lax.all_to_all(outgoing, "samples", split_axis=0, concat_axis=0, tiled=True)
    ones_row = jnp.ones((shard_count,), jnp.bfloat16)
    received = jnp.einsum(
        "k,kuad->uad", ones_row, arrived, preferred_element_type=jnp.float32
    ).astype(jnp.bfloat16)
    placed = jnp.einsum("at,mad->mtd", select, received, preferred_element_type=jnp.float32)
    kept = jnp.where(region_mask[None, :, None] > 0, jnp.zeros_like(out_store), out_store)
    site_cot = (kept.astype(jnp.float32) + placed).astype(jnp.bfloat16)
    cotangents = jnp.where(section_index == 0, site_cot, out_store)
    onehot = (spins[:, :, None] == jnp.arange(SPINS)[None, None, :]).astype(jnp.bfloat16)
    embed_term = jnp.einsum("mtv,mtd->vd", onehot, site_cot, preferred_element_type=jnp.float32)
    embed_term = jnp.where(section_index == 0, embed_term, jnp.zeros_like(embed_term))
    embed_grad = lax.psum(embed_term, ("samples", "section"))
    return (summed_weight[None], cotangents[None], embed_grad)


def ring_sample(place, count):
    return jnp.where(place < count // 2, 2 * place, 2 * (count - place) - 1)


def ring_place(sample, count):
    return jnp.where(lax.rem(sample, 2) == 0, sample // 2, count - 1 - sample // 2)


def ring_route(count, distance):
    order = list(range(0, count, 2)) + list(range(1, count, 2))[::-1]
    return [(order[i], order[(i - distance) % count]) for i in range(count)]


def own_place(count):
    return ring_place(lax.axis_index("samples"), count)


def peer_at(place, distance, count):
    return ring_sample(lax.rem(place + distance + count, count), count)


def partner_of(slot):
    return jnp.bitwise_xor(lax.axis_index("samples"), slot)


def far_first(count):
    return [*range(count // 2, count), *range(count // 2)]


def columns(index, size):
    return pl.ds(pl.multiple_of(index * size, size), size)


def in_vmem(count):
    return [pl.BlockSpec(memory_space=pltpu.VMEM)] * count


def in_smem(count):
    return [pl.BlockSpec(memory_space=pltpu.SMEM)] * count


def on_core(body, out_shapes, in_specs, scratch=(), micros=1, vmem=16):
    return pl.pallas_call(
        body,
        out_shape=out_shapes,
        in_specs=in_specs,
        out_specs=jax.tree.map(lambda _: pl.BlockSpec(memory_space=pltpu.VMEM), out_shapes),
        scratch_shapes=list(scratch),
        compiler_params=pltpu.CompilerParams(vmem_limit_bytes=vmem << 20),
        cost_estimate=pl.CostEstimate(
            flops=int(micros * FLOPS_PER_MICRO), bytes_accessed=1 << 16, transcendentals=0
        ),
    )


def matmul(left, right):
    return jnp.dot(left, right, preferred_element_type=jnp.float32)


def matmul_t(left, right):
    return lax.dot_general(
        left, right, (((1,), (1,)), ((), ())), preferred_element_type=jnp.float32
    )


def pack_kernel(count, share_axis, x_ref, w_ref, spins_ref, *refs):
    outs, sems = refs[:-1], refs[-1]
    seq_len = x_ref.shape[2]
    skipped = seq_len + TAIL
    sent = outs[0].shape[0] - skipped
    rows = columns(lax.axis_index(share_axis), sent) if share_axis else slice(None)
    copies = []
    for slot in range(count):
        cols = columns(partner_of(slot), HEAD)
        head, weight = outs[slot].at[0:seq_len, :], outs[slot].at[skipped:, :]
        copies.append(pltpu.make_async_copy(x_ref.at[0, 0, :, cols], head, sems.at[0, slot]))
        copies.append(pltpu.make_async_copy(w_ref.at[0, rows, cols], weight, sems.at[1, slot]))
    for copy in copies:
        copy.start()
    spin_rows = jnp.broadcast_to(spins_ref[...].astype(jnp.float32), (TAIL, seq_len))
    for slot in range(count):
        outs[slot][seq_len:skipped, :] = spin_rows.astype(jnp.bfloat16)
    for copy in copies:
        copy.wait()


def collect_kernel(count, *refs):
    heads_ref, rows_ref = refs[count:]
    sent = rows_ref.shape[1]
    for slot in range(count):
        peer = partner_of(slot)
        heads_ref[peer] = refs[slot][...]
        rows_ref[peer] = refs[slot][-sent:, :]


def forward_kernel(count, scale, *refs):
    heads_ref, shared, layout_ref = refs[0], refs[1:-6], refs[-4]
    probs_ref, turned_ref, bundle_ref = refs[-3:]
    seq_len = probs_ref.shape[1]
    lines = seq_len + TAIL
    half = lax.axis_index("mp")
    parts = count // 2
    sent = heads_ref.shape[1] - lines
    for part in range(parts):
        shard = (1 - half) * parts + part
        for piece, value in enumerate((heads_ref[shard, lines:, :], *(ref[shard] for ref in shared))):
            first = count * seq_len + (piece * parts + part) * sent
            bundle_ref[first : first + sent, :] = value
    blocks = layout_ref.shape[1]
    rows = lax.broadcasted_iota(jnp.int32, (seq_len, seq_len), 0) // BLOCK
    cols = lax.broadcasted_iota(jnp.int32, (seq_len, seq_len), 1) // BLOCK
    seen = rows == cols
    for q in range(blocks):
        for k in range(blocks):
            if q != k:
                seen = seen | ((rows == q) & (cols == k) & (layout_ref[0, q, k] > 0))
    xs = [heads_ref[slot, 0:seq_len, :] for slot in range(count)]
    scores = [jnp.where(seen, matmul_t(x, x) * scale, -jnp.inf) for x in xs]
    tops = [jnp.max(score, axis=-1, keepdims=True) for score in scores]
    terms = [jnp.exp(score - top) for score, top in zip(scores, tops)]
    sums = [jnp.sum(term, axis=-1, keepdims=True) for term in terms]
    for slot in range(count):
        probs = terms[slot] / sums[slot]
        low = probs.astype(jnp.bfloat16)
        probs_ref[slot] = probs
        attended = matmul(low, xs[slot]).astype(jnp.bfloat16)
        bundle_ref[slot * seq_len : (slot + 1) * seq_len, :] = attended
        turned_ref[slot] = transposed(low)


def lay_weights(weights, shares, share_axis):
    index = lax.axis_index(share_axis) if share_axis else 0
    pieces = len(shares) // 2
    parts = len(shares[0])
    for number, share in enumerate(shares):
        head, piece = number % 2, number // 2
        place = index if piece == 0 else 1 - index
        for part, value in enumerate(share):
            sent = value.shape[0]
            rows = pl.ds(pl.multiple_of((part * pieces + place) * sent, sent), sent)
            weights[rows, head * HEAD : (head + 1) * HEAD] = value


def weight_term(pieces, left, cols):
    total = None
    for index, first in enumerate(range(0, len(pieces), 2)):
        rows = [piece[:, cols] for slot in pieces[first : first + 2] for piece in slot]
        term = matmul(left[index], jnp.concatenate(rows, axis=0))
        total = term if total is None else total + term
    return total


def both_heads(own_ref, sibling_ref, samples, seq_len):
    rows = [
        jnp.concatenate(
            [ref[columns(sample, seq_len), :] for ref in (own_ref, sibling_ref)], axis=1
        )
        for sample in samples
    ]
    return transposed(jnp.concatenate(rows, axis=0))


def transposed(value):
    return value.astype(jnp.float32).T.astype(jnp.bfloat16)


def attention_back(scale, xs, probs, turned, grads, above):
    grad_probs = [matmul_t(grad, x) for grad, x in zip(grads, xs)]
    inner = [jnp.sum(grad * prob, axis=-1, keepdims=True) for grad, prob in zip(grad_probs, probs)]
    grad_scores = [
        (prob * (grad - total)).astype(jnp.bfloat16)
        for prob, grad, total in zip(probs, grad_probs, inner)
    ]
    both = [jnp.concatenate([grad, transposed(grad)], axis=1) for grad in grad_scores]
    results = []
    for index, x in enumerate(xs):
        through = matmul(turned[index], grads[index])
        through = through + scale * matmul(both[index], jnp.concatenate([x, x], axis=0))
        results.append((above[index].astype(jnp.float32) + through).astype(jnp.bfloat16))
    return results


def near_slots(count):
    return [slot for slot in range(count) if slot != count // 2]


def near_products_kernel(count, share_axis, *refs):
    pieces = [refs[index : index + 1] for index in range(count - 1)]
    bundle_ref, sibling_ref, heads_ref = refs[count - 1 : count + 2]
    shared = refs[count + 2 : -5]
    partial_ref, own_ref, other_ref, above_ref, weights = refs[-5:]
    place = own_place(count)
    shard = lax.axis_index("samples")
    parts, _, shard_rows = partial_ref.shape
    seq_len = pieces[0][0].shape[0]
    lines = seq_len + TAIL
    sent = heads_ref.shape[1] - lines
    half = lax.axis_index("mp")
    sample_of = [peer_at(place, slot, count) for slot in near_slots(count)]
    shares = []
    for piece, ref in enumerate((heads_ref, *shared)):
        skipped = lines if piece == 0 else 0
        shares.append([ref[half * parts + part, skipped:, :] for part in range(parts)])
        firsts = [count * seq_len + (piece * parts + part) * sent for part in range(parts)]
        shares.append([sibling_ref[first : first + sent, :] for first in firsts])
    lay_weights(weights, shares, share_axis)
    left = [
        both_heads(bundle_ref, sibling_ref, sample_of[first : first + 2], seq_len)
        for first in range(0, count - 1, 2)
    ]
    for part in range(parts):
        cols = slice(part * shard_rows, (part + 1) * shard_rows)
        partial_ref[part] = weight_term(pieces, left, cols)
    for first in range(0, count - 1, 2):
        rows = [piece[...] for slot in pieces[first : first + 2] for piece in slot]
        total = matmul(jnp.concatenate(rows, axis=0), weights[...])
        lines = slice(first * seq_len, first * seq_len + total.shape[0])
        own_ref[lines, :] = total[:, :HEAD]
        other_ref[lines, :] = total[:, HEAD:].astype(jnp.bfloat16)
    for index, slot in enumerate(pieces):
        above_ref[index * seq_len : (index + 1) * seq_len, :] = slot[0][:, columns(shard, HEAD)]


def near_back_kernel(count, scale, *refs):
    heads_ref, probs_ref, turned_ref, own_ref, other_ref, above_ref = refs[:6]
    grads_ref = refs[-1]
    place = own_place(count)
    seq_len = probs_ref.shape[1]
    sample_of = [peer_at(place, slot, count) for slot in near_slots(count)]
    lines = [slice(index * seq_len, (index + 1) * seq_len) for index in range(count - 1)]
    results = attention_back(
        scale,
        [heads_ref[sample, 0:seq_len, :] for sample in sample_of],
        [probs_ref[sample] for sample in sample_of],
        [turned_ref[sample] for sample in sample_of],
        [
            (own_ref[line, :] + other_ref[line, :].astype(jnp.float32)).astype(jnp.bfloat16)
            for line in lines
        ],
        [above_ref[line, :] for line in lines],
    )
    for index, result in enumerate(results):
        grads_ref[index] = result


def far_products_kernel(count, *refs):
    piece, refs = refs[:2], refs[2:]
    bundle_ref, sibling_ref, partial_ref, weights_ref = refs[:4]
    send_ref, keep_ref, own_ref, above_ref = refs[4:]
    sample = peer_at(own_place(count), count // 2, count)
    shard = lax.axis_index("samples")
    parts, _, shard_rows = partial_ref.shape
    left = [both_heads(bundle_ref, sibling_ref, [sample], 2 * piece[0].shape[0])]
    for part in range(parts):
        cols = slice(part * shard_rows, (part + 1) * shard_rows)
        total = transposed(partial_ref[part] + weight_term([piece], left, cols))
        keep_ref[part] = total[:, :HEAD]
        send_ref[cols, :] = total[:, HEAD:]
    total = matmul(jnp.concatenate([rows[...] for rows in piece], axis=0), weights_ref[...])
    own_ref[...] = total[:, :HEAD]
    send_ref[parts * shard_rows :, :] = total[:, HEAD:].astype(jnp.bfloat16)
    cols = columns(shard, HEAD)
    above_ref[...] = jnp.concatenate([rows[:, cols] for rows in piece], axis=0)


def far_kernel(count, scale, *refs):
    came_ref, keep_ref, own_ref, above_ref, heads_ref, probs_ref, turned_ref = refs[:7]
    near_ref, mask_ref, partner_ref = refs[7:10]
    outs, (grads, terms) = refs[10:-2], refs[-2:]
    place = own_place(count)
    half = lax.axis_index("mp")
    seq_len = probs_ref.shape[1]
    skipped = seq_len + TAIL
    parts, shard_rows = keep_ref.shape[:2]
    for part in range(parts):
        terms[half * parts + part] = keep_ref[part]
        lines = slice(part * shard_rows, (part + 1) * shard_rows)
        terms[(1 - half) * parts + part] = came_ref[lines, :]
    for index, slot in enumerate(near_slots(count)):
        grads[peer_at(place, slot, count)] = near_ref[index]
    sample = peer_at(place, count // 2, count)
    other = came_ref[parts * shard_rows :, :].astype(jnp.float32)
    (grads[sample],) = attention_back(
        scale,
        [heads_ref[sample, 0:seq_len, :]],
        [probs_ref[sample]],
        [turned_ref[sample]],
        [(own_ref[...] + other).astype(jnp.bfloat16)],
        [above_ref[...]],
    )
    region = jnp.broadcast_to(mask_ref[...].astype(jnp.float32), (HEAD, seq_len)).T > 0.5
    which = lax.broadcasted_iota(jnp.int32, (TAIL, seq_len), 0).astype(jnp.float32)
    embed = jnp.zeros((TAIL, HEAD), jnp.float32)
    for slot in range(count):
        sample = partner_of(slot)
        swapped = grads[partner_ref[sample]].astype(jnp.float32)
        site = jnp.where(region, swapped, grads[sample].astype(jnp.float32)).astype(jnp.bfloat16)
        outs[slot][0:seq_len, :] = site
        outs[slot][skipped:, :] = terms[sample]
        spin = heads_ref[sample, seq_len:skipped, :].astype(jnp.float32)
        embed = embed + matmul((spin == which).astype(jnp.bfloat16), site)
    high = embed.astype(jnp.bfloat16).astype(jnp.float32)
    low = embed - high
    tail = jnp.concatenate([high[: TAIL // 2], low[: TAIL // 2]], axis=0).astype(jnp.bfloat16)
    for slot in range(count):
        outs[slot][seq_len:skipped, :] = tail


def unpack_kernel(count, *refs):
    weight_ref, site_ref, embed_ref = refs[count:]
    refs = dict(zip(far_first(count), refs))
    seq_len = site_ref.shape[2]
    skipped = seq_len + TAIL
    for slot in range(count):
        cols = columns(partner_of(slot), HEAD)
        weight_ref[0, :, cols] = refs[slot][skipped:, :].astype(jnp.float32)
        site_ref[0, 0, :, cols] = refs[slot][0:seq_len, :]
        tail = refs[slot][seq_len:skipped, :].astype(jnp.float32)
        embed_ref[:, cols] = (tail[: TAIL // 2] + tail[TAIL // 2 :])[:SPINS]


def spread(blocks):
    count = len(blocks)
    came = [blocks[0]]
    for slot in range(1, count):
        route = [(shard, shard ^ slot) for shard in range(count)]
        came.append(lax.ppermute(blocks[slot], "samples", route))
    return came


def head_sharded(
    stored_inputs, top_cotangent, layer_weights, block_layout, region_mask, partner_samples, spins
):
    count = lax.axis_size("samples")
    seq_len = stored_inputs.shape[2]
    shard_rows, half_width = layer_weights.shape[1:]
    scale = 4.0 / HEAD
    bf16, f32 = jnp.bfloat16, jnp.float32
    per_head = (count, seq_len, HEAD)
    lines = seq_len + TAIL
    share_axis = "groups" if lax.axis_size("groups") == 2 else None
    sent = shard_rows // 2 if share_axis else shard_rows
    parts = count // 2
    swap = [(0, 1), (1, 0)]

    up, down = ring_route(count, -1), ring_route(count, 1)
    block = top_cotangent[0]
    rows = seq_len // 2
    packed = on_core(
        functools.partial(pack_kernel, count, share_axis),
        [jax.ShapeDtypeStruct((lines + sent, HEAD), bf16)] * count,
        [pl.BlockSpec(memory_space=pltpu.HBM)] * 2 + in_vmem(1),
        [pltpu.SemaphoreType.DMA((2, count))],
        micros=1,
        vmem=60,
    )(stored_inputs, layer_weights, spins)
    heads, weight_rows = on_core(
        functools.partial(collect_kernel, count),
        [
            jax.ShapeDtypeStruct((count, lines + sent, HEAD), bf16),
            jax.ShapeDtypeStruct((count, sent, HEAD), bf16),
        ],
        in_vmem(count),
        micros=0.4,
    )(*spread(packed))
    slots = {0: block}
    ahead, back = block, block
    for step in range(1, count // 2):
        ahead = lax.ppermute(ahead, "samples", up)
        back = lax.ppermute(back, "samples", down)
        slots[count - step], slots[step] = ahead, back
    far = (
        lax.ppermute(ahead[:rows], "samples", up),
        lax.ppermute(back[rows:], "samples", down),
    )
    near = [slots[slot] for slot in near_slots(count)]
    small = (region_mask.reshape(1, seq_len), partner_samples)
    shared = []
    if share_axis:
        shared = [lax.ppermute(weight_rows, share_axis, swap)]
    probs, turned, bundle = on_core(
        functools.partial(forward_kernel, count, scale),
        [
            jax.ShapeDtypeStruct(per_head, f32),
            jax.ShapeDtypeStruct(per_head, bf16),
            jax.ShapeDtypeStruct((count * seq_len + half_width, HEAD), bf16),
        ],
        in_vmem(2 + len(shared)) + in_smem(2),
        micros=1.2,
    )(heads, *shared, *small, block_layout)
    sibling = lax.ppermute(bundle, "mp", swap)
    near_lines = (count - 1) * seq_len
    partial, near_own, near_other, near_above, weights = on_core(
        functools.partial(near_products_kernel, count, share_axis),
        [
            jax.ShapeDtypeStruct((parts, 2 * HEAD, shard_rows), f32),
            jax.ShapeDtypeStruct((near_lines, HEAD), f32),
            jax.ShapeDtypeStruct((near_lines, HEAD), bf16),
            jax.ShapeDtypeStruct((near_lines, HEAD), bf16),
            jax.ShapeDtypeStruct((half_width, 2 * HEAD), bf16),
        ],
        in_vmem(count + 2 + len(shared)),
        micros=1.4,
    )(*near, bundle, sibling, heads, *shared)
    near_other = lax.ppermute(near_other, "mp", swap)
    near_grads = on_core(
        functools.partial(near_back_kernel, count, scale),
        jax.ShapeDtypeStruct((count - 1, seq_len, HEAD), bf16),
        in_vmem(7) + in_smem(1),
        micros=1.8,
    )(heads, probs, turned, near_own, near_other, near_above, *small)
    far_send, far_keep, far_own, far_above = on_core(
        functools.partial(far_products_kernel, count),
        [
            jax.ShapeDtypeStruct((half_width + seq_len, HEAD), bf16),
            jax.ShapeDtypeStruct((parts, shard_rows, HEAD), bf16),
            jax.ShapeDtypeStruct((seq_len, HEAD), f32),
            jax.ShapeDtypeStruct((seq_len, HEAD), bf16),
        ],
        in_vmem(6),
        micros=0.5,
    )(*far, bundle, sibling, partial, weights)
    far_came = lax.ppermute(far_send, "mp", swap)
    terms = on_core(
        functools.partial(far_kernel, count, scale),
        [jax.ShapeDtypeStruct((lines + shard_rows, HEAD), bf16)] * count,
        in_vmem(9) + in_smem(1),
        [pltpu.VMEM(per_head, bf16), pltpu.VMEM((count, shard_rows, HEAD), bf16)],
        micros=1.2,
    )(far_came, far_keep, far_own, far_above, heads, probs, turned, near_grads, *small)
    came = spread(terms)
    return on_core(
        functools.partial(unpack_kernel, count),
        [
            jax.ShapeDtypeStruct((1, shard_rows, half_width), f32),
            jax.ShapeDtypeStruct((1, 1, seq_len, half_width), bf16),
            jax.ShapeDtypeStruct((SPINS, half_width), f32),
        ],
        in_vmem(count),
        micros=1.2,
    )(*[came[slot] for slot in far_first(count)])


def solution(mesh):
    in_specs = (
        P("section", ("groups", "samples"), None, "mp"),
        P(("groups", "samples"), None, "mp"),
        P("section", "samples", "mp"),
        P("section", None, None),
        P(),
        P("groups"),
        P(("groups", "samples"), None),
    )
    out_specs = (
        P(("groups", "section"), "samples", "mp"),
        P("section", ("groups", "samples"), None, "mp"),
        P("groups", "mp"),
    )
    shards = mesh.shape["samples"]

    def whole(stored_inputs, top_cotangent, *rest):
        samples, _, width = top_cotangent.shape
        layer_count = stored_inputs.shape[0]
        one_each = samples == mesh.shape["groups"] * shards and layer_count == 1
        by_heads = one_each and shards > 1 and shards & (shards - 1) == 0 and width == mesh.shape["mp"] * shards * HEAD
        return jax.shard_map(
            head_sharded if by_heads else local,
            mesh=mesh,
            in_specs=in_specs,
            out_specs=out_specs,
            check_vma=False,
        )(stored_inputs, top_cotangent, *rest)

    return whole
```

```python
import functools

import jax
import jax.numpy as jnp
from jax import lax
from jax.experimental import pallas as pl
from jax.experimental.pallas import tpu as pltpu
from jax.sharding import PartitionSpec as P

HEAD = 128
BLOCK = 64
SPINS = 2
TAIL = 16
FLOPS_PER_MICRO = 1.15e9


def for_sending(value):

    def short(part):
        return part.astype(jnp.bfloat16) if part.dtype == jnp.float32 else part

    return jax.tree.map(short, value)


def passed_along(block, axis, distance):
    devices = range(lax.axis_size(axis))
    route = [(i - distance, i) for i in devices if i - distance in devices]
    return lax.ppermute(block, axis, route)


def softmax_parts(inputs_h, allowed, attention_scale):
    scores = (
        jnp.einsum("qhd,khd->hqk", inputs_h, inputs_h, preferred_element_type=jnp.float32)
        * attention_scale
    )
    scores = jnp.where(allowed[None], scores, -jnp.inf)
    top_score = jnp.max(scores, axis=-1, keepdims=True)
    expo_terms = jnp.exp(scores - top_score)
    probs = expo_terms / jnp.sum(expo_terms, axis=-1, keepdims=True)
    return (probs, probs.astype(jnp.bfloat16))


def local(
    stored_inputs, top_cotangent, layer_weights, block_layout, region_mask, partner_samples, spins
):
    section_index = lax.axis_index("section")
    section_count = lax.axis_size("section")
    micro_count = stored_inputs.shape[1]
    seq_len = stored_inputs.shape[2]
    half_width = stored_inputs.shape[3]
    head_count = half_width // HEAD
    attention_scale = 4.0 / HEAD
    weights = lax.all_gather(layer_weights[0], "samples", axis=0, tiled=True)
    pos_block = jnp.arange(seq_len) // BLOCK
    block_onehot = (pos_block[:, None] == jnp.arange(block_layout.shape[1])[None, :]).astype(
        jnp.float32
    )
    linked = jnp.dot(jnp.dot(block_onehot, block_layout[0].astype(jnp.float32)), block_onehot.T)
    allowed = (linked > 0.5) | (pos_block[:, None] == pos_block[None, :])
    every_layer_input = stored_inputs[0]
    inputs_h = every_layer_input[0].reshape(seq_len, head_count, HEAD)
    probs, probs_low = softmax_parts(inputs_h, allowed, attention_scale)
    attended = jnp.einsum(
        "hqk,khd->qhd", probs_low, inputs_h, preferred_element_type=jnp.float32
    ).astype(jnp.bfloat16)
    probs_list = [probs]
    low_list = [probs_low]
    attend_list = [attended.reshape(seq_len, half_width)]
    probs_all = jnp.stack(probs_list)
    low_all = jnp.stack(low_list)
    attend_store = jnp.stack(attend_list)

    def layer_back(grad_full, grad_own, inputs, probs, probs_low):
        grad_attn = jnp.dot(grad_full, weights, preferred_element_type=jnp.float32).astype(
            jnp.bfloat16
        )
        inputs_h = inputs.reshape(seq_len, head_count, HEAD)
        grad_h = grad_attn.reshape(seq_len, head_count, HEAD)
        grad_probs = jnp.einsum(
            "qhd,khd->hqk", grad_h, inputs_h, preferred_element_type=jnp.float32
        )
        grad_scores = (
            probs * (grad_probs - jnp.sum(grad_probs * probs, axis=-1, keepdims=True))
        ).astype(jnp.bfloat16)
        through = jnp.einsum("hqk,qhd->khd", probs_low, grad_h, preferred_element_type=jnp.float32)
        through = through + attention_scale * (
            jnp.einsum("hqk,khd->qhd", grad_scores, inputs_h, preferred_element_type=jnp.float32)
            + jnp.einsum("hqk,qhd->khd", grad_scores, inputs_h, preferred_element_type=jnp.float32)
        )
        grad_in = grad_own.astype(jnp.float32) + through.reshape(seq_len, half_width)
        return grad_in.astype(jnp.bfloat16)

    def resting(grad_full, grad_own, inputs, probs, probs_low):
        return jnp.zeros((seq_len, half_width), jnp.bfloat16)

    carried_state = jnp.zeros((seq_len, half_width), jnp.bfloat16)
    out_list = []
    grad_list = []
    total_steps = micro_count + section_count - 1
    for step_number in range(total_steps):
        micro_index = step_number - (section_count - 1 - section_index)
        active = (micro_index >= 0) & (micro_index < micro_count)
        slot_index = jnp.clip(micro_index, 0, micro_count - 1)
        from_top = lax.dynamic_index_in_dim(top_cotangent, slot_index, 0, keepdims=False)
        incoming = jnp.where(section_index == section_count - 1, from_top, carried_state)
        grad_full = lax.all_gather(incoming, "mp", axis=1, tiled=True)
        inputs_now = lax.dynamic_index_in_dim(every_layer_input, slot_index, 0, keepdims=False)
        probs_now = lax.dynamic_index_in_dim(probs_all, slot_index, 0, keepdims=False)
        low_now = lax.dynamic_index_in_dim(low_all, slot_index, 0, keepdims=False)
        grad_in = lax.cond(
            active, layer_back, resting, grad_full, incoming, inputs_now, probs_now, low_now
        )
        out_list.append(grad_in)
        grad_list.append(grad_full)
        if step_number < total_steps - 1:
            carried_state = jax.tree.map(
                lambda part, own: part.astype(own.dtype),
                passed_along(for_sending(grad_in), "section", -1),
                grad_in,
            )
    offset = section_count - 1 - section_index
    out_store = lax.dynamic_slice_in_dim(jnp.stack(out_list), offset, micro_count, 0)
    grad_store = lax.dynamic_slice_in_dim(jnp.stack(grad_list), offset, micro_count, 0)
    summed_weight = lax.psum_scatter(
        jnp.einsum(
            "mtf,mta->fa", grad_store, attend_store, preferred_element_type=jnp.float32
        ).astype(jnp.bfloat16),
        "samples",
        scatter_dimension=0,
        tiled=True,
    ).astype(jnp.float32)
    region_count = seq_len // 2
    rank_in_region = jnp.cumsum(region_mask) - 1
    select = (
        (rank_in_region[None, :] == jnp.arange(region_count)[:, None]) & (region_mask[None, :] > 0)
    ).astype(jnp.bfloat16)
    tiles = jnp.einsum("at,mtd->mad", select, out_store, preferred_element_type=jnp.float32).astype(
        jnp.bfloat16
    )
    shard_index = lax.axis_index("samples")
    my_partners = lax.dynamic_slice_in_dim(
        partner_samples, shard_index * micro_count, micro_count, 0
    )
    shard_count = lax.axis_size("samples")
    dest_shard = my_partners // micro_count
    dest_slot = my_partners % micro_count
    route = (
        (dest_shard[:, None, None] == jnp.arange(shard_count)[None, :, None])
        & (dest_slot[:, None, None] == jnp.arange(micro_count)[None, None, :])
    ).astype(jnp.bfloat16)
    outgoing = jnp.einsum("mku,mad->kuad", route, tiles, preferred_element_type=jnp.float32).astype(
        jnp.bfloat16
    )
    arrived = lax.all_to_all(outgoing, "samples", split_axis=0, concat_axis=0, tiled=True)
    ones_row = jnp.ones((shard_count,), jnp.bfloat16)
    received = jnp.einsum(
        "k,kuad->uad", ones_row, arrived, preferred_element_type=jnp.float32
    ).astype(jnp.bfloat16)
    placed = jnp.einsum("at,mad->mtd", select, received, preferred_element_type=jnp.float32)
    kept = jnp.where(region_mask[None, :, None] > 0, jnp.zeros_like(out_store), out_store)
    site_cot = (kept.astype(jnp.float32) + placed).astype(jnp.bfloat16)
    cotangents = jnp.where(section_index == 0, site_cot, out_store)
    onehot = (spins[:, :, None] == jnp.arange(SPINS)[None, None, :]).astype(jnp.bfloat16)
    embed_term = jnp.einsum("mtv,mtd->vd", onehot, site_cot, preferred_element_type=jnp.float32)
    embed_term = jnp.where(section_index == 0, embed_term, jnp.zeros_like(embed_term))
    embed_grad = lax.psum(embed_term, ("samples", "section"))
    return (summed_weight[None], cotangents[None], embed_grad)


def ring_sample(place, count):
    return jnp.where(place < count // 2, 2 * place, 2 * (count - place) - 1)


def ring_place(sample, count):
    return jnp.where(lax.rem(sample, 2) == 0, sample // 2, count - 1 - sample // 2)


def ring_route(count, distance):
    order = list(range(0, count, 2)) + list(range(1, count, 2))[::-1]
    return [(order[i], order[(i - distance) % count]) for i in range(count)]


def own_place(count):
    return ring_place(lax.axis_index("samples"), count)


def peer_at(place, distance, count):
    return ring_sample(lax.rem(place + distance + count, count), count)


def partner_of(slot):
    return jnp.bitwise_xor(lax.axis_index("samples"), slot)


def sending_order(count):
    near, far, order = list(range(1, count // 2)), list(range(count // 2, count)), []
    while near or far:
        order += near[:1] + far[:2]
        near, far = near[1:], far[2:]
    return [*order, 0]


def columns(index, size):
    return pl.ds(pl.multiple_of(index * size, size), size)


def in_vmem(count):
    return [pl.BlockSpec(memory_space=pltpu.VMEM)] * count


def in_smem(count):
    return [pl.BlockSpec(memory_space=pltpu.SMEM)] * count


def on_core(body, out_shapes, in_specs, scratch=(), micros=1, vmem=16):
    return pl.pallas_call(
        body,
        out_shape=out_shapes,
        in_specs=in_specs,
        out_specs=jax.tree.map(lambda _: pl.BlockSpec(memory_space=pltpu.VMEM), out_shapes),
        scratch_shapes=list(scratch),
        compiler_params=pltpu.CompilerParams(vmem_limit_bytes=vmem << 20),
        cost_estimate=pl.CostEstimate(
            flops=int(micros * FLOPS_PER_MICRO), bytes_accessed=1 << 16, transcendentals=0
        ),
    )


def matmul(left, right):
    return jnp.dot(left, right, preferred_element_type=jnp.float32)


def matmul_t(left, right):
    return lax.dot_general(
        left, right, (((1,), (1,)), ((), ())), preferred_element_type=jnp.float32
    )


def pack_kernel(count, share_axis, x_ref, w_ref, spins_ref, *refs):
    outs, sems = refs[:-1], refs[-1]
    seq_len = x_ref.shape[2]
    skipped = seq_len + TAIL
    sent = outs[0].shape[0] - skipped
    rows = columns(lax.axis_index(share_axis), sent) if share_axis else slice(None)
    copies = []
    for slot in range(count):
        cols = columns(partner_of(slot), HEAD)
        head, weight = outs[slot].at[0:seq_len, :], outs[slot].at[skipped:, :]
        copies.append(pltpu.make_async_copy(x_ref.at[0, 0, :, cols], head, sems.at[0, slot]))
        copies.append(pltpu.make_async_copy(w_ref.at[0, rows, cols], weight, sems.at[1, slot]))
    for copy in copies:
        copy.start()
    spin_rows = jnp.broadcast_to(spins_ref[...].astype(jnp.float32), (TAIL, seq_len))
    for slot in range(count):
        outs[slot][seq_len:skipped, :] = spin_rows.astype(jnp.bfloat16)
    for copy in copies:
        copy.wait()


def collect_kernel(count, *refs):
    heads_ref, rows_ref = refs[count:]
    refs = dict(zip(sending_order(count), refs))
    sent = rows_ref.shape[1]
    for slot in range(count):
        peer = partner_of(slot)
        heads_ref[peer] = refs[slot][...]
        rows_ref[peer] = refs[slot][-sent:, :]


def forward_kernel(count, scale, *refs):
    heads_ref, shared, layout_ref = refs[0], refs[1:-6], refs[-4]
    probs_ref, turned_ref, bundle_ref = refs[-3:]
    seq_len = probs_ref.shape[1]
    lines = seq_len + TAIL
    half = lax.axis_index("mp")
    parts = count // 2
    sent = heads_ref.shape[1] - lines
    for part in range(parts):
        shard = (1 - half) * parts + part
        for piece, value in enumerate((heads_ref[shard, lines:, :], *(ref[shard] for ref in shared))):
            first = count * seq_len + (piece * parts + part) * sent
            bundle_ref[first : first + sent, :] = value
    blocks = layout_ref.shape[1]
    rows = lax.broadcasted_iota(jnp.int32, (seq_len, seq_len), 0) // BLOCK
    cols = lax.broadcasted_iota(jnp.int32, (seq_len, seq_len), 1) // BLOCK
    seen = rows == cols
    for q in range(blocks):
        for k in range(blocks):
            if q != k:
                seen = seen | ((rows == q) & (cols == k) & (layout_ref[0, q, k] > 0))
    xs = [heads_ref[slot, 0:seq_len, :] for slot in range(count)]
    scores = [jnp.where(seen, matmul_t(x, x) * scale, -jnp.inf) for x in xs]
    tops = [jnp.max(score, axis=-1, keepdims=True) for score in scores]
    terms = [jnp.exp(score - top) for score, top in zip(scores, tops)]
    sums = [jnp.sum(term, axis=-1, keepdims=True) for term in terms]
    for slot in range(count):
        probs = terms[slot] / sums[slot]
        low = probs.astype(jnp.bfloat16)
        probs_ref[slot] = probs
        attended = matmul(low, xs[slot]).astype(jnp.bfloat16)
        bundle_ref[slot * seq_len : (slot + 1) * seq_len, :] = attended
        turned_ref[slot] = transposed(low)


def lay_weights(weights, shares, share_axis):
    index = lax.axis_index(share_axis) if share_axis else 0
    pieces = len(shares) // 2
    parts = len(shares[0])
    for number, share in enumerate(shares):
        head, piece = number % 2, number // 2
        place = index if piece == 0 else 1 - index
        for part, value in enumerate(share):
            sent = value.shape[0]
            rows = pl.ds(pl.multiple_of((part * pieces + place) * sent, sent), sent)
            weights[rows, head * HEAD : (head + 1) * HEAD] = value


def weight_term(pieces, left, cols):
    total = None
    for index, first in enumerate(range(0, len(pieces), 2)):
        rows = [piece[:, cols] for slot in pieces[first : first + 2] for piece in slot]
        term = matmul(left[index], jnp.concatenate(rows, axis=0))
        total = term if total is None else total + term
    return total


def both_heads(own_ref, sibling_ref, samples, seq_len):
    rows = [
        jnp.concatenate(
            [ref[columns(sample, seq_len), :] for ref in (own_ref, sibling_ref)], axis=1
        )
        for sample in samples
    ]
    return transposed(jnp.concatenate(rows, axis=0))


def transposed(value):
    return value.astype(jnp.float32).T.astype(jnp.bfloat16)


def attention_back(scale, xs, probs, turned, grads, above):
    grad_probs = [matmul_t(grad, x) for grad, x in zip(grads, xs)]
    inner = [jnp.sum(grad * prob, axis=-1, keepdims=True) for grad, prob in zip(grad_probs, probs)]
    grad_scores = [
        (prob * (grad - total)).astype(jnp.bfloat16)
        for prob, grad, total in zip(probs, grad_probs, inner)
    ]
    both = [jnp.concatenate([grad, transposed(grad)], axis=1) for grad in grad_scores]
    results = []
    for index, x in enumerate(xs):
        through = matmul(turned[index], grads[index])
        through = through + scale * matmul(both[index], jnp.concatenate([x, x], axis=0))
        results.append((above[index].astype(jnp.float32) + through).astype(jnp.bfloat16))
    return results


def near_slots(count):
    return [slot for slot in range(count) if slot != count // 2]


def near_products_kernel(count, share_axis, *refs):
    pieces = [refs[index : index + 1] for index in range(count - 1)]
    bundle_ref, sibling_ref, heads_ref = refs[count - 1 : count + 2]
    shared = refs[count + 2 : -5]
    partial_ref, own_ref, other_ref, above_ref, weights = refs[-5:]
    place = own_place(count)
    shard = lax.axis_index("samples")
    parts, _, shard_rows = partial_ref.shape
    seq_len = pieces[0][0].shape[0]
    lines = seq_len + TAIL
    sent = heads_ref.shape[1] - lines
    half = lax.axis_index("mp")
    sample_of = [peer_at(place, slot, count) for slot in near_slots(count)]
    shares = []
    for piece, ref in enumerate((heads_ref, *shared)):
        skipped = lines if piece == 0 else 0
        shares.append([ref[half * parts + part, skipped:, :] for part in range(parts)])
        firsts = [count * seq_len + (piece * parts + part) * sent for part in range(parts)]
        shares.append([sibling_ref[first : first + sent, :] for first in firsts])
    lay_weights(weights, shares, share_axis)
    left = [
        both_heads(bundle_ref, sibling_ref, sample_of[first : first + 2], seq_len)
        for first in range(0, count - 1, 2)
    ]
    for part in range(parts):
        cols = slice(part * shard_rows, (part + 1) * shard_rows)
        partial_ref[part] = weight_term(pieces, left, cols)
    for first in range(0, count - 1, 2):
        rows = [piece[...] for slot in pieces[first : first + 2] for piece in slot]
        total = matmul(jnp.concatenate(rows, axis=0), weights[...])
        lines = slice(first * seq_len, first * seq_len + total.shape[0])
        own_ref[lines, :] = total[:, :HEAD]
        other_ref[lines, :] = total[:, HEAD:].astype(jnp.bfloat16)
    for index, slot in enumerate(pieces):
        above_ref[index * seq_len : (index + 1) * seq_len, :] = slot[0][:, columns(shard, HEAD)]


def near_back_kernel(count, scale, *refs):
    heads_ref, probs_ref, turned_ref, own_ref, other_ref, above_ref = refs[:6]
    grads_ref = refs[-1]
    place = own_place(count)
    seq_len = probs_ref.shape[1]
    sample_of = [peer_at(place, slot, count) for slot in near_slots(count)]
    lines = [slice(index * seq_len, (index + 1) * seq_len) for index in range(count - 1)]
    results = attention_back(
        scale,
        [heads_ref[sample, 0:seq_len, :] for sample in sample_of],
        [probs_ref[sample] for sample in sample_of],
        [turned_ref[sample] for sample in sample_of],
        [
            (own_ref[line, :] + other_ref[line, :].astype(jnp.float32)).astype(jnp.bfloat16)
            for line in lines
        ],
        [above_ref[line, :] for line in lines],
    )
    for index, result in enumerate(results):
        grads_ref[index] = result


def far_products_kernel(count, *refs):
    piece, refs = refs[:2], refs[2:]
    bundle_ref, sibling_ref, partial_ref, weights_ref = refs[:4]
    send_ref, keep_ref, own_ref, above_ref = refs[4:]
    sample = peer_at(own_place(count), count // 2, count)
    shard = lax.axis_index("samples")
    parts, _, shard_rows = partial_ref.shape
    left = [both_heads(bundle_ref, sibling_ref, [sample], 2 * piece[0].shape[0])]
    for part in range(parts):
        cols = slice(part * shard_rows, (part + 1) * shard_rows)
        total = transposed(partial_ref[part] + weight_term([piece], left, cols))
        keep_ref[part] = total[:, :HEAD]
        send_ref[cols, :] = total[:, HEAD:]
    total = matmul(jnp.concatenate([rows[...] for rows in piece], axis=0), weights_ref[...])
    own_ref[...] = total[:, :HEAD]
    send_ref[parts * shard_rows :, :] = total[:, HEAD:].astype(jnp.bfloat16)
    cols = columns(shard, HEAD)
    above_ref[...] = jnp.concatenate([rows[:, cols] for rows in piece], axis=0)


def far_kernel(count, scale, *refs):
    came_ref, keep_ref, own_ref, above_ref, heads_ref, probs_ref, turned_ref = refs[:7]
    near_ref, mask_ref, partner_ref = refs[7:10]
    outs, (grads, terms) = refs[10:-2], refs[-2:]
    place = own_place(count)
    half = lax.axis_index("mp")
    seq_len = probs_ref.shape[1]
    skipped = seq_len + TAIL
    parts, shard_rows = keep_ref.shape[:2]
    for part in range(parts):
        terms[half * parts + part] = keep_ref[part]
        lines = slice(part * shard_rows, (part + 1) * shard_rows)
        terms[(1 - half) * parts + part] = came_ref[lines, :]
    for index, slot in enumerate(near_slots(count)):
        grads[peer_at(place, slot, count)] = near_ref[index]
    sample = peer_at(place, count // 2, count)
    other = came_ref[parts * shard_rows :, :].astype(jnp.float32)
    (grads[sample],) = attention_back(
        scale,
        [heads_ref[sample, 0:seq_len, :]],
        [probs_ref[sample]],
        [turned_ref[sample]],
        [(own_ref[...] + other).astype(jnp.bfloat16)],
        [above_ref[...]],
    )
    region = jnp.broadcast_to(mask_ref[...].astype(jnp.float32), (HEAD, seq_len)).T > 0.5
    which = lax.broadcasted_iota(jnp.int32, (TAIL, seq_len), 0).astype(jnp.float32)
    embed = jnp.zeros((TAIL, HEAD), jnp.float32)
    for slot in range(count):
        sample = partner_of(slot)
        swapped = grads[partner_ref[sample]].astype(jnp.float32)
        site = jnp.where(region, swapped, grads[sample].astype(jnp.float32)).astype(jnp.bfloat16)
        outs[slot][0:seq_len, :] = site
        outs[slot][skipped:, :] = terms[sample]
        spin = heads_ref[sample, seq_len:skipped, :].astype(jnp.float32)
        embed = embed + matmul((spin == which).astype(jnp.bfloat16), site)
    high = embed.astype(jnp.bfloat16).astype(jnp.float32)
    low = embed - high
    tail = jnp.concatenate([high[: TAIL // 2], low[: TAIL // 2]], axis=0).astype(jnp.bfloat16)
    for slot in range(count):
        outs[slot][seq_len:skipped, :] = tail


def unpack_kernel(count, *refs):
    weight_ref, site_ref, embed_ref = refs[count:]
    refs = dict(zip(sending_order(count), refs))
    seq_len = site_ref.shape[2]
    skipped = seq_len + TAIL
    for slot in range(count):
        cols = columns(partner_of(slot), HEAD)
        weight_ref[0, :, cols] = refs[slot][skipped:, :].astype(jnp.float32)
        site_ref[0, 0, :, cols] = refs[slot][0:seq_len, :]
        tail = refs[slot][seq_len:skipped, :].astype(jnp.float32)
        embed_ref[:, cols] = (tail[: TAIL // 2] + tail[TAIL // 2 :])[:SPINS]


def spread(blocks):
    count = len(blocks)
    came = [blocks[0]]
    for slot in range(1, count):
        route = [(shard, shard ^ slot) for shard in range(count)]
        came.append(lax.ppermute(blocks[slot], "samples", route))
    return came


def head_sharded(
    stored_inputs, top_cotangent, layer_weights, block_layout, region_mask, partner_samples, spins
):
    count = lax.axis_size("samples")
    seq_len = stored_inputs.shape[2]
    shard_rows, half_width = layer_weights.shape[1:]
    scale = 4.0 / HEAD
    bf16, f32 = jnp.bfloat16, jnp.float32
    per_head = (count, seq_len, HEAD)
    lines = seq_len + TAIL
    share_axis = "groups" if lax.axis_size("groups") == 2 else None
    sent = shard_rows // 2 if share_axis else shard_rows
    parts = count // 2
    swap = [(0, 1), (1, 0)]

    up, down = ring_route(count, -1), ring_route(count, 1)
    block = top_cotangent[0]
    rows = seq_len // 2
    packed = on_core(
        functools.partial(pack_kernel, count, share_axis),
        [jax.ShapeDtypeStruct((lines + sent, HEAD), bf16)] * count,
        [pl.BlockSpec(memory_space=pltpu.HBM)] * 2 + in_vmem(1),
        [pltpu.SemaphoreType.DMA((2, count))],
        micros=1,
        vmem=60,
    )(stored_inputs, layer_weights, spins)
    arrived = spread(packed)
    heads, weight_rows = on_core(
        functools.partial(collect_kernel, count),
        [
            jax.ShapeDtypeStruct((count, lines + sent, HEAD), bf16),
            jax.ShapeDtypeStruct((count, sent, HEAD), bf16),
        ],
        in_vmem(count),
        micros=0.4,
    )(*[arrived[slot] for slot in sending_order(count)])
    slots = {0: block}
    ahead, back = block, block
    for step in range(1, count // 2):
        ahead = lax.ppermute(ahead, "samples", up)
        back = lax.ppermute(back, "samples", down)
        slots[count - step], slots[step] = ahead, back
    far = (
        lax.ppermute(ahead[:rows], "samples", up),
        lax.ppermute(back[rows:], "samples", down),
    )
    near = [slots[slot] for slot in near_slots(count)]
    small = (region_mask.reshape(1, seq_len), partner_samples)
    shared = []
    if share_axis:
        shared = [lax.ppermute(weight_rows, share_axis, swap)]
    probs, turned, bundle = on_core(
        functools.partial(forward_kernel, count, scale),
        [
            jax.ShapeDtypeStruct(per_head, f32),
            jax.ShapeDtypeStruct(per_head, bf16),
            jax.ShapeDtypeStruct((count * seq_len + half_width, HEAD), bf16),
        ],
        in_vmem(2 + len(shared)) + in_smem(2),
        micros=1.2,
    )(heads, *shared, *small, block_layout)
    sibling = lax.ppermute(bundle, "mp", swap)
    near_lines = (count - 1) * seq_len
    partial, near_own, near_other, near_above, weights = on_core(
        functools.partial(near_products_kernel, count, share_axis),
        [
            jax.ShapeDtypeStruct((parts, 2 * HEAD, shard_rows), f32),
            jax.ShapeDtypeStruct((near_lines, HEAD), f32),
            jax.ShapeDtypeStruct((near_lines, HEAD), bf16),
            jax.ShapeDtypeStruct((near_lines, HEAD), bf16),
            jax.ShapeDtypeStruct((half_width, 2 * HEAD), bf16),
        ],
        in_vmem(count + 2 + len(shared)),
        micros=1.4,
    )(*near, bundle, sibling, heads, *shared)
    near_other = lax.ppermute(near_other, "mp", swap)
    near_grads = on_core(
        functools.partial(near_back_kernel, count, scale),
        jax.ShapeDtypeStruct((count - 1, seq_len, HEAD), bf16),
        in_vmem(7) + in_smem(1),
        micros=1.8,
    )(heads, probs, turned, near_own, near_other, near_above, *small)
    far_send, far_keep, far_own, far_above = on_core(
        functools.partial(far_products_kernel, count),
        [
            jax.ShapeDtypeStruct((half_width + seq_len, HEAD), bf16),
            jax.ShapeDtypeStruct((parts, shard_rows, HEAD), bf16),
            jax.ShapeDtypeStruct((seq_len, HEAD), f32),
            jax.ShapeDtypeStruct((seq_len, HEAD), bf16),
        ],
        in_vmem(6),
        micros=0.5,
    )(*far, bundle, sibling, partial, weights)
    far_came = lax.ppermute(far_send, "mp", swap)
    terms = on_core(
        functools.partial(far_kernel, count, scale),
        [jax.ShapeDtypeStruct((lines + shard_rows, HEAD), bf16)] * count,
        in_vmem(9) + in_smem(1),
        [pltpu.VMEM(per_head, bf16), pltpu.VMEM((count, shard_rows, HEAD), bf16)],
        micros=1.2,
    )(far_came, far_keep, far_own, far_above, heads, probs, turned, near_grads, *small)
    came = spread(terms)
    return on_core(
        functools.partial(unpack_kernel, count),
        [
            jax.ShapeDtypeStruct((1, shard_rows, half_width), f32),
            jax.ShapeDtypeStruct((1, 1, seq_len, half_width), bf16),
            jax.ShapeDtypeStruct((SPINS, half_width), f32),
        ],
        in_vmem(count),
        micros=1.2,
    )(*[came[slot] for slot in sending_order(count)])


def solution(mesh):
    in_specs = (
        P("section", ("groups", "samples"), None, "mp"),
        P(("groups", "samples"), None, "mp"),
        P("section", "samples", "mp"),
        P("section", None, None),
        P(),
        P("groups"),
        P(("groups", "samples"), None),
    )
    out_specs = (
        P(("groups", "section"), "samples", "mp"),
        P("section", ("groups", "samples"), None, "mp"),
        P("groups", "mp"),
    )
    shards = mesh.shape["samples"]

    def whole(stored_inputs, top_cotangent, *rest):
        samples, _, width = top_cotangent.shape
        layer_count = stored_inputs.shape[0]
        one_each = samples == mesh.shape["groups"] * shards and layer_count == 1
        by_heads = one_each and shards > 1 and shards & (shards - 1) == 0 and width == mesh.shape["mp"] * shards * HEAD
        return jax.shard_map(
            head_sharded if by_heads else local,
            mesh=mesh,
            in_specs=in_specs,
            out_specs=out_specs,
            check_vma=False,
        )(stored_inputs, top_cotangent, *rest)

    return whole
```

```python
import functools

import jax
import jax.numpy as jnp
from jax import lax
from jax.experimental import pallas as pl
from jax.experimental.pallas import tpu as pltpu
from jax.sharding import PartitionSpec as P

HEAD = 128
BLOCK = 64
SPINS = 2
TAIL = 16
FLOPS_PER_MICRO = 1.15e9


def for_sending(value):

    def short(part):
        return part.astype(jnp.bfloat16) if part.dtype == jnp.float32 else part

    return jax.tree.map(short, value)


def passed_along(block, axis, distance):
    devices = range(lax.axis_size(axis))
    route = [(i - distance, i) for i in devices if i - distance in devices]
    return lax.ppermute(block, axis, route)


def softmax_parts(inputs_h, allowed, attention_scale):
    scores = (
        jnp.einsum("qhd,khd->hqk", inputs_h, inputs_h, preferred_element_type=jnp.float32)
        * attention_scale
    )
    scores = jnp.where(allowed[None], scores, -jnp.inf)
    top_score = jnp.max(scores, axis=-1, keepdims=True)
    expo_terms = jnp.exp(scores - top_score)
    probs = expo_terms / jnp.sum(expo_terms, axis=-1, keepdims=True)
    return (probs, probs.astype(jnp.bfloat16))


def local(
    stored_inputs, top_cotangent, layer_weights, block_layout, region_mask, partner_samples, spins
):
    section_index = lax.axis_index("section")
    section_count = lax.axis_size("section")
    micro_count = stored_inputs.shape[1]
    seq_len = stored_inputs.shape[2]
    half_width = stored_inputs.shape[3]
    head_count = half_width // HEAD
    attention_scale = 4.0 / HEAD
    weights = lax.all_gather(layer_weights[0], "samples", axis=0, tiled=True)
    pos_block = jnp.arange(seq_len) // BLOCK
    block_onehot = (pos_block[:, None] == jnp.arange(block_layout.shape[1])[None, :]).astype(
        jnp.float32
    )
    linked = jnp.dot(jnp.dot(block_onehot, block_layout[0].astype(jnp.float32)), block_onehot.T)
    allowed = (linked > 0.5) | (pos_block[:, None] == pos_block[None, :])
    every_layer_input = stored_inputs[0]
    inputs_h = every_layer_input[0].reshape(seq_len, head_count, HEAD)
    probs, probs_low = softmax_parts(inputs_h, allowed, attention_scale)
    attended = jnp.einsum(
        "hqk,khd->qhd", probs_low, inputs_h, preferred_element_type=jnp.float32
    ).astype(jnp.bfloat16)
    probs_list = [probs]
    low_list = [probs_low]
    attend_list = [attended.reshape(seq_len, half_width)]
    probs_all = jnp.stack(probs_list)
    low_all = jnp.stack(low_list)
    attend_store = jnp.stack(attend_list)

    def layer_back(grad_full, grad_own, inputs, probs, probs_low):
        grad_attn = jnp.dot(grad_full, weights, preferred_element_type=jnp.float32).astype(
            jnp.bfloat16
        )
        inputs_h = inputs.reshape(seq_len, head_count, HEAD)
        grad_h = grad_attn.reshape(seq_len, head_count, HEAD)
        grad_probs = jnp.einsum(
            "qhd,khd->hqk", grad_h, inputs_h, preferred_element_type=jnp.float32
        )
        grad_scores = (
            probs * (grad_probs - jnp.sum(grad_probs * probs, axis=-1, keepdims=True))
        ).astype(jnp.bfloat16)
        through = jnp.einsum("hqk,qhd->khd", probs_low, grad_h, preferred_element_type=jnp.float32)
        through = through + attention_scale * (
            jnp.einsum("hqk,khd->qhd", grad_scores, inputs_h, preferred_element_type=jnp.float32)
            + jnp.einsum("hqk,qhd->khd", grad_scores, inputs_h, preferred_element_type=jnp.float32)
        )
        grad_in = grad_own.astype(jnp.float32) + through.reshape(seq_len, half_width)
        return grad_in.astype(jnp.bfloat16)

    def resting(grad_full, grad_own, inputs, probs, probs_low):
        return jnp.zeros((seq_len, half_width), jnp.bfloat16)

    carried_state = jnp.zeros((seq_len, half_width), jnp.bfloat16)
    out_list = []
    grad_list = []
    total_steps = micro_count + section_count - 1
    for step_number in range(total_steps):
        micro_index = step_number - (section_count - 1 - section_index)
        active = (micro_index >= 0) & (micro_index < micro_count)
        slot_index = jnp.clip(micro_index, 0, micro_count - 1)
        from_top = lax.dynamic_index_in_dim(top_cotangent, slot_index, 0, keepdims=False)
        incoming = jnp.where(section_index == section_count - 1, from_top, carried_state)
        grad_full = lax.all_gather(incoming, "mp", axis=1, tiled=True)
        inputs_now = lax.dynamic_index_in_dim(every_layer_input, slot_index, 0, keepdims=False)
        probs_now = lax.dynamic_index_in_dim(probs_all, slot_index, 0, keepdims=False)
        low_now = lax.dynamic_index_in_dim(low_all, slot_index, 0, keepdims=False)
        grad_in = lax.cond(
            active, layer_back, resting, grad_full, incoming, inputs_now, probs_now, low_now
        )
        out_list.append(grad_in)
        grad_list.append(grad_full)
        if step_number < total_steps - 1:
            carried_state = jax.tree.map(
                lambda part, own: part.astype(own.dtype),
                passed_along(for_sending(grad_in), "section", -1),
                grad_in,
            )
    offset = section_count - 1 - section_index
    out_store = lax.dynamic_slice_in_dim(jnp.stack(out_list), offset, micro_count, 0)
    grad_store = lax.dynamic_slice_in_dim(jnp.stack(grad_list), offset, micro_count, 0)
    summed_weight = lax.psum_scatter(
        jnp.einsum(
            "mtf,mta->fa", grad_store, attend_store, preferred_element_type=jnp.float32
        ).astype(jnp.bfloat16),
        "samples",
        scatter_dimension=0,
        tiled=True,
    ).astype(jnp.float32)
    region_count = seq_len // 2
    rank_in_region = jnp.cumsum(region_mask) - 1
    select = (
        (rank_in_region[None, :] == jnp.arange(region_count)[:, None]) & (region_mask[None, :] > 0)
    ).astype(jnp.bfloat16)
    tiles = jnp.einsum("at,mtd->mad", select, out_store, preferred_element_type=jnp.float32).astype(
        jnp.bfloat16
    )
    shard_index = lax.axis_index("samples")
    my_partners = lax.dynamic_slice_in_dim(
        partner_samples, shard_index * micro_count, micro_count, 0
    )
    shard_count = lax.axis_size("samples")
    dest_shard = my_partners // micro_count
    dest_slot = my_partners % micro_count
    route = (
        (dest_shard[:, None, None] == jnp.arange(shard_count)[None, :, None])
        & (dest_slot[:, None, None] == jnp.arange(micro_count)[None, None, :])
    ).astype(jnp.bfloat16)
    outgoing = jnp.einsum("mku,mad->kuad", route, tiles, preferred_element_type=jnp.float32).astype(
        jnp.bfloat16
    )
    arrived = lax.all_to_all(outgoing, "samples", split_axis=0, concat_axis=0, tiled=True)
    ones_row = jnp.ones((shard_count,), jnp.bfloat16)
    received = jnp.einsum(
        "k,kuad->uad", ones_row, arrived, preferred_element_type=jnp.float32
    ).astype(jnp.bfloat16)
    placed = jnp.einsum("at,mad->mtd", select, received, preferred_element_type=jnp.float32)
    kept = jnp.where(region_mask[None, :, None] > 0, jnp.zeros_like(out_store), out_store)
    site_cot = (kept.astype(jnp.float32) + placed).astype(jnp.bfloat16)
    cotangents = jnp.where(section_index == 0, site_cot, out_store)
    onehot = (spins[:, :, None] == jnp.arange(SPINS)[None, None, :]).astype(jnp.bfloat16)
    embed_term = jnp.einsum("mtv,mtd->vd", onehot, site_cot, preferred_element_type=jnp.float32)
    embed_term = jnp.where(section_index == 0, embed_term, jnp.zeros_like(embed_term))
    embed_grad = lax.psum(embed_term, ("samples", "section"))
    return (summed_weight[None], cotangents[None], embed_grad)


def ring_sample(place, count):
    return jnp.where(place < count // 2, 2 * place, 2 * (count - place) - 1)


def ring_place(sample, count):
    return jnp.where(lax.rem(sample, 2) == 0, sample // 2, count - 1 - sample // 2)


def ring_route(count, distance):
    order = list(range(0, count, 2)) + list(range(1, count, 2))[::-1]
    return [(order[i], order[(i - distance) % count]) for i in range(count)]


def own_place(count):
    return ring_place(lax.axis_index("samples"), count)


def peer_at(place, distance, count):
    return ring_sample(lax.rem(place + distance + count, count), count)


def partner_of(slot):
    return jnp.bitwise_xor(lax.axis_index("samples"), slot)


def sending_order(count, run=2):
    near, far, order = list(range(1, count // 2)), list(range(count // 2, count)), []
    while near or far:
        order += near[:1] + far[:run]
        near, far = near[1:], far[run:]
    return [*order, 0]


def columns(index, size):
    return pl.ds(pl.multiple_of(index * size, size), size)


def in_vmem(count):
    return [pl.BlockSpec(memory_space=pltpu.VMEM)] * count


def in_smem(count):
    return [pl.BlockSpec(memory_space=pltpu.SMEM)] * count


def on_core(body, out_shapes, in_specs, scratch=(), micros=1, vmem=16):
    return pl.pallas_call(
        body,
        out_shape=out_shapes,
        in_specs=in_specs,
        out_specs=jax.tree.map(lambda _: pl.BlockSpec(memory_space=pltpu.VMEM), out_shapes),
        scratch_shapes=list(scratch),
        compiler_params=pltpu.CompilerParams(vmem_limit_bytes=vmem << 20),
        cost_estimate=pl.CostEstimate(
            flops=int(micros * FLOPS_PER_MICRO), bytes_accessed=1 << 16, transcendentals=0
        ),
    )


def matmul(left, right):
    return jnp.dot(left, right, preferred_element_type=jnp.float32)


def matmul_t(left, right):
    return lax.dot_general(
        left, right, (((1,), (1,)), ((), ())), preferred_element_type=jnp.float32
    )


def pack_kernel(count, share_axis, x_ref, w_ref, spins_ref, *refs):
    outs, sems = refs[:-1], refs[-1]
    seq_len = x_ref.shape[2]
    skipped = seq_len + TAIL
    sent = outs[0].shape[0] - skipped
    rows = columns(lax.axis_index(share_axis), sent) if share_axis else slice(None)
    copies = []
    for slot in range(count):
        cols = columns(partner_of(slot), HEAD)
        head, weight = outs[slot].at[0:seq_len, :], outs[slot].at[skipped:, :]
        copies.append(pltpu.make_async_copy(x_ref.at[0, 0, :, cols], head, sems.at[0, slot]))
        copies.append(pltpu.make_async_copy(w_ref.at[0, rows, cols], weight, sems.at[1, slot]))
    for copy in copies:
        copy.start()
    spin_rows = jnp.broadcast_to(spins_ref[...].astype(jnp.float32), (TAIL, seq_len))
    for slot in range(count):
        outs[slot][seq_len:skipped, :] = spin_rows.astype(jnp.bfloat16)
    for copy in copies:
        copy.wait()


def collect_kernel(count, *refs):
    heads_ref, rows_ref = refs[count:]
    refs = dict(zip(sending_order(count), refs))
    sent = rows_ref.shape[1]
    for slot in range(count):
        peer = partner_of(slot)
        heads_ref[peer] = refs[slot][...]
        rows_ref[peer] = refs[slot][-sent:, :]


def forward_kernel(count, scale, *refs):
    heads_ref, shared, layout_ref = refs[0], refs[1:-6], refs[-4]
    probs_ref, turned_ref, bundle_ref = refs[-3:]
    seq_len = probs_ref.shape[1]
    lines = seq_len + TAIL
    half = lax.axis_index("mp")
    parts = count // 2
    sent = heads_ref.shape[1] - lines
    for part in range(parts):
        shard = (1 - half) * parts + part
        for piece, value in enumerate((heads_ref[shard, lines:, :], *(ref[shard] for ref in shared))):
            first = count * seq_len + (piece * parts + part) * sent
            bundle_ref[first : first + sent, :] = value
    blocks = layout_ref.shape[1]
    rows = lax.broadcasted_iota(jnp.int32, (seq_len, seq_len), 0) // BLOCK
    cols = lax.broadcasted_iota(jnp.int32, (seq_len, seq_len), 1) // BLOCK
    seen = rows == cols
    for q in range(blocks):
        for k in range(blocks):
            if q != k:
                seen = seen | ((rows == q) & (cols == k) & (layout_ref[0, q, k] > 0))
    xs = [heads_ref[slot, 0:seq_len, :] for slot in range(count)]
    scores = [jnp.where(seen, matmul_t(x, x) * scale, -jnp.inf) for x in xs]
    tops = [jnp.max(score, axis=-1, keepdims=True) for score in scores]
    terms = [jnp.exp(score - top) for score, top in zip(scores, tops)]
    sums = [jnp.sum(term, axis=-1, keepdims=True) for term in terms]
    for slot in range(count):
        probs = terms[slot] / sums[slot]
        low = probs.astype(jnp.bfloat16)
        probs_ref[slot] = probs
        attended = matmul(low, xs[slot]).astype(jnp.bfloat16)
        bundle_ref[slot * seq_len : (slot + 1) * seq_len, :] = attended
        turned_ref[slot] = transposed(low)


def lay_weights(weights, shares, share_axis):
    index = lax.axis_index(share_axis) if share_axis else 0
    pieces = len(shares) // 2
    parts = len(shares[0])
    for number, share in enumerate(shares):
        head, piece = number % 2, number // 2
        place = index if piece == 0 else 1 - index
        for part, value in enumerate(share):
            sent = value.shape[0]
            rows = pl.ds(pl.multiple_of((part * pieces + place) * sent, sent), sent)
            weights[rows, head * HEAD : (head + 1) * HEAD] = value


def weight_term(pieces, left, cols):
    total = None
    for index, first in enumerate(range(0, len(pieces), 2)):
        rows = [piece[:, cols] for slot in pieces[first : first + 2] for piece in slot]
        term = matmul(left[index], jnp.concatenate(rows, axis=0))
        total = term if total is None else total + term
    return total


def both_heads(own_ref, sibling_ref, samples, seq_len):
    rows = [
        jnp.concatenate(
            [ref[columns(sample, seq_len), :] for ref in (own_ref, sibling_ref)], axis=1
        )
        for sample in samples
    ]
    return transposed(jnp.concatenate(rows, axis=0))


def transposed(value):
    return value.astype(jnp.float32).T.astype(jnp.bfloat16)


def attention_back(scale, xs, probs, turned, grads, above):
    grad_probs = [matmul_t(grad, x) for grad, x in zip(grads, xs)]
    inner = [jnp.sum(grad * prob, axis=-1, keepdims=True) for grad, prob in zip(grad_probs, probs)]
    grad_scores = [
        (prob * (grad - total)).astype(jnp.bfloat16)
        for prob, grad, total in zip(probs, grad_probs, inner)
    ]
    both = [jnp.concatenate([grad, transposed(grad)], axis=1) for grad in grad_scores]
    results = []
    for index, x in enumerate(xs):
        through = matmul(turned[index], grads[index])
        through = through + scale * matmul(both[index], jnp.concatenate([x, x], axis=0))
        results.append((above[index].astype(jnp.float32) + through).astype(jnp.bfloat16))
    return results


def near_slots(count):
    return [slot for slot in range(count) if slot != count // 2]


def near_products_kernel(count, share_axis, *refs):
    pieces = [refs[index : index + 1] for index in range(count - 1)]
    bundle_ref, sibling_ref, heads_ref = refs[count - 1 : count + 2]
    shared = refs[count + 2 : -5]
    partial_ref, own_ref, other_ref, above_ref, weights = refs[-5:]
    place = own_place(count)
    shard = lax.axis_index("samples")
    parts, _, shard_rows = partial_ref.shape
    seq_len = pieces[0][0].shape[0]
    lines = seq_len + TAIL
    sent = heads_ref.shape[1] - lines
    half = lax.axis_index("mp")
    sample_of = [peer_at(place, slot, count) for slot in near_slots(count)]
    shares = []
    for piece, ref in enumerate((heads_ref, *shared)):
        skipped = lines if piece == 0 else 0
        shares.append([ref[half * parts + part, skipped:, :] for part in range(parts)])
        firsts = [count * seq_len + (piece * parts + part) * sent for part in range(parts)]
        shares.append([sibling_ref[first : first + sent, :] for first in firsts])
    lay_weights(weights, shares, share_axis)
    left = [
        both_heads(bundle_ref, sibling_ref, sample_of[first : first + 2], seq_len)
        for first in range(0, count - 1, 2)
    ]
    for part in range(parts):
        cols = slice(part * shard_rows, (part + 1) * shard_rows)
        partial_ref[part] = weight_term(pieces, left, cols)
    for first in range(0, count - 1, 2):
        rows = [piece[...] for slot in pieces[first : first + 2] for piece in slot]
        total = matmul(jnp.concatenate(rows, axis=0), weights[...])
        lines = slice(first * seq_len, first * seq_len + total.shape[0])
        own_ref[lines, :] = total[:, :HEAD]
        other_ref[lines, :] = total[:, HEAD:].astype(jnp.bfloat16)
    for index, slot in enumerate(pieces):
        above_ref[index * seq_len : (index + 1) * seq_len, :] = slot[0][:, columns(shard, HEAD)]


def near_back_kernel(count, scale, *refs):
    heads_ref, probs_ref, turned_ref, own_ref, other_ref, above_ref = refs[:6]
    grads_ref = refs[-1]
    place = own_place(count)
    seq_len = probs_ref.shape[1]
    sample_of = [peer_at(place, slot, count) for slot in near_slots(count)]
    lines = [slice(index * seq_len, (index + 1) * seq_len) for index in range(count - 1)]
    results = attention_back(
        scale,
        [heads_ref[sample, 0:seq_len, :] for sample in sample_of],
        [probs_ref[sample] for sample in sample_of],
        [turned_ref[sample] for sample in sample_of],
        [
            (own_ref[line, :] + other_ref[line, :].astype(jnp.float32)).astype(jnp.bfloat16)
            for line in lines
        ],
        [above_ref[line, :] for line in lines],
    )
    for index, result in enumerate(results):
        grads_ref[index] = result


def far_products_kernel(count, *refs):
    piece, refs = refs[:2], refs[2:]
    bundle_ref, sibling_ref, partial_ref, weights_ref = refs[:4]
    send_ref, keep_ref, own_ref, above_ref = refs[4:]
    sample = peer_at(own_place(count), count // 2, count)
    shard = lax.axis_index("samples")
    parts, _, shard_rows = partial_ref.shape
    left = [both_heads(bundle_ref, sibling_ref, [sample], 2 * piece[0].shape[0])]
    for part in range(parts):
        cols = slice(part * shard_rows, (part + 1) * shard_rows)
        total = transposed(partial_ref[part] + weight_term([piece], left, cols))
        keep_ref[part] = total[:, :HEAD]
        send_ref[cols, :] = total[:, HEAD:]
    total = matmul(jnp.concatenate([rows[...] for rows in piece], axis=0), weights_ref[...])
    own_ref[...] = total[:, :HEAD]
    send_ref[parts * shard_rows :, :] = total[:, HEAD:].astype(jnp.bfloat16)
    cols = columns(shard, HEAD)
    above_ref[...] = jnp.concatenate([rows[:, cols] for rows in piece], axis=0)


def far_kernel(count, scale, *refs):
    came_ref, keep_ref, own_ref, above_ref, heads_ref, probs_ref, turned_ref = refs[:7]
    near_ref, mask_ref, partner_ref = refs[7:10]
    outs, (grads, terms) = refs[10:-2], refs[-2:]
    place = own_place(count)
    half = lax.axis_index("mp")
    seq_len = probs_ref.shape[1]
    skipped = seq_len + TAIL
    parts, shard_rows = keep_ref.shape[:2]
    for part in range(parts):
        terms[half * parts + part] = keep_ref[part]
        lines = slice(part * shard_rows, (part + 1) * shard_rows)
        terms[(1 - half) * parts + part] = came_ref[lines, :]
    for index, slot in enumerate(near_slots(count)):
        grads[peer_at(place, slot, count)] = near_ref[index]
    sample = peer_at(place, count // 2, count)
    other = came_ref[parts * shard_rows :, :].astype(jnp.float32)
    (grads[sample],) = attention_back(
        scale,
        [heads_ref[sample, 0:seq_len, :]],
        [probs_ref[sample]],
        [turned_ref[sample]],
        [(own_ref[...] + other).astype(jnp.bfloat16)],
        [above_ref[...]],
    )
    region = jnp.broadcast_to(mask_ref[...].astype(jnp.float32), (HEAD, seq_len)).T > 0.5
    which = lax.broadcasted_iota(jnp.int32, (TAIL, seq_len), 0).astype(jnp.float32)
    embed = jnp.zeros((TAIL, HEAD), jnp.float32)
    for slot in range(count):
        sample = partner_of(slot)
        swapped = grads[partner_ref[sample]].astype(jnp.float32)
        site = jnp.where(region, swapped, grads[sample].astype(jnp.float32)).astype(jnp.bfloat16)
        outs[slot][0:seq_len, :] = site
        outs[slot][skipped:, :] = terms[sample]
        spin = heads_ref[sample, seq_len:skipped, :].astype(jnp.float32)
        embed = embed + matmul((spin == which).astype(jnp.bfloat16), site)
    high = embed.astype(jnp.bfloat16).astype(jnp.float32)
    low = embed - high
    tail = jnp.concatenate([high[: TAIL // 2], low[: TAIL // 2]], axis=0).astype(jnp.bfloat16)
    for slot in range(count):
        outs[slot][seq_len:skipped, :] = tail


def unpack_kernel(count, *refs):
    weight_ref, site_ref, embed_ref = refs[count:]
    refs = dict(zip(sending_order(count, 1), refs))
    seq_len = site_ref.shape[2]
    skipped = seq_len + TAIL
    for slot in range(count):
        cols = columns(partner_of(slot), HEAD)
        weight_ref[0, :, cols] = refs[slot][skipped:, :].astype(jnp.float32)
        site_ref[0, 0, :, cols] = refs[slot][0:seq_len, :]
        tail = refs[slot][seq_len:skipped, :].astype(jnp.float32)
        embed_ref[:, cols] = (tail[: TAIL // 2] + tail[TAIL // 2 :])[:SPINS]


def spread(blocks):
    count = len(blocks)
    came = [blocks[0]]
    for slot in range(1, count):
        route = [(shard, shard ^ slot) for shard in range(count)]
        came.append(lax.ppermute(blocks[slot], "samples", route))
    return came


def head_sharded(
    stored_inputs, top_cotangent, layer_weights, block_layout, region_mask, partner_samples, spins
):
    count = lax.axis_size("samples")
    seq_len = stored_inputs.shape[2]
    shard_rows, half_width = layer_weights.shape[1:]
    scale = 4.0 / HEAD
    bf16, f32 = jnp.bfloat16, jnp.float32
    per_head = (count, seq_len, HEAD)
    lines = seq_len + TAIL
    share_axis = "groups" if lax.axis_size("groups") == 2 else None
    sent = shard_rows // 2 if share_axis else shard_rows
    parts = count // 2
    swap = [(0, 1), (1, 0)]

    up, down = ring_route(count, -1), ring_route(count, 1)
    block = top_cotangent[0]
    rows = seq_len // 2
    packed = on_core(
        functools.partial(pack_kernel, count, share_axis),
        [jax.ShapeDtypeStruct((lines + sent, HEAD), bf16)] * count,
        [pl.BlockSpec(memory_space=pltpu.HBM)] * 2 + in_vmem(1),
        [pltpu.SemaphoreType.DMA((2, count))],
        micros=1,
        vmem=60,
    )(stored_inputs, layer_weights, spins)
    arrived = spread(packed)
    heads, weight_rows = on_core(
        functools.partial(collect_kernel, count),
        [
            jax.ShapeDtypeStruct((count, lines + sent, HEAD), bf16),
            jax.ShapeDtypeStruct((count, sent, HEAD), bf16),
        ],
        in_vmem(count),
        micros=0.4,
    )(*[arrived[slot] for slot in sending_order(count)])
    slots = {0: block}
    ahead, back = block, block
    for step in range(1, count // 2):
        ahead = lax.ppermute(ahead, "samples", up)
        back = lax.ppermute(back, "samples", down)
        slots[count - step], slots[step] = ahead, back
    far = (
        lax.ppermute(ahead[:rows], "samples", up),
        lax.ppermute(back[rows:], "samples", down),
    )
    near = [slots[slot] for slot in near_slots(count)]
    small = (region_mask.reshape(1, seq_len), partner_samples)
    shared = []
    if share_axis:
        shared = [lax.ppermute(weight_rows, share_axis, swap)]
    probs, turned, bundle = on_core(
        functools.partial(forward_kernel, count, scale),
        [
            jax.ShapeDtypeStruct(per_head, f32),
            jax.ShapeDtypeStruct(per_head, bf16),
            jax.ShapeDtypeStruct((count * seq_len + half_width, HEAD), bf16),
        ],
        in_vmem(2 + len(shared)) + in_smem(2),
        micros=1.2,
    )(heads, *shared, *small, block_layout)
    sibling = lax.ppermute(bundle, "mp", swap)
    near_lines = (count - 1) * seq_len
    partial, near_own, near_other, near_above, weights = on_core(
        functools.partial(near_products_kernel, count, share_axis),
        [
            jax.ShapeDtypeStruct((parts, 2 * HEAD, shard_rows), f32),
            jax.ShapeDtypeStruct((near_lines, HEAD), f32),
            jax.ShapeDtypeStruct((near_lines, HEAD), bf16),
            jax.ShapeDtypeStruct((near_lines, HEAD), bf16),
            jax.ShapeDtypeStruct((half_width, 2 * HEAD), bf16),
        ],
        in_vmem(count + 2 + len(shared)),
        micros=1.4,
    )(*near, bundle, sibling, heads, *shared)
    near_other = lax.ppermute(near_other, "mp", swap)
    near_grads = on_core(
        functools.partial(near_back_kernel, count, scale),
        jax.ShapeDtypeStruct((count - 1, seq_len, HEAD), bf16),
        in_vmem(7) + in_smem(1),
        micros=1.8,
    )(heads, probs, turned, near_own, near_other, near_above, *small)
    far_send, far_keep, far_own, far_above = on_core(
        functools.partial(far_products_kernel, count),
        [
            jax.ShapeDtypeStruct((half_width + seq_len, HEAD), bf16),
            jax.ShapeDtypeStruct((parts, shard_rows, HEAD), bf16),
            jax.ShapeDtypeStruct((seq_len, HEAD), f32),
            jax.ShapeDtypeStruct((seq_len, HEAD), bf16),
        ],
        in_vmem(6),
        micros=0.5,
    )(*far, bundle, sibling, partial, weights)
    far_came = lax.ppermute(far_send, "mp", swap)
    terms = on_core(
        functools.partial(far_kernel, count, scale),
        [jax.ShapeDtypeStruct((lines + shard_rows, HEAD), bf16)] * count,
        in_vmem(9) + in_smem(1),
        [pltpu.VMEM(per_head, bf16), pltpu.VMEM((count, shard_rows, HEAD), bf16)],
        micros=1.2,
    )(far_came, far_keep, far_own, far_above, heads, probs, turned, near_grads, *small)
    came = spread(terms)
    return on_core(
        functools.partial(unpack_kernel, count),
        [
            jax.ShapeDtypeStruct((1, shard_rows, half_width), f32),
            jax.ShapeDtypeStruct((1, 1, seq_len, half_width), bf16),
            jax.ShapeDtypeStruct((SPINS, half_width), f32),
        ],
        in_vmem(count),
        micros=1.2,
    )(*[came[slot] for slot in sending_order(count, 1)])


def solution(mesh):
    in_specs = (
        P("section", ("groups", "samples"), None, "mp"),
        P(("groups", "samples"), None, "mp"),
        P("section", "samples", "mp"),
        P("section", None, None),
        P(),
        P("groups"),
        P(("groups", "samples"), None),
    )
    out_specs = (
        P(("groups", "section"), "samples", "mp"),
        P("section", ("groups", "samples"), None, "mp"),
        P("groups", "mp"),
    )
    shards = mesh.shape["samples"]

    def whole(stored_inputs, top_cotangent, *rest):
        samples, _, width = top_cotangent.shape
        layer_count = stored_inputs.shape[0]
        one_each = samples == mesh.shape["groups"] * shards and layer_count == 1
        by_heads = one_each and shards > 1 and shards & (shards - 1) == 0 and width == mesh.shape["mp"] * shards * HEAD
        return jax.shard_map(
            head_sharded if by_heads else local,
            mesh=mesh,
            in_specs=in_specs,
            out_specs=out_specs,
            check_vma=False,
        )(stored_inputs, top_cotangent, *rest)

    return whole
```

```python
import functools

import jax
import jax.numpy as jnp
from jax import lax
from jax.experimental import pallas as pl
from jax.experimental.pallas import tpu as pltpu
from jax.sharding import PartitionSpec as P

HEAD = 128
BLOCK = 64
SPINS = 2
TAIL = 16
FLOPS_PER_MICRO = 1.15e9


def for_sending(value):

    def short(part):
        return part.astype(jnp.bfloat16) if part.dtype == jnp.float32 else part

    return jax.tree.map(short, value)


def passed_along(block, axis, distance):
    devices = range(lax.axis_size(axis))
    route = [(i - distance, i) for i in devices if i - distance in devices]
    return lax.ppermute(block, axis, route)


def softmax_parts(inputs_h, allowed, attention_scale):
    scores = (
        jnp.einsum("qhd,khd->hqk", inputs_h, inputs_h, preferred_element_type=jnp.float32)
        * attention_scale
    )
    scores = jnp.where(allowed[None], scores, -jnp.inf)
    top_score = jnp.max(scores, axis=-1, keepdims=True)
    expo_terms = jnp.exp(scores - top_score)
    probs = expo_terms / jnp.sum(expo_terms, axis=-1, keepdims=True)
    return (probs, probs.astype(jnp.bfloat16))


def local(
    stored_inputs, top_cotangent, layer_weights, block_layout, region_mask, partner_samples, spins
):
    section_index = lax.axis_index("section")
    section_count = lax.axis_size("section")
    micro_count = stored_inputs.shape[1]
    seq_len = stored_inputs.shape[2]
    half_width = stored_inputs.shape[3]
    head_count = half_width // HEAD
    attention_scale = 4.0 / HEAD
    weights = lax.all_gather(layer_weights[0], "samples", axis=0, tiled=True)
    pos_block = jnp.arange(seq_len) // BLOCK
    block_onehot = (pos_block[:, None] == jnp.arange(block_layout.shape[1])[None, :]).astype(
        jnp.float32
    )
    linked = jnp.dot(jnp.dot(block_onehot, block_layout[0].astype(jnp.float32)), block_onehot.T)
    allowed = (linked > 0.5) | (pos_block[:, None] == pos_block[None, :])
    every_layer_input = stored_inputs[0]
    inputs_h = every_layer_input[0].reshape(seq_len, head_count, HEAD)
    probs, probs_low = softmax_parts(inputs_h, allowed, attention_scale)
    attended = jnp.einsum(
        "hqk,khd->qhd", probs_low, inputs_h, preferred_element_type=jnp.float32
    ).astype(jnp.bfloat16)
    probs_list = [probs]
    low_list = [probs_low]
    attend_list = [attended.reshape(seq_len, half_width)]
    probs_all = jnp.stack(probs_list)
    low_all = jnp.stack(low_list)
    attend_store = jnp.stack(attend_list)

    def layer_back(grad_full, grad_own, inputs, probs, probs_low):
        grad_attn = jnp.dot(grad_full, weights, preferred_element_type=jnp.float32).astype(
            jnp.bfloat16
        )
        inputs_h = inputs.reshape(seq_len, head_count, HEAD)
        grad_h = grad_attn.reshape(seq_len, head_count, HEAD)
        grad_probs = jnp.einsum(
            "qhd,khd->hqk", grad_h, inputs_h, preferred_element_type=jnp.float32
        )
        grad_scores = (
            probs * (grad_probs - jnp.sum(grad_probs * probs, axis=-1, keepdims=True))
        ).astype(jnp.bfloat16)
        through = jnp.einsum("hqk,qhd->khd", probs_low, grad_h, preferred_element_type=jnp.float32)
        through = through + attention_scale * (
            jnp.einsum("hqk,khd->qhd", grad_scores, inputs_h, preferred_element_type=jnp.float32)
            + jnp.einsum("hqk,qhd->khd", grad_scores, inputs_h, preferred_element_type=jnp.float32)
        )
        grad_in = grad_own.astype(jnp.float32) + through.reshape(seq_len, half_width)
        return grad_in.astype(jnp.bfloat16)

    def resting(grad_full, grad_own, inputs, probs, probs_low):
        return jnp.zeros((seq_len, half_width), jnp.bfloat16)

    carried_state = jnp.zeros((seq_len, half_width), jnp.bfloat16)
    out_list = []
    grad_list = []
    total_steps = micro_count + section_count - 1
    for step_number in range(total_steps):
        micro_index = step_number - (section_count - 1 - section_index)
        active = (micro_index >= 0) & (micro_index < micro_count)
        slot_index = jnp.clip(micro_index, 0, micro_count - 1)
        from_top = lax.dynamic_index_in_dim(top_cotangent, slot_index, 0, keepdims=False)
        incoming = jnp.where(section_index == section_count - 1, from_top, carried_state)
        grad_full = lax.all_gather(incoming, "mp", axis=1, tiled=True)
        inputs_now = lax.dynamic_index_in_dim(every_layer_input, slot_index, 0, keepdims=False)
        probs_now = lax.dynamic_index_in_dim(probs_all, slot_index, 0, keepdims=False)
        low_now = lax.dynamic_index_in_dim(low_all, slot_index, 0, keepdims=False)
        grad_in = lax.cond(
            active, layer_back, resting, grad_full, incoming, inputs_now, probs_now, low_now
        )
        out_list.append(grad_in)
        grad_list.append(grad_full)
        if step_number < total_steps - 1:
            carried_state = jax.tree.map(
                lambda part, own: part.astype(own.dtype),
                passed_along(for_sending(grad_in), "section", -1),
                grad_in,
            )
    offset = section_count - 1 - section_index
    out_store = lax.dynamic_slice_in_dim(jnp.stack(out_list), offset, micro_count, 0)
    grad_store = lax.dynamic_slice_in_dim(jnp.stack(grad_list), offset, micro_count, 0)
    summed_weight = lax.psum_scatter(
        jnp.einsum(
            "mtf,mta->fa", grad_store, attend_store, preferred_element_type=jnp.float32
        ).astype(jnp.bfloat16),
        "samples",
        scatter_dimension=0,
        tiled=True,
    ).astype(jnp.float32)
    region_count = seq_len // 2
    rank_in_region = jnp.cumsum(region_mask) - 1
    select = (
        (rank_in_region[None, :] == jnp.arange(region_count)[:, None]) & (region_mask[None, :] > 0)
    ).astype(jnp.bfloat16)
    tiles = jnp.einsum("at,mtd->mad", select, out_store, preferred_element_type=jnp.float32).astype(
        jnp.bfloat16
    )
    shard_index = lax.axis_index("samples")
    my_partners = lax.dynamic_slice_in_dim(
        partner_samples, shard_index * micro_count, micro_count, 0
    )
    shard_count = lax.axis_size("samples")
    dest_shard = my_partners // micro_count
    dest_slot = my_partners % micro_count
    route = (
        (dest_shard[:, None, None] == jnp.arange(shard_count)[None, :, None])
        & (dest_slot[:, None, None] == jnp.arange(micro_count)[None, None, :])
    ).astype(jnp.bfloat16)
    outgoing = jnp.einsum("mku,mad->kuad", route, tiles, preferred_element_type=jnp.float32).astype(
        jnp.bfloat16
    )
    arrived = lax.all_to_all(outgoing, "samples", split_axis=0, concat_axis=0, tiled=True)
    ones_row = jnp.ones((shard_count,), jnp.bfloat16)
    received = jnp.einsum(
        "k,kuad->uad", ones_row, arrived, preferred_element_type=jnp.float32
    ).astype(jnp.bfloat16)
    placed = jnp.einsum("at,mad->mtd", select, received, preferred_element_type=jnp.float32)
    kept = jnp.where(region_mask[None, :, None] > 0, jnp.zeros_like(out_store), out_store)
    site_cot = (kept.astype(jnp.float32) + placed).astype(jnp.bfloat16)
    cotangents = jnp.where(section_index == 0, site_cot, out_store)
    onehot = (spins[:, :, None] == jnp.arange(SPINS)[None, None, :]).astype(jnp.bfloat16)
    embed_term = jnp.einsum("mtv,mtd->vd", onehot, site_cot, preferred_element_type=jnp.float32)
    embed_term = jnp.where(section_index == 0, embed_term, jnp.zeros_like(embed_term))
    embed_grad = lax.psum(embed_term, ("samples", "section"))
    return (summed_weight[None], cotangents[None], embed_grad)


def ring_sample(place, count):
    return jnp.where(place < count // 2, 2 * place, 2 * (count - place) - 1)


def ring_place(sample, count):
    return jnp.where(lax.rem(sample, 2) == 0, sample // 2, count - 1 - sample // 2)


def ring_route(count, distance):
    order = list(range(0, count, 2)) + list(range(1, count, 2))[::-1]
    return [(order[i], order[(i - distance) % count]) for i in range(count)]


def own_place(count):
    return ring_place(lax.axis_index("samples"), count)


def peer_at(place, distance, count):
    return ring_sample(lax.rem(place + distance + count, count), count)


def partner_of(slot):
    return jnp.bitwise_xor(lax.axis_index("samples"), slot)


def sending_order(count, run=1):
    near, far, order = list(range(1, count // 2)), list(range(count // 2, count)), []
    while near or far:
        order += near[:1] + far[:run]
        near, far = near[1:], far[run:]
    return [*order, 0]


def columns(index, size):
    return pl.ds(pl.multiple_of(index * size, size), size)


def in_vmem(count):
    return [pl.BlockSpec(memory_space=pltpu.VMEM)] * count


def in_smem(count):
    return [pl.BlockSpec(memory_space=pltpu.SMEM)] * count


def on_core(body, out_shapes, in_specs, scratch=(), micros=1, vmem=16):
    return pl.pallas_call(
        body,
        out_shape=out_shapes,
        in_specs=in_specs,
        out_specs=jax.tree.map(lambda _: pl.BlockSpec(memory_space=pltpu.VMEM), out_shapes),
        scratch_shapes=list(scratch),
        compiler_params=pltpu.CompilerParams(vmem_limit_bytes=vmem << 20),
        cost_estimate=pl.CostEstimate(
            flops=int(micros * FLOPS_PER_MICRO), bytes_accessed=1 << 16, transcendentals=0
        ),
    )


def matmul(left, right):
    return jnp.dot(left, right, preferred_element_type=jnp.float32)


def matmul_t(left, right):
    return lax.dot_general(
        left, right, (((1,), (1,)), ((), ())), preferred_element_type=jnp.float32
    )


def pack_kernel(count, share_axis, x_ref, w_ref, spins_ref, *refs):
    outs, sems = refs[:-1], refs[-1]
    seq_len = x_ref.shape[2]
    skipped = seq_len + TAIL
    sent = outs[0].shape[0] - skipped
    rows = columns(lax.axis_index(share_axis), sent) if share_axis else slice(None)
    copies = []
    for slot in range(count):
        cols = columns(partner_of(slot), HEAD)
        head, weight = outs[slot].at[0:seq_len, :], outs[slot].at[skipped:, :]
        copies.append(pltpu.make_async_copy(x_ref.at[0, 0, :, cols], head, sems.at[0, slot]))
        copies.append(pltpu.make_async_copy(w_ref.at[0, rows, cols], weight, sems.at[1, slot]))
    for copy in copies:
        copy.start()
    spin_rows = jnp.broadcast_to(spins_ref[...].astype(jnp.float32), (TAIL, seq_len))
    for slot in range(count):
        outs[slot][seq_len:skipped, :] = spin_rows.astype(jnp.bfloat16)
    for copy in copies:
        copy.wait()


def collect_kernel(count, *refs):
    heads_ref, rows_ref = refs[count:]
    refs = dict(zip(sending_order(count), refs))
    sent = rows_ref.shape[1]
    for slot in range(count):
        peer = partner_of(slot)
        heads_ref[peer] = refs[slot][...]
        rows_ref[peer] = refs[slot][-sent:, :]


def forward_kernel(count, scale, *refs):
    heads_ref, shared, layout_ref = refs[0], refs[1:-6], refs[-4]
    probs_ref, turned_ref, bundle_ref = refs[-3:]
    seq_len = probs_ref.shape[1]
    lines = seq_len + TAIL
    half = lax.axis_index("mp")
    parts = count // 2
    sent = heads_ref.shape[1] - lines
    for part in range(parts):
        shard = (1 - half) * parts + part
        for piece, value in enumerate((heads_ref[shard, lines:, :], *(ref[shard] for ref in shared))):
            first = count * seq_len + (piece * parts + part) * sent
            bundle_ref[first : first + sent, :] = value
    blocks = layout_ref.shape[1]
    rows = lax.broadcasted_iota(jnp.int32, (seq_len, seq_len), 0) // BLOCK
    cols = lax.broadcasted_iota(jnp.int32, (seq_len, seq_len), 1) // BLOCK
    seen = rows == cols
    for q in range(blocks):
        for k in range(blocks):
            if q != k:
                seen = seen | ((rows == q) & (cols == k) & (layout_ref[0, q, k] > 0))
    xs = [heads_ref[slot, 0:seq_len, :] for slot in range(count)]
    scores = [jnp.where(seen, matmul_t(x, x) * scale, -jnp.inf) for x in xs]
    tops = [jnp.max(score, axis=-1, keepdims=True) for score in scores]
    terms = [jnp.exp(score - top) for score, top in zip(scores, tops)]
    sums = [jnp.sum(term, axis=-1, keepdims=True) for term in terms]
    for slot in range(count):
        probs = terms[slot] / sums[slot]
        low = probs.astype(jnp.bfloat16)
        probs_ref[slot] = probs
        attended = matmul(low, xs[slot]).astype(jnp.bfloat16)
        bundle_ref[slot * seq_len : (slot + 1) * seq_len, :] = attended
        turned_ref[slot] = transposed(low)


def lay_weights(weights, shares, share_axis):
    index = lax.axis_index(share_axis) if share_axis else 0
    pieces = len(shares) // 2
    parts = len(shares[0])
    for number, share in enumerate(shares):
        head, piece = number % 2, number // 2
        place = index if piece == 0 else 1 - index
        for part, value in enumerate(share):
            sent = value.shape[0]
            rows = pl.ds(pl.multiple_of((part * pieces + place) * sent, sent), sent)
            weights[rows, head * HEAD : (head + 1) * HEAD] = value


def weight_term(pieces, left, cols):
    total = None
    for index, first in enumerate(range(0, len(pieces), 2)):
        rows = [piece[:, cols] for slot in pieces[first : first + 2] for piece in slot]
        term = matmul(left[index], jnp.concatenate(rows, axis=0))
        total = term if total is None else total + term
    return total


def both_heads(own_ref, sibling_ref, samples, seq_len):
    rows = [
        jnp.concatenate(
            [ref[columns(sample, seq_len), :] for ref in (own_ref, sibling_ref)], axis=1
        )
        for sample in samples
    ]
    return transposed(jnp.concatenate(rows, axis=0))


def transposed(value):
    return value.astype(jnp.float32).T.astype(jnp.bfloat16)


def attention_back(scale, xs, probs, turned, grads, above):
    grad_probs = [matmul_t(grad, x) for grad, x in zip(grads, xs)]
    inner = [jnp.sum(grad * prob, axis=-1, keepdims=True) for grad, prob in zip(grad_probs, probs)]
    grad_scores = [
        (prob * (grad - total)).astype(jnp.bfloat16)
        for prob, grad, total in zip(probs, grad_probs, inner)
    ]
    both = [jnp.concatenate([grad, transposed(grad)], axis=1) for grad in grad_scores]
    results = []
    for index, x in enumerate(xs):
        through = matmul(turned[index], grads[index])
        through = through + scale * matmul(both[index], jnp.concatenate([x, x], axis=0))
        results.append((above[index].astype(jnp.float32) + through).astype(jnp.bfloat16))
    return results


def near_slots(count):
    return [slot for slot in range(count) if slot != count // 2]


def near_products_kernel(count, share_axis, *refs):
    pieces = [refs[index : index + 1] for index in range(count - 1)]
    bundle_ref, sibling_ref, heads_ref = refs[count - 1 : count + 2]
    shared = refs[count + 2 : -5]
    partial_ref, own_ref, other_ref, above_ref, weights = refs[-5:]
    place = own_place(count)
    shard = lax.axis_index("samples")
    parts, _, shard_rows = partial_ref.shape
    seq_len = pieces[0][0].shape[0]
    lines = seq_len + TAIL
    sent = heads_ref.shape[1] - lines
    half = lax.axis_index("mp")
    sample_of = [peer_at(place, slot, count) for slot in near_slots(count)]
    shares = []
    for piece, ref in enumerate((heads_ref, *shared)):
        skipped = lines if piece == 0 else 0
        shares.append([ref[half * parts + part, skipped:, :] for part in range(parts)])
        firsts = [count * seq_len + (piece * parts + part) * sent for part in range(parts)]
        shares.append([sibling_ref[first : first + sent, :] for first in firsts])
    lay_weights(weights, shares, share_axis)
    left = [
        both_heads(bundle_ref, sibling_ref, sample_of[first : first + 2], seq_len)
        for first in range(0, count - 1, 2)
    ]
    for part in range(parts):
        cols = slice(part * shard_rows, (part + 1) * shard_rows)
        partial_ref[part] = weight_term(pieces, left, cols)
    for first in range(0, count - 1, 2):
        rows = [piece[...] for slot in pieces[first : first + 2] for piece in slot]
        total = matmul(jnp.concatenate(rows, axis=0), weights[...])
        lines = slice(first * seq_len, first * seq_len + total.shape[0])
        own_ref[lines, :] = total[:, :HEAD]
        other_ref[lines, :] = total[:, HEAD:].astype(jnp.bfloat16)
    for index, slot in enumerate(pieces):
        above_ref[index * seq_len : (index + 1) * seq_len, :] = slot[0][:, columns(shard, HEAD)]


def near_back_kernel(count, scale, *refs):
    heads_ref, probs_ref, turned_ref, own_ref, other_ref, above_ref = refs[:6]
    grads_ref = refs[-1]
    place = own_place(count)
    seq_len = probs_ref.shape[1]
    sample_of = [peer_at(place, slot, count) for slot in near_slots(count)]
    lines = [slice(index * seq_len, (index + 1) * seq_len) for index in range(count - 1)]
    results = attention_back(
        scale,
        [heads_ref[sample, 0:seq_len, :] for sample in sample_of],
        [probs_ref[sample] for sample in sample_of],
        [turned_ref[sample] for sample in sample_of],
        [
            (own_ref[line, :] + other_ref[line, :].astype(jnp.float32)).astype(jnp.bfloat16)
            for line in lines
        ],
        [above_ref[line, :] for line in lines],
    )
    for index, result in enumerate(results):
        grads_ref[index] = result


def far_products_kernel(count, *refs):
    piece, refs = refs[:2], refs[2:]
    bundle_ref, sibling_ref, partial_ref, weights_ref = refs[:4]
    send_ref, keep_ref, own_ref, above_ref = refs[4:]
    sample = peer_at(own_place(count), count // 2, count)
    shard = lax.axis_index("samples")
    parts, _, shard_rows = partial_ref.shape
    left = [both_heads(bundle_ref, sibling_ref, [sample], 2 * piece[0].shape[0])]
    for part in range(parts):
        cols = slice(part * shard_rows, (part + 1) * shard_rows)
        total = transposed(partial_ref[part] + weight_term([piece], left, cols))
        keep_ref[part] = total[:, :HEAD]
        send_ref[cols, :] = total[:, HEAD:]
    total = matmul(jnp.concatenate([rows[...] for rows in piece], axis=0), weights_ref[...])
    own_ref[...] = total[:, :HEAD]
    send_ref[parts * shard_rows :, :] = total[:, HEAD:].astype(jnp.bfloat16)
    cols = columns(shard, HEAD)
    above_ref[...] = jnp.concatenate([rows[:, cols] for rows in piece], axis=0)


def far_kernel(count, scale, *refs):
    came_ref, keep_ref, own_ref, above_ref, heads_ref, probs_ref, turned_ref = refs[:7]
    near_ref, mask_ref, partner_ref = refs[7:10]
    outs, (grads, terms) = refs[10:-2], refs[-2:]
    place = own_place(count)
    half = lax.axis_index("mp")
    seq_len = probs_ref.shape[1]
    skipped = seq_len + TAIL
    parts, shard_rows = keep_ref.shape[:2]
    for part in range(parts):
        terms[half * parts + part] = keep_ref[part]
        lines = slice(part * shard_rows, (part + 1) * shard_rows)
        terms[(1 - half) * parts + part] = came_ref[lines, :]
    for index, slot in enumerate(near_slots(count)):
        grads[peer_at(place, slot, count)] = near_ref[index]
    sample = peer_at(place, count // 2, count)
    other = came_ref[parts * shard_rows :, :].astype(jnp.float32)
    (grads[sample],) = attention_back(
        scale,
        [heads_ref[sample, 0:seq_len, :]],
        [probs_ref[sample]],
        [turned_ref[sample]],
        [(own_ref[...] + other).astype(jnp.bfloat16)],
        [above_ref[...]],
    )
    region = jnp.broadcast_to(mask_ref[...].astype(jnp.float32), (HEAD, seq_len)).T > 0.5
    which = lax.broadcasted_iota(jnp.int32, (TAIL, seq_len), 0).astype(jnp.float32)
    embed = jnp.zeros((TAIL, HEAD), jnp.float32)
    for slot in range(count):
        sample = partner_of(slot)
        swapped = grads[partner_ref[sample]].astype(jnp.float32)
        site = jnp.where(region, swapped, grads[sample].astype(jnp.float32)).astype(jnp.bfloat16)
        outs[slot][0:seq_len, :] = site
        outs[slot][skipped:, :] = terms[sample]
        spin = heads_ref[sample, seq_len:skipped, :].astype(jnp.float32)
        embed = embed + matmul((spin == which).astype(jnp.bfloat16), site)
    high = embed.astype(jnp.bfloat16).astype(jnp.float32)
    low = embed - high
    tail = jnp.concatenate([high[: TAIL // 2], low[: TAIL // 2]], axis=0).astype(jnp.bfloat16)
    for slot in range(count):
        outs[slot][seq_len:skipped, :] = tail


def unpack_kernel(count, *refs):
    weight_ref, site_ref, embed_ref = refs[count:]
    refs = dict(zip(sending_order(count), refs))
    seq_len = site_ref.shape[2]
    skipped = seq_len + TAIL
    for slot in range(count):
        cols = columns(partner_of(slot), HEAD)
        weight_ref[0, :, cols] = refs[slot][skipped:, :].astype(jnp.float32)
        site_ref[0, 0, :, cols] = refs[slot][0:seq_len, :]
        tail = refs[slot][seq_len:skipped, :].astype(jnp.float32)
        embed_ref[:, cols] = (tail[: TAIL // 2] + tail[TAIL // 2 :])[:SPINS]


def spread(blocks):
    count = len(blocks)
    came = [blocks[0]]
    for slot in range(1, count):
        route = [(shard, shard ^ slot) for shard in range(count)]
        came.append(lax.ppermute(blocks[slot], "samples", route))
    return came


def head_sharded(
    stored_inputs, top_cotangent, layer_weights, block_layout, region_mask, partner_samples, spins
):
    count = lax.axis_size("samples")
    seq_len = stored_inputs.shape[2]
    shard_rows, half_width = layer_weights.shape[1:]
    scale = 4.0 / HEAD
    bf16, f32 = jnp.bfloat16, jnp.float32
    per_head = (count, seq_len, HEAD)
    lines = seq_len + TAIL
    share_axis = "groups" if lax.axis_size("groups") == 2 else None
    sent = shard_rows // 2 if share_axis else shard_rows
    parts = count // 2
    swap = [(0, 1), (1, 0)]

    up, down = ring_route(count, -1), ring_route(count, 1)
    block = top_cotangent[0]
    rows = seq_len // 2
    packed = on_core(
        functools.partial(pack_kernel, count, share_axis),
        [jax.ShapeDtypeStruct((lines + sent, HEAD), bf16)] * count,
        [pl.BlockSpec(memory_space=pltpu.HBM)] * 2 + in_vmem(1),
        [pltpu.SemaphoreType.DMA((2, count))],
        micros=1,
        vmem=60,
    )(stored_inputs, layer_weights, spins)
    arrived = spread(packed)
    heads, weight_rows = on_core(
        functools.partial(collect_kernel, count),
        [
            jax.ShapeDtypeStruct((count, lines + sent, HEAD), bf16),
            jax.ShapeDtypeStruct((count, sent, HEAD), bf16),
        ],
        in_vmem(count),
        micros=0.4,
    )(*[arrived[slot] for slot in sending_order(count)])
    slots = {0: block}
    ahead, back = block, block
    for step in range(1, count // 2):
        ahead = lax.ppermute(ahead, "samples", up)
        back = lax.ppermute(back, "samples", down)
        slots[count - step], slots[step] = ahead, back
    far = (
        lax.ppermute(ahead[:rows], "samples", up),
        lax.ppermute(back[rows:], "samples", down),
    )
    near = [slots[slot] for slot in near_slots(count)]
    small = (region_mask.reshape(1, seq_len), partner_samples)
    shared = []
    if share_axis:
        shared = [lax.ppermute(weight_rows, share_axis, swap)]
    probs, turned, bundle = on_core(
        functools.partial(forward_kernel, count, scale),
        [
            jax.ShapeDtypeStruct(per_head, f32),
            jax.ShapeDtypeStruct(per_head, bf16),
            jax.ShapeDtypeStruct((count * seq_len + half_width, HEAD), bf16),
        ],
        in_vmem(2 + len(shared)) + in_smem(2),
        micros=1.2,
    )(heads, *shared, *small, block_layout)
    sibling = lax.ppermute(bundle, "mp", swap)
    near_lines = (count - 1) * seq_len
    partial, near_own, near_other, near_above, weights = on_core(
        functools.partial(near_products_kernel, count, share_axis),
        [
            jax.ShapeDtypeStruct((parts, 2 * HEAD, shard_rows), f32),
            jax.ShapeDtypeStruct((near_lines, HEAD), f32),
            jax.ShapeDtypeStruct((near_lines, HEAD), bf16),
            jax.ShapeDtypeStruct((near_lines, HEAD), bf16),
            jax.ShapeDtypeStruct((half_width, 2 * HEAD), bf16),
        ],
        in_vmem(count + 2 + len(shared)),
        micros=1.4,
    )(*near, bundle, sibling, heads, *shared)
    near_other = lax.ppermute(near_other, "mp", swap)
    near_grads = on_core(
        functools.partial(near_back_kernel, count, scale),
        jax.ShapeDtypeStruct((count - 1, seq_len, HEAD), bf16),
        in_vmem(7) + in_smem(1),
        micros=1.8,
    )(heads, probs, turned, near_own, near_other, near_above, *small)
    far_send, far_keep, far_own, far_above = on_core(
        functools.partial(far_products_kernel, count),
        [
            jax.ShapeDtypeStruct((half_width + seq_len, HEAD), bf16),
            jax.ShapeDtypeStruct((parts, shard_rows, HEAD), bf16),
            jax.ShapeDtypeStruct((seq_len, HEAD), f32),
            jax.ShapeDtypeStruct((seq_len, HEAD), bf16),
        ],
        in_vmem(6),
        micros=0.5,
    )(*far, bundle, sibling, partial, weights)
    far_came = lax.ppermute(far_send, "mp", swap)
    terms = on_core(
        functools.partial(far_kernel, count, scale),
        [jax.ShapeDtypeStruct((lines + shard_rows, HEAD), bf16)] * count,
        in_vmem(9) + in_smem(1),
        [pltpu.VMEM(per_head, bf16), pltpu.VMEM((count, shard_rows, HEAD), bf16)],
        micros=1.2,
    )(far_came, far_keep, far_own, far_above, heads, probs, turned, near_grads, *small)
    came = spread(terms)
    return on_core(
        functools.partial(unpack_kernel, count),
        [
            jax.ShapeDtypeStruct((1, shard_rows, half_width), f32),
            jax.ShapeDtypeStruct((1, 1, seq_len, half_width), bf16),
            jax.ShapeDtypeStruct((SPINS, half_width), f32),
        ],
        in_vmem(count),
        micros=1.2,
    )(*[came[slot] for slot in sending_order(count)])


def solution(mesh):
    in_specs = (
        P("section", ("groups", "samples"), None, "mp"),
        P(("groups", "samples"), None, "mp"),
        P("section", "samples", "mp"),
        P("section", None, None),
        P(),
        P("groups"),
        P(("groups", "samples"), None),
    )
    out_specs = (
        P(("groups", "section"), "samples", "mp"),
        P("section", ("groups", "samples"), None, "mp"),
        P("groups", "mp"),
    )
    shards = mesh.shape["samples"]

    def whole(stored_inputs, top_cotangent, *rest):
        samples, _, width = top_cotangent.shape
        layer_count = stored_inputs.shape[0]
        one_each = samples == mesh.shape["groups"] * shards and layer_count == 1
        by_heads = one_each and shards > 1 and shards & (shards - 1) == 0 and width == mesh.shape["mp"] * shards * HEAD
        return jax.shard_map(
            head_sharded if by_heads else local,
            mesh=mesh,
            in_specs=in_specs,
            out_specs=out_specs,
            check_vma=False,
        )(stored_inputs, top_cotangent, *rest)

    return whole
```
